32 devices in a mesh: dp: 8 (over y, x, core), mp: 4 (over z).
Axes of the slice: x: 2, y: 2, z: 4, core: 2. Of those that a mesh axis runs over, the one named last changes fastest.
Arguments:
- tokens: bfloat16 [16384, 2048], P('dp'), may hold values from -6 to 6
- cotangent: bfloat16 [16384, 2048], P('dp'), may hold values from -6 to 6
- seq_len: int32 [32], replicated, may hold values from 0 to 2048, as said below
- seq_device: int32 [32], replicated, may hold values from 0 to 7, as said below
- owner_map: int32 [192], replicated, may hold values from 0 to 191, as said below
- weight_blocks: float32 [4, 192, 256, 256], P('mp', 'dp')
- left_stat: float32 [4, 192, 256, 256], P('mp', 'dp'), as said below
- right_stat: float32 [4, 192, 256, 256], P('mp', 'dp'), as said below
- left_root: float32 [4, 192, 256, 256], P('mp', 'dp'), as said below
- right_root: float32 [4, 192, 256, 256], P('mp', 'dp'), as said below
- vectors: float32 [6, 2048], replicated
- vector_stat: float32 [6, 2048], replicated, as said below
- unit_bias: float32 [4, 3584], P('mp'), may hold values from -1.5 to 1.5
- unit_stat: float32 [4, 3584], P('mp'), as said below
Outputs:
- block_out: bfloat16 [16384, 2048], P('dp')
- input_grad: bfloat16 [16384, 2048], P('dp')
- block_grad: float32 [4, 192, 256, 256], P('mp', 'dp')
- left_new: float32 [4, 192, 256, 256], P('mp', 'dp')
- right_new: float32 [4, 192, 256, 256], P('mp', 'dp')
- weight_new: float32 [4, 192, 256, 256], P('mp', 'dp')
- vector_grad: float32 [6, 2048], replicated
- vector_stat_new: float32 [6, 2048], replicated
- vector_new: float32 [6, 2048], replicated
- unit_grad: float32 [4, 3584], P('mp')
- unit_stat_new: float32 [4, 3584], P('mp')
- unit_new: float32 [4, 3584], P('mp')
The draws below stay inside these ranges and needn't reach their ends.
Inputs may be any that keep to these rules, and one draw needn't show every extreme that they name: `seq_len`: the lengths of the sequences of one dp index sum to 2048 or less; one index holds a single sequence of exactly 2048. `seq_device`: each dp index is named by exactly 4 sequences. `owner_map`: a permutation; slot s lies on dp index s // 24. `left_stat`: symmetric. `right_stat`: symmetric. `left_root`: symmetric. `right_root`: symmetric. `vector_stat`: every entry is positive. `unit_stat`: every entry is positive.
All inputs are finite; a program needn't handle non-finite values.
Results may differ from the reference program's by a relative error of at most 0.012.
Values may be sent and summed in bfloat16 or wider, within the bound.
A program may use at most 384 MiB of HBM per device.

```python
import math
import jax
import jax.numpy as jnp
from jax import lax

D = 2048
HEADS = 8
HD = 256
ROT = 64
FF = 8192
TOK_DEV = 2048
SLOTS = 4
B = 256
TOKENS = 16384
QKV_DEV = 1536
D_DEV = 512
FF_DEV = 2048
UB_DEV = 3584
BLOCKS = 192
N_DP = 8
N_MP = 4


grad_share = [0.5, 0.1, 0.3, 0.65]


weight_spread = [1.0, 8.0, 1.0, 1.0]


def sequence_layout(key):
    key = jax.random.fold_in(key, 101)
    keys = jax.random.split(key, 5)
    devices = jnp.arange(N_DP, dtype=jnp.int32)
    full_device = jax.random.randint(keys[0], (), 0, N_DP)
    totals = jax.random.randint(keys[1], (N_DP,), TOK_DEV // 2, TOK_DEV + 1)
    counts = jax.random.randint(keys[2], (N_DP,), 1, SLOTS + 1)
    totals = jnp.where(devices == full_device, TOK_DEV, totals).astype(jnp.int32)
    counts = jnp.where(devices == full_device, 1, counts)
    cut_points = jax.random.randint(keys[3], (N_DP, SLOTS - 1), 1, totals[:, None])
    in_use = jnp.arange(SLOTS - 1)[None, :] < counts[:, None] - 1
    cut_points = jnp.sort(jnp.where(in_use, cut_points, totals[:, None]), axis=1).astype(jnp.int32)
    bounds = jnp.concatenate([jnp.zeros((N_DP, 1), jnp.int32), cut_points, totals[:, None]], axis=1)
    lengths = (bounds[:, 1:] - bounds[:, :-1]).reshape(-1)
    shuffle = jax.random.permutation(keys[4], N_DP * SLOTS)
    seq_len = jnp.zeros((N_DP * SLOTS,), jnp.int32).at[shuffle].set(lengths)
    owner_of = jnp.zeros((N_DP * SLOTS,), jnp.int32).at[shuffle].set(jnp.repeat(devices, SLOTS))
    return (seq_len, owner_of)


def block_owner(key):
    return jax.random.permutation(jax.random.fold_in(key, 202), BLOCKS).astype(jnp.int32)


def block_type(key):
    source = jnp.argsort(block_owner(key))
    qkv_end = D // B * (QKV_DEV // B)
    out_end = qkv_end + D_DEV // B * (D // B)
    up_end = out_end + D // B * (FF_DEV // B)
    return (source >= qkv_end).astype(jnp.int32) + (source >= out_end).astype(jnp.int32) + (source >= up_end).astype(jnp.int32)


def shaped_matrix(diagonal, jitter, scale_level):
    identity = (jnp.arange(B)[:, None] == jnp.arange(B)[None, :]).astype(jnp.float32)
    off_part = (jitter + jnp.swapaxes(jitter, -1, -2)) * (0.5 / math.sqrt(2.0 * B))
    return scale_level[None, :, None, None] * (identity * diagonal + (1.0 - identity) * off_part)


def draw_seq_len(key, part):
    return sequence_layout(key)[0]


def draw_seq_device(key, part):
    return sequence_layout(key)[1]


def draw_owner_map(key, part):
    return block_owner(key)


def draw_weight_blocks(key, part):
    kinds = block_type(key)
    key = jax.random.fold_in(key, 3)
    spreads = jnp.array(weight_spread, jnp.float32) * jnp.array([D ** (-0.5), D ** (-0.5), D ** (-0.5), FF ** (-0.5)], jnp.float32)
    base = jax.random.normal(key, (N_MP, BLOCKS, B, B))
    return base * spreads[kinds][None, :, None, None]


def stat_matrix(key, scale_level, low_end, high_end):
    first_key, second_key = jax.random.split(key)
    diagonal = jax.random.uniform(first_key, (N_MP, BLOCKS, 1, B), minval=low_end, maxval=high_end)
    jitter = jax.random.normal(second_key, (N_MP, BLOCKS, B, B))
    return shaped_matrix(diagonal, jitter, scale_level)


def draw_left_stat(key, part):
    kinds = block_type(key)
    key = jax.random.fold_in(key, 5)
    scale_level = B * TOKENS * jnp.array(grad_share, jnp.float32)[kinds] ** 2
    return stat_matrix(key, scale_level, 1.0, 4.0)


def draw_right_stat(key, part):
    kinds = block_type(key)
    key = jax.random.fold_in(key, 6)
    scale_level = B * TOKENS * jnp.array(grad_share, jnp.float32)[kinds] ** 2
    return stat_matrix(key, scale_level, 1.0, 4.0)


def draw_left_root(key, part):
    kinds = block_type(key)
    key = jax.random.fold_in(key, 7)
    scale_level = (B * TOKENS * jnp.array(grad_share, jnp.float32)[kinds] ** 2) ** (-0.25)
    return stat_matrix(key, scale_level, 0.5, 2.0)


def draw_right_root(key, part):
    kinds = block_type(key)
    key = jax.random.fold_in(key, 8)
    scale_level = (B * TOKENS * jnp.array(grad_share, jnp.float32)[kinds] ** 2) ** (-0.25)
    return stat_matrix(key, scale_level, 0.5, 2.0)


def draw_vectors(key, part):
    key = jax.random.fold_in(key, 9)
    jitter = jax.random.normal(key, (6, D))
    centre = jnp.array([1.0, 0.0, 1.0, 0.0, 0.0, 0.0], jnp.float32)[:, None]
    spread = jnp.array([0.15, 0.1, 0.15, 0.1, 0.1, 0.1], jnp.float32)[:, None]
    return centre + spread * jitter


def draw_vector_stat(key, part):
    key = jax.random.fold_in(key, 10)
    factor = jax.random.uniform(key, (6, D), minval=1.0, maxval=4.0)
    scale_level = TOKENS * jnp.array([1.0, 1.0, 0.36, 0.36, 1.0, 1.0], jnp.float32)[:, None]
    return scale_level * factor


def draw_unit_stat(key, part):
    key = jax.random.fold_in(key, 11)
    factor = jax.random.uniform(key, (N_MP, UB_DEV), minval=1.0, maxval=4.0)
    scale_level = TOKENS * jnp.where(jnp.arange(UB_DEV) < QKV_DEV, 0.25, 0.09)
    return scale_level[None, :] * factor


def levels(stream_key, dims, shards, least, largest):
    def one(dim, blocks):
        heights = jax.random.uniform(jax.random.fold_in(jax.random.fold_in(stream_key, 6), dim), (blocks,), jnp.float32, least / len(shards), largest / len(shards))
        return jnp.repeat(jnp.exp(heights), dims[dim] // blocks).reshape((-1,) + (1,) * (len(dims) - dim - 1))

    level = one(*shards[0])
    for cut in shards[1:]:
        level = level * one(*cut)
    return level


def bell_draw(stream_key, dims, scale, most, pieces=(), kind=jnp.bfloat16):
    values = scale * jax.random.normal(stream_key, dims, jnp.float32)
    if pieces:
        values = values * levels(stream_key, dims, pieces, -0.22, 0.18)
    return jnp.clip(values, -most, most).astype(kind)


def setup_inputs(seed: int = 0) -> dict:
    arg_keys = jax.random.split(jax.random.key(seed), 15)
    return {
        "tokens": bell_draw(arg_keys[0], (TOKENS, D), 1.0, 6.0, ((0, 8),)),
        "cotangent": bell_draw(arg_keys[1], (TOKENS, D), 1.0, 6.0, ((0, 8),)),
        "seq_len": draw_seq_len(jax.random.fold_in(arg_keys[14], 71), 0),
        "seq_device": draw_seq_device(jax.random.fold_in(arg_keys[14], 71), 0),
        "owner_map": draw_owner_map(jax.random.fold_in(arg_keys[14], 71), 0),
        "weight_blocks": draw_weight_blocks(jax.random.fold_in(arg_keys[14], 71), 0),
        "left_stat": draw_left_stat(jax.random.fold_in(arg_keys[14], 71), 0),
        "right_stat": draw_right_stat(jax.random.fold_in(arg_keys[14], 71), 0),
        "left_root": draw_left_root(jax.random.fold_in(arg_keys[14], 71), 0),
        "right_root": draw_right_root(jax.random.fold_in(arg_keys[14], 71), 0),
        "vectors": draw_vectors(jax.random.fold_in(arg_keys[14], 71), 0),
        "vector_stat": draw_vector_stat(jax.random.fold_in(arg_keys[14], 71), 0),
        "unit_bias": bell_draw(arg_keys[12], (N_MP, UB_DEV), 0.1, 1.5, ((0, 4),), jnp.float32),
        "unit_stat": draw_unit_stat(jax.random.fold_in(arg_keys[14], 71), 0),
    }


highest = lax.Precision.HIGHEST
norm_eps = 1e-05
step_share = 0.5
vector_rate = 0.15
masked_score = -1e+30

@jax.custom_vjp
def low(v):
    return lax.optimization_barrier(v.astype(jnp.bfloat16)).astype(jnp.float32)

@jax.custom_vjp
def low_back(v):
    return v

def low_keep(v):
    return (low(v), None)

def low_pass(kept, grad):
    return (grad,)

def back_keep(v):
    return (v, None)

def back_low(kept, grad):
    return (low(grad),)
low.defvjp(low_keep, low_pass)
low_back.defvjp(back_keep, back_low)

def layer_norm(values, gain, shift):
    center = values - lax.optimization_barrier(jnp.mean(values, axis=-1, keepdims=True))
    spread = lax.optimization_barrier(jnp.mean(center * center, axis=-1, keepdims=True))
    return center * lax.rsqrt(spread + norm_eps) * gain + shift

def segment_layout(seq_len, seq_device, device, row_count):
    is_mine = seq_device == device
    lengths = jnp.where(is_mine, seq_len, 0).astype(jnp.int32)
    seq_ends = jnp.cumsum(lengths).astype(jnp.int32)
    row_index = jnp.arange(row_count, dtype=jnp.int32)
    passed = is_mine[None, :] & (seq_ends[None, :] <= row_index[:, None])
    segment = lax.optimization_barrier(jnp.sum(passed.astype(jnp.int32), axis=1)).astype(jnp.int32)
    seq_start = lax.optimization_barrier(jnp.max(jnp.where(passed, seq_ends[None, :], 0), axis=1)).astype(jnp.int32)
    return (segment, row_index - seq_start)

def rotary_tables(position):
    half_rot = ROT // 2
    frequency = 10000.0 ** (-2.0 * jnp.arange(half_rot, dtype=jnp.float32) / ROT)
    angles = position.astype(jnp.float32)[:, None] * frequency[None, :]
    cosine_table = jnp.concatenate([jnp.cos(angles), jnp.cos(angles)], axis=1)
    sine_table = jnp.concatenate([jnp.sin(angles), jnp.sin(angles)], axis=1)
    return (cosine_table, sine_table)

def rotate(values, cosine_table, sine_table):
    rot_dims = cosine_table.shape[1]
    half_rot = rot_dims // 2
    leading = values[..., :rot_dims]
    turned = jnp.concatenate([-leading[..., half_rot:], leading[..., :half_rot]], axis=-1)
    rotated = leading * cosine_table[:, None, :] + turned * sine_table[:, None, :]
    return jnp.concatenate([rotated, values[..., rot_dims:]], axis=-1)

def blocks_to_matrix(blocks, across):
    down_count = blocks.shape[0] // across
    return blocks.reshape(down_count, across, B, B).transpose(0, 2, 1, 3).reshape(down_count * B, across * B)

def matrix_to_blocks(matrix):
    down_count = matrix.shape[0] // B
    across = matrix.shape[1] // B
    return matrix.reshape(down_count, B, across, B).transpose(0, 2, 1, 3).reshape(down_count * across, B, B)

def split_blocks(blocks, qkv_cols, head_cols, unit_cols):
    qkv_end = D // B * (qkv_cols // B)
    out_end = qkv_end + head_cols // B * (D // B)
    up_end = out_end + D // B * (unit_cols // B)
    qkv_w = blocks_to_matrix(blocks[:qkv_end], qkv_cols // B)
    out_w = blocks_to_matrix(blocks[qkv_end:out_end], D // B)
    up_w = blocks_to_matrix(blocks[out_end:up_end], unit_cols // B)
    down_w = blocks_to_matrix(blocks[up_end:], D // B)
    return (qkv_w, out_w, up_w, down_w)

def apply_step(weight, direction):
    weight_size = jnp.sqrt(lax.optimization_barrier(jnp.mean(weight * weight, axis=(-2, -1), keepdims=True)))
    step_size = jnp.sqrt(lax.optimization_barrier(jnp.mean(direction * direction, axis=(-2, -1), keepdims=True)) + 1e-06)
    return weight - step_share * weight_size * direction / step_size

def vector_update(values, old_stat, gradient):
    new_stat = 0.5 * old_stat + 0.5 * gradient * gradient
    return (new_stat, values - vector_rate * gradient * lax.rsqrt(new_stat))

def attention(queries, keys_low, values_low, segment):
    row_count = queries.shape[0]
    block_rows = min(512, row_count)
    block_count = row_count // block_rows
    column = jnp.arange(row_count, dtype=jnp.int32)
    score_scale = 1.0 / math.sqrt(HD)

    def one_block(inputs):
        block_query, block_segment, block_row = inputs
        scores = low_back(jnp.einsum('qhd,khd->hqk', block_query, keys_low, precision=highest) * score_scale)
        allowed = (block_segment[:, None] == segment[None, :]) & (column[None, :] <= block_row[:, None])
        scores = jnp.where(allowed[None], scores, masked_score)
        log_total = jax.nn.logsumexp(scores, axis=-1, keepdims=True)
        weights = low(jnp.exp(scores - log_total))
        return jnp.einsum('hqk,khd->qhd', weights, values_low, precision=highest)
    outputs = lax.map(jax.checkpoint(one_block), (queries.reshape(block_count, block_rows, HEADS, HD), segment.reshape(block_count, block_rows), column.reshape(block_count, block_rows)))
    return outputs.reshape(row_count, HEADS, HD)

def forward(inputs, qkv_w, out_w, up_w, down_w, unit_shift, vectors, segment, cosine_table, sine_table):
    row_count = inputs.shape[0]
    normed_one = low(layer_norm(inputs, vectors[0], vectors[1]))
    normed_two = low(layer_norm(inputs, vectors[2], vectors[3]))
    qkv_proj = jnp.einsum('td,gde->tge', normed_one, qkv_w, precision=highest) + unit_shift[None, :, :QKV_DEV]
    qkv_proj = low_back(qkv_proj).reshape(row_count, HEADS, 3, HD)
    turned = rotate(qkv_proj[:, :, :2].reshape(row_count, 2 * HEADS, HD), cosine_table, sine_table)
    turned = turned.reshape(row_count, HEADS, 2, HD)
    queries = low(turned[:, :, 0])
    keys_low = low(turned[:, :, 1])
    values_low = low(qkv_proj[:, :, 2])
    context = attention(queries, keys_low, values_low, segment).reshape(row_count, N_MP, D_DEV)
    context = low(low_back(context))
    hidden = low_back(jnp.einsum('td,gdf->tgf', normed_two, up_w, precision=highest) + unit_shift[None, :, QKV_DEV:])
    active = low(jax.nn.gelu(hidden, approximate=False))
    partial_out = jnp.einsum('tgi,gid->tgd', context, out_w, precision=highest) + jnp.einsum('tgf,gfd->tgd', active, down_w, precision=highest)
    return inputs + lax.optimization_barrier(jnp.sum(low(partial_out), axis=1)) + vectors[4] + vectors[5]

def reference(tokens, cotangent, seq_len, seq_device, owner_map, weight_blocks, left_stat, right_stat, left_root, right_root, vectors, vector_stat, unit_bias, unit_stat):
    canonical = low(weight_blocks[:, owner_map])
    qkv_w, out_w, up_w, down_w = jax.vmap(lambda blocks: split_blocks(blocks, QKV_DEV, D_DEV, FF_DEV))(canonical)
    parameters = (qkv_w, out_w, up_w, down_w, unit_bias, vectors)

    def device_step(totals, inputs):
        block_tokens, block_cot, device = inputs
        segment, position = segment_layout(seq_len, seq_device, device, TOK_DEV)
        cosine_table, sine_table = rotary_tables(position)

        def local_pass(values, qkv_m, out_m, up_m, down_m, unit_m, vector_m):
            return forward(values, qkv_m, out_m, up_m, down_m, unit_m, vector_m, segment, cosine_table, sine_table)
        result, pull_back = jax.vjp(local_pass, block_tokens.astype(jnp.float32), qkv_w, out_w, up_w, down_w, unit_bias, vectors)
        gradients = pull_back(block_cot.astype(jnp.float32))
        totals = jax.tree.map(lambda left_part, right_part: left_part + right_part, totals, tuple(gradients[1:]))
        return (totals, (result.astype(jnp.bfloat16), gradients[0].astype(jnp.bfloat16)))
    zero_totals = jax.tree.map(jnp.zeros_like, parameters)
    totals, outputs = lax.scan(device_step, zero_totals, (tokens.reshape(N_DP, TOK_DEV, D), cotangent.reshape(N_DP, TOK_DEV, D), jnp.arange(N_DP, dtype=jnp.int32)))
    block_out = outputs[0].reshape(TOKENS, D)
    input_grad = outputs[1].reshape(TOKENS, D)
    qkv_g, out_g, up_g, down_g, unit_grad, vector_grad = totals
    canonical_grad = jnp.concatenate([jax.vmap(matrix_to_blocks)(matrix) for matrix in (qkv_g, out_g, up_g, down_g)], axis=1)
    block_grad = jnp.zeros_like(canonical_grad).at[:, owner_map].set(canonical_grad)
    left_new = 0.5 * left_stat + 0.5 * jnp.einsum('gnij,gnkj->gnik', block_grad, block_grad, precision=highest)
    right_new = 0.5 * right_stat + 0.5 * jnp.einsum('gnji,gnjk->gnik', block_grad, block_grad, precision=highest)
    direction = jnp.einsum('gnij,gnjk->gnik', left_root, block_grad, precision=highest)
    direction = jnp.einsum('gnij,gnjk->gnik', direction, right_root, precision=highest)
    weight_new = apply_step(weight_blocks, direction)
    vector_stat_new, vector_new = vector_update(vectors, vector_stat, vector_grad)
    unit_stat_new, unit_new = vector_update(unit_bias, unit_stat, unit_grad)
    return (block_out, input_grad, block_grad, left_new, right_new, weight_new, vector_grad, vector_stat_new, vector_new, unit_grad, unit_stat_new, unit_new)
```

```python
import functools
import math

import jax
import jax.numpy as jnp
from jax import lax
from jax.experimental import pallas as pl
from jax.experimental.pallas import tpu as pltpu
from jax.sharding import PartitionSpec as P

D = 2048
HEADS = 8
HD = 256
ROT = 64
FF = 8192
B = 256


highest = lax.Precision.HIGHEST
norm_eps = 1e-05
step_share = 0.5
vector_rate = 0.15
masked_score = -1e30


def layer_norm(values, gain, shift):
    center = values - jnp.mean(values, axis=-1, keepdims=True)
    spread = jnp.mean(center * center, axis=-1, keepdims=True)
    return center * lax.rsqrt(spread + norm_eps) * gain + shift


def gelu_exact(values):
    return jax.nn.gelu(values, approximate=False)


def segment_layout(seq_len, seq_device, device, row_count):
    is_mine = seq_device == device
    lengths = jnp.where(is_mine, seq_len, 0)
    seq_ends = jnp.cumsum(lengths)
    row_index = jnp.arange(row_count, dtype=jnp.int32)
    passed = is_mine[None, :] & (seq_ends[None, :] <= row_index[:, None])
    segment = jnp.sum(passed.astype(jnp.int32), axis=1)
    seq_start = jnp.max(jnp.where(passed, seq_ends[None, :], 0), axis=1)
    return (segment, row_index - seq_start)


def rotary_tables(position):
    half_rot = ROT // 2
    frequency = 10000.0 ** (-2.0 * jnp.arange(half_rot, dtype=jnp.float32) / ROT)
    angles = position.astype(jnp.float32)[:, None] * frequency[None, :]
    cosine_table = jnp.concatenate([jnp.cos(angles), jnp.cos(angles)], axis=1)
    sine_table = jnp.concatenate([jnp.sin(angles), jnp.sin(angles)], axis=1)
    return (cosine_table, sine_table)


def rotate(values, cosine_table, sine_table):
    rot_dims = cosine_table.shape[1]
    half_rot = rot_dims // 2
    leading = values[..., :rot_dims]
    turned = jnp.concatenate([-leading[..., half_rot:], leading[..., :half_rot]], axis=-1)
    rotated = leading * cosine_table[:, None, :] + turned * sine_table[:, None, :]
    return jnp.concatenate([rotated, values[..., rot_dims:]], axis=-1)


def blocks_to_matrix(blocks, across):
    down_count = blocks.shape[0] // across
    return (
        blocks.reshape(down_count, across, B, B)
        .transpose(0, 2, 1, 3)
        .reshape(down_count * B, across * B)
    )


def matrix_to_blocks(matrix):
    down_count = matrix.shape[0] // B
    across = matrix.shape[1] // B
    return (
        matrix.reshape(down_count, B, across, B)
        .transpose(0, 2, 1, 3)
        .reshape(down_count * across, B, B)
    )


def split_blocks(blocks, qkv_cols, head_cols, unit_cols):
    qkv_end = D // B * (qkv_cols // B)
    out_end = qkv_end + head_cols // B * (D // B)
    up_end = out_end + D // B * (unit_cols // B)
    qkv_w = blocks_to_matrix(blocks[:qkv_end], qkv_cols // B)
    out_w = blocks_to_matrix(blocks[qkv_end:out_end], D // B)
    up_w = blocks_to_matrix(blocks[out_end:up_end], unit_cols // B)
    down_w = blocks_to_matrix(blocks[up_end:], D // B)
    return (qkv_w, out_w, up_w, down_w)


def apply_step(weight, direction):
    weight_size = jnp.sqrt(jnp.mean(weight * weight, axis=(-2, -1), keepdims=True))
    step_size = jnp.sqrt(jnp.mean(direction * direction, axis=(-2, -1), keepdims=True) + 1e-06)
    return weight - step_share * weight_size * direction / step_size


def vector_update(values, old_stat, gradient):
    new_stat = 0.5 * old_stat + 0.5 * gradient * gradient
    return (new_stat, values - vector_rate * gradient * lax.rsqrt(new_stat))


def block_mask(block_segment, block_row, segment, column):
    return (block_segment[:, None] == segment[None, :]) & (column[None, :] <= block_row[:, None])


def attention_forward(queries, keys_low, values_low, segment):
    row_count, head_count, head_dim = queries.shape
    block_rows = min(512, row_count)
    block_count = row_count // block_rows
    score_scale = 1.0 / math.sqrt(head_dim)
    column = jnp.arange(row_count, dtype=jnp.int32)

    def one_block(inputs):
        block_query, block_segment, block_row = inputs
        scores = (
            jnp.einsum("qhd,khd->hqk", block_query, keys_low, preferred_element_type=jnp.float32)
            * score_scale
        )
        scores = jnp.where(
            block_mask(block_segment, block_row, segment, column)[None], scores, masked_score
        )
        log_total = jax.nn.logsumexp(scores, axis=-1)
        weights = jnp.exp(scores - log_total[:, :, None]).astype(jnp.bfloat16)
        context = jnp.einsum(
            "hqk,khd->qhd", weights, values_low, preferred_element_type=jnp.float32
        )
        return (context, log_total)

    contexts, log_totals = lax.map(
        one_block,
        (
            queries.reshape(block_count, block_rows, head_count, head_dim),
            segment.reshape(block_count, block_rows),
            column.reshape(block_count, block_rows),
        ),
    )
    return (contexts.reshape(row_count, head_count, head_dim), log_totals)


def attention_backward(queries, keys_low, values_low, context_grad, log_totals, segment):
    row_count, head_count, head_dim = queries.shape
    block_rows = min(512, row_count)
    block_count = row_count // block_rows
    score_scale = 1.0 / math.sqrt(head_dim)
    column = jnp.arange(row_count, dtype=jnp.int32)

    def one_block(totals, inputs):
        key_grad, value_grad = totals
        block_query, block_grad, block_total, block_segment, block_row = inputs
        scores = (
            jnp.einsum("qhd,khd->hqk", block_query, keys_low, preferred_element_type=jnp.float32)
            * score_scale
        )
        scores = jnp.where(
            block_mask(block_segment, block_row, segment, column)[None], scores, masked_score
        )
        probs = jnp.exp(scores - block_total[:, :, None])
        weights = probs.astype(jnp.bfloat16)
        prob_grad = jnp.einsum(
            "qhd,khd->hqk", block_grad, values_low, preferred_element_type=jnp.float32
        )
        delta = jnp.sum(probs * prob_grad, axis=-1, keepdims=True)
        score_grad = (probs * (prob_grad - delta)).astype(jnp.bfloat16)
        query_grad = (
            jnp.einsum("hqk,khd->qhd", score_grad, keys_low, preferred_element_type=jnp.float32)
            * score_scale
        )
        key_grad = (
            key_grad
            + jnp.einsum(
                "hqk,qhd->khd", score_grad, block_query, preferred_element_type=jnp.float32
            )
            * score_scale
        )
        value_grad = value_grad + jnp.einsum(
            "hqk,qhd->khd", weights, block_grad, preferred_element_type=jnp.float32
        )
        return ((key_grad, value_grad), query_grad)

    zeros_start = jnp.zeros((row_count, head_count, head_dim), jnp.float32)
    (key_grad, value_grad), query_grad = lax.scan(
        one_block,
        (zeros_start, zeros_start),
        (
            queries.reshape(block_count, block_rows, head_count, head_dim),
            context_grad.reshape(block_count, block_rows, head_count, head_dim),
            log_totals,
            segment.reshape(block_count, block_rows),
            column.reshape(block_count, block_rows),
        ),
    )
    return (query_grad.reshape(row_count, head_count, head_dim), key_grad, value_grad)


def per_device(
    tokens,
    cotangent,
    seq_len,
    seq_device,
    owner_map,
    weight_blocks,
    left_stat,
    right_stat,
    left_root,
    right_root,
    vectors,
    vector_stat,
    unit_bias,
    unit_stat,
):
    groups = lax.axis_size("mp")
    device = lax.axis_index("dp")
    row_count = tokens.shape[0]
    heads_here = HEADS // groups
    qkv_cols = 3 * D // groups
    head_cols = D // groups
    unit_cols = FF // groups
    slot_count = weight_blocks.shape[1]
    sent_blocks = weight_blocks[0].astype(jnp.bfloat16)
    gathered = lax.all_gather(sent_blocks, "dp", axis=0, tiled=True)
    qkv_w, out_w, up_w, down_w = split_blocks(gathered[owner_map], qkv_cols, head_cols, unit_cols)
    segment, position = segment_layout(seq_len, seq_device, device, row_count)
    cosine_table, sine_table = rotary_tables(position)
    unit_shift = unit_bias[0]
    inputs = tokens.astype(jnp.float32)
    normed_one = layer_norm(inputs, vectors[0], vectors[1]).astype(jnp.bfloat16)
    normed_two = layer_norm(inputs, vectors[2], vectors[3]).astype(jnp.bfloat16)
    qkv_proj = (
        jnp.dot(normed_one, qkv_w, preferred_element_type=jnp.float32) + unit_shift[:qkv_cols]
    )
    qkv_proj = qkv_proj.reshape(row_count, heads_here, 3, HD)

    def turn_pair(values):
        return rotate(values.reshape(row_count, 2 * heads_here, HD), cosine_table, sine_table)

    turned, turn_back = jax.vjp(turn_pair, qkv_proj[:, :, :2])
    turned = turned.reshape(row_count, heads_here, 2, HD).astype(jnp.bfloat16)
    queries = turned[:, :, 0]
    keys_low = turned[:, :, 1]
    values_low = qkv_proj[:, :, 2].astype(jnp.bfloat16)
    context, log_totals = attention_forward(queries, keys_low, values_low, segment)
    context_low = context.reshape(row_count, head_cols).astype(jnp.bfloat16)
    hidden = jnp.dot(normed_two, up_w, preferred_element_type=jnp.float32) + unit_shift[qkv_cols:]
    active, gelu_back = jax.vjp(gelu_exact, hidden)
    active_low = active.astype(jnp.bfloat16)
    partial_out = jnp.dot(context_low, out_w, preferred_element_type=jnp.float32) + jnp.dot(
        active_low, down_w, preferred_element_type=jnp.float32
    )
    branch = lax.psum(partial_out.astype(jnp.bfloat16), "mp").astype(jnp.float32)
    block_out = (inputs + branch + (vectors[4] + vectors[5])).astype(jnp.bfloat16)
    grad_full = cotangent.astype(jnp.float32)
    act_grad = jnp.einsum("td,fd->tf", cotangent, down_w, preferred_element_type=jnp.float32)
    hidden_grad = gelu_back(act_grad)[0].astype(jnp.bfloat16)
    context_grad = jnp.einsum(
        "td,id->ti", cotangent, out_w, preferred_element_type=jnp.float32
    ).astype(jnp.bfloat16)
    query_grad, key_grad, value_grad = attention_backward(
        queries,
        keys_low,
        values_low,
        context_grad.reshape(row_count, heads_here, HD),
        log_totals,
        segment,
    )
    pair_grad = turn_back(
        jnp.stack([query_grad, key_grad], axis=2).reshape(row_count, 2 * heads_here, HD)
    )[0]
    qkv_grad = (
        jnp.concatenate([pair_grad, value_grad[:, :, None]], axis=2)
        .reshape(row_count, qkv_cols)
        .astype(jnp.bfloat16)
    )
    one_grad = jnp.einsum("te,de->td", qkv_grad, qkv_w, preferred_element_type=jnp.float32)
    two_grad = jnp.einsum("tf,df->td", hidden_grad, up_w, preferred_element_type=jnp.float32)
    norm_back_one = jax.vjp(layer_norm, inputs, vectors[0], vectors[1])[1]
    norm_back_two = jax.vjp(layer_norm, inputs, vectors[2], vectors[3])[1]
    input_one, gain_one, shift_one = norm_back_one(one_grad)
    input_two, gain_two, shift_two = norm_back_two(two_grad)
    input_part = input_one + input_two
    norm_part = jnp.stack([gain_one, shift_one, gain_two, shift_two])
    input_sum, norm_sum = lax.psum((input_part, norm_part), "mp")
    input_grad = (grad_full + input_sum).astype(jnp.bfloat16)
    qkv_w_grad = jnp.einsum("td,te->de", normed_one, qkv_grad, preferred_element_type=jnp.float32)
    out_w_grad = jnp.einsum("ti,td->id", context_low, cotangent, preferred_element_type=jnp.float32)
    up_w_grad = jnp.einsum("td,tf->df", normed_two, hidden_grad, preferred_element_type=jnp.float32)
    down_w_grad = jnp.einsum("tf,td->fd", active_low, cotangent, preferred_element_type=jnp.float32)
    canonical_grad = jnp.concatenate(
        [matrix_to_blocks(matrix) for matrix in (qkv_w_grad, out_w_grad, up_w_grad, down_w_grad)],
        axis=0,
    )
    slot_grads = canonical_grad[jnp.argsort(owner_map)]
    out_sum = jnp.sum(grad_full, axis=0)
    vector_part = jnp.concatenate([norm_sum, jnp.stack([out_sum, out_sum])], axis=0)
    unit_part = jnp.concatenate(
        [
            jnp.sum(qkv_grad.astype(jnp.float32), axis=0),
            jnp.sum(hidden_grad.astype(jnp.float32), axis=0),
        ]
    )
    summed, vector_grad, unit_grad = lax.psum((slot_grads, vector_part, unit_part), "dp")
    owned = lax.dynamic_slice_in_dim(summed, device * slot_count, slot_count, 0)
    left_new = 0.5 * left_stat[0] + 0.5 * jnp.einsum(
        "nij,nkj->nik", owned, owned, precision=highest
    )
    right_new = 0.5 * right_stat[0] + 0.5 * jnp.einsum(
        "nji,njk->nik", owned, owned, precision=highest
    )
    direction = jnp.einsum("nij,njk->nik", left_root[0], owned, precision=highest)
    direction = jnp.einsum("nij,njk->nik", direction, right_root[0], precision=highest)
    weight_new = apply_step(weight_blocks[0], direction)
    vector_stat_new, vector_new = vector_update(vectors, vector_stat, vector_grad)
    unit_stat_new, unit_new = vector_update(unit_shift, unit_stat[0], unit_grad)
    return (
        block_out,
        input_grad,
        owned[None],
        left_new[None],
        right_new[None],
        weight_new[None],
        vector_grad,
        vector_stat_new,
        vector_new,
        unit_grad[None],
        unit_stat_new[None],
        unit_new[None],
    )


LOW = jnp.bfloat16
WIDE = jnp.float32
MESH = pl.DeviceIdType.MESH
ANY = pl.BlockSpec(memory_space=pl.ANY)
STEP = 256
SUB = 64
PAIRS = 16
STEPS = 8
VMEM_BYTES = 60 * 1024 * 1024


def dot(left, right):
    return lax.dot_general(left, right, (((1,), (0,)), ((), ())), preferred_element_type=WIDE)


def dot_nt(left, right):
    return lax.dot_general(left, right, (((1,), (1,)), ((), ())), preferred_element_type=WIDE)


def dot_tn(left, right):
    return lax.dot_general(left, right, (((0,), (0,)), ((), ())), preferred_element_type=WIDE)


def resident(shape):
    return pl.BlockSpec(shape, lambda *_: (0,) * len(shape), pipeline_mode=pl.Buffered(1))


def tile_of(refs, widths, block):
    for ref, (rows, cols) in zip(refs, widths):
        count = (rows // B) * (cols // B)
        if block < count:
            i, j = divmod(block, cols // B)
            return ref.at[pl.ds(i * B, B), pl.ds(j * B, B)]
        block -= count


def move_blocks(copies_in, copies_out):
    for copy in copies_in:
        copy.start()
    for first, second in zip(copies_in, copies_out):
        first.wait()
        second.start()
    for copy in copies_out:
        copy.wait()


def place_kernel(shapes, order_ref, slots_ref, *refs):
    mats, (hold, sem_in, sem_out) = refs[:-3], refs[-3:]
    total = slots_ref.shape[0]
    move_blocks(
        [
            pltpu.make_async_copy(slots_ref.at[order_ref[b]], hold.at[b], sem_in.at[b])
            for b in range(total)
        ],
        [
            pltpu.make_async_copy(hold.at[b], tile_of(mats, shapes, b), sem_out.at[b])
            for b in range(total)
        ],
    )


def block_scratch(total):
    return [
        pltpu.VMEM((total, B, B), LOW),
        pltpu.SemaphoreType.DMA((total,)),
        pltpu.SemaphoreType.DMA((total,)),
    ]


def place_blocks(slots, order, shapes):
    total = slots.shape[0]
    return pl.pallas_call(
        functools.partial(place_kernel, shapes),
        grid_spec=pltpu.PrefetchScalarGridSpec(
            num_scalar_prefetch=1,
            grid=(1,),
            in_specs=[ANY],
            out_specs=[ANY] * len(shapes),
            scratch_shapes=block_scratch(total),
        ),
        out_shape=[jax.ShapeDtypeStruct(s, LOW) for s in shapes],
        compiler_params=pltpu.CompilerParams(vmem_limit_bytes=VMEM_BYTES),
        name="place_blocks",
    )(order, slots)


def unplace_kernel(shapes, order_ref, *refs):
    mats, (slots_ref, hold, sem_in, sem_out) = refs[:-4], refs[-4:]
    total = slots_ref.shape[0]
    move_blocks(
        [
            pltpu.make_async_copy(tile_of(mats, shapes, b), hold.at[b], sem_in.at[b])
            for b in range(total)
        ],
        [
            pltpu.make_async_copy(hold.at[b], slots_ref.at[order_ref[b]], sem_out.at[b])
            for b in range(total)
        ],
    )


def unplace_blocks(mats, order):
    shapes = [m.shape for m in mats]
    total = order.shape[0]
    return pl.pallas_call(
        functools.partial(unplace_kernel, shapes),
        grid_spec=pltpu.PrefetchScalarGridSpec(
            num_scalar_prefetch=1,
            grid=(1,),
            in_specs=[ANY] * len(mats),
            out_specs=ANY,
            scratch_shapes=block_scratch(total),
        ),
        out_shape=jax.ShapeDtypeStruct((total, B, B), LOW),
        compiler_params=pltpu.CompilerParams(vmem_limit_bytes=VMEM_BYTES),
        name="unplace_blocks",
    )(order, *mats)


def turn(values, cos, sin_high, sin_low):
    return (
        values * cos
        + pltpu.roll(values, 32, 1) * sin_high
        - pltpu.roll(values, 96, 1) * sin_low
    )


def turn_back(values, cos, sin_high, sin_low):
    return (
        values * cos
        - pltpu.roll(values, 32, 1) * sin_high
        + pltpu.roll(values, 96, 1) * sin_low
    )


def qkv_kernel(scale, h_ref, w_ref, bias_ref, cos_ref, high_ref, low_ref, q_ref, k_ref, v_ref):
    for j in range(w_ref.shape[1] // HD):
        head, part = divmod(j, 3)
        cols = slice(head * HD, head * HD + HD)
        proj = dot(h_ref[...], w_ref[:, j * HD : (j + 1) * HD]) + bias_ref[:, j * HD : (j + 1) * HD]
        if part == 2:
            v_ref[:, cols] = proj.astype(LOW)
            continue
        front = turn(proj[:, :128], cos_ref[...], high_ref[...], low_ref[...])
        turned = jnp.concatenate([front, proj[:, 128:]], axis=1).astype(LOW)
        if part == 0:
            q_ref[:, cols] = (turned.astype(WIDE) * scale).astype(LOW)
        else:
            k_ref[:, cols] = turned


def project_qkv(h1, qkv_w, bias, tables):
    rows, d = h1.shape
    cols = qkv_w.shape[1]
    out_cols = cols // 3
    tile = 512
    row_spec = lambda width: pl.BlockSpec((tile, width), lambda i: (i, 0))
    return pl.pallas_call(
        functools.partial(qkv_kernel, 1.0 / math.sqrt(HD)),
        grid=(rows // tile,),
        in_specs=[row_spec(d), resident((d, cols)), resident((1, cols))] + [row_spec(128)] * 3,
        out_specs=[row_spec(out_cols)] * 3,
        out_shape=[jax.ShapeDtypeStruct((rows, out_cols), LOW)] * 3,
        compiler_params=pltpu.CompilerParams(vmem_limit_bytes=VMEM_BYTES),
        name="project_qkv",
    )(h1, qkv_w, bias, *tables)


def attention_kernel(
    tile,
    start_ref,
    q_ref,
    k_ref,
    v_ref,
    g_ref,
    cos_ref,
    high_ref,
    low_ref,
    ctx_ref,
    grad_ref,
    p_scr,
    dp_scr,
    dk_scr,
    dv_scr,
):
    step = pl.program_id(1)
    count = pl.num_programs(1)
    scale = 1.0 / math.sqrt(HD)

    @pl.when(step == 0)
    def _():
        dk_scr[...] = jnp.zeros_like(dk_scr)
        dv_scr[...] = jnp.zeros_like(dv_scr)

    def rows(c):
        q = q_ref[...]
        g = g_ref[...]
        first = start_ref[...]
        top = jnp.full((tile, 1), masked_score, WIDE)
        for j in range(c + 1):
            keys = slice(j * tile, (j + 1) * tile)
            s = dot_nt(q, k_ref[keys, :])
            col = lax.broadcasted_iota(jnp.int32, (tile, tile), 1) + j * tile
            ok = col >= first
            if j == c:
                row = lax.broadcasted_iota(jnp.int32, (tile, tile), 0) + c * tile
                ok = ok & (col <= row)
            s = jnp.where(ok, s, masked_score)
            p_scr[:, keys] = s
            top = jnp.maximum(top, jnp.max(s, axis=1, keepdims=True))
        total = jnp.zeros((tile, 1), WIDE)
        for j in range(c + 1):
            keys = slice(j * tile, (j + 1) * tile)
            e = jnp.exp(p_scr[:, keys] - top)
            p_scr[:, keys] = e
            total = total + jnp.sum(e, axis=1, keepdims=True)
        inverse = 1.0 / total
        ctx = jnp.zeros((tile, HD), WIDE)
        delta = jnp.zeros((tile, 1), WIDE)
        for j in range(c + 1):
            keys = slice(j * tile, (j + 1) * tile)
            p = p_scr[:, keys] * inverse
            p_scr[:, keys] = p
            pb = p.astype(LOW)
            dp = dot_nt(g, v_ref[keys, :])
            dp_scr[:, keys] = dp
            delta = delta + jnp.sum(p * dp, axis=1, keepdims=True)
            ctx = ctx + dot(pb, v_ref[keys, :])
            dv_scr[keys, :] += dot_tn(pb, g)
        ctx_ref[...] = ctx.astype(LOW)
        dq = jnp.zeros((tile, HD), WIDE)
        for j in range(c + 1):
            keys = slice(j * tile, (j + 1) * tile)
            ds = (p_scr[:, keys] * (dp_scr[:, keys] - delta)).astype(LOW)
            dq = dq + dot(ds, k_ref[keys, :])
            dk_scr[keys, :] += dot_tn(ds, q)
        dq = dq * scale
        here = slice(c * tile, (c + 1) * tile)
        front = turn_back(dq[:, :128], cos_ref[here, :], high_ref[here, :], low_ref[here, :])
        grad_ref[here, 0:128] = front.astype(LOW)
        grad_ref[here, 128:HD] = dq[:, 128:].astype(LOW)

    for c in range(dk_scr.shape[0] // tile):
        pl.when(step == c)(functools.partial(rows, c))

    @pl.when(step == count - 1)
    def _():
        dk = dk_scr[...]
        front = turn_back(dk[:, :128], cos_ref[...], high_ref[...], low_ref[...])
        grad_ref[:, HD : HD + 128] = front.astype(LOW)
        grad_ref[:, HD + 128 : 2 * HD] = dk[:, 128:].astype(LOW)
        grad_ref[:, 2 * HD :] = dv_scr[...].astype(LOW)


def attention_both(start, q, k, v, ctx_grad, tables):
    rows, cols = q.shape
    heads = cols // HD
    tile = 512
    tile_spec = pl.BlockSpec((tile, HD), lambda h, i: (i, h))
    full_spec = pl.BlockSpec((rows, HD), lambda h, i: (0, h))
    flops = heads * rows * rows * HD * 6
    return pl.pallas_call(
        functools.partial(attention_kernel, tile),
        grid=(heads, rows // tile),
        in_specs=[pl.BlockSpec((tile, 1), lambda h, i: (i, 0)), tile_spec, full_spec, full_spec, tile_spec]
        + [resident((rows, 128))] * 3,
        out_specs=[tile_spec, pl.BlockSpec((rows, 3 * HD), lambda h, i: (0, h))],
        out_shape=[
            jax.ShapeDtypeStruct((rows, cols), LOW),
            jax.ShapeDtypeStruct((rows, 3 * cols), LOW),
        ],
        scratch_shapes=[
            pltpu.VMEM((tile, rows), WIDE),
            pltpu.VMEM((tile, rows), WIDE),
            pltpu.VMEM((rows, HD), WIDE),
            pltpu.VMEM((rows, HD), WIDE),
        ],
        compiler_params=pltpu.CompilerParams(vmem_limit_bytes=VMEM_BYTES),
        cost_estimate=pl.CostEstimate(flops=flops, bytes_accessed=30 << 20, transcendentals=0),
        name="attention_both",
    )(start, q, k, v, ctx_grad, *tables)


class Line:
    def __init__(self, out, part, got, across, sems):
        self.out, self.part, self.got, self.across = out, part, got, across
        (
            self.up_send,
            self.up_recv,
            self.far_send,
            self.far_recv,
            self.over_send,
            self.over_recv,
            self.down_send,
            self.down_recv,
            self.relay_send,
            self.relay_recv,
            self.own,
        ) = [sems.at[i] for i in range(11)]
        z = lax.axis_index("mp")
        self.inner = (z == 1) | (z == 2)
        self.near = (z >= 2).astype(jnp.int32)
        self.far = 1 - self.near
        self.partner = jnp.where(self.inner, jnp.where(z == 1, 0, 3), jnp.where(z == 0, 1, 2))
        self.other = 3 - z

    def rows(self, pair, which):
        return self.out.at[pl.ds(pl.multiple_of(pair * (2 * SUB) + which * SUB, SUB), SUB), :]

    def greet(self):
        barrier = pltpu.get_barrier_semaphore()
        pl.semaphore_signal(barrier, inc=1, device_id={"mp": self.partner}, device_id_type=MESH)

        @pl.when(self.inner)
        def _():
            pl.semaphore_signal(barrier, inc=1, device_id={"mp": self.other}, device_id_type=MESH)
            pl.semaphore_wait(barrier, 2)

        @pl.when(jnp.logical_not(self.inner))
        def _():
            pl.semaphore_wait(barrier, 1)

    def copy(self, src, dst, send, recv, pair, target):
        return pltpu.make_async_remote_copy(
            src_ref=src,
            dst_ref=dst,
            send_sem=send.at[pair],
            recv_sem=recv.at[pair],
            device_id={"mp": target},
            device_id_type=MESH,
        )

    def up(self, pair):
        return self.copy(self.part.at[pair], self.got.at[pair], self.up_send, self.up_recv, pair, self.partner)

    def far_sum(self, pair):
        return self.copy(
            self.part.at[pair, self.far], self.across.at[pair], self.far_send, self.far_recv, pair, self.other
        )

    def over(self, pair, which):
        src = self.part.at[pair, self.near]
        return self.copy(src, self.rows(pair, which), self.over_send, self.over_recv, pair, self.other)

    def down(self, pair):
        src = self.part.at[pair, self.near]
        return self.copy(
            src, self.rows(pair, self.near), self.down_send, self.down_recv, pair, self.partner
        )

    def relay(self, pair):
        far = self.rows(pair, self.far)
        return self.copy(far, far, self.relay_send, self.relay_recv, pair, self.partner)

    def keep(self, pair):
        src = self.part.at[pair, self.near]
        return pltpu.make_async_copy(src, self.rows(pair, self.near), self.own.at[pair])

    def send_up(self, pair):
        @pl.when(jnp.logical_not(self.inner))
        def _():
            self.up(pair).start()

    def add_far(self, pair):
        self.up(pair).wait_recv()
        far = self.part[pair, self.far].astype(WIDE) + self.got[pair, self.far].astype(WIDE)
        self.part[pair, self.far] = far.astype(LOW)
        self.far_sum(pair).start()

    def finish_near(self, pair, base):
        self.far_sum(pair).wait_recv()
        total = (
            self.part[pair, self.near].astype(WIDE)
            + self.got[pair, self.near].astype(WIDE)
            + self.across[pair].astype(WIDE)
        )
        self.part[pair, self.near] = (base + total).astype(LOW)
        self.over(pair, self.near).start()
        self.down(pair).start()
        self.keep(pair).start()

    def send_relay(self, pair):
        self.over(pair, self.far).wait_recv()
        self.relay(pair).start()

    def drain(self):
        @pl.when(self.inner)
        def _():
            @pl.loop(0, PAIRS)
            def _(pair):
                self.far_sum(pair).wait_send()
                self.over(pair, self.near).wait_send()
                self.down(pair).wait_send()
                self.relay(pair).wait_send()
                self.keep(pair).wait()

        @pl.when(jnp.logical_not(self.inner))
        def _():
            @pl.loop(0, PAIRS)
            def _(pair):
                self.up(pair).wait_send()
                self.down(pair).wait_recv()
                self.relay(pair).wait_recv()

    def tick(self, step, base_of):
        @pl.when(self.inner & (step >= 1) & (step < STEPS + 1))
        def _():
            for s in range(2):
                self.add_far((step - 1) * 2 + s)

        @pl.when(self.inner & (step >= 2) & (step < STEPS + 2))
        def _():
            for s in range(2):
                offset = pl.multiple_of(s * 2 * SUB + self.near * SUB, SUB)
                self.finish_near((step - 2) * 2 + s, base_of(offset))

        @pl.when(self.inner & (step >= 3) & (step < STEPS + 3))
        def _():
            for s in range(2):
                self.send_relay((step - 3) * 2 + s)


LINE_STEPS = STEPS + 3


def line_scratch(d):
    return [
        pltpu.VMEM((PAIRS, 2, SUB, d), LOW),
        pltpu.VMEM((PAIRS, 2, SUB, d), LOW),
        pltpu.VMEM((PAIRS, SUB, d), LOW),
        pltpu.SemaphoreType.DMA((11, PAIRS)),
    ]


def now(step):
    return jnp.minimum(step, STEPS - 1)


def later(step):
    return jnp.clip(step - 2, 0, STEPS - 1)


def row_block(width, at):
    return pl.BlockSpec((STEP, width), lambda i: (at(i), 0))


def gelu_parts(z):
    e = jnp.exp(z * z * -0.5)
    t = 1.0 / (1.0 + jnp.abs(z) * (0.3275911 * math.sqrt(0.5)))
    poly = t * (
        0.5 * 0.254829592
        + t
        * (
            0.5 * -0.284496736
            + t * (0.5 * 1.421413741 + t * (0.5 * -1.453152027 + t * (0.5 * 1.061405429)))
        )
    )
    below = poly * e
    cdf = jnp.where(z >= 0, 1.0 - below, below)
    return cdf, e * (1.0 / math.sqrt(2.0 * math.pi))


def store_part(part_ref, step, cols, value):
    part_ref[pl.ds(step * 2, 2), :, :, cols] = value.astype(LOW).reshape(2, 2, SUB, value.shape[1])


def forward_kernel(
    h_ref,
    g_ref,
    ctx_ref,
    x_ref,
    up_ref,
    od_ref,
    bias_ref,
    shift_ref,
    act_ref,
    hg_ref,
    out_ref,
    part,
    got,
    across,
    sems,
):
    step = pl.program_id(0)
    line = Line(out_ref, part, got, across, sems)
    heads = ctx_ref.shape[1]
    width = 512

    @pl.when(step == 0)
    def _():
        line.greet()

    @pl.when(step < STEPS)
    def _():
        for n in range(up_ref.shape[1] // width):
            cols = slice(n * width, (n + 1) * width)
            hidden = dot(h_ref[...], up_ref[:, cols]) + bias_ref[:, cols]
            act_grad = dot_nt(g_ref[...], od_ref[heads + n * width : heads + (n + 1) * width, :])
            cdf, density = gelu_parts(hidden)
            act_ref[:, cols] = (hidden * cdf).astype(LOW)
            hg_ref[:, cols] = (act_grad * (cdf + hidden * density)).astype(LOW)
        for n in range(od_ref.shape[1] // width):
            cols = slice(n * width, (n + 1) * width)
            value = dot(ctx_ref[...], od_ref[:heads, cols]) + dot(act_ref[...], od_ref[heads:, cols])
            store_part(part, step, cols, value)
        for s in range(2):
            line.send_up(step * 2 + s)

    line.tick(
        step, lambda offset: x_ref[pl.ds(offset, SUB), :].astype(WIDE) + shift_ref[...]
    )

    @pl.when(step == LINE_STEPS - 1)
    def _():
        line.drain()


def forward_line(h2, cotangent, ctx, tokens, up_w, od_w, bias, shift):
    rows, d = tokens.shape
    units = up_w.shape[1]
    return pl.pallas_call(
        forward_kernel,
        grid=(LINE_STEPS,),
        in_specs=[
            row_block(d, now),
            row_block(d, now),
            row_block(ctx.shape[1], now),
            row_block(d, later),
            resident(up_w.shape),
            resident(od_w.shape),
            resident(bias.shape),
            resident(shift.shape),
        ],
        out_specs=[row_block(units, now), row_block(units, now), ANY],
        out_shape=[
            jax.ShapeDtypeStruct((rows, units), LOW),
            jax.ShapeDtypeStruct((rows, units), LOW),
            jax.ShapeDtypeStruct((rows, d), LOW),
        ],
        scratch_shapes=line_scratch(d),
        compiler_params=pltpu.CompilerParams(
            vmem_limit_bytes=VMEM_BYTES, collective_id=1, has_side_effects=True
        ),
        cost_estimate=pl.CostEstimate(
            flops=200_000_000_000, bytes_accessed=80 << 20, transcendentals=0
        ),
        name="forward_line",
    )(h2, cotangent, ctx, tokens, up_w, od_w, bias, shift)


def backward_kernel(
    qg_ref,
    hg_ref,
    x_ref,
    g_ref,
    qkv_ref,
    up_ref,
    one_ref,
    two_ref,
    norm_ref,
    out_ref,
    gc_scr,
    xhat_scr,
    part,
    got,
    across,
    sems,
):
    step = pl.program_id(0)
    line = Line(out_ref, part, got, across, sems)
    d = x_ref.shape[1]
    width = 512

    @pl.when(step == 0)
    def _():
        line.greet()
        norm_ref[...] = jnp.zeros_like(norm_ref)

    @pl.when(step < STEPS)
    def _():
        x = x_ref[...].astype(WIDE)
        center = x - jnp.mean(x, axis=1, keepdims=True)
        scale = lax.rsqrt(jnp.mean(center * center, axis=1, keepdims=True) + norm_eps)
        xhat_scr[...] = center * scale
        mean = jnp.zeros((STEP, 1), WIDE)
        slope = jnp.zeros((STEP, 1), WIDE)
        for n in range(d // width):
            cols = slice(n * width, (n + 1) * width)
            e1 = dot_nt(qg_ref[...], qkv_ref[cols, :])
            e2 = dot_nt(hg_ref[...], up_ref[cols, :])
            xhat = xhat_scr[:, cols]
            gc = e1 * one_ref[:, cols] + e2 * two_ref[:, cols]
            gc_scr[:, cols] = gc
            mean = mean + jnp.sum(gc, axis=1, keepdims=True)
            slope = slope + jnp.sum(gc * xhat, axis=1, keepdims=True)
            norm_ref[0:1, cols] += jnp.sum(e1 * xhat, axis=0, keepdims=True)
            norm_ref[1:2, cols] += jnp.sum(e1, axis=0, keepdims=True)
            norm_ref[2:3, cols] += jnp.sum(e2 * xhat, axis=0, keepdims=True)
            norm_ref[3:4, cols] += jnp.sum(e2, axis=0, keepdims=True)
        mean = mean * (1.0 / d)
        slope = slope * (1.0 / d)
        for n in range(d // width):
            cols = slice(n * width, (n + 1) * width)
            value = (gc_scr[:, cols] - mean - xhat_scr[:, cols] * slope) * scale
            store_part(part, step, cols, value)
        for s in range(2):
            line.send_up(step * 2 + s)

    line.tick(step, lambda offset: g_ref[pl.ds(offset, SUB), :].astype(WIDE))

    @pl.when(step == LINE_STEPS - 1)
    def _():
        line.drain()


def backward_line(qkv_grad, hidden_grad, tokens, cotangent, qkv_w, up_w, gain_one, gain_two):
    rows, d = tokens.shape
    return pl.pallas_call(
        backward_kernel,
        grid=(LINE_STEPS,),
        in_specs=[
            row_block(qkv_grad.shape[1], now),
            row_block(hidden_grad.shape[1], now),
            row_block(d, now),
            row_block(d, later),
            resident(qkv_w.shape),
            resident(up_w.shape),
            resident((1, d)),
            resident((1, d)),
        ],
        out_specs=[pl.BlockSpec((8, d), lambda i: (0, 0)), ANY],
        out_shape=[jax.ShapeDtypeStruct((8, d), WIDE), jax.ShapeDtypeStruct((rows, d), LOW)],
        scratch_shapes=[pltpu.VMEM((STEP, d), WIDE), pltpu.VMEM((STEP, d), WIDE)] + line_scratch(d),
        compiler_params=pltpu.CompilerParams(
            vmem_limit_bytes=VMEM_BYTES, collective_id=2, has_side_effects=True
        ),
        cost_estimate=pl.CostEstimate(
            flops=200_000_000_000, bytes_accessed=60 << 20, transcendentals=0
        ),
        name="backward_line",
    )(qkv_grad, hidden_grad, tokens, cotangent, qkv_w, up_w, gain_one, gain_two)


def halves(values):
    high = values.astype(LOW)
    return high, (values - high.astype(WIDE)).astype(LOW)


def shampoo_kernel(
    g_ref, w_ref, ls_ref, rs_ref, lr_ref, rr_ref, grad_ref, left_ref, right_ref, weight_ref
):
    for n in range(g_ref.shape[0]):
        g = g_ref[n]
        grad_ref[n] = g.astype(WIDE)
        left_ref[n] = 0.5 * ls_ref[n] + 0.5 * dot_nt(g, g)
        right_ref[n] = 0.5 * rs_ref[n] + 0.5 * dot_tn(g, g)
        l_high, l_low = halves(lr_ref[n])
        r_high, r_low = halves(rr_ref[n])
        d_high, d_low = halves(dot(l_high, g) + dot(l_low, g))
        direction = dot(d_high, r_high) + dot(d_low, r_high) + dot(d_high, r_low)
        weight = w_ref[n]
        size = 1.0 / (B * B)
        weight_size = jnp.sqrt(jnp.sum(weight * weight, keepdims=True) * size)
        step_size = jnp.sqrt(jnp.sum(direction * direction, keepdims=True) * size + 1e-06)
        weight_ref[n] = weight - direction * (step_share * weight_size / step_size)


def shampoo(grads, weights, left_stat, right_stat, left_root, right_root):
    count = grads.shape[0]
    group = 2
    spec = pl.BlockSpec((group, B, B), lambda i: (i, 0, 0))
    return pl.pallas_call(
        shampoo_kernel,
        grid=(count // group,),
        in_specs=[spec] * 6,
        out_specs=[spec] * 4,
        out_shape=[jax.ShapeDtypeStruct((count, B, B), WIDE)] * 4,
        compiler_params=pltpu.CompilerParams(vmem_limit_bytes=VMEM_BYTES),
        name="shampoo",
    )(grads, weights, left_stat, right_stat, left_root, right_root)


def per_device_line(
    tokens,
    cotangent,
    seq_len,
    seq_device,
    owner_map,
    weight_blocks,
    left_stat,
    right_stat,
    left_root,
    right_root,
    vectors,
    vector_stat,
    unit_bias,
    unit_stat,
):
    groups = lax.axis_size("mp")
    device = lax.axis_index("dp")
    row_count, d = tokens.shape
    qkv_cols = 3 * d // groups
    head_cols = d // groups
    unit_cols = FF // groups
    gathered = lax.all_gather(weight_blocks[0].astype(LOW), "dp", axis=0, tiled=True)

    segment, position = segment_layout(seq_len, seq_device, device, row_count)
    start = (jnp.arange(row_count, dtype=jnp.int32) - position)[:, None]
    frequency = 10000.0 ** (-2.0 * jnp.arange(ROT // 2, dtype=WIDE) / ROT)
    angles = position.astype(WIDE)[:, None] * frequency[None, :]
    cos, sin = jnp.cos(angles), jnp.sin(angles)
    pad = jnp.zeros((row_count, 128 - ROT), WIDE)
    empty = jnp.zeros_like(sin)
    tables = (
        jnp.concatenate([cos, cos, pad + 1.0], axis=1),
        jnp.concatenate([empty, sin, pad], axis=1),
        jnp.concatenate([sin, empty, pad], axis=1),
    )
    inputs = tokens.astype(WIDE)
    normed_one = layer_norm(inputs, vectors[0], vectors[1]).astype(LOW)
    normed_two = layer_norm(inputs, vectors[2], vectors[3]).astype(LOW)
    out_sum = jnp.sum(cotangent.astype(WIDE), axis=0)
    shift = (vectors[4] + vectors[5])[None]
    unit_shift = unit_bias[0]

    shapes = ((d, qkv_cols), (head_cols + unit_cols, d), (d, unit_cols))
    blocks = [(a // B) * (b // B) for a, b in ((d, qkv_cols), (head_cols, d), (d, unit_cols))]
    order = jnp.concatenate(
        [
            owner_map[: blocks[0] + blocks[1]],
            owner_map[blocks[0] + blocks[1] + blocks[2] :],
            owner_map[blocks[0] + blocks[1] : blocks[0] + blocks[1] + blocks[2]],
        ]
    )
    qkv_w, od_w, up_w = place_blocks(gathered, order, shapes)

    q, k, v = project_qkv(normed_one, qkv_w, unit_shift[None, :qkv_cols], tables)
    ctx_grad = jnp.einsum(
        "td,id->ti", cotangent, od_w[:head_cols], preferred_element_type=WIDE
    ).astype(LOW)
    ctx, qkv_grad = attention_both(start, q, k, v, ctx_grad, tables)
    act, hidden_grad, block_out = forward_line(
        normed_two, cotangent, ctx, tokens, up_w, od_w, unit_shift[None, qkv_cols:], shift
    )
    mats = [
        lax.dot_general(a, b, (((0,), (0,)), ((), ())), preferred_element_type=WIDE).astype(LOW)
        for a, b in (
            (normed_one, qkv_grad),
            (ctx, cotangent),
            (normed_two, hidden_grad),
            (act, cotangent),
        )
    ]
    slots = unplace_blocks(mats, owner_map)
    owned = lax.psum_scatter(slots, "dp", scatter_dimension=0, tiled=True)
    qkv_grad, hidden_grad, slots = lax.optimization_barrier((qkv_grad, hidden_grad, slots))
    norm_part, input_grad = backward_line(
        qkv_grad,
        hidden_grad,
        tokens,
        cotangent,
        qkv_w,
        up_w,
        vectors[0:1],
        vectors[2:3],
    )
    block_grad, left_new, right_new, weight_new = shampoo(
        owned, weight_blocks[0], left_stat[0], right_stat[0], left_root[0], right_root[0]
    )
    unit_part = jnp.concatenate(
        [
            jnp.sum(qkv_grad.astype(WIDE), axis=0),
            jnp.sum(hidden_grad.astype(WIDE), axis=0),
        ]
    )
    norm_sum = lax.psum(norm_part[:4], "mp")
    vector_part = jnp.concatenate([norm_sum, jnp.stack([out_sum, out_sum])], axis=0)
    vector_grad, unit_grad = lax.psum((vector_part, unit_part), "dp")
    vector_stat_new, vector_new = vector_update(vectors, vector_stat, vector_grad)
    unit_stat_new, unit_new = vector_update(unit_shift, unit_stat[0], unit_grad)
    return (
        block_out,
        input_grad,
        block_grad[None],
        left_new[None],
        right_new[None],
        weight_new[None],
        vector_grad,
        vector_stat_new,
        vector_new,
        unit_grad[None],
        unit_stat_new[None],
        unit_new[None],
    )


def solution(mesh):
    placed = (
        P("dp", None),
        P("dp", None),
        P(),
        P(),
        P(),
        P("mp", "dp", None, None),
        P("mp", "dp", None, None),
        P("mp", "dp", None, None),
        P("mp", "dp", None, None),
        P("mp", "dp", None, None),
        P(),
        P(),
        P("mp", None),
        P("mp", None),
    )
    body = per_device
    if mesh.shape["dp"] == 8 and mesh.shape["mp"] == 4:
        body = per_device_line
    return jax.shard_map(
        body,
        mesh=mesh,
        in_specs=placed,
        out_specs=(
            P("dp", None),
            P("dp", None),
            P("mp", "dp", None, None),
            P("mp", "dp", None, None),
            P("mp", "dp", None, None),
            P("mp", "dp", None, None),
            P(),
            P(),
            P(),
            P("mp", None),
            P("mp", None),
            P("mp", None),
        ),
        check_vma=False,
    )
```

```python
import functools
import math

import jax
import jax.numpy as jnp
from jax import lax
from jax.experimental import pallas as pl
from jax.experimental.pallas import tpu as pltpu
from jax.sharding import PartitionSpec as P

D = 2048
HEADS = 8
HD = 256
ROT = 64
FF = 8192
B = 256


highest = lax.Precision.HIGHEST
norm_eps = 1e-05
step_share = 0.5
vector_rate = 0.15
masked_score = -1e30


def layer_norm(values, gain, shift):
    center = values - jnp.mean(values, axis=-1, keepdims=True)
    spread = jnp.mean(center * center, axis=-1, keepdims=True)
    return center * lax.rsqrt(spread + norm_eps) * gain + shift


def gelu_exact(values):
    return jax.nn.gelu(values, approximate=False)


def segment_layout(seq_len, seq_device, device, row_count):
    is_mine = seq_device == device
    lengths = jnp.where(is_mine, seq_len, 0)
    seq_ends = jnp.cumsum(lengths)
    row_index = jnp.arange(row_count, dtype=jnp.int32)
    passed = is_mine[None, :] & (seq_ends[None, :] <= row_index[:, None])
    segment = jnp.sum(passed.astype(jnp.int32), axis=1)
    seq_start = jnp.max(jnp.where(passed, seq_ends[None, :], 0), axis=1)
    return (segment, row_index - seq_start)


def rotary_tables(position):
    half_rot = ROT // 2
    frequency = 10000.0 ** (-2.0 * jnp.arange(half_rot, dtype=jnp.float32) / ROT)
    angles = position.astype(jnp.float32)[:, None] * frequency[None, :]
    cosine_table = jnp.concatenate([jnp.cos(angles), jnp.cos(angles)], axis=1)
    sine_table = jnp.concatenate([jnp.sin(angles), jnp.sin(angles)], axis=1)
    return (cosine_table, sine_table)


def rotate(values, cosine_table, sine_table):
    rot_dims = cosine_table.shape[1]
    half_rot = rot_dims // 2
    leading = values[..., :rot_dims]
    turned = jnp.concatenate([-leading[..., half_rot:], leading[..., :half_rot]], axis=-1)
    rotated = leading * cosine_table[:, None, :] + turned * sine_table[:, None, :]
    return jnp.concatenate([rotated, values[..., rot_dims:]], axis=-1)


def blocks_to_matrix(blocks, across):
    down_count = blocks.shape[0] // across
    return (
        blocks.reshape(down_count, across, B, B)
        .transpose(0, 2, 1, 3)
        .reshape(down_count * B, across * B)
    )


def matrix_to_blocks(matrix):
    down_count = matrix.shape[0] // B
    across = matrix.shape[1] // B
    return (
        matrix.reshape(down_count, B, across, B)
        .transpose(0, 2, 1, 3)
        .reshape(down_count * across, B, B)
    )


def split_blocks(blocks, qkv_cols, head_cols, unit_cols):
    qkv_end = D // B * (qkv_cols // B)
    out_end = qkv_end + head_cols // B * (D // B)
    up_end = out_end + D // B * (unit_cols // B)
    qkv_w = blocks_to_matrix(blocks[:qkv_end], qkv_cols // B)
    out_w = blocks_to_matrix(blocks[qkv_end:out_end], D // B)
    up_w = blocks_to_matrix(blocks[out_end:up_end], unit_cols // B)
    down_w = blocks_to_matrix(blocks[up_end:], D // B)
    return (qkv_w, out_w, up_w, down_w)


def apply_step(weight, direction):
    weight_size = jnp.sqrt(jnp.mean(weight * weight, axis=(-2, -1), keepdims=True))
    step_size = jnp.sqrt(jnp.mean(direction * direction, axis=(-2, -1), keepdims=True) + 1e-06)
    return weight - step_share * weight_size * direction / step_size


def vector_update(values, old_stat, gradient):
    new_stat = 0.5 * old_stat + 0.5 * gradient * gradient
    return (new_stat, values - vector_rate * gradient * lax.rsqrt(new_stat))


def block_mask(block_segment, block_row, segment, column):
    return (block_segment[:, None] == segment[None, :]) & (column[None, :] <= block_row[:, None])


def attention_forward(queries, keys_low, values_low, segment):
    row_count, head_count, head_dim = queries.shape
    block_rows = min(512, row_count)
    block_count = row_count // block_rows
    score_scale = 1.0 / math.sqrt(head_dim)
    column = jnp.arange(row_count, dtype=jnp.int32)

    def one_block(inputs):
        block_query, block_segment, block_row = inputs
        scores = (
            jnp.einsum("qhd,khd->hqk", block_query, keys_low, preferred_element_type=jnp.float32)
            * score_scale
        )
        scores = jnp.where(
            block_mask(block_segment, block_row, segment, column)[None], scores, masked_score
        )
        log_total = jax.nn.logsumexp(scores, axis=-1)
        weights = jnp.exp(scores - log_total[:, :, None]).astype(jnp.bfloat16)
        context = jnp.einsum(
            "hqk,khd->qhd", weights, values_low, preferred_element_type=jnp.float32
        )
        return (context, log_total)

    contexts, log_totals = lax.map(
        one_block,
        (
            queries.reshape(block_count, block_rows, head_count, head_dim),
            segment.reshape(block_count, block_rows),
            column.reshape(block_count, block_rows),
        ),
    )
    return (contexts.reshape(row_count, head_count, head_dim), log_totals)


def attention_backward(queries, keys_low, values_low, context_grad, log_totals, segment):
    row_count, head_count, head_dim = queries.shape
    block_rows = min(512, row_count)
    block_count = row_count // block_rows
    score_scale = 1.0 / math.sqrt(head_dim)
    column = jnp.arange(row_count, dtype=jnp.int32)

    def one_block(totals, inputs):
        key_grad, value_grad = totals
        block_query, block_grad, block_total, block_segment, block_row = inputs
        scores = (
            jnp.einsum("qhd,khd->hqk", block_query, keys_low, preferred_element_type=jnp.float32)
            * score_scale
        )
        scores = jnp.where(
            block_mask(block_segment, block_row, segment, column)[None], scores, masked_score
        )
        probs = jnp.exp(scores - block_total[:, :, None])
        weights = probs.astype(jnp.bfloat16)
        prob_grad = jnp.einsum(
            "qhd,khd->hqk", block_grad, values_low, preferred_element_type=jnp.float32
        )
        delta = jnp.sum(probs * prob_grad, axis=-1, keepdims=True)
        score_grad = (probs * (prob_grad - delta)).astype(jnp.bfloat16)
        query_grad = (
            jnp.einsum("hqk,khd->qhd", score_grad, keys_low, preferred_element_type=jnp.float32)
            * score_scale
        )
        key_grad = (
            key_grad
            + jnp.einsum(
                "hqk,qhd->khd", score_grad, block_query, preferred_element_type=jnp.float32
            )
            * score_scale
        )
        value_grad = value_grad + jnp.einsum(
            "hqk,qhd->khd", weights, block_grad, preferred_element_type=jnp.float32
        )
        return ((key_grad, value_grad), query_grad)

    zeros_start = jnp.zeros((row_count, head_count, head_dim), jnp.float32)
    (key_grad, value_grad), query_grad = lax.scan(
        one_block,
        (zeros_start, zeros_start),
        (
            queries.reshape(block_count, block_rows, head_count, head_dim),
            context_grad.reshape(block_count, block_rows, head_count, head_dim),
            log_totals,
            segment.reshape(block_count, block_rows),
            column.reshape(block_count, block_rows),
        ),
    )
    return (query_grad.reshape(row_count, head_count, head_dim), key_grad, value_grad)


def per_device(
    tokens,
    cotangent,
    seq_len,
    seq_device,
    owner_map,
    weight_blocks,
    left_stat,
    right_stat,
    left_root,
    right_root,
    vectors,
    vector_stat,
    unit_bias,
    unit_stat,
):
    groups = lax.axis_size("mp")
    device = lax.axis_index("dp")
    row_count = tokens.shape[0]
    heads_here = HEADS // groups
    qkv_cols = 3 * D // groups
    head_cols = D // groups
    unit_cols = FF // groups
    slot_count = weight_blocks.shape[1]
    sent_blocks = weight_blocks[0].astype(jnp.bfloat16)
    gathered = lax.all_gather(sent_blocks, "dp", axis=0, tiled=True)
    qkv_w, out_w, up_w, down_w = split_blocks(gathered[owner_map], qkv_cols, head_cols, unit_cols)
    segment, position = segment_layout(seq_len, seq_device, device, row_count)
    cosine_table, sine_table = rotary_tables(position)
    unit_shift = unit_bias[0]
    inputs = tokens.astype(jnp.float32)
    normed_one = layer_norm(inputs, vectors[0], vectors[1]).astype(jnp.bfloat16)
    normed_two = layer_norm(inputs, vectors[2], vectors[3]).astype(jnp.bfloat16)
    qkv_proj = (
        jnp.dot(normed_one, qkv_w, preferred_element_type=jnp.float32) + unit_shift[:qkv_cols]
    )
    qkv_proj = qkv_proj.reshape(row_count, heads_here, 3, HD)

    def turn_pair(values):
        return rotate(values.reshape(row_count, 2 * heads_here, HD), cosine_table, sine_table)

    turned, turn_back = jax.vjp(turn_pair, qkv_proj[:, :, :2])
    turned = turned.reshape(row_count, heads_here, 2, HD).astype(jnp.bfloat16)
    queries = turned[:, :, 0]
    keys_low = turned[:, :, 1]
    values_low = qkv_proj[:, :, 2].astype(jnp.bfloat16)
    context, log_totals = attention_forward(queries, keys_low, values_low, segment)
    context_low = context.reshape(row_count, head_cols).astype(jnp.bfloat16)
    hidden = jnp.dot(normed_two, up_w, preferred_element_type=jnp.float32) + unit_shift[qkv_cols:]
    active, gelu_back = jax.vjp(gelu_exact, hidden)
    active_low = active.astype(jnp.bfloat16)
    partial_out = jnp.dot(context_low, out_w, preferred_element_type=jnp.float32) + jnp.dot(
        active_low, down_w, preferred_element_type=jnp.float32
    )
    branch = lax.psum(partial_out.astype(jnp.bfloat16), "mp").astype(jnp.float32)
    block_out = (inputs + branch + (vectors[4] + vectors[5])).astype(jnp.bfloat16)
    grad_full = cotangent.astype(jnp.float32)
    act_grad = jnp.einsum("td,fd->tf", cotangent, down_w, preferred_element_type=jnp.float32)
    hidden_grad = gelu_back(act_grad)[0].astype(jnp.bfloat16)
    context_grad = jnp.einsum(
        "td,id->ti", cotangent, out_w, preferred_element_type=jnp.float32
    ).astype(jnp.bfloat16)
    query_grad, key_grad, value_grad = attention_backward(
        queries,
        keys_low,
        values_low,
        context_grad.reshape(row_count, heads_here, HD),
        log_totals,
        segment,
    )
    pair_grad = turn_back(
        jnp.stack([query_grad, key_grad], axis=2).reshape(row_count, 2 * heads_here, HD)
    )[0]
    qkv_grad = (
        jnp.concatenate([pair_grad, value_grad[:, :, None]], axis=2)
        .reshape(row_count, qkv_cols)
        .astype(jnp.bfloat16)
    )
    one_grad = jnp.einsum("te,de->td", qkv_grad, qkv_w, preferred_element_type=jnp.float32)
    two_grad = jnp.einsum("tf,df->td", hidden_grad, up_w, preferred_element_type=jnp.float32)
    norm_back_one = jax.vjp(layer_norm, inputs, vectors[0], vectors[1])[1]
    norm_back_two = jax.vjp(layer_norm, inputs, vectors[2], vectors[3])[1]
    input_one, gain_one, shift_one = norm_back_one(one_grad)
    input_two, gain_two, shift_two = norm_back_two(two_grad)
    input_part = input_one + input_two
    norm_part = jnp.stack([gain_one, shift_one, gain_two, shift_two])
    input_sum, norm_sum = lax.psum((input_part, norm_part), "mp")
    input_grad = (grad_full + input_sum).astype(jnp.bfloat16)
    qkv_w_grad = jnp.einsum("td,te->de", normed_one, qkv_grad, preferred_element_type=jnp.float32)
    out_w_grad = jnp.einsum("ti,td->id", context_low, cotangent, preferred_element_type=jnp.float32)
    up_w_grad = jnp.einsum("td,tf->df", normed_two, hidden_grad, preferred_element_type=jnp.float32)
    down_w_grad = jnp.einsum("tf,td->fd", active_low, cotangent, preferred_element_type=jnp.float32)
    canonical_grad = jnp.concatenate(
        [matrix_to_blocks(matrix) for matrix in (qkv_w_grad, out_w_grad, up_w_grad, down_w_grad)],
        axis=0,
    )
    slot_grads = canonical_grad[jnp.argsort(owner_map)]
    out_sum = jnp.sum(grad_full, axis=0)
    vector_part = jnp.concatenate([norm_sum, jnp.stack([out_sum, out_sum])], axis=0)
    unit_part = jnp.concatenate(
        [
            jnp.sum(qkv_grad.astype(jnp.float32), axis=0),
            jnp.sum(hidden_grad.astype(jnp.float32), axis=0),
        ]
    )
    summed, vector_grad, unit_grad = lax.psum((slot_grads, vector_part, unit_part), "dp")
    owned = lax.dynamic_slice_in_dim(summed, device * slot_count, slot_count, 0)
    left_new = 0.5 * left_stat[0] + 0.5 * jnp.einsum(
        "nij,nkj->nik", owned, owned, precision=highest
    )
    right_new = 0.5 * right_stat[0] + 0.5 * jnp.einsum(
        "nji,njk->nik", owned, owned, precision=highest
    )
    direction = jnp.einsum("nij,njk->nik", left_root[0], owned, precision=highest)
    direction = jnp.einsum("nij,njk->nik", direction, right_root[0], precision=highest)
    weight_new = apply_step(weight_blocks[0], direction)
    vector_stat_new, vector_new = vector_update(vectors, vector_stat, vector_grad)
    unit_stat_new, unit_new = vector_update(unit_shift, unit_stat[0], unit_grad)
    return (
        block_out,
        input_grad,
        owned[None],
        left_new[None],
        right_new[None],
        weight_new[None],
        vector_grad,
        vector_stat_new,
        vector_new,
        unit_grad[None],
        unit_stat_new[None],
        unit_new[None],
    )


LOW = jnp.bfloat16
WIDE = jnp.float32
MESH = pl.DeviceIdType.MESH
ANY = pl.BlockSpec(memory_space=pl.ANY)
STEP = 256
SUB = 64
PAIRS = 16
STEPS = 8
VMEM_BYTES = 60 * 1024 * 1024
FORWARD_VMEM = 63 * 1024 * 1024


def dot(left, right):
    return lax.dot_general(left, right, (((1,), (0,)), ((), ())), preferred_element_type=WIDE)


def dot_nt(left, right):
    return lax.dot_general(left, right, (((1,), (1,)), ((), ())), preferred_element_type=WIDE)


def dot_tn(left, right):
    return lax.dot_general(left, right, (((0,), (0,)), ((), ())), preferred_element_type=WIDE)


def resident(shape):
    return pl.BlockSpec(shape, lambda *_: (0,) * len(shape), pipeline_mode=pl.Buffered(1))


def tile_of(refs, widths, block):
    for ref, (rows, cols) in zip(refs, widths):
        count = (rows // B) * (cols // B)
        if block < count:
            i, j = divmod(block, cols // B)
            return ref.at[pl.ds(i * B, B), pl.ds(j * B, B)]
        block -= count


def move_blocks(copies_in, copies_out):
    for copy in copies_in:
        copy.start()
    for first, second in zip(copies_in, copies_out):
        first.wait()
        second.start()
    for copy in copies_out:
        copy.wait()


def place_kernel(shapes, order_ref, slots_ref, *refs):
    mats, (hold, sem_in, sem_out) = refs[:-3], refs[-3:]
    total = slots_ref.shape[0]
    move_blocks(
        [
            pltpu.make_async_copy(slots_ref.at[order_ref[b]], hold.at[b], sem_in.at[b])
            for b in range(total)
        ],
        [
            pltpu.make_async_copy(hold.at[b], tile_of(mats, shapes, b), sem_out.at[b])
            for b in range(total)
        ],
    )


def block_scratch(total):
    return [
        pltpu.VMEM((total, B, B), LOW),
        pltpu.SemaphoreType.DMA((total,)),
        pltpu.SemaphoreType.DMA((total,)),
    ]


def place_blocks(slots, order, shapes):
    total = slots.shape[0]
    return pl.pallas_call(
        functools.partial(place_kernel, shapes),
        grid_spec=pltpu.PrefetchScalarGridSpec(
            num_scalar_prefetch=1,
            grid=(1,),
            in_specs=[ANY],
            out_specs=[ANY] * len(shapes),
            scratch_shapes=block_scratch(total),
        ),
        out_shape=[jax.ShapeDtypeStruct(s, LOW) for s in shapes],
        compiler_params=pltpu.CompilerParams(vmem_limit_bytes=VMEM_BYTES),
        name="place_blocks",
    )(order, slots)


def unplace_kernel(shapes, order_ref, *refs):
    mats, (slots_ref, hold, sem_in, sem_out) = refs[:-4], refs[-4:]
    total = slots_ref.shape[0]
    move_blocks(
        [
            pltpu.make_async_copy(tile_of(mats, shapes, b), hold.at[b], sem_in.at[b])
            for b in range(total)
        ],
        [
            pltpu.make_async_copy(hold.at[b], slots_ref.at[order_ref[b]], sem_out.at[b])
            for b in range(total)
        ],
    )


def unplace_blocks(mats, order):
    shapes = [m.shape for m in mats]
    total = order.shape[0]
    return pl.pallas_call(
        functools.partial(unplace_kernel, shapes),
        grid_spec=pltpu.PrefetchScalarGridSpec(
            num_scalar_prefetch=1,
            grid=(1,),
            in_specs=[ANY] * len(mats),
            out_specs=ANY,
            scratch_shapes=block_scratch(total),
        ),
        out_shape=jax.ShapeDtypeStruct((total, B, B), LOW),
        compiler_params=pltpu.CompilerParams(vmem_limit_bytes=VMEM_BYTES),
        name="unplace_blocks",
    )(order, *mats)


def turn(values, cos, sin_high, sin_low):
    return (
        values * cos
        + pltpu.roll(values, 32, 1) * sin_high
        - pltpu.roll(values, 96, 1) * sin_low
    )


def turn_back(values, cos, sin_high, sin_low):
    return (
        values * cos
        - pltpu.roll(values, 32, 1) * sin_high
        + pltpu.roll(values, 96, 1) * sin_low
    )


def qkv_kernel(scale, h_ref, w_ref, bias_ref, cos_ref, high_ref, low_ref, q_ref, k_ref, v_ref):
    for j in range(w_ref.shape[1] // HD):
        head, part = divmod(j, 3)
        cols = slice(head * HD, head * HD + HD)
        proj = dot(h_ref[...], w_ref[:, j * HD : (j + 1) * HD]) + bias_ref[:, j * HD : (j + 1) * HD]
        if part == 2:
            v_ref[:, cols] = proj.astype(LOW)
            continue
        front = turn(proj[:, :128], cos_ref[...], high_ref[...], low_ref[...])
        turned = jnp.concatenate([front, proj[:, 128:]], axis=1).astype(LOW)
        if part == 0:
            q_ref[:, cols] = (turned.astype(WIDE) * scale).astype(LOW)
        else:
            k_ref[:, cols] = turned


def project_qkv(h1, qkv_w, bias, tables):
    rows, d = h1.shape
    cols = qkv_w.shape[1]
    out_cols = cols // 3
    tile = 512
    row_spec = lambda width: pl.BlockSpec((tile, width), lambda i: (i, 0))
    return pl.pallas_call(
        functools.partial(qkv_kernel, 1.0 / math.sqrt(HD)),
        grid=(rows // tile,),
        in_specs=[row_spec(d), resident((d, cols)), resident((1, cols))] + [row_spec(128)] * 3,
        out_specs=[row_spec(out_cols)] * 3,
        out_shape=[jax.ShapeDtypeStruct((rows, out_cols), LOW)] * 3,
        compiler_params=pltpu.CompilerParams(vmem_limit_bytes=VMEM_BYTES),
        name="project_qkv",
    )(h1, qkv_w, bias, *tables)


def attention_kernel(
    tile,
    start_ref,
    q_ref,
    k_ref,
    v_ref,
    cot_ref,
    out_ref,
    cos_ref,
    high_ref,
    low_ref,
    ctx_ref,
    grad_ref,
    sums_ref,
    p_scr,
    dp_scr,
    dk_scr,
    dv_scr,
):
    step = pl.program_id(1)
    count = pl.num_programs(1)
    scale = 1.0 / math.sqrt(HD)

    @pl.when(step == 0)
    def _():
        dk_scr[...] = jnp.zeros_like(dk_scr)
        dv_scr[...] = jnp.zeros_like(dv_scr)

    def rows(c):
        q = q_ref[...]
        g = dot_nt(cot_ref[...], out_ref[...]).astype(LOW)
        first = start_ref[...]
        top = jnp.full((tile, 1), masked_score, WIDE)
        for j in range(c + 1):
            keys = slice(j * tile, (j + 1) * tile)
            s = dot_nt(q, k_ref[keys, :])
            col = lax.broadcasted_iota(jnp.int32, (tile, tile), 1) + j * tile
            ok = col >= first
            if j == c:
                row = lax.broadcasted_iota(jnp.int32, (tile, tile), 0) + c * tile
                ok = ok & (col <= row)
            s = jnp.where(ok, s, masked_score)
            p_scr[:, keys] = s
            top = jnp.maximum(top, jnp.max(s, axis=1, keepdims=True))
        total = jnp.zeros((tile, 1), WIDE)
        for j in range(c + 1):
            keys = slice(j * tile, (j + 1) * tile)
            e = jnp.exp(p_scr[:, keys] - top)
            p_scr[:, keys] = e
            total = total + jnp.sum(e, axis=1, keepdims=True)
        inverse = 1.0 / total
        ctx = jnp.zeros((tile, HD), WIDE)
        delta = jnp.zeros((tile, 1), WIDE)
        for j in range(c + 1):
            keys = slice(j * tile, (j + 1) * tile)
            p = p_scr[:, keys] * inverse
            p_scr[:, keys] = p
            pb = p.astype(LOW)
            dp = dot_nt(g, v_ref[keys, :])
            dp_scr[:, keys] = dp
            delta = delta + jnp.sum(p * dp, axis=1, keepdims=True)
            ctx = ctx + dot(pb, v_ref[keys, :])
            dv_scr[keys, :] += dot_tn(pb, g)
        ctx_ref[...] = ctx.astype(LOW)
        dq = jnp.zeros((tile, HD), WIDE)
        for j in range(c + 1):
            keys = slice(j * tile, (j + 1) * tile)
            ds = (p_scr[:, keys] * (dp_scr[:, keys] - delta)).astype(LOW)
            dq = dq + dot(ds, k_ref[keys, :])
            dk_scr[keys, :] += dot_tn(ds, q)
        dq = dq * scale
        here = slice(c * tile, (c + 1) * tile)
        front = turn_back(dq[:, :128], cos_ref[here, :], high_ref[here, :], low_ref[here, :])
        grad_ref[here, 0:128] = front.astype(LOW)
        grad_ref[here, 128:HD] = dq[:, 128:].astype(LOW)

    for c in range(dk_scr.shape[0] // tile):
        pl.when(step == c)(functools.partial(rows, c))

    @pl.when(step == count - 1)
    def _():
        dk = dk_scr[...]
        front = turn_back(dk[:, :128], cos_ref[...], high_ref[...], low_ref[...])
        grad_ref[:, HD : HD + 128] = front.astype(LOW)
        grad_ref[:, HD + 128 : 2 * HD] = dk[:, 128:].astype(LOW)
        grad_ref[:, 2 * HD :] = dv_scr[...].astype(LOW)
        total = jnp.sum(grad_ref[...].astype(WIDE), axis=0, keepdims=True)
        sums_ref[...] = jnp.broadcast_to(total, sums_ref.shape)


def attention_both(start, q, k, v, cotangent, od_w, tables):
    rows, cols = q.shape
    d = cotangent.shape[1]
    heads = cols // HD
    tile = 512
    tile_spec = pl.BlockSpec((tile, HD), lambda h, i: (i, h))
    full_spec = pl.BlockSpec((rows, HD), lambda h, i: (0, h))
    flops = heads * rows * rows * HD * 6
    return pl.pallas_call(
        functools.partial(attention_kernel, tile),
        grid=(heads, rows // tile),
        in_specs=[
            pl.BlockSpec((tile, 1), lambda h, i: (i, 0)),
            tile_spec,
            full_spec,
            full_spec,
            pl.BlockSpec((tile, d), lambda h, i: (i, 0)),
            pl.BlockSpec((HD, d), lambda h, i: (h, 0)),
        ]
        + [resident((rows, 128))] * 3,
        out_specs=[
            tile_spec,
            pl.BlockSpec((rows, 3 * HD), lambda h, i: (0, h)),
            pl.BlockSpec((8, 3 * HD), lambda h, i: (0, h)),
        ],
        out_shape=[
            jax.ShapeDtypeStruct((rows, cols), LOW),
            jax.ShapeDtypeStruct((rows, 3 * cols), LOW),
            jax.ShapeDtypeStruct((8, 3 * cols), WIDE),
        ],
        scratch_shapes=[
            pltpu.VMEM((tile, rows), WIDE),
            pltpu.VMEM((tile, rows), WIDE),
            pltpu.VMEM((rows, HD), WIDE),
            pltpu.VMEM((rows, HD), WIDE),
        ],
        compiler_params=pltpu.CompilerParams(vmem_limit_bytes=VMEM_BYTES),
        cost_estimate=pl.CostEstimate(flops=flops, bytes_accessed=30 << 20, transcendentals=0),
        name="attention_both",
    )(start, q, k, v, cotangent, od_w, *tables)


class Line:
    def __init__(self, out, part, got, across, sems):
        self.out, self.part, self.got, self.across = out, part, got, across
        (
            self.up_send,
            self.up_recv,
            self.far_send,
            self.far_recv,
            self.over_send,
            self.over_recv,
            self.down_send,
            self.down_recv,
            self.relay_send,
            self.relay_recv,
            self.own,
        ) = [sems.at[i] for i in range(11)]
        z = lax.axis_index("mp")
        self.inner = (z == 1) | (z == 2)
        self.near = (z >= 2).astype(jnp.int32)
        self.far = 1 - self.near
        self.partner = jnp.where(self.inner, jnp.where(z == 1, 0, 3), jnp.where(z == 0, 1, 2))
        self.other = 3 - z

    def rows(self, pair, which):
        return self.out.at[pl.ds(pl.multiple_of(pair * (2 * SUB) + which * SUB, SUB), SUB), :]

    def greet(self):
        barrier = pltpu.get_barrier_semaphore()
        pl.semaphore_signal(barrier, inc=1, device_id={"mp": self.partner}, device_id_type=MESH)

        @pl.when(self.inner)
        def _():
            pl.semaphore_signal(barrier, inc=1, device_id={"mp": self.other}, device_id_type=MESH)
            pl.semaphore_wait(barrier, 2)

        @pl.when(jnp.logical_not(self.inner))
        def _():
            pl.semaphore_wait(barrier, 1)

    def copy(self, src, dst, send, recv, pair, target):
        return pltpu.make_async_remote_copy(
            src_ref=src,
            dst_ref=dst,
            send_sem=send.at[pair],
            recv_sem=recv.at[pair],
            device_id={"mp": target},
            device_id_type=MESH,
        )

    def up(self, pair):
        return self.copy(self.part.at[pair], self.got.at[pair], self.up_send, self.up_recv, pair, self.partner)

    def far_sum(self, pair):
        return self.copy(
            self.part.at[pair, self.far], self.across.at[pair], self.far_send, self.far_recv, pair, self.other
        )

    def over(self, pair, which):
        src = self.part.at[pair, self.near]
        return self.copy(src, self.rows(pair, which), self.over_send, self.over_recv, pair, self.other)

    def down(self, pair):
        src = self.part.at[pair, self.near]
        return self.copy(
            src, self.rows(pair, self.near), self.down_send, self.down_recv, pair, self.partner
        )

    def relay(self, pair):
        far = self.rows(pair, self.far)
        return self.copy(far, far, self.relay_send, self.relay_recv, pair, self.partner)

    def keep(self, pair):
        src = self.part.at[pair, self.near]
        return pltpu.make_async_copy(src, self.rows(pair, self.near), self.own.at[pair])

    def send_up(self, pair):
        @pl.when(jnp.logical_not(self.inner))
        def _():
            self.up(pair).start()

    def add_far(self, pair):
        self.up(pair).wait_recv()
        far = self.part[pair, self.far].astype(WIDE) + self.got[pair, self.far].astype(WIDE)
        self.part[pair, self.far] = far.astype(LOW)
        self.far_sum(pair).start()

    def finish_near(self, pair, base):
        self.far_sum(pair).wait_recv()
        total = (
            self.part[pair, self.near].astype(WIDE)
            + self.got[pair, self.near].astype(WIDE)
            + self.across[pair].astype(WIDE)
        )
        self.part[pair, self.near] = (base + total).astype(LOW)
        self.over(pair, self.near).start()
        self.down(pair).start()
        self.keep(pair).start()

    def send_relay(self, pair):
        self.over(pair, self.far).wait_recv()
        self.relay(pair).start()

    def drain(self):
        @pl.when(self.inner)
        def _():
            @pl.loop(0, PAIRS)
            def _(pair):
                self.far_sum(pair).wait_send()
                self.over(pair, self.near).wait_send()
                self.down(pair).wait_send()
                self.relay(pair).wait_send()
                self.keep(pair).wait()

        @pl.when(jnp.logical_not(self.inner))
        def _():
            @pl.loop(0, PAIRS)
            def _(pair):
                self.up(pair).wait_send()
                self.down(pair).wait_recv()
                self.relay(pair).wait_recv()

    def tick(self, step, lag, base):
        @pl.when(self.inner & (step >= lag + 2) & (step < lag + 2 + PAIRS))
        def _():
            self.send_relay(step - lag - 2)

        @pl.when(self.inner & (step >= lag + 1) & (step < lag + 1 + PAIRS))
        def _():
            self.finish_near(step - lag - 1, base())

        @pl.when(self.inner & (step >= lag) & (step < lag + PAIRS))
        def _():
            self.add_far(step - lag)


def line_scratch(d):
    return [
        pltpu.VMEM((PAIRS, 2, SUB, d), LOW),
        pltpu.VMEM((PAIRS, 2, SUB, d), LOW),
        pltpu.VMEM((PAIRS, SUB, d), LOW),
        pltpu.SemaphoreType.DMA((11, PAIRS)),
    ]


def now(step):
    return jnp.minimum(step, STEPS - 1)


def row_block(width):
    return pl.BlockSpec((STEP, width), lambda i: (now(i), 0))


def base_block(width, lag):
    return pl.BlockSpec((2 * SUB, width), lambda i: (jnp.clip(i - lag - 1, 0, PAIRS - 1), 0))


def lane(start):
    return pl.ds(pl.multiple_of(start, B), B)


def gelu_parts(z):
    e = jnp.exp(z * z * -0.5)
    t = 1.0 / (1.0 + jnp.abs(z) * (0.3275911 * math.sqrt(0.5)))
    poly = t * (
        0.5 * 0.254829592
        + t
        * (
            0.5 * -0.284496736
            + t * (0.5 * 1.421413741 + t * (0.5 * -1.453152027 + t * (0.5 * 1.061405429)))
        )
    )
    below = poly * e
    cdf = jnp.where(z >= 0, 1.0 - below, below)
    return cdf, e * (1.0 / math.sqrt(2.0 * math.pi))


def store_part(part_ref, step, cols, value):
    part_ref[pl.ds(step * 2, 2), :, :, cols] = value.astype(LOW).reshape(2, 2, SUB, value.shape[1])


FORWARD_LAG = 2
FORWARD_GRID = FORWARD_LAG + PAIRS + 2


def weight_unit(a_t, b_ref, cols, stage, slot):
    for n in range(cols // 512):
        part = slice(n * 512, (n + 1) * 512)
        stage[pl.ds(pl.multiple_of(slot * B, B), B), part] = dot(a_t, b_ref[:, part]).astype(LOW)


def forward_kernel(
    h_ref,
    g_ref,
    ctx_ref,
    x_ref,
    bias_ref,
    shift_ref,
    up_hbm,
    od_hbm,
    h1_hbm,
    h2_hbm,
    ctx_hbm,
    cot_hbm,
    qg_hbm,
    out_ref,
    hg_hbm,
    wq_hbm,
    wo_hbm,
    wu_hbm,
    sums_ref,
    up_buf,
    od_buf,
    act_all,
    hg_all,
    part,
    got,
    across,
    sems,
    load_sem,
    panel_sem,
    stage_sem,
    hg_sem,
):
    step = pl.program_id(0)
    line = Line(out_ref, part, got, across, sems)
    heads = ctx_ref.shape[1]
    rows, units = act_all.shape
    qkv_cols = qg_hbm.shape[1]
    width = 512
    tiles = units // width
    stage = od_buf.at[pl.ds(rows, 2 * B), :]

    def load_up(n):
        cols = pl.ds(n * width, width)
        return pltpu.make_async_copy(up_hbm.at[:, cols], up_buf.at[:, cols], load_sem.at[n])

    def load_down(n):
        part_rows = pl.ds(heads + n * width, width)
        return pltpu.make_async_copy(
            od_hbm.at[part_rows, :], od_buf.at[part_rows, :], load_sem.at[tiles + n]
        )

    def load_out():
        part_rows = pl.ds(0, heads)
        return pltpu.make_async_copy(
            od_hbm.at[part_rows, :], od_buf.at[part_rows, :], load_sem.at[2 * tiles]
        )

    def load_cot():
        return pltpu.make_async_copy(
            cot_hbm, od_buf.at[pl.ds(0, rows), :], load_sem.at[2 * tiles + 1]
        )

    def load_qg():
        return pltpu.make_async_copy(
            qg_hbm, up_buf.at[:, pl.ds(0, qkv_cols)], load_sem.at[2 * tiles + 2]
        )

    def panel_cols(slot):
        return lane(qkv_cols + slot * B)

    def panel(src, i, slot):
        return pltpu.make_async_copy(
            src.at[:, lane(i * B)], up_buf.at[:, panel_cols(slot)], panel_sem.at[slot]
        )

    def store_hg(i):
        part_rows = pl.ds(pl.multiple_of(i * STEP, STEP), STEP)
        return pltpu.make_async_copy(
            hg_all.at[part_rows, :], hg_hbm.at[part_rows, :], hg_sem.at[i]
        )

    def stage_out(dst, row, cols, slot):
        return pltpu.make_async_copy(
            stage.at[lane(slot * B), pl.ds(0, cols)],
            dst.at[lane(row), :],
            stage_sem.at[slot],
        )

    @pl.when(step == 0)
    def _():
        for n in range(tiles):
            load_up(n).start()
            load_down(n).start()
        load_out().start()
        line.greet()
        sums_ref[...] = jnp.zeros_like(sums_ref)

    @pl.when(step < STEPS)
    def _():
        here = pl.ds(pl.multiple_of(step * STEP, STEP), STEP)
        for n in range(tiles):
            cols = slice(n * width, (n + 1) * width)

            @pl.when(step == 0)
            def _():
                load_up(n).wait()
                load_down(n).wait()

            hidden = dot(h_ref[...], up_buf[:, cols]) + bias_ref[:, cols]
            act_grad = dot_nt(g_ref[...], od_buf[heads + n * width : heads + (n + 1) * width, :])
            cdf, density = gelu_parts(hidden)
            act_all[here, cols] = (hidden * cdf).astype(LOW)
            grad = (act_grad * (cdf + hidden * density)).astype(LOW)
            hg_all[here, cols] = grad
            sums_ref[0:1, cols] += jnp.sum(grad.astype(WIDE), axis=0, keepdims=True)

        @pl.when(step == 0)
        def _():
            load_out().wait()

        store_hg(step).start()
        for n in range(od_buf.shape[1] // width):
            cols = slice(n * width, (n + 1) * width)
            value = dot(ctx_ref[...], od_buf[:heads, cols]) + dot(
                act_all[here, :], od_buf[heads:, cols]
            )
            store_part(part, step, cols, value)
        for s in range(2):
            line.send_up(step * 2 + s)

    @pl.when(step == STEPS - 1)
    def _():
        panel(h2_hbm, 0, 0).start()
        load_cot().start()
        load_qg().start()

    def unit(index, a_t, b_ref, cols, dst, row):
        slot = index % 2

        @pl.when(index >= 2)
        def _():
            stage_out(dst, row, cols, slot).wait()

        weight_unit(a_t, b_ref, cols, stage, slot)
        stage_out(dst, row, cols, slot).start()

    def settle(dst, cols):
        for slot in range(2):
            stage_out(dst, 0, cols, slot).wait()

    @pl.when((step == 8) | (step == 9))
    def _():
        @pl.loop(0, 4)
        def _(k):
            i = (step - 8) * 4 + k
            panel(h2_hbm, i, i % 2).wait()

            @pl.when(i < 7)
            def _():
                panel(h2_hbm, i + 1, (i + 1) % 2).start()

            unit(i, up_buf[:, panel_cols(i % 2)].T, hg_all, units, wu_hbm, i * B)

    @pl.when(step == 10)
    def _():
        settle(wu_hbm, units)
        load_cot().wait()

    @pl.when((step == 10) | (step == 11))
    def _():
        @pl.loop(0, 4)
        def _(k):
            i = (step - 10) * 4 + k
            cot = od_buf.at[pl.ds(0, rows), :]
            unit(i, act_all[:, lane(i * B)].T, cot, units, wo_hbm, heads + i * B)

    @pl.when(step == 12)
    def _():
        settle(wo_hbm, units)
        for j in range(2):
            panel(ctx_hbm, j, j).start()
        load_qg().wait()
        for j in range(2):
            panel(ctx_hbm, j, j).wait()

        @pl.loop(0, 2)
        def _(j):
            cot = od_buf.at[pl.ds(0, rows), :]
            unit(j, up_buf[:, panel_cols(j)].T, cot, units, wo_hbm, j * B)

        settle(wo_hbm, units)
        panel(h1_hbm, 0, 0).start()

    @pl.when((step == 13) | (step == 14))
    def _():
        @pl.loop(0, 4)
        def _(k):
            i = (step - 13) * 4 + k
            panel(h1_hbm, i, i % 2).wait()

            @pl.when(i < 7)
            def _():
                panel(h1_hbm, i + 1, (i + 1) % 2).start()

            grads = up_buf.at[:, pl.ds(0, qkv_cols)]
            unit(i, up_buf[:, panel_cols(i % 2)].T, grads, qkv_cols, wq_hbm, i * B)

    @pl.when(step == 15)
    def _():
        settle(wq_hbm, qkv_cols)

        @pl.loop(0, STEPS)
        def _(i):
            store_hg(i).wait()

    def base():
        near = pl.ds(pl.multiple_of(line.near * SUB, SUB), SUB)
        return x_ref[near, :].astype(WIDE) + shift_ref[...]

    line.tick(step, FORWARD_LAG, base)

    @pl.when(step == FORWARD_GRID - 1)
    def _():
        line.drain()


def forward_line(h1, h2, cotangent, ctx, qkv_grad, tokens, up_w, od_w, bias, shift):
    rows, d = tokens.shape
    units = up_w.shape[1]
    qkv_cols = qkv_grad.shape[1]
    return pl.pallas_call(
        forward_kernel,
        grid=(FORWARD_GRID,),
        in_specs=[
            row_block(d),
            row_block(d),
            row_block(ctx.shape[1]),
            base_block(d, FORWARD_LAG),
            resident(bias.shape),
            resident(shift.shape),
        ]
        + [ANY] * 7,
        out_specs=[ANY] * 5 + [pl.BlockSpec((8, units), lambda i: (0, 0))],
        out_shape=[
            jax.ShapeDtypeStruct((rows, d), LOW),
            jax.ShapeDtypeStruct((rows, units), LOW),
            jax.ShapeDtypeStruct((d, qkv_cols), LOW),
            jax.ShapeDtypeStruct(od_w.shape, LOW),
            jax.ShapeDtypeStruct((d, units), LOW),
            jax.ShapeDtypeStruct((8, units), WIDE),
        ],
        scratch_shapes=[
            pltpu.VMEM(up_w.shape, LOW),
            pltpu.VMEM(od_w.shape, LOW),
            pltpu.VMEM((rows, units), LOW),
            pltpu.VMEM((rows, units), LOW),
        ]
        + line_scratch(d)
        + [
            pltpu.SemaphoreType.DMA((11,)),
            pltpu.SemaphoreType.DMA((2,)),
            pltpu.SemaphoreType.DMA((2,)),
            pltpu.SemaphoreType.DMA((STEPS,)),
        ],
        compiler_params=pltpu.CompilerParams(
            vmem_limit_bytes=FORWARD_VMEM, collective_id=1, has_side_effects=True
        ),
        cost_estimate=pl.CostEstimate(
            flops=200_000_000_000, bytes_accessed=80 << 20, transcendentals=0
        ),
        name="forward_line",
    )(h2, cotangent, ctx, tokens, bias, shift, up_w, od_w, h1, h2, ctx, cotangent, qkv_grad)


BACKWARD_LAG = 1
BACKWARD_GRID = BACKWARD_LAG + PAIRS + 2


class Spread:
    def __init__(self, own, along_mp, along_dp, sems):
        self.own = own
        self.stages = [
            ("dp", along_dp, sems.at[0], sems.at[1]),
            ("mp", along_mp, sems.at[2], sems.at[3]),
        ]

    def others(self, stage):
        axis, buf, send, recv = self.stages[stage]
        me = lax.axis_index(axis)
        return axis, buf, send, recv, me, [lax.rem(me + k, buf.shape[0]) for k in range(1, buf.shape[0])]

    def greet(self):
        barrier = pltpu.get_barrier_semaphore()
        count = 0
        for stage in range(2):
            axis, _, _, _, _, others = self.others(stage)
            for other in others:
                pl.semaphore_signal(barrier, inc=1, device_id={axis: other}, device_id_type=MESH)
            count += len(others)
        pl.semaphore_wait(barrier, count)

    def copies(self, stage):
        axis, buf, send, recv, me, others = self.others(stage)
        return [
            (
                pltpu.make_async_remote_copy(
                    src_ref=self.own,
                    dst_ref=buf.at[me],
                    send_sem=send.at[k],
                    recv_sem=recv.at[me],
                    device_id={axis: other},
                    device_id_type=MESH,
                ),
                pltpu.make_async_remote_copy(
                    src_ref=self.own,
                    dst_ref=buf.at[other],
                    send_sem=send.at[k],
                    recv_sem=recv.at[other],
                    device_id={axis: other},
                    device_id_type=MESH,
                ),
            )
            for k, other in enumerate(others)
        ]

    def start(self, stage):
        _, buf, _, _, me, _ = self.others(stage)
        buf[me] = self.own[...]
        for out, _ in self.copies(stage):
            out.start()

    def finish(self, stage):
        _, buf, _, _, _, _ = self.others(stage)
        for out, back in self.copies(stage):
            out.wait_send()
            back.wait_recv()
        total = buf[0]
        for i in range(1, buf.shape[0]):
            total = total + buf[i]
        return total


def backward_kernel(
    qg_ref,
    hg_ref,
    x_ref,
    g_ref,
    qkv_ref,
    up_ref,
    one_ref,
    two_ref,
    sums_in,
    sums_ref,
    out_ref,
    gc_scr,
    xhat_scr,
    own,
    along_mp,
    along_dp,
    spread_sems,
    part,
    got,
    across,
    sems,
):
    step = pl.program_id(0)
    line = Line(out_ref, part, got, across, sems)
    spread = Spread(own, along_mp, along_dp, spread_sems)
    d = x_ref.shape[1]
    width = 512

    @pl.when(step == 0)
    def _():
        spread.greet()
        own[...] = sums_in[...]

    @pl.when(step < STEPS)
    def _():
        x = x_ref[...].astype(WIDE)
        center = x - jnp.mean(x, axis=1, keepdims=True)
        scale = lax.rsqrt(jnp.mean(center * center, axis=1, keepdims=True) + norm_eps)
        xhat_scr[...] = center * scale
        mean = jnp.zeros((STEP, 1), WIDE)
        slope = jnp.zeros((STEP, 1), WIDE)
        for n in range(d // width):
            cols = slice(n * width, (n + 1) * width)
            e1 = dot_nt(qg_ref[...], qkv_ref[cols, :])
            e2 = dot_nt(hg_ref[...], up_ref[cols, :])
            xhat = xhat_scr[:, cols]
            gc = e1 * one_ref[:, cols] + e2 * two_ref[:, cols]
            gc_scr[:, cols] = gc
            mean = mean + jnp.sum(gc, axis=1, keepdims=True)
            slope = slope + jnp.sum(gc * xhat, axis=1, keepdims=True)
            own[0:1, cols] += jnp.sum(e1 * xhat, axis=0, keepdims=True)
            own[1:2, cols] += jnp.sum(e1, axis=0, keepdims=True)
            own[2:3, cols] += jnp.sum(e2 * xhat, axis=0, keepdims=True)
            own[3:4, cols] += jnp.sum(e2, axis=0, keepdims=True)
        mean = mean * (1.0 / d)
        slope = slope * (1.0 / d)
        for n in range(d // width):
            cols = slice(n * width, (n + 1) * width)
            value = (gc_scr[:, cols] - mean - xhat_scr[:, cols] * slope) * scale
            store_part(part, step, cols, value)
        for s in range(2):
            line.send_up(step * 2 + s)

    @pl.when(step == STEPS)
    def _():
        spread.start(0)

    @pl.when(step == STEPS + 4)
    def _():
        own[...] = spread.finish(0)
        spread.start(1)

    def base():
        near = pl.ds(pl.multiple_of(line.near * SUB, SUB), SUB)
        return g_ref[near, :].astype(WIDE)

    line.tick(step, BACKWARD_LAG, base)

    @pl.when(step == BACKWARD_GRID - 1)
    def _():
        line.drain()
        total = spread.finish(1)
        row = lax.broadcasted_iota(jnp.int32, total.shape, 0)
        sums_ref[...] = jnp.where(row < 4, total, own[...])


def backward_line(qkv_grad, hidden_grad, tokens, cotangent, qkv_w, up_w, gain_one, gain_two, sums):
    rows, d = tokens.shape
    small = sums.shape
    return pl.pallas_call(
        backward_kernel,
        grid=(BACKWARD_GRID,),
        in_specs=[
            row_block(qkv_grad.shape[1]),
            row_block(hidden_grad.shape[1]),
            row_block(d),
            base_block(d, BACKWARD_LAG),
            resident(qkv_w.shape),
            resident(up_w.shape),
            resident((1, d)),
            resident((1, d)),
            resident(small),
        ],
        out_specs=[pl.BlockSpec(small, lambda i: (0, 0)), ANY],
        out_shape=[jax.ShapeDtypeStruct(small, WIDE), jax.ShapeDtypeStruct((rows, d), LOW)],
        scratch_shapes=[
            pltpu.VMEM((STEP, d), WIDE),
            pltpu.VMEM((STEP, d), WIDE),
            pltpu.VMEM(small, WIDE),
            pltpu.VMEM((4,) + small, WIDE),
            pltpu.VMEM((8,) + small, WIDE),
            pltpu.SemaphoreType.DMA((4, 8)),
        ]
        + line_scratch(d),
        compiler_params=pltpu.CompilerParams(
            vmem_limit_bytes=VMEM_BYTES, collective_id=2, has_side_effects=True
        ),
        cost_estimate=pl.CostEstimate(
            flops=200_000_000_000, bytes_accessed=60 << 20, transcendentals=0
        ),
        name="backward_line",
    )(
        qkv_grad, hidden_grad, tokens, cotangent, qkv_w, up_w, gain_one, gain_two, sums
    )


def halves(values):
    high = values.astype(LOW)
    return high, (values - high.astype(WIDE)).astype(LOW)


def shampoo_kernel(
    g_ref,
    w_ref,
    ls_ref,
    rs_ref,
    lr_ref,
    rr_ref,
    one_in,
    two_in,
    grad_ref,
    left_ref,
    right_ref,
    weight_ref,
    one_out,
    two_out,
    hold,
    sems,
):
    step = pl.program_id(0)
    pairs = ((one_in, one_out), (two_in, two_out))
    fetch = [pltpu.make_async_copy(a, hold.at[i], sems.at[0, i]) for i, (a, _) in enumerate(pairs)]
    store = [pltpu.make_async_copy(hold.at[i], b, sems.at[1, i]) for i, (_, b) in enumerate(pairs)]

    @pl.when(step == 0)
    def _():
        for copy in fetch:
            copy.start()

    for i in range(2):

        @pl.when(step == pl.num_programs(0) * (i + 1) // 3)
        def _():
            fetch[i].wait()
            store[i].start()

    @pl.when(step == pl.num_programs(0) - 1)
    def _():
        for copy in store:
            copy.wait()

    for n in range(g_ref.shape[0]):
        g = g_ref[n]
        grad_ref[n] = g.astype(WIDE)
        left_ref[n] = 0.5 * ls_ref[n] + 0.5 * dot_nt(g, g)
        right_ref[n] = 0.5 * rs_ref[n] + 0.5 * dot_tn(g, g)
        l_high, l_low = halves(lr_ref[n])
        r_high, r_low = halves(rr_ref[n])
        d_high, d_low = halves(dot(l_high, g) + dot(l_low, g))
        direction = dot(d_high, r_high) + dot(d_low, r_high) + dot(d_high, r_low)
        weight = w_ref[n]
        size = 1.0 / (B * B)
        weight_size = jnp.sqrt(jnp.sum(weight * weight, keepdims=True) * size)
        step_size = jnp.sqrt(jnp.sum(direction * direction, keepdims=True) * size + 1e-06)
        weight_ref[n] = weight - direction * (step_share * weight_size / step_size)


def shampoo(grads, weights, left_stat, right_stat, left_root, right_root, one, two):
    count = grads.shape[0]
    group = 2
    spec = pl.BlockSpec((group, B, B), lambda i: (i, 0, 0))
    return pl.pallas_call(
        shampoo_kernel,
        grid=(count // group,),
        in_specs=[spec] * 6 + [ANY] * 2,
        out_specs=[spec] * 4 + [ANY] * 2,
        out_shape=[jax.ShapeDtypeStruct((count, B, B), WIDE)] * 4
        + [jax.ShapeDtypeStruct(one.shape, one.dtype)] * 2,
        scratch_shapes=[
            pltpu.VMEM((2,) + one.shape, one.dtype),
            pltpu.SemaphoreType.DMA((2, 2)),
        ],
        compiler_params=pltpu.CompilerParams(vmem_limit_bytes=VMEM_BYTES),
        name="shampoo",
    )(grads, weights, left_stat, right_stat, left_root, right_root, one, two)


def per_device_line(
    tokens,
    cotangent,
    seq_len,
    seq_device,
    owner_map,
    weight_blocks,
    left_stat,
    right_stat,
    left_root,
    right_root,
    vectors,
    vector_stat,
    unit_bias,
    unit_stat,
):
    groups = lax.axis_size("mp")
    device = lax.axis_index("dp")
    row_count, d = tokens.shape
    qkv_cols = 3 * d // groups
    head_cols = d // groups
    unit_cols = FF // groups
    gathered = lax.all_gather(weight_blocks[0].astype(LOW), "dp", axis=0, tiled=True)

    segment, position = segment_layout(seq_len, seq_device, device, row_count)
    start = (jnp.arange(row_count, dtype=jnp.int32) - position)[:, None]
    frequency = 10000.0 ** (-2.0 * jnp.arange(ROT // 2, dtype=WIDE) / ROT)
    angles = position.astype(WIDE)[:, None] * frequency[None, :]
    cos, sin = jnp.cos(angles), jnp.sin(angles)
    pad = jnp.zeros((row_count, 128 - ROT), WIDE)
    empty = jnp.zeros_like(sin)
    tables = (
        jnp.concatenate([cos, cos, pad + 1.0], axis=1),
        jnp.concatenate([empty, sin, pad], axis=1),
        jnp.concatenate([sin, empty, pad], axis=1),
    )
    inputs = tokens.astype(WIDE)
    normed_one = layer_norm(inputs, vectors[0], vectors[1]).astype(LOW)
    normed_two = layer_norm(inputs, vectors[2], vectors[3]).astype(LOW)
    out_sum = jnp.sum(cotangent.astype(WIDE), axis=0, keepdims=True)
    normed_one, normed_two, out_sum = lax.optimization_barrier((normed_one, normed_two, out_sum))
    shift = (vectors[4] + vectors[5])[None]
    unit_shift = unit_bias[0]

    shapes = ((d, qkv_cols), (head_cols + unit_cols, d), (d, unit_cols))
    blocks = [(a // B) * (b // B) for a, b in ((d, qkv_cols), (head_cols, d), (d, unit_cols))]
    order = jnp.concatenate(
        [
            owner_map[: blocks[0] + blocks[1]],
            owner_map[blocks[0] + blocks[1] + blocks[2] :],
            owner_map[blocks[0] + blocks[1] : blocks[0] + blocks[1] + blocks[2]],
        ]
    )
    qkv_w, od_w, up_w = place_blocks(gathered, order, shapes)

    q, k, v = project_qkv(normed_one, qkv_w, unit_shift[None, :qkv_cols], tables)
    ctx, qkv_grad, qkv_sums = attention_both(start, q, k, v, cotangent, od_w, tables)
    block_out, hidden_grad, qkv_wg, od_wg, up_wg, hidden_sums = forward_line(
        normed_one,
        normed_two,
        cotangent,
        ctx,
        qkv_grad,
        tokens,
        up_w,
        od_w,
        unit_shift[None, qkv_cols:],
        shift,
    )
    slots = unplace_blocks([qkv_wg, od_wg, up_wg], order)
    owned = lax.psum_scatter(slots, "dp", scatter_dimension=0, tiled=True)
    qkv_grad, hidden_grad, slots = lax.optimization_barrier((qkv_grad, hidden_grad, slots))
    sums = jnp.concatenate(
        [
            jnp.zeros((4, d), WIDE),
            out_sum,
            jnp.pad(qkv_sums[:1], ((0, 0), (0, d - qkv_cols))),
            jnp.pad(hidden_sums[:1], ((0, 0), (0, d - unit_cols))),
            jnp.zeros((1, d), WIDE),
        ],
        axis=0,
    )
    sums, input_grad = backward_line(
        qkv_grad,
        hidden_grad,
        tokens,
        cotangent,
        qkv_w,
        up_w,
        vectors[0:1],
        vectors[2:3],
        sums,
    )
    block_grad, left_new, right_new, weight_new, block_out, input_grad = shampoo(
        owned,
        weight_blocks[0],
        left_stat[0],
        right_stat[0],
        left_root[0],
        right_root[0],
        block_out,
        input_grad,
    )
    vector_grad = jnp.concatenate([sums[:5], sums[4:5]], axis=0)
    unit_grad = jnp.concatenate([sums[5, :qkv_cols], sums[6, :unit_cols]])
    vector_stat_new, vector_new = vector_update(vectors, vector_stat, vector_grad)
    unit_stat_new, unit_new = vector_update(unit_shift, unit_stat[0], unit_grad)
    return (
        block_out,
        input_grad,
        block_grad[None],
        left_new[None],
        right_new[None],
        weight_new[None],
        vector_grad,
        vector_stat_new,
        vector_new,
        unit_grad[None],
        unit_stat_new[None],
        unit_new[None],
    )


def solution(mesh):
    placed = (
        P("dp", None),
        P("dp", None),
        P(),
        P(),
        P(),
        P("mp", "dp", None, None),
        P("mp", "dp", None, None),
        P("mp", "dp", None, None),
        P("mp", "dp", None, None),
        P("mp", "dp", None, None),
        P(),
        P(),
        P("mp", None),
        P("mp", None),
    )
    body = per_device
    if mesh.shape["dp"] == 8 and mesh.shape["mp"] == 4:
        body = per_device_line
    return jax.shard_map(
        body,
        mesh=mesh,
        in_specs=placed,
        out_specs=(
            P("dp", None),
            P("dp", None),
            P("mp", "dp", None, None),
            P("mp", "dp", None, None),
            P("mp", "dp", None, None),
            P("mp", "dp", None, None),
            P(),
            P(),
            P(),
            P("mp", None),
            P("mp", None),
            P("mp", None),
        ),
        check_vma=False,
    )
```

```python
import functools
import math

import jax
import jax.numpy as jnp
from jax import lax
from jax.experimental import pallas as pl
from jax.experimental.pallas import tpu as pltpu
from jax.sharding import PartitionSpec as P

D = 2048
HEADS = 8
HD = 256
ROT = 64
FF = 8192
B = 256


highest = lax.Precision.HIGHEST
norm_eps = 1e-05
step_share = 0.5
vector_rate = 0.15
masked_score = -1e30


def layer_norm(values, gain, shift):
    center = values - jnp.mean(values, axis=-1, keepdims=True)
    spread = jnp.mean(center * center, axis=-1, keepdims=True)
    return center * lax.rsqrt(spread + norm_eps) * gain + shift


def gelu_exact(values):
    return jax.nn.gelu(values, approximate=False)


def segment_layout(seq_len, seq_device, device, row_count):
    is_mine = seq_device == device
    lengths = jnp.where(is_mine, seq_len, 0)
    seq_ends = jnp.cumsum(lengths)
    row_index = jnp.arange(row_count, dtype=jnp.int32)
    passed = is_mine[None, :] & (seq_ends[None, :] <= row_index[:, None])
    segment = jnp.sum(passed.astype(jnp.int32), axis=1)
    seq_start = jnp.max(jnp.where(passed, seq_ends[None, :], 0), axis=1)
    return (segment, row_index - seq_start)


def rotary_tables(position):
    half_rot = ROT // 2
    frequency = 10000.0 ** (-2.0 * jnp.arange(half_rot, dtype=jnp.float32) / ROT)
    angles = position.astype(jnp.float32)[:, None] * frequency[None, :]
    cosine_table = jnp.concatenate([jnp.cos(angles), jnp.cos(angles)], axis=1)
    sine_table = jnp.concatenate([jnp.sin(angles), jnp.sin(angles)], axis=1)
    return (cosine_table, sine_table)


def rotate(values, cosine_table, sine_table):
    rot_dims = cosine_table.shape[1]
    half_rot = rot_dims // 2
    leading = values[..., :rot_dims]
    turned = jnp.concatenate([-leading[..., half_rot:], leading[..., :half_rot]], axis=-1)
    rotated = leading * cosine_table[:, None, :] + turned * sine_table[:, None, :]
    return jnp.concatenate([rotated, values[..., rot_dims:]], axis=-1)


def blocks_to_matrix(blocks, across):
    down_count = blocks.shape[0] // across
    return (
        blocks.reshape(down_count, across, B, B)
        .transpose(0, 2, 1, 3)
        .reshape(down_count * B, across * B)
    )


def matrix_to_blocks(matrix):
    down_count = matrix.shape[0] // B
    across = matrix.shape[1] // B
    return (
        matrix.reshape(down_count, B, across, B)
        .transpose(0, 2, 1, 3)
        .reshape(down_count * across, B, B)
    )


def split_blocks(blocks, qkv_cols, head_cols, unit_cols):
    qkv_end = D // B * (qkv_cols // B)
    out_end = qkv_end + head_cols // B * (D // B)
    up_end = out_end + D // B * (unit_cols // B)
    qkv_w = blocks_to_matrix(blocks[:qkv_end], qkv_cols // B)
    out_w = blocks_to_matrix(blocks[qkv_end:out_end], D // B)
    up_w = blocks_to_matrix(blocks[out_end:up_end], unit_cols // B)
    down_w = blocks_to_matrix(blocks[up_end:], D // B)
    return (qkv_w, out_w, up_w, down_w)


def apply_step(weight, direction):
    weight_size = jnp.sqrt(jnp.mean(weight * weight, axis=(-2, -1), keepdims=True))
    step_size = jnp.sqrt(jnp.mean(direction * direction, axis=(-2, -1), keepdims=True) + 1e-06)
    return weight - step_share * weight_size * direction / step_size


def vector_update(values, old_stat, gradient):
    new_stat = 0.5 * old_stat + 0.5 * gradient * gradient
    return (new_stat, values - vector_rate * gradient * lax.rsqrt(new_stat))


def block_mask(block_segment, block_row, segment, column):
    return (block_segment[:, None] == segment[None, :]) & (column[None, :] <= block_row[:, None])


def attention_forward(queries, keys_low, values_low, segment):
    row_count, head_count, head_dim = queries.shape
    block_rows = min(512, row_count)
    block_count = row_count // block_rows
    score_scale = 1.0 / math.sqrt(head_dim)
    column = jnp.arange(row_count, dtype=jnp.int32)

    def one_block(inputs):
        block_query, block_segment, block_row = inputs
        scores = (
            jnp.einsum("qhd,khd->hqk", block_query, keys_low, preferred_element_type=jnp.float32)
            * score_scale
        )
        scores = jnp.where(
            block_mask(block_segment, block_row, segment, column)[None], scores, masked_score
        )
        log_total = jax.nn.logsumexp(scores, axis=-1)
        weights = jnp.exp(scores - log_total[:, :, None]).astype(jnp.bfloat16)
        context = jnp.einsum(
            "hqk,khd->qhd", weights, values_low, preferred_element_type=jnp.float32
        )
        return (context, log_total)

    contexts, log_totals = lax.map(
        one_block,
        (
            queries.reshape(block_count, block_rows, head_count, head_dim),
            segment.reshape(block_count, block_rows),
            column.reshape(block_count, block_rows),
        ),
    )
    return (contexts.reshape(row_count, head_count, head_dim), log_totals)


def attention_backward(queries, keys_low, values_low, context_grad, log_totals, segment):
    row_count, head_count, head_dim = queries.shape
    block_rows = min(512, row_count)
    block_count = row_count // block_rows
    score_scale = 1.0 / math.sqrt(head_dim)
    column = jnp.arange(row_count, dtype=jnp.int32)

    def one_block(totals, inputs):
        key_grad, value_grad = totals
        block_query, block_grad, block_total, block_segment, block_row = inputs
        scores = (
            jnp.einsum("qhd,khd->hqk", block_query, keys_low, preferred_element_type=jnp.float32)
            * score_scale
        )
        scores = jnp.where(
            block_mask(block_segment, block_row, segment, column)[None], scores, masked_score
        )
        probs = jnp.exp(scores - block_total[:, :, None])
        weights = probs.astype(jnp.bfloat16)
        prob_grad = jnp.einsum(
            "qhd,khd->hqk", block_grad, values_low, preferred_element_type=jnp.float32
        )
        delta = jnp.sum(probs * prob_grad, axis=-1, keepdims=True)
        score_grad = (probs * (prob_grad - delta)).astype(jnp.bfloat16)
        query_grad = (
            jnp.einsum("hqk,khd->qhd", score_grad, keys_low, preferred_element_type=jnp.float32)
            * score_scale
        )
        key_grad = (
            key_grad
            + jnp.einsum(
                "hqk,qhd->khd", score_grad, block_query, preferred_element_type=jnp.float32
            )
            * score_scale
        )
        value_grad = value_grad + jnp.einsum(
            "hqk,qhd->khd", weights, block_grad, preferred_element_type=jnp.float32
        )
        return ((key_grad, value_grad), query_grad)

    zeros_start = jnp.zeros((row_count, head_count, head_dim), jnp.float32)
    (key_grad, value_grad), query_grad = lax.scan(
        one_block,
        (zeros_start, zeros_start),
        (
            queries.reshape(block_count, block_rows, head_count, head_dim),
            context_grad.reshape(block_count, block_rows, head_count, head_dim),
            log_totals,
            segment.reshape(block_count, block_rows),
            column.reshape(block_count, block_rows),
        ),
    )
    return (query_grad.reshape(row_count, head_count, head_dim), key_grad, value_grad)


def per_device(
    tokens,
    cotangent,
    seq_len,
    seq_device,
    owner_map,
    weight_blocks,
    left_stat,
    right_stat,
    left_root,
    right_root,
    vectors,
    vector_stat,
    unit_bias,
    unit_stat,
):
    groups = lax.axis_size("mp")
    device = lax.axis_index("dp")
    row_count = tokens.shape[0]
    heads_here = HEADS // groups
    qkv_cols = 3 * D // groups
    head_cols = D // groups
    unit_cols = FF // groups
    slot_count = weight_blocks.shape[1]
    sent_blocks = weight_blocks[0].astype(jnp.bfloat16)
    gathered = lax.all_gather(sent_blocks, "dp", axis=0, tiled=True)
    qkv_w, out_w, up_w, down_w = split_blocks(gathered[owner_map], qkv_cols, head_cols, unit_cols)
    segment, position = segment_layout(seq_len, seq_device, device, row_count)
    cosine_table, sine_table = rotary_tables(position)
    unit_shift = unit_bias[0]
    inputs = tokens.astype(jnp.float32)
    normed_one = layer_norm(inputs, vectors[0], vectors[1]).astype(jnp.bfloat16)
    normed_two = layer_norm(inputs, vectors[2], vectors[3]).astype(jnp.bfloat16)
    qkv_proj = (
        jnp.dot(normed_one, qkv_w, preferred_element_type=jnp.float32) + unit_shift[:qkv_cols]
    )
    qkv_proj = qkv_proj.reshape(row_count, heads_here, 3, HD)

    def turn_pair(values):
        return rotate(values.reshape(row_count, 2 * heads_here, HD), cosine_table, sine_table)

    turned, turn_back = jax.vjp(turn_pair, qkv_proj[:, :, :2])
    turned = turned.reshape(row_count, heads_here, 2, HD).astype(jnp.bfloat16)
    queries = turned[:, :, 0]
    keys_low = turned[:, :, 1]
    values_low = qkv_proj[:, :, 2].astype(jnp.bfloat16)
    context, log_totals = attention_forward(queries, keys_low, values_low, segment)
    context_low = context.reshape(row_count, head_cols).astype(jnp.bfloat16)
    hidden = jnp.dot(normed_two, up_w, preferred_element_type=jnp.float32) + unit_shift[qkv_cols:]
    active, gelu_back = jax.vjp(gelu_exact, hidden)
    active_low = active.astype(jnp.bfloat16)
    partial_out = jnp.dot(context_low, out_w, preferred_element_type=jnp.float32) + jnp.dot(
        active_low, down_w, preferred_element_type=jnp.float32
    )
    branch = lax.psum(partial_out.astype(jnp.bfloat16), "mp").astype(jnp.float32)
    block_out = (inputs + branch + (vectors[4] + vectors[5])).astype(jnp.bfloat16)
    grad_full = cotangent.astype(jnp.float32)
    act_grad = jnp.einsum("td,fd->tf", cotangent, down_w, preferred_element_type=jnp.float32)
    hidden_grad = gelu_back(act_grad)[0].astype(jnp.bfloat16)
    context_grad = jnp.einsum(
        "td,id->ti", cotangent, out_w, preferred_element_type=jnp.float32
    ).astype(jnp.bfloat16)
    query_grad, key_grad, value_grad = attention_backward(
        queries,
        keys_low,
        values_low,
        context_grad.reshape(row_count, heads_here, HD),
        log_totals,
        segment,
    )
    pair_grad = turn_back(
        jnp.stack([query_grad, key_grad], axis=2).reshape(row_count, 2 * heads_here, HD)
    )[0]
    qkv_grad = (
        jnp.concatenate([pair_grad, value_grad[:, :, None]], axis=2)
        .reshape(row_count, qkv_cols)
        .astype(jnp.bfloat16)
    )
    one_grad = jnp.einsum("te,de->td", qkv_grad, qkv_w, preferred_element_type=jnp.float32)
    two_grad = jnp.einsum("tf,df->td", hidden_grad, up_w, preferred_element_type=jnp.float32)
    norm_back_one = jax.vjp(layer_norm, inputs, vectors[0], vectors[1])[1]
    norm_back_two = jax.vjp(layer_norm, inputs, vectors[2], vectors[3])[1]
    input_one, gain_one, shift_one = norm_back_one(one_grad)
    input_two, gain_two, shift_two = norm_back_two(two_grad)
    input_part = input_one + input_two
    norm_part = jnp.stack([gain_one, shift_one, gain_two, shift_two])
    input_sum, norm_sum = lax.psum((input_part, norm_part), "mp")
    input_grad = (grad_full + input_sum).astype(jnp.bfloat16)
    qkv_w_grad = jnp.einsum("td,te->de", normed_one, qkv_grad, preferred_element_type=jnp.float32)
    out_w_grad = jnp.einsum("ti,td->id", context_low, cotangent, preferred_element_type=jnp.float32)
    up_w_grad = jnp.einsum("td,tf->df", normed_two, hidden_grad, preferred_element_type=jnp.float32)
    down_w_grad = jnp.einsum("tf,td->fd", active_low, cotangent, preferred_element_type=jnp.float32)
    canonical_grad = jnp.concatenate(
        [matrix_to_blocks(matrix) for matrix in (qkv_w_grad, out_w_grad, up_w_grad, down_w_grad)],
        axis=0,
    )
    slot_grads = canonical_grad[jnp.argsort(owner_map)]
    out_sum = jnp.sum(grad_full, axis=0)
    vector_part = jnp.concatenate([norm_sum, jnp.stack([out_sum, out_sum])], axis=0)
    unit_part = jnp.concatenate(
        [
            jnp.sum(qkv_grad.astype(jnp.float32), axis=0),
            jnp.sum(hidden_grad.astype(jnp.float32), axis=0),
        ]
    )
    summed, vector_grad, unit_grad = lax.psum((slot_grads, vector_part, unit_part), "dp")
    owned = lax.dynamic_slice_in_dim(summed, device * slot_count, slot_count, 0)
    left_new = 0.5 * left_stat[0] + 0.5 * jnp.einsum(
        "nij,nkj->nik", owned, owned, precision=highest
    )
    right_new = 0.5 * right_stat[0] + 0.5 * jnp.einsum(
        "nji,njk->nik", owned, owned, precision=highest
    )
    direction = jnp.einsum("nij,njk->nik", left_root[0], owned, precision=highest)
    direction = jnp.einsum("nij,njk->nik", direction, right_root[0], precision=highest)
    weight_new = apply_step(weight_blocks[0], direction)
    vector_stat_new, vector_new = vector_update(vectors, vector_stat, vector_grad)
    unit_stat_new, unit_new = vector_update(unit_shift, unit_stat[0], unit_grad)
    return (
        block_out,
        input_grad,
        owned[None],
        left_new[None],
        right_new[None],
        weight_new[None],
        vector_grad,
        vector_stat_new,
        vector_new,
        unit_grad[None],
        unit_stat_new[None],
        unit_new[None],
    )


LOW = jnp.bfloat16
WIDE = jnp.float32
MESH = pl.DeviceIdType.MESH
ANY = pl.BlockSpec(memory_space=pl.ANY)
STEP = 256
SUB = 32
PAIRS = 32
STEPS = 8
PER_STEP = PAIRS // STEPS
TICKS = PAIRS // 2
GOT = 16
ACROSS = 8
VMEM_BYTES = 60 * 1024 * 1024
FORWARD_VMEM = 63 * 1024 * 1024


def dot(left, right):
    return lax.dot_general(left, right, (((1,), (0,)), ((), ())), preferred_element_type=WIDE)


def dot_nt(left, right):
    return lax.dot_general(left, right, (((1,), (1,)), ((), ())), preferred_element_type=WIDE)


def dot_tn(left, right):
    return lax.dot_general(left, right, (((0,), (0,)), ((), ())), preferred_element_type=WIDE)


def resident(shape):
    return pl.BlockSpec(shape, lambda *_: (0,) * len(shape), pipeline_mode=pl.Buffered(1))


def tile_of(refs, widths, block):
    for ref, (rows, cols) in zip(refs, widths):
        count = (rows // B) * (cols // B)
        if block < count:
            i, j = divmod(block, cols // B)
            return ref.at[pl.ds(i * B, B), pl.ds(j * B, B)]
        block -= count


def move_blocks(copies_in, copies_out):
    for copy in copies_in:
        copy.start()
    for first, second in zip(copies_in, copies_out):
        first.wait()
        second.start()
    for copy in copies_out:
        copy.wait()


def block_scratch(total):
    return [
        pltpu.VMEM((total, B, B), LOW),
        pltpu.SemaphoreType.DMA((total,)),
        pltpu.SemaphoreType.DMA((total,)),
    ]


def unplace_kernel(shapes, order_ref, *refs):
    mats, (slots_ref, hold, sem_in, sem_out) = refs[:-4], refs[-4:]
    total = slots_ref.shape[0]
    move_blocks(
        [
            pltpu.make_async_copy(tile_of(mats, shapes, b), hold.at[b], sem_in.at[b])
            for b in range(total)
        ],
        [
            pltpu.make_async_copy(hold.at[b], slots_ref.at[order_ref[b]], sem_out.at[b])
            for b in range(total)
        ],
    )


def unplace_blocks(mats, order):
    shapes = [m.shape for m in mats]
    total = order.shape[0]
    return pl.pallas_call(
        functools.partial(unplace_kernel, shapes),
        grid_spec=pltpu.PrefetchScalarGridSpec(
            num_scalar_prefetch=1,
            grid=(1,),
            in_specs=[ANY] * len(mats),
            out_specs=ANY,
            scratch_shapes=block_scratch(total),
        ),
        out_shape=jax.ShapeDtypeStruct((total, B, B), LOW),
        compiler_params=pltpu.CompilerParams(vmem_limit_bytes=VMEM_BYTES),
        name="unplace_blocks",
    )(order, *mats)


PIECES = 4
ROUTES = ((0, 2), (0, 4), (0, 1), (2, 4), (4, 2), (2, 1), (4, 1), (6, 1))


def flip(index, mask):
    for bit in range(3):
        if mask >> bit & 1:
            unit = 2**bit
            index = index + (1 - 2 * lax.rem(lax.div(index, unit), 2)) * unit
    return index


def gather_kernel(
    shapes,
    order_ref,
    vec_ref,
    w_hbm,
    x_hbm,
    cot_hbm,
    qkv_hbm,
    od_hbm,
    up_hbm,
    h1_hbm,
    h2_hbm,
    sum_ref,
    slots,
    wide,
    x_buf,
    c_buf,
    h_buf,
    stage,
    send_sem,
    recv_sem,
    load_sem,
    row_sem,
    norm_sem,
    stage_sem,
):
    me = lax.axis_index("dp")
    each = w_hbm.shape[0]
    size = each // PIECES
    steps = x_hbm.shape[0] // STEP

    def piece(mask, q):
        return slots.at[pl.ds(flip(me, mask) * each + q * size, size)]

    def send(source, target, q):
        return pltpu.make_async_remote_copy(
            src_ref=piece(source, q),
            dst_ref=piece(source, q),
            send_sem=send_sem.at[ROUTES.index((source, target)), q],
            recv_sem=recv_sem.at[source ^ target, q],
            device_id={"dp": flip(me, target)},
            device_id_type=MESH,
        )

    def arrived(source, q):
        pltpu.make_async_remote_copy(
            src_ref=piece(source, q),
            dst_ref=piece(source, q),
            send_sem=send_sem.at[0, q],
            recv_sem=recv_sem.at[source, q],
            device_id={"dp": flip(me, 1)},
            device_id_type=MESH,
        ).wait_recv()

    def load(q):
        return pltpu.make_async_copy(
            w_hbm.at[pl.ds(q * size, size)], wide.at[q % 2], load_sem.at[q % 2]
        )

    def tile(i):
        return pl.ds(pl.multiple_of(i * STEP, STEP), STEP)

    def fetch(i, slot):
        return (
            pltpu.make_async_copy(x_hbm.at[tile(i), :], x_buf.at[slot], row_sem.at[0, slot]),
            pltpu.make_async_copy(cot_hbm.at[tile(i), :], c_buf.at[slot], row_sem.at[1, slot]),
        )

    def keep(i, slot):
        return (
            pltpu.make_async_copy(h_buf.at[slot, 0], h1_hbm.at[tile(i), :], norm_sem.at[0, slot]),
            pltpu.make_async_copy(h_buf.at[slot, 1], h2_hbm.at[tile(i), :], norm_sem.at[1, slot]),
        )

    def norm_step(i, slot, first):
        for copy in fetch(i, slot):
            copy.wait()

        @pl.when(jnp.logical_not(first))
        def _():
            for copy in keep(i, slot):
                copy.wait()

        x = x_buf[slot].astype(WIDE)
        center = x - jnp.mean(x, axis=1, keepdims=True)
        scale = lax.rsqrt(jnp.mean(center * center, axis=1, keepdims=True) + norm_eps)
        xhat = center * scale
        h_buf[slot, 0] = (xhat * vec_ref[0:1, :] + vec_ref[1:2, :]).astype(LOW)
        h_buf[slot, 1] = (xhat * vec_ref[2:3, :] + vec_ref[3:4, :]).astype(LOW)
        sum_ref[0:1, :] += jnp.sum(c_buf[slot].astype(WIDE), axis=0, keepdims=True)
        for copy in keep(i, slot):
            copy.start()

    for q in range(2):
        load(q).start()
    for slot in range(2):
        for copy in fetch(slot, slot):
            copy.start()
    barrier = pltpu.get_barrier_semaphore()
    for target in (1, 2, 4):
        pl.semaphore_signal(
            barrier, inc=1, device_id={"dp": flip(me, target)}, device_id_type=MESH
        )
    sum_ref[...] = jnp.zeros_like(sum_ref)
    for q in range(PIECES):
        load(q).wait()
        slots[pl.ds(me * each + q * size, size)] = wide[q % 2].astype(LOW)
        if q + 2 < PIECES:
            load(q + 2).start()
        if q == 0:
            pl.semaphore_wait(barrier, 3)
        for target in (2, 4, 1):
            send(0, target, q).start()

    for q in range(PIECES):

        @pl.loop(0, steps // (2 * PIECES))
        def _(k):
            i = (q * (steps // (2 * PIECES)) + k) * 2
            for slot in range(2):
                norm_step(i + slot, slot, i == 0)

                @pl.when(i + slot + 2 < steps)
                def _():
                    for copy in fetch(i + slot + 2, slot):
                        copy.start()

        arrived(2, q)
        if q % 2:
            send(2, 4, q).start()
        send(2, 1, q).start()
        arrived(4, q)
        if q % 2 == 0:
            send(4, 2, q).start()
        send(4, 1, q).start()
    for slot in range(2):
        for copy in keep(slot, slot):
            copy.wait()
    for q in range(PIECES):
        arrived(6, q)
        send(6, 1, q).start()
    for source in (1, 3, 5, 7):
        for q in range(PIECES):
            arrived(source, q)

    block = 0
    for ref, (rows, cols) in zip((qkv_hbm, od_hbm, up_hbm), shapes):
        across = cols // B

        def panel(i, slot):
            return pltpu.make_async_copy(
                stage.at[slot, :, pl.ds(0, cols)], ref.at[lane(i * B), :], stage_sem.at[slot]
            )

        @pl.loop(0, rows // B // 2)
        def _(k):
            for slot in range(2):
                i = k * 2 + slot

                @pl.when(k > 0)
                def _():
                    panel(i, slot).wait()

                for j in range(across):
                    stage[slot, :, j * B : (j + 1) * B] = slots[order_ref[block + i * across + j]]
                panel(i, slot).start()

        for slot in range(2):
            panel(slot, slot).wait()
        block += rows // B * across

    for source, target in ROUTES:
        for q in range(PIECES):
            if (source, target) == (2, 4) and q % 2 == 0:
                continue
            if (source, target) == (4, 2) and q % 2:
                continue
            send(source, target, q).wait_send()


def gather_weights(blocks, order, tokens, cotangent, vectors, shapes):
    rows, d = tokens.shape
    each = blocks.shape[0]
    return pl.pallas_call(
        functools.partial(gather_kernel, shapes),
        in_specs=[
            pl.BlockSpec(memory_space=pltpu.SMEM),
            pl.BlockSpec(memory_space=pltpu.VMEM),
            ANY,
            ANY,
            ANY,
        ],
        out_specs=[ANY] * 5 + [pl.BlockSpec(memory_space=pltpu.VMEM)],
        out_shape=[jax.ShapeDtypeStruct(s, LOW) for s in shapes]
        + [jax.ShapeDtypeStruct((rows, d), LOW)] * 2
        + [jax.ShapeDtypeStruct((8, d), WIDE)],
        scratch_shapes=[
            pltpu.VMEM((order.shape[0], B, B), LOW),
            pltpu.VMEM((2, each // PIECES, B, B), WIDE),
            pltpu.VMEM((2, STEP, d), LOW),
            pltpu.VMEM((2, STEP, d), LOW),
            pltpu.VMEM((2, 2, STEP, d), LOW),
            pltpu.VMEM((2, B, d), LOW),
            pltpu.SemaphoreType.DMA((8, PIECES)),
            pltpu.SemaphoreType.DMA((8, PIECES)),
            pltpu.SemaphoreType.DMA((2,)),
            pltpu.SemaphoreType.DMA((2, 2)),
            pltpu.SemaphoreType.DMA((2, 2)),
            pltpu.SemaphoreType.DMA((2,)),
        ],
        compiler_params=pltpu.CompilerParams(
            vmem_limit_bytes=VMEM_BYTES, collective_id=3, has_side_effects=True
        ),
        cost_estimate=pl.CostEstimate(
            flops=100_000_000_000, bytes_accessed=80 << 20, transcendentals=0
        ),
        name="gather_weights",
    )(order, vectors, blocks, tokens, cotangent)


def turn(values, cos, sin, back=False):
    lanes = lax.broadcasted_iota(jnp.int32, values.shape, 1)
    lower, upper = pltpu.roll(values, 96, 1), pltpu.roll(values, 32, 1)
    other = jnp.where(lanes < 32, -lower, upper)
    return values * cos - other * sin if back else values * cos + other * sin


def qkv_kernel(scale, h_ref, w_ref, bias_ref, cos_ref, sin_ref, q_ref, k_ref, v_ref):
    for j in range(w_ref.shape[1] // HD):
        head, part = divmod(j, 3)
        cols = slice(head * HD, head * HD + HD)
        proj = dot(h_ref[...], w_ref[:, j * HD : (j + 1) * HD]) + bias_ref[:, j * HD : (j + 1) * HD]
        if part == 2:
            v_ref[:, cols] = proj.astype(LOW)
            continue
        front = turn(proj[:, :128], cos_ref[...], sin_ref[...])
        turned = jnp.concatenate([front, proj[:, 128:]], axis=1).astype(LOW)
        if part == 0:
            q_ref[:, cols] = (turned.astype(WIDE) * scale).astype(LOW)
        else:
            k_ref[:, cols] = turned


def project_qkv(h1, qkv_w, bias, tables):
    rows, d = h1.shape
    cols = qkv_w.shape[1]
    out_cols = cols // 3
    tile = 512
    row_spec = lambda width: pl.BlockSpec((tile, width), lambda i: (i, 0))
    return pl.pallas_call(
        functools.partial(qkv_kernel, 1.0 / math.sqrt(HD)),
        grid=(rows // tile,),
        in_specs=[row_spec(d), resident((d, cols)), resident((1, cols))] + [row_spec(128)] * 2,
        out_specs=[row_spec(out_cols)] * 3,
        out_shape=[jax.ShapeDtypeStruct((rows, out_cols), LOW)] * 3,
        compiler_params=pltpu.CompilerParams(vmem_limit_bytes=VMEM_BYTES),
        name="project_qkv",
    )(h1, qkv_w, bias, *tables)


def attention_kernel(
    tile,
    start_ref,
    q_ref,
    k_ref,
    v_ref,
    cot_ref,
    out_ref,
    ctx_ref,
    grad_ref,
    stats_ref,
    s_scr,
):
    step = pl.program_id(1)

    def rows(c):
        q = q_ref[...]
        first = start_ref[...]
        top = jnp.full((tile, 1), masked_score, WIDE)
        for j in range(c + 1):
            keys = slice(j * tile, (j + 1) * tile)
            s = dot_nt(q, k_ref[keys, :])
            col = lax.broadcasted_iota(jnp.int32, (tile, tile), 1) + j * tile
            ok = col >= first
            if j == c:
                row = lax.broadcasted_iota(jnp.int32, (tile, tile), 0) + c * tile
                ok = ok & (col <= row)
            s = jnp.where(ok, s, masked_score)
            s_scr[:, keys] = s
            top = jnp.maximum(top, jnp.max(s, axis=1, keepdims=True))
        total = jnp.zeros((tile, 1), WIDE)
        ctx = jnp.zeros((tile, HD), WIDE)
        for j in range(c + 1):
            keys = slice(j * tile, (j + 1) * tile)
            e = jnp.exp(s_scr[:, keys] - top)
            total = total + jnp.sum(e, axis=1, keepdims=True)
            ctx = ctx + dot(e.astype(LOW), v_ref[keys, :])
        ctx = ctx * (1.0 / total)
        grad = dot_nt(cot_ref[...], out_ref[...]).astype(LOW)
        delta = jnp.sum(ctx * grad.astype(WIDE), axis=1, keepdims=True)
        ctx_ref[...] = ctx.astype(LOW)
        grad_ref[...] = grad
        lanes = lax.broadcasted_iota(jnp.int32, (tile, 128), 1)
        stats_ref[...] = jnp.where(
            lanes == 0, top + jnp.log(total), jnp.where(lanes == 1, delta, first.astype(WIDE))
        )

    for c in range(k_ref.shape[0] // tile):
        pl.when(step == c)(functools.partial(rows, c))


def attention_forward_rows(start, q, k, v, cotangent, od_w):
    rows, cols = q.shape
    d = cotangent.shape[1]
    heads = cols // HD
    tile = 512
    tile_spec = pl.BlockSpec((tile, HD), lambda h, i: (i, h))
    full_spec = pl.BlockSpec((rows, HD), lambda h, i: (0, h))
    flops = heads * rows * rows * HD * 3
    return pl.pallas_call(
        functools.partial(attention_kernel, tile),
        grid=(heads, rows // tile),
        in_specs=[
            pl.BlockSpec((tile, 1), lambda h, i: (i, 0)),
            tile_spec,
            full_spec,
            full_spec,
            pl.BlockSpec((tile, d), lambda h, i: (i, 0)),
            pl.BlockSpec((HD, d), lambda h, i: (h, 0)),
        ],
        out_specs=[tile_spec, tile_spec, pl.BlockSpec((tile, 128), lambda h, i: (i, h))],
        out_shape=[
            jax.ShapeDtypeStruct((rows, cols), LOW),
            jax.ShapeDtypeStruct((rows, cols), LOW),
            jax.ShapeDtypeStruct((rows, heads * 128), WIDE),
        ],
        scratch_shapes=[pltpu.VMEM((tile, rows), WIDE)],
        compiler_params=pltpu.CompilerParams(vmem_limit_bytes=VMEM_BYTES),
        cost_estimate=pl.CostEstimate(flops=flops, bytes_accessed=30 << 20, transcendentals=0),
        name="attention_forward",
    )(start, q, k, v, cotangent, od_w)


class Line:
    def __init__(self, out, part, got, across, sems):
        self.out, self.part, self.got, self.across = out, part, got, across
        (
            self.up_send,
            self.up_recv,
            self.far_send,
            self.far_recv,
            self.over_send,
            self.over_recv,
            self.down_send,
            self.down_recv,
            self.relay_send,
            self.relay_recv,
            self.own,
        ) = [sems.at[i] for i in range(11)]
        z = lax.axis_index("mp")
        self.inner = (z == 1) | (z == 2)
        self.near = (z >= 2).astype(jnp.int32)
        self.far = 1 - self.near
        self.partner = jnp.where(self.inner, jnp.where(z == 1, 0, 3), jnp.where(z == 0, 1, 2))
        self.other = 3 - z

    def rows(self, pair, which):
        return self.out.at[pl.ds(pl.multiple_of(pair * (2 * SUB) + which * SUB, SUB), SUB), :]

    def greet(self):
        barrier = pltpu.get_barrier_semaphore()
        pl.semaphore_signal(barrier, inc=1, device_id={"mp": self.partner}, device_id_type=MESH)

        @pl.when(self.inner)
        def _():
            pl.semaphore_signal(barrier, inc=1, device_id={"mp": self.other}, device_id_type=MESH)
            pl.semaphore_wait(barrier, 2)

        @pl.when(jnp.logical_not(self.inner))
        def _():
            pl.semaphore_wait(barrier, 1)

    def copy(self, src, dst, send, recv, pair, target):
        return pltpu.make_async_remote_copy(
            src_ref=src,
            dst_ref=dst,
            send_sem=send.at[pair],
            recv_sem=recv.at[pair],
            device_id={"mp": target},
            device_id_type=MESH,
        )

    def up(self, pair):
        return self.copy(
            self.part.at[pair], self.got.at[pair % GOT], self.up_send, self.up_recv, pair, self.partner
        )

    def far_sum(self, pair):
        src, dst = self.part.at[pair, self.far], self.across.at[pair % ACROSS]
        return self.copy(src, dst, self.far_send, self.far_recv, pair, self.other)

    def over(self, pair, which):
        src = self.part.at[pair, self.near]
        return self.copy(src, self.rows(pair, which), self.over_send, self.over_recv, pair, self.other)

    def down(self, pair):
        src = self.part.at[pair, self.near]
        return self.copy(
            src, self.rows(pair, self.near), self.down_send, self.down_recv, pair, self.partner
        )

    def relay(self, pair):
        far = self.rows(pair, self.far)
        return self.copy(far, far, self.relay_send, self.relay_recv, pair, self.partner)

    def keep(self, pair):
        src = self.part.at[pair, self.near]
        return pltpu.make_async_copy(src, self.rows(pair, self.near), self.own.at[pair])

    def send_up(self, pair):
        @pl.when(pair >= GOT)
        def _():
            self.down(pair - GOT).wait_recv()

        self.up(pair).start()

    def add_far(self, pair):
        self.up(pair).wait_recv()
        far = self.part[pair, self.far].astype(WIDE) + self.got[pair % GOT, self.far].astype(WIDE)
        self.part[pair, self.far] = far.astype(LOW)
        self.far_sum(pair).start()

    def finish_near(self, pair, base):
        self.far_sum(pair).wait_recv()
        total = (
            self.part[pair, self.near].astype(WIDE)
            + self.got[pair % GOT, self.near].astype(WIDE)
            + self.across[pair % ACROSS].astype(WIDE)
        )
        self.part[pair, self.near] = (base + total).astype(LOW)
        self.over(pair, self.near).start()
        self.down(pair).start()
        self.keep(pair).start()

    def send_relay(self, pair):
        self.over(pair, self.far).wait_recv()
        self.relay(pair).start()

    def drain(self):
        @pl.when(self.inner)
        def _():
            @pl.loop(0, PAIRS)
            def _(pair):
                self.far_sum(pair).wait_send()
                self.over(pair, self.near).wait_send()
                self.down(pair).wait_send()
                self.relay(pair).wait_send()
                self.keep(pair).wait()

        @pl.when(jnp.logical_not(self.inner))
        def _():
            @pl.loop(0, PAIRS)
            def _(pair):
                self.up(pair).wait_send()
                self.relay(pair).wait_recv()

            @pl.loop(PAIRS - GOT, PAIRS)
            def _(pair):
                self.down(pair).wait_recv()

    def tick(self, step, lag, base):
        @pl.when(jnp.logical_not(self.inner) & (step < TICKS))
        def _():
            for s in range(2):
                self.send_up(step * 2 + s)

        @pl.when(self.inner & (step >= lag + 2) & (step < lag + 2 + TICKS))
        def _():
            for s in range(2):
                self.send_relay((step - lag - 2) * 2 + s)

        @pl.when(self.inner & (step >= lag + 1) & (step < lag + 1 + TICKS))
        def _():
            for s in range(2):
                self.finish_near((step - lag - 1) * 2 + s, base(s))

        @pl.when(self.inner & (step >= lag) & (step < lag + TICKS))
        def _():
            for s in range(2):
                self.add_far((step - lag) * 2 + s)


def line_scratch(d):
    return [
        pltpu.VMEM((PAIRS, 2, SUB, d), LOW),
        pltpu.VMEM((GOT, 2, SUB, d), LOW),
        pltpu.VMEM((ACROSS, SUB, d), LOW),
        pltpu.SemaphoreType.DMA((11, PAIRS)),
    ]


def now(step):
    return jnp.minimum(step, STEPS - 1)


def row_block(width):
    return pl.BlockSpec((STEP, width), lambda i: (now(i), 0))


def base_block(width, lag):
    return pl.BlockSpec((4 * SUB, width), lambda i: (jnp.clip(i - lag - 1, 0, TICKS - 1), 0))


def lane(start):
    return pl.ds(pl.multiple_of(start, B), B)


def gelu_parts(z):
    e = jnp.exp(z * z * -0.5)
    t = 1.0 / (1.0 + jnp.abs(z) * (0.3275911 * math.sqrt(0.5)))
    poly = t * (
        0.5 * 0.254829592
        + t
        * (
            0.5 * -0.284496736
            + t * (0.5 * 1.421413741 + t * (0.5 * -1.453152027 + t * (0.5 * 1.061405429)))
        )
    )
    below = poly * e
    cdf = jnp.where(z >= 0, 1.0 - below, below)
    return cdf, e * (1.0 / math.sqrt(2.0 * math.pi))


def store_part(part_ref, step, cols, value):
    value = value.astype(LOW).reshape(PER_STEP, 2, SUB, value.shape[1])
    part_ref[pl.ds(step * PER_STEP, PER_STEP), :, :, cols] = value


FORWARD_LAG = 2
FORWARD_GRID = FORWARD_LAG + TICKS + 2


def weight_unit(a_t, b_ref, cols, stage, slot):
    for n in range(cols // 512):
        part = slice(n * 512, (n + 1) * 512)
        stage[pl.ds(pl.multiple_of(slot * B, B), B), part] = dot(a_t, b_ref[:, part]).astype(LOW)


def forward_kernel(
    h_ref,
    g_ref,
    ctx_ref,
    x_ref,
    bias_ref,
    shift_ref,
    cos_ref,
    sin_ref,
    up_hbm,
    od_hbm,
    h1_hbm,
    h2_hbm,
    ctx_hbm,
    cot_hbm,
    q_hbm,
    k_hbm,
    v_hbm,
    cg_hbm,
    stats_hbm,
    out_ref,
    hg_hbm,
    qg_hbm,
    wq_hbm,
    wo_hbm,
    wu_hbm,
    sums_ref,
    qkv_sums_ref,
    up_buf,
    od_buf,
    act_all,
    hg_all,
    part,
    got,
    across,
    sems,
    stats,
    dq_scr,
    dk_scr,
    dv_scr,
    load_sem,
    panel_sem,
    stage_sem,
    hg_sem,
    head_sem,
):
    step = pl.program_id(0)
    line = Line(out_ref, part, got, across, sems)
    heads = ctx_ref.shape[1]
    rows, units = act_all.shape
    qkv_cols = qg_hbm.shape[1]
    width = 512
    tiles = units // width
    stage = od_buf.at[pl.ds(rows, 2 * B), :]

    def load_up(n):
        cols = pl.ds(n * width, width)
        return pltpu.make_async_copy(up_hbm.at[:, cols], up_buf.at[:, cols], load_sem.at[n])

    def load_down(n):
        part_rows = pl.ds(heads + n * width, width)
        return pltpu.make_async_copy(
            od_hbm.at[part_rows, :], od_buf.at[part_rows, :], load_sem.at[tiles + n]
        )

    def load_out():
        part_rows = pl.ds(0, heads)
        return pltpu.make_async_copy(
            od_hbm.at[part_rows, :], od_buf.at[part_rows, :], load_sem.at[2 * tiles]
        )

    def load_cot():
        return pltpu.make_async_copy(
            cot_hbm, od_buf.at[pl.ds(0, rows), :], load_sem.at[2 * tiles + 1]
        )

    def load_head(h):
        cols = pl.ds(pl.multiple_of(h * HD, HD), HD)
        copies = [
            pltpu.make_async_copy(
                src.at[:, cols], act_all.at[:, pl.ds(i * HD, HD)], head_sem.at[i]
            )
            for i, src in enumerate((q_hbm, k_hbm, v_hbm, cg_hbm))
        ]
        lanes = pl.ds(pl.multiple_of(h * 128, 128), 128)
        copies.append(pltpu.make_async_copy(stats_hbm.at[:, lanes], stats, head_sem.at[4]))
        return copies

    def store_qg():
        return pltpu.make_async_copy(hg_all.at[:, pl.ds(0, qkv_cols)], qg_hbm, head_sem.at[5])

    def panel_cols(slot):
        return lane(qkv_cols + slot * B)

    def panel(src, i, slot):
        return pltpu.make_async_copy(
            src.at[:, lane(i * B)], up_buf.at[:, panel_cols(slot)], panel_sem.at[slot]
        )

    def store_hg(i):
        part_rows = pl.ds(pl.multiple_of(i * STEP, STEP), STEP)
        return pltpu.make_async_copy(
            hg_all.at[part_rows, :], hg_hbm.at[part_rows, :], hg_sem.at[i]
        )

    def stage_out(dst, row, cols, slot):
        return pltpu.make_async_copy(
            stage.at[lane(slot * B), pl.ds(0, cols)],
            dst.at[lane(row), :],
            stage_sem.at[slot],
        )

    @pl.when(step == 0)
    def _():
        for n in range(tiles):
            load_up(n).start()
            load_down(n).start()
        load_out().start()
        line.greet()
        sums_ref[...] = jnp.zeros_like(sums_ref)

    @pl.when(step < STEPS)
    def _():
        here = pl.ds(pl.multiple_of(step * STEP, STEP), STEP)
        for n in range(tiles):
            cols = slice(n * width, (n + 1) * width)

            @pl.when(step == 0)
            def _():
                load_up(n).wait()
                load_down(n).wait()

            hidden = dot(h_ref[...], up_buf[:, cols]) + bias_ref[:, cols]
            act_grad = dot_nt(g_ref[...], od_buf[heads + n * width : heads + (n + 1) * width, :])
            cdf, density = gelu_parts(hidden)
            act_all[here, cols] = (hidden * cdf).astype(LOW)
            grad = (act_grad * (cdf + hidden * density)).astype(LOW)
            hg_all[here, cols] = grad
            sums_ref[0:1, cols] += jnp.sum(grad.astype(WIDE), axis=0, keepdims=True)

        @pl.when(step == 0)
        def _():
            load_out().wait()

        store_hg(step).start()
        for n in range(od_buf.shape[1] // width):
            cols = slice(n * width, (n + 1) * width)
            value = dot(ctx_ref[...], od_buf[:heads, cols]) + dot(
                act_all[here, :], od_buf[heads:, cols]
            )
            store_part(part, step, cols, value)

    @pl.when(step == STEPS - 1)
    def _():
        panel(h2_hbm, 0, 0).start()
        load_cot().start()

    def unit(index, a_t, b_ref, cols, dst, row):
        slot = index % 2

        @pl.when(index >= 2)
        def _():
            stage_out(dst, row, cols, slot).wait()

        weight_unit(a_t, b_ref, cols, stage, slot)
        stage_out(dst, row, cols, slot).start()

    def settle(dst, cols):
        for slot in range(2):
            stage_out(dst, 0, cols, slot).wait()

    @pl.when((step == 8) | (step == 9))
    def _():
        @pl.loop(0, 4)
        def _(k):
            i = (step - 8) * 4 + k
            panel(h2_hbm, i, i % 2).wait()

            @pl.when(i < 7)
            def _():
                panel(h2_hbm, i + 1, (i + 1) % 2).start()

            unit(i, up_buf[:, panel_cols(i % 2)].T, hg_all, units, wu_hbm, i * B)

    @pl.when(step == 10)
    def _():
        settle(wu_hbm, units)
        load_cot().wait()

    @pl.when((step == 10) | (step == 11))
    def _():
        @pl.loop(0, 4)
        def _(k):
            i = (step - 10) * 4 + k
            cot = od_buf.at[pl.ds(0, rows), :]
            unit(i, act_all[:, lane(i * B)].T, cot, units, wo_hbm, heads + i * B)

    @pl.when(step == 11)
    def _():
        for copy in load_head(0):
            copy.start()

    @pl.when(step == 12)
    def _():
        settle(wo_hbm, units)

        @pl.loop(0, STEPS)
        def _(i):
            store_hg(i).wait()

    def head_grads(h, start, stop):
        tile = 512
        count = rows // tile

        def tile_rows(i):
            return pl.ds(pl.multiple_of(i * tile, tile), tile)

        def put(i, part, values):
            cols = pl.ds(pl.multiple_of(h * 3 * HD + part * HD, HD), HD)
            hg_all[tile_rows(i), cols] = values.astype(LOW)

        def turned_back(i, values):
            front = turn(values[:, :128], cos_ref[tile_rows(i), :], sin_ref[tile_rows(i), :], True)
            return jnp.concatenate([front, values[:, 128:]], axis=1)

        @pl.loop(start, stop)
        def _(j):
            keys = act_all[tile_rows(j), HD : 2 * HD]
            values = act_all[tile_rows(j), 2 * HD : 3 * HD]
            dk_scr[...] = jnp.zeros_like(dk_scr)
            dv_scr[...] = jnp.zeros_like(dv_scr)

            @pl.loop(j, count)
            def _(i):
                q = act_all[tile_rows(i), 0:HD]
                g = act_all[tile_rows(i), 3 * HD : 4 * HD]
                info = stats[tile_rows(i), :]
                log_total, delta = info[:, 0:1], info[:, 1:2]
                first = info[:, 2:3].astype(jnp.int32) - j * tile
                col = lax.broadcasted_iota(jnp.int32, (tile, tile), 1)
                row = lax.broadcasted_iota(jnp.int32, (tile, tile), 0) + (i - j) * tile
                ok = (col >= first) & (col <= row)
                p = jnp.where(ok, jnp.exp(dot_nt(q, keys) - log_total), 0.0)
                ds = (p * (dot_nt(g, values) - delta)).astype(LOW)
                dv_scr[...] += dot_tn(p.astype(LOW), g)
                dk_scr[...] += dot_tn(ds, q)
                dq_scr[tile_rows(i), :] += dot(ds, keys)

            put(j, 1, turned_back(j, dk_scr[...]))
            put(j, 2, dv_scr[...])

        @pl.when(stop == count)
        def _():
            @pl.loop(0, count)
            def _(i):
                put(i, 0, turned_back(i, dq_scr[tile_rows(i), :] * (1.0 / math.sqrt(HD))))

    @pl.when((step == 12) | (step == 14))
    def _():
        for copy in load_head((step - 12) // 2):
            copy.wait()
        dq_scr[...] = jnp.zeros_like(dq_scr)

    @pl.when((step >= 12) & (step < 16))
    def _():
        second = (step - 12) % 2
        head_grads((step - 12) // 2, second, 1 + 3 * second)

    @pl.when(step == 13)
    def _():
        for copy in load_head(1):
            copy.start()

    @pl.when(step == 16)
    def _():
        store_qg().start()
        for j in range(2):
            panel(ctx_hbm, j, j).start()
        total = jnp.zeros((1, qkv_cols), WIDE)
        for i in range(rows // 512):
            part_rows = slice(i * 512, (i + 1) * 512)
            total = total + jnp.sum(hg_all[part_rows, :qkv_cols].astype(WIDE), axis=0, keepdims=True)
        qkv_sums_ref[...] = jnp.broadcast_to(total, qkv_sums_ref.shape)
        for j in range(2):
            panel(ctx_hbm, j, j).wait()

        @pl.loop(0, 2)
        def _(j):
            cot = od_buf.at[pl.ds(0, rows), :]
            unit(j, up_buf[:, panel_cols(j)].T, cot, units, wo_hbm, j * B)

        settle(wo_hbm, units)
        panel(h1_hbm, 0, 0).start()

    @pl.when((step == 17) | (step == 18))
    def _():
        @pl.loop(0, 4)
        def _(k):
            i = (step - 17) * 4 + k
            panel(h1_hbm, i, i % 2).wait()

            @pl.when(i < 7)
            def _():
                panel(h1_hbm, i + 1, (i + 1) % 2).start()

            grads = hg_all.at[:, pl.ds(0, qkv_cols)]
            unit(i, up_buf[:, panel_cols(i % 2)].T, grads, qkv_cols, wq_hbm, i * B)

    @pl.when(step == 19)
    def _():
        settle(wq_hbm, qkv_cols)
        store_qg().wait()

    def base(s):
        near = pl.ds(pl.multiple_of(s * 2 * SUB + line.near * SUB, SUB), SUB)
        return x_ref[near, :].astype(WIDE) + shift_ref[...]

    line.tick(step, FORWARD_LAG, base)

    @pl.when(step == FORWARD_GRID - 1)
    def _():
        line.drain()


def forward_line(
    h1, h2, cotangent, ctx, heads, stats, tables, tokens, up_w, od_w, bias, shift
):
    rows, d = tokens.shape
    units = up_w.shape[1]
    qkv_cols = 3 * ctx.shape[1]
    return pl.pallas_call(
        forward_kernel,
        grid=(FORWARD_GRID,),
        in_specs=[
            row_block(d),
            row_block(d),
            row_block(ctx.shape[1]),
            base_block(d, FORWARD_LAG),
            resident(bias.shape),
            resident(shift.shape),
            resident((rows, 128)),
            resident((rows, 128)),
        ]
        + [ANY] * 11,
        out_specs=[ANY] * 6
        + [pl.BlockSpec((8, units), lambda i: (0, 0)), pl.BlockSpec((8, qkv_cols), lambda i: (0, 0))],
        out_shape=[
            jax.ShapeDtypeStruct((rows, d), LOW),
            jax.ShapeDtypeStruct((rows, units), LOW),
            jax.ShapeDtypeStruct((rows, qkv_cols), LOW),
            jax.ShapeDtypeStruct((d, qkv_cols), LOW),
            jax.ShapeDtypeStruct(od_w.shape, LOW),
            jax.ShapeDtypeStruct((d, units), LOW),
            jax.ShapeDtypeStruct((8, units), WIDE),
            jax.ShapeDtypeStruct((8, qkv_cols), WIDE),
        ],
        scratch_shapes=[
            pltpu.VMEM(up_w.shape, LOW),
            pltpu.VMEM(od_w.shape, LOW),
            pltpu.VMEM((rows, units), LOW),
            pltpu.VMEM((rows, units), LOW),
        ]
        + line_scratch(d)
        + [
            pltpu.VMEM((rows, 128), WIDE),
            pltpu.VMEM((rows, HD), WIDE),
            pltpu.VMEM((512, HD), WIDE),
            pltpu.VMEM((512, HD), WIDE),
            pltpu.SemaphoreType.DMA((10,)),
            pltpu.SemaphoreType.DMA((2,)),
            pltpu.SemaphoreType.DMA((2,)),
            pltpu.SemaphoreType.DMA((STEPS,)),
            pltpu.SemaphoreType.DMA((6,)),
        ],
        compiler_params=pltpu.CompilerParams(
            vmem_limit_bytes=FORWARD_VMEM, collective_id=1, has_side_effects=True
        ),
        cost_estimate=pl.CostEstimate(
            flops=200_000_000_000, bytes_accessed=80 << 20, transcendentals=0
        ),
        name="forward_line",
    )(
        h2,
        cotangent,
        ctx,
        tokens,
        bias,
        shift,
        *tables,
        up_w,
        od_w,
        h1,
        h2,
        ctx,
        cotangent,
        *heads,
        stats,
    )


BACKWARD_LAG = 1
BACKWARD_GRID = BACKWARD_LAG + TICKS + 2


class Spread:
    def __init__(self, own, along_mp, along_dp, sems):
        self.own = own
        self.stages = [
            ("dp", along_dp, sems.at[0], sems.at[1]),
            ("mp", along_mp, sems.at[2], sems.at[3]),
        ]

    def others(self, stage):
        axis, buf, send, recv = self.stages[stage]
        me = lax.axis_index(axis)
        return axis, buf, send, recv, me, [lax.rem(me + k, buf.shape[0]) for k in range(1, buf.shape[0])]

    def greet(self):
        barrier = pltpu.get_barrier_semaphore()
        count = 0
        for stage in range(2):
            axis, _, _, _, _, others = self.others(stage)
            for other in others:
                pl.semaphore_signal(barrier, inc=1, device_id={axis: other}, device_id_type=MESH)
            count += len(others)
        pl.semaphore_wait(barrier, count)

    def copies(self, stage):
        axis, buf, send, recv, me, others = self.others(stage)
        return [
            (
                pltpu.make_async_remote_copy(
                    src_ref=self.own,
                    dst_ref=buf.at[me],
                    send_sem=send.at[k],
                    recv_sem=recv.at[me],
                    device_id={axis: other},
                    device_id_type=MESH,
                ),
                pltpu.make_async_remote_copy(
                    src_ref=self.own,
                    dst_ref=buf.at[other],
                    send_sem=send.at[k],
                    recv_sem=recv.at[other],
                    device_id={axis: other},
                    device_id_type=MESH,
                ),
            )
            for k, other in enumerate(others)
        ]

    def start(self, stage):
        _, buf, _, _, me, _ = self.others(stage)
        buf[me] = self.own[...]
        for out, _ in self.copies(stage):
            out.start()

    def finish(self, stage):
        _, buf, _, _, _, _ = self.others(stage)
        for out, back in self.copies(stage):
            out.wait_send()
            back.wait_recv()
        total = buf[0]
        for i in range(1, buf.shape[0]):
            total = total + buf[i]
        return total


def backward_kernel(
    qg_ref,
    hg_ref,
    x_ref,
    g_ref,
    qkv_ref,
    up_ref,
    one_ref,
    two_ref,
    sums_in,
    sums_ref,
    out_ref,
    gc_scr,
    xhat_scr,
    own,
    along_mp,
    along_dp,
    spread_sems,
    part,
    got,
    across,
    sems,
):
    step = pl.program_id(0)
    line = Line(out_ref, part, got, across, sems)
    spread = Spread(own, along_mp, along_dp, spread_sems)
    d = x_ref.shape[1]
    width = 512

    @pl.when(step == 0)
    def _():
        spread.greet()
        own[...] = sums_in[...]

    @pl.when(step < STEPS)
    def _():
        x = x_ref[...].astype(WIDE)
        center = x - jnp.mean(x, axis=1, keepdims=True)
        scale = lax.rsqrt(jnp.mean(center * center, axis=1, keepdims=True) + norm_eps)
        xhat_scr[...] = center * scale
        mean = jnp.zeros((STEP, 1), WIDE)
        slope = jnp.zeros((STEP, 1), WIDE)
        for n in range(d // width):
            cols = slice(n * width, (n + 1) * width)
            e1 = dot_nt(qg_ref[...], qkv_ref[cols, :])
            e2 = dot_nt(hg_ref[...], up_ref[cols, :])
            xhat = xhat_scr[:, cols]
            gc = e1 * one_ref[:, cols] + e2 * two_ref[:, cols]
            gc_scr[:, cols] = gc
            mean = mean + jnp.sum(gc, axis=1, keepdims=True)
            slope = slope + jnp.sum(gc * xhat, axis=1, keepdims=True)
            own[0:1, cols] += jnp.sum(e1 * xhat, axis=0, keepdims=True)
            own[1:2, cols] += jnp.sum(e1, axis=0, keepdims=True)
            own[2:3, cols] += jnp.sum(e2 * xhat, axis=0, keepdims=True)
            own[3:4, cols] += jnp.sum(e2, axis=0, keepdims=True)
        mean = mean * (1.0 / d)
        slope = slope * (1.0 / d)
        for n in range(d // width):
            cols = slice(n * width, (n + 1) * width)
            value = (gc_scr[:, cols] - mean - xhat_scr[:, cols] * slope) * scale
            store_part(part, step, cols, value)

    @pl.when(step == STEPS)
    def _():
        spread.start(0)

    @pl.when(step == STEPS + 4)
    def _():
        own[...] = spread.finish(0)
        spread.start(1)

    def base(s):
        near = pl.ds(pl.multiple_of(s * 2 * SUB + line.near * SUB, SUB), SUB)
        return g_ref[near, :].astype(WIDE)

    line.tick(step, BACKWARD_LAG, base)

    @pl.when(step == BACKWARD_GRID - 1)
    def _():
        line.drain()
        total = spread.finish(1)
        row = lax.broadcasted_iota(jnp.int32, total.shape, 0)
        sums_ref[...] = jnp.where(row < 4, total, own[...])


def backward_line(qkv_grad, hidden_grad, tokens, cotangent, qkv_w, up_w, gain_one, gain_two, sums):
    rows, d = tokens.shape
    small = sums.shape
    return pl.pallas_call(
        backward_kernel,
        grid=(BACKWARD_GRID,),
        in_specs=[
            row_block(qkv_grad.shape[1]),
            row_block(hidden_grad.shape[1]),
            row_block(d),
            base_block(d, BACKWARD_LAG),
            resident(qkv_w.shape),
            resident(up_w.shape),
            resident((1, d)),
            resident((1, d)),
            resident(small),
        ],
        out_specs=[pl.BlockSpec(small, lambda i: (0, 0)), ANY],
        out_shape=[jax.ShapeDtypeStruct(small, WIDE), jax.ShapeDtypeStruct((rows, d), LOW)],
        scratch_shapes=[
            pltpu.VMEM((STEP, d), WIDE),
            pltpu.VMEM((STEP, d), WIDE),
            pltpu.VMEM(small, WIDE),
            pltpu.VMEM((4,) + small, WIDE),
            pltpu.VMEM((8,) + small, WIDE),
            pltpu.SemaphoreType.DMA((4, 8)),
        ]
        + line_scratch(d),
        compiler_params=pltpu.CompilerParams(
            vmem_limit_bytes=VMEM_BYTES, collective_id=2, has_side_effects=True
        ),
        cost_estimate=pl.CostEstimate(
            flops=200_000_000_000, bytes_accessed=60 << 20, transcendentals=0
        ),
        name="backward_line",
    )(
        qkv_grad, hidden_grad, tokens, cotangent, qkv_w, up_w, gain_one, gain_two, sums
    )


def halves(values):
    high = values.astype(LOW)
    return high, (values - high.astype(WIDE)).astype(LOW)


def shampoo_kernel(
    g_ref,
    w_ref,
    ls_ref,
    rs_ref,
    lr_ref,
    rr_ref,
    one_in,
    two_in,
    grad_ref,
    left_ref,
    right_ref,
    weight_ref,
    one_out,
    two_out,
    hold,
    sems,
):
    step = pl.program_id(0)
    pairs = ((one_in, one_out), (two_in, two_out))
    fetch = [pltpu.make_async_copy(a, hold.at[i], sems.at[0, i]) for i, (a, _) in enumerate(pairs)]
    store = [pltpu.make_async_copy(hold.at[i], b, sems.at[1, i]) for i, (_, b) in enumerate(pairs)]

    @pl.when(step == 0)
    def _():
        for copy in fetch:
            copy.start()

    for i in range(2):

        @pl.when(step == pl.num_programs(0) * (i + 1) // 3)
        def _():
            fetch[i].wait()
            store[i].start()

    @pl.when(step == pl.num_programs(0) - 1)
    def _():
        for copy in store:
            copy.wait()

    for n in range(g_ref.shape[0]):
        g = g_ref[n]
        grad_ref[n] = g.astype(WIDE)
        left_ref[n] = 0.5 * ls_ref[n] + 0.5 * dot_nt(g, g)
        right_ref[n] = 0.5 * rs_ref[n] + 0.5 * dot_tn(g, g)
        l_high, l_low = halves(lr_ref[n])
        r_high, r_low = halves(rr_ref[n])
        d_high, d_low = halves(dot(l_high, g) + dot(l_low, g))
        direction = dot(d_high, r_high) + dot(d_low, r_high) + dot(d_high, r_low)
        weight = w_ref[n]
        size = 1.0 / (B * B)
        weight_size = jnp.sqrt(jnp.sum(weight * weight, keepdims=True) * size)
        step_size = jnp.sqrt(jnp.sum(direction * direction, keepdims=True) * size + 1e-06)
        weight_ref[n] = weight - direction * (step_share * weight_size / step_size)


def shampoo(grads, weights, left_stat, right_stat, left_root, right_root, one, two):
    count = grads.shape[0]
    group = 2
    spec = pl.BlockSpec((group, B, B), lambda i: (i, 0, 0))
    return pl.pallas_call(
        shampoo_kernel,
        grid=(count // group,),
        in_specs=[spec] * 6 + [ANY] * 2,
        out_specs=[spec] * 4 + [ANY] * 2,
        out_shape=[jax.ShapeDtypeStruct((count, B, B), WIDE)] * 4
        + [jax.ShapeDtypeStruct(one.shape, one.dtype)] * 2,
        scratch_shapes=[
            pltpu.VMEM((2,) + one.shape, one.dtype),
            pltpu.SemaphoreType.DMA((2, 2)),
        ],
        compiler_params=pltpu.CompilerParams(vmem_limit_bytes=VMEM_BYTES),
        name="shampoo",
    )(grads, weights, left_stat, right_stat, left_root, right_root, one, two)


def per_device_line(
    tokens,
    cotangent,
    seq_len,
    seq_device,
    owner_map,
    weight_blocks,
    left_stat,
    right_stat,
    left_root,
    right_root,
    vectors,
    vector_stat,
    unit_bias,
    unit_stat,
):
    groups = lax.axis_size("mp")
    device = lax.axis_index("dp")
    row_count, d = tokens.shape
    qkv_cols = 3 * d // groups
    head_cols = d // groups
    unit_cols = FF // groups
    segment, position = segment_layout(seq_len, seq_device, device, row_count)
    start = (jnp.arange(row_count, dtype=jnp.int32) - position)[:, None]
    frequency = 10000.0 ** (-2.0 * jnp.arange(ROT // 2, dtype=WIDE) / ROT)
    angles = position.astype(WIDE)[:, None] * frequency[None, :]
    cos, sin = jnp.cos(angles), jnp.sin(angles)
    pad = jnp.zeros((row_count, 128 - ROT), WIDE)
    tables = (
        jnp.concatenate([cos, cos, pad + 1.0], axis=1),
        jnp.concatenate([sin, sin, pad], axis=1),
    )
    shift = (vectors[4] + vectors[5])[None]
    unit_shift = unit_bias[0]

    shapes = ((d, qkv_cols), (head_cols + unit_cols, d), (d, unit_cols))
    blocks = [(a // B) * (b // B) for a, b in ((d, qkv_cols), (head_cols, d), (d, unit_cols))]
    order = jnp.concatenate(
        [
            owner_map[: blocks[0] + blocks[1]],
            owner_map[blocks[0] + blocks[1] + blocks[2] :],
            owner_map[blocks[0] + blocks[1] : blocks[0] + blocks[1] + blocks[2]],
        ]
    )
    qkv_w, od_w, up_w, normed_one, normed_two, out_sum = gather_weights(
        weight_blocks[0], order, tokens, cotangent, vectors, shapes
    )

    q, k, v = project_qkv(normed_one, qkv_w, unit_shift[None, :qkv_cols], tables)
    ctx, ctx_grad, stats = attention_forward_rows(start, q, k, v, cotangent, od_w)
    block_out, hidden_grad, qkv_grad, qkv_wg, od_wg, up_wg, hidden_sums, qkv_sums = forward_line(
        normed_one,
        normed_two,
        cotangent,
        ctx,
        (q, k, v, ctx_grad),
        stats,
        tables,
        tokens,
        up_w,
        od_w,
        unit_shift[None, qkv_cols:],
        shift,
    )
    slots = unplace_blocks([qkv_wg, od_wg, up_wg], order)
    owned = lax.psum_scatter(slots, "dp", scatter_dimension=0, tiled=True)
    qkv_grad, hidden_grad, slots = lax.optimization_barrier((qkv_grad, hidden_grad, slots))
    sums = jnp.concatenate(
        [
            jnp.zeros((4, d), WIDE),
            out_sum[:1],
            jnp.pad(qkv_sums[:1], ((0, 0), (0, d - qkv_cols))),
            jnp.pad(hidden_sums[:1], ((0, 0), (0, d - unit_cols))),
            jnp.zeros((1, d), WIDE),
        ],
        axis=0,
    )
    sums, input_grad = backward_line(
        qkv_grad,
        hidden_grad,
        tokens,
        cotangent,
        qkv_w,
        up_w,
        vectors[0:1],
        vectors[2:3],
        sums,
    )
    block_grad, left_new, right_new, weight_new, block_out, input_grad = shampoo(
        owned,
        weight_blocks[0],
        left_stat[0],
        right_stat[0],
        left_root[0],
        right_root[0],
        block_out,
        input_grad,
    )
    vector_grad = jnp.concatenate([sums[:5], sums[4:5]], axis=0)
    unit_grad = jnp.concatenate([sums[5, :qkv_cols], sums[6, :unit_cols]])
    vector_stat_new, vector_new = vector_update(vectors, vector_stat, vector_grad)
    unit_stat_new, unit_new = vector_update(unit_shift, unit_stat[0], unit_grad)
    return (
        block_out,
        input_grad,
        block_grad[None],
        left_new[None],
        right_new[None],
        weight_new[None],
        vector_grad,
        vector_stat_new,
        vector_new,
        unit_grad[None],
        unit_stat_new[None],
        unit_new[None],
    )


def solution(mesh):
    placed = (
        P("dp", None),
        P("dp", None),
        P(),
        P(),
        P(),
        P("mp", "dp", None, None),
        P("mp", "dp", None, None),
        P("mp", "dp", None, None),
        P("mp", "dp", None, None),
        P("mp", "dp", None, None),
        P(),
        P(),
        P("mp", None),
        P("mp", None),
    )
    body = per_device
    if mesh.shape["dp"] == 8 and mesh.shape["mp"] == 4:
        body = per_device_line
    return jax.shard_map(
        body,
        mesh=mesh,
        in_specs=placed,
        out_specs=(
            P("dp", None),
            P("dp", None),
            P("mp", "dp", None, None),
            P("mp", "dp", None, None),
            P("mp", "dp", None, None),
            P("mp", "dp", None, None),
            P(),
            P(),
            P(),
            P("mp", None),
            P("mp", None),
            P("mp", None),
        ),
        check_vma=False,
    )
```

```python
import functools
import math

import jax
import jax.numpy as jnp
from jax import lax
from jax.experimental import pallas as pl
from jax.experimental.pallas import tpu as pltpu
from jax.sharding import PartitionSpec as P

D = 2048
HEADS = 8
HD = 256
ROT = 64
FF = 8192
B = 256


highest = lax.Precision.HIGHEST
norm_eps = 1e-05
step_share = 0.5
vector_rate = 0.15
masked_score = -1e30


def layer_norm(values, gain, shift):
    center = values - jnp.mean(values, axis=-1, keepdims=True)
    spread = jnp.mean(center * center, axis=-1, keepdims=True)
    return center * lax.rsqrt(spread + norm_eps) * gain + shift


def gelu_exact(values):
    return jax.nn.gelu(values, approximate=False)


def segment_layout(seq_len, seq_device, device, row_count):
    is_mine = seq_device == device
    lengths = jnp.where(is_mine, seq_len, 0)
    seq_ends = jnp.cumsum(lengths)
    row_index = jnp.arange(row_count, dtype=jnp.int32)
    passed = is_mine[None, :] & (seq_ends[None, :] <= row_index[:, None])
    segment = jnp.sum(passed.astype(jnp.int32), axis=1)
    seq_start = jnp.max(jnp.where(passed, seq_ends[None, :], 0), axis=1)
    return (segment, row_index - seq_start)


def rotary_tables(position):
    half_rot = ROT // 2
    frequency = 10000.0 ** (-2.0 * jnp.arange(half_rot, dtype=jnp.float32) / ROT)
    angles = position.astype(jnp.float32)[:, None] * frequency[None, :]
    cosine_table = jnp.concatenate([jnp.cos(angles), jnp.cos(angles)], axis=1)
    sine_table = jnp.concatenate([jnp.sin(angles), jnp.sin(angles)], axis=1)
    return (cosine_table, sine_table)


def rotate(values, cosine_table, sine_table):
    rot_dims = cosine_table.shape[1]
    half_rot = rot_dims // 2
    leading = values[..., :rot_dims]
    turned = jnp.concatenate([-leading[..., half_rot:], leading[..., :half_rot]], axis=-1)
    rotated = leading * cosine_table[:, None, :] + turned * sine_table[:, None, :]
    return jnp.concatenate([rotated, values[..., rot_dims:]], axis=-1)


def blocks_to_matrix(blocks, across):
    down_count = blocks.shape[0] // across
    return (
        blocks.reshape(down_count, across, B, B)
        .transpose(0, 2, 1, 3)
        .reshape(down_count * B, across * B)
    )


def matrix_to_blocks(matrix):
    down_count = matrix.shape[0] // B
    across = matrix.shape[1] // B
    return (
        matrix.reshape(down_count, B, across, B)
        .transpose(0, 2, 1, 3)
        .reshape(down_count * across, B, B)
    )


def split_blocks(blocks, qkv_cols, head_cols, unit_cols):
    qkv_end = D // B * (qkv_cols // B)
    out_end = qkv_end + head_cols // B * (D // B)
    up_end = out_end + D // B * (unit_cols // B)
    qkv_w = blocks_to_matrix(blocks[:qkv_end], qkv_cols // B)
    out_w = blocks_to_matrix(blocks[qkv_end:out_end], D // B)
    up_w = blocks_to_matrix(blocks[out_end:up_end], unit_cols // B)
    down_w = blocks_to_matrix(blocks[up_end:], D // B)
    return (qkv_w, out_w, up_w, down_w)


def apply_step(weight, direction):
    weight_size = jnp.sqrt(jnp.mean(weight * weight, axis=(-2, -1), keepdims=True))
    step_size = jnp.sqrt(jnp.mean(direction * direction, axis=(-2, -1), keepdims=True) + 1e-06)
    return weight - step_share * weight_size * direction / step_size


def vector_update(values, old_stat, gradient):
    new_stat = 0.5 * old_stat + 0.5 * gradient * gradient
    return (new_stat, values - vector_rate * gradient * lax.rsqrt(new_stat))


def block_mask(block_segment, block_row, segment, column):
    return (block_segment[:, None] == segment[None, :]) & (column[None, :] <= block_row[:, None])


def attention_forward(queries, keys_low, values_low, segment):
    row_count, head_count, head_dim = queries.shape
    block_rows = min(512, row_count)
    block_count = row_count // block_rows
    score_scale = 1.0 / math.sqrt(head_dim)
    column = jnp.arange(row_count, dtype=jnp.int32)

    def one_block(inputs):
        block_query, block_segment, block_row = inputs
        scores = (
            jnp.einsum("qhd,khd->hqk", block_query, keys_low, preferred_element_type=jnp.float32)
            * score_scale
        )
        scores = jnp.where(
            block_mask(block_segment, block_row, segment, column)[None], scores, masked_score
        )
        log_total = jax.nn.logsumexp(scores, axis=-1)
        weights = jnp.exp(scores - log_total[:, :, None]).astype(jnp.bfloat16)
        context = jnp.einsum(
            "hqk,khd->qhd", weights, values_low, preferred_element_type=jnp.float32
        )
        return (context, log_total)

    contexts, log_totals = lax.map(
        one_block,
        (
            queries.reshape(block_count, block_rows, head_count, head_dim),
            segment.reshape(block_count, block_rows),
            column.reshape(block_count, block_rows),
        ),
    )
    return (contexts.reshape(row_count, head_count, head_dim), log_totals)


def attention_backward(queries, keys_low, values_low, context_grad, log_totals, segment):
    row_count, head_count, head_dim = queries.shape
    block_rows = min(512, row_count)
    block_count = row_count // block_rows
    score_scale = 1.0 / math.sqrt(head_dim)
    column = jnp.arange(row_count, dtype=jnp.int32)

    def one_block(totals, inputs):
        key_grad, value_grad = totals
        block_query, block_grad, block_total, block_segment, block_row = inputs
        scores = (
            jnp.einsum("qhd,khd->hqk", block_query, keys_low, preferred_element_type=jnp.float32)
            * score_scale
        )
        scores = jnp.where(
            block_mask(block_segment, block_row, segment, column)[None], scores, masked_score
        )
        probs = jnp.exp(scores - block_total[:, :, None])
        weights = probs.astype(jnp.bfloat16)
        prob_grad = jnp.einsum(
            "qhd,khd->hqk", block_grad, values_low, preferred_element_type=jnp.float32
        )
        delta = jnp.sum(probs * prob_grad, axis=-1, keepdims=True)
        score_grad = (probs * (prob_grad - delta)).astype(jnp.bfloat16)
        query_grad = (
            jnp.einsum("hqk,khd->qhd", score_grad, keys_low, preferred_element_type=jnp.float32)
            * score_scale
        )
        key_grad = (
            key_grad
            + jnp.einsum(
                "hqk,qhd->khd", score_grad, block_query, preferred_element_type=jnp.float32
            )
            * score_scale
        )
        value_grad = value_grad + jnp.einsum(
            "hqk,qhd->khd", weights, block_grad, preferred_element_type=jnp.float32
        )
        return ((key_grad, value_grad), query_grad)

    zeros_start = jnp.zeros((row_count, head_count, head_dim), jnp.float32)
    (key_grad, value_grad), query_grad = lax.scan(
        one_block,
        (zeros_start, zeros_start),
        (
            queries.reshape(block_count, block_rows, head_count, head_dim),
            context_grad.reshape(block_count, block_rows, head_count, head_dim),
            log_totals,
            segment.reshape(block_count, block_rows),
            column.reshape(block_count, block_rows),
        ),
    )
    return (query_grad.reshape(row_count, head_count, head_dim), key_grad, value_grad)


def per_device(
    tokens,
    cotangent,
    seq_len,
    seq_device,
    owner_map,
    weight_blocks,
    left_stat,
    right_stat,
    left_root,
    right_root,
    vectors,
    vector_stat,
    unit_bias,
    unit_stat,
):
    groups = lax.axis_size("mp")
    device = lax.axis_index("dp")
    row_count = tokens.shape[0]
    heads_here = HEADS // groups
    qkv_cols = 3 * D // groups
    head_cols = D // groups
    unit_cols = FF // groups
    slot_count = weight_blocks.shape[1]
    sent_blocks = weight_blocks[0].astype(jnp.bfloat16)
    gathered = lax.all_gather(sent_blocks, "dp", axis=0, tiled=True)
    qkv_w, out_w, up_w, down_w = split_blocks(gathered[owner_map], qkv_cols, head_cols, unit_cols)
    segment, position = segment_layout(seq_len, seq_device, device, row_count)
    cosine_table, sine_table = rotary_tables(position)
    unit_shift = unit_bias[0]
    inputs = tokens.astype(jnp.float32)
    normed_one = layer_norm(inputs, vectors[0], vectors[1]).astype(jnp.bfloat16)
    normed_two = layer_norm(inputs, vectors[2], vectors[3]).astype(jnp.bfloat16)
    qkv_proj = (
        jnp.dot(normed_one, qkv_w, preferred_element_type=jnp.float32) + unit_shift[:qkv_cols]
    )
    qkv_proj = qkv_proj.reshape(row_count, heads_here, 3, HD)

    def turn_pair(values):
        return rotate(values.reshape(row_count, 2 * heads_here, HD), cosine_table, sine_table)

    turned, turn_back = jax.vjp(turn_pair, qkv_proj[:, :, :2])
    turned = turned.reshape(row_count, heads_here, 2, HD).astype(jnp.bfloat16)
    queries = turned[:, :, 0]
    keys_low = turned[:, :, 1]
    values_low = qkv_proj[:, :, 2].astype(jnp.bfloat16)
    context, log_totals = attention_forward(queries, keys_low, values_low, segment)
    context_low = context.reshape(row_count, head_cols).astype(jnp.bfloat16)
    hidden = jnp.dot(normed_two, up_w, preferred_element_type=jnp.float32) + unit_shift[qkv_cols:]
    active, gelu_back = jax.vjp(gelu_exact, hidden)
    active_low = active.astype(jnp.bfloat16)
    partial_out = jnp.dot(context_low, out_w, preferred_element_type=jnp.float32) + jnp.dot(
        active_low, down_w, preferred_element_type=jnp.float32
    )
    branch = lax.psum(partial_out.astype(jnp.bfloat16), "mp").astype(jnp.float32)
    block_out = (inputs + branch + (vectors[4] + vectors[5])).astype(jnp.bfloat16)
    grad_full = cotangent.astype(jnp.float32)
    act_grad = jnp.einsum("td,fd->tf", cotangent, down_w, preferred_element_type=jnp.float32)
    hidden_grad = gelu_back(act_grad)[0].astype(jnp.bfloat16)
    context_grad = jnp.einsum(
        "td,id->ti", cotangent, out_w, preferred_element_type=jnp.float32
    ).astype(jnp.bfloat16)
    query_grad, key_grad, value_grad = attention_backward(
        queries,
        keys_low,
        values_low,
        context_grad.reshape(row_count, heads_here, HD),
        log_totals,
        segment,
    )
    pair_grad = turn_back(
        jnp.stack([query_grad, key_grad], axis=2).reshape(row_count, 2 * heads_here, HD)
    )[0]
    qkv_grad = (
        jnp.concatenate([pair_grad, value_grad[:, :, None]], axis=2)
        .reshape(row_count, qkv_cols)
        .astype(jnp.bfloat16)
    )
    one_grad = jnp.einsum("te,de->td", qkv_grad, qkv_w, preferred_element_type=jnp.float32)
    two_grad = jnp.einsum("tf,df->td", hidden_grad, up_w, preferred_element_type=jnp.float32)
    norm_back_one = jax.vjp(layer_norm, inputs, vectors[0], vectors[1])[1]
    norm_back_two = jax.vjp(layer_norm, inputs, vectors[2], vectors[3])[1]
    input_one, gain_one, shift_one = norm_back_one(one_grad)
    input_two, gain_two, shift_two = norm_back_two(two_grad)
    input_part = input_one + input_two
    norm_part = jnp.stack([gain_one, shift_one, gain_two, shift_two])
    input_sum, norm_sum = lax.psum((input_part, norm_part), "mp")
    input_grad = (grad_full + input_sum).astype(jnp.bfloat16)
    qkv_w_grad = jnp.einsum("td,te->de", normed_one, qkv_grad, preferred_element_type=jnp.float32)
    out_w_grad = jnp.einsum("ti,td->id", context_low, cotangent, preferred_element_type=jnp.float32)
    up_w_grad = jnp.einsum("td,tf->df", normed_two, hidden_grad, preferred_element_type=jnp.float32)
    down_w_grad = jnp.einsum("tf,td->fd", active_low, cotangent, preferred_element_type=jnp.float32)
    canonical_grad = jnp.concatenate(
        [matrix_to_blocks(matrix) for matrix in (qkv_w_grad, out_w_grad, up_w_grad, down_w_grad)],
        axis=0,
    )
    slot_grads = canonical_grad[jnp.argsort(owner_map)]
    out_sum = jnp.sum(grad_full, axis=0)
    vector_part = jnp.concatenate([norm_sum, jnp.stack([out_sum, out_sum])], axis=0)
    unit_part = jnp.concatenate(
        [
            jnp.sum(qkv_grad.astype(jnp.float32), axis=0),
            jnp.sum(hidden_grad.astype(jnp.float32), axis=0),
        ]
    )
    summed, vector_grad, unit_grad = lax.psum((slot_grads, vector_part, unit_part), "dp")
    owned = lax.dynamic_slice_in_dim(summed, device * slot_count, slot_count, 0)
    left_new = 0.5 * left_stat[0] + 0.5 * jnp.einsum(
        "nij,nkj->nik", owned, owned, precision=highest
    )
    right_new = 0.5 * right_stat[0] + 0.5 * jnp.einsum(
        "nji,njk->nik", owned, owned, precision=highest
    )
    direction = jnp.einsum("nij,njk->nik", left_root[0], owned, precision=highest)
    direction = jnp.einsum("nij,njk->nik", direction, right_root[0], precision=highest)
    weight_new = apply_step(weight_blocks[0], direction)
    vector_stat_new, vector_new = vector_update(vectors, vector_stat, vector_grad)
    unit_stat_new, unit_new = vector_update(unit_shift, unit_stat[0], unit_grad)
    return (
        block_out,
        input_grad,
        owned[None],
        left_new[None],
        right_new[None],
        weight_new[None],
        vector_grad,
        vector_stat_new,
        vector_new,
        unit_grad[None],
        unit_stat_new[None],
        unit_new[None],
    )


LOW = jnp.bfloat16
WIDE = jnp.float32
MESH = pl.DeviceIdType.MESH
ANY = pl.BlockSpec(memory_space=pl.ANY)
STEP = 256
SUB = 32
PAIRS = 32
STEPS = 8
PER_STEP = PAIRS // STEPS
TICKS = PAIRS // 2
GOT = 8
ACROSS = 4
VMEM_BYTES = 60 * 1024 * 1024
FORWARD_VMEM = 63 * 1024 * 1024


def dot(left, right):
    return lax.dot_general(left, right, (((1,), (0,)), ((), ())), preferred_element_type=WIDE)


def dot_nt(left, right):
    return lax.dot_general(left, right, (((1,), (1,)), ((), ())), preferred_element_type=WIDE)


def dot_tn(left, right):
    return lax.dot_general(left, right, (((0,), (0,)), ((), ())), preferred_element_type=WIDE)


def resident(shape):
    return pl.BlockSpec(shape, lambda *_: (0,) * len(shape), pipeline_mode=pl.Buffered(1))


def unplace_kernel(order_ref, blocks_ref, slots_ref, hold, sem_in, sem_out):
    total = blocks_ref.shape[0]
    chunk = total // sem_in.shape[0]

    def read(i):
        part = pl.ds(i * chunk, chunk)
        return pltpu.make_async_copy(blocks_ref.at[part], hold.at[part], sem_in.at[i])

    def write(b):
        return pltpu.make_async_copy(hold.at[b], slots_ref.at[order_ref[b]], sem_out.at[b])

    for i in range(total // chunk):
        read(i).start()
    for i in range(total // chunk):
        read(i).wait()
        for b in range(i * chunk, (i + 1) * chunk):
            write(b).start()
    for b in range(total):
        write(b).wait()


def unplace_blocks(blocks, order):
    total = order.shape[0]
    return pl.pallas_call(
        unplace_kernel,
        grid_spec=pltpu.PrefetchScalarGridSpec(
            num_scalar_prefetch=1,
            grid=(1,),
            in_specs=[ANY],
            out_specs=ANY,
            scratch_shapes=[
                pltpu.VMEM((total, B, B), LOW),
                pltpu.SemaphoreType.DMA((48,)),
                pltpu.SemaphoreType.DMA((total,)),
            ],
        ),
        out_shape=jax.ShapeDtypeStruct((total, B, B), LOW),
        compiler_params=pltpu.CompilerParams(vmem_limit_bytes=VMEM_BYTES),
        name="unplace_blocks",
    )(order, blocks)


PIECES = 4
ROUTES = ((0, 2), (0, 4), (0, 1), (2, 4), (4, 2), (2, 1), (4, 1), (6, 1))


def flip(index, mask):
    for bit in range(3):
        if mask >> bit & 1:
            unit = 2**bit
            index = index + (1 - 2 * lax.rem(lax.div(index, unit), 2)) * unit
    return index


def segments(qkv, od, up):
    wide, down = od.shape[1] // B, up.shape[1] // B
    out = od.shape[0] // B - down
    deep, cols = qkv.shape[0] // B, qkv.shape[1] // B
    starts = [deep * cols, out * wide, deep * down]
    return (
        (qkv, 0, deep, cols, 0),
        (od, 0, out, wide, starts[0]),
        (up, 0, deep, down, sum(starts[:2])),
        (od, out, down, wide, sum(starts)),
    )


def gather_kernel(
    order_ref,
    len_ref,
    place_ref,
    vec_ref,
    freq_ref,
    w_hbm,
    x_hbm,
    cot_hbm,
    qkv_hbm,
    od_hbm,
    up_hbm,
    h1_hbm,
    h2_hbm,
    table_hbm,
    sum_ref,
    slots,
    wide,
    x_buf,
    c_buf,
    h_buf,
    table_buf,
    stage,
    send_sem,
    recv_sem,
    load_sem,
    row_sem,
    norm_sem,
    stage_sem,
):
    me = lax.axis_index("dp")
    each = w_hbm.shape[0]
    size = each // PIECES
    steps = x_hbm.shape[0] // STEP

    def piece(mask, q):
        return slots.at[pl.ds(flip(me, mask) * each + q * size, size)]

    def send(source, target, q):
        return pltpu.make_async_remote_copy(
            src_ref=piece(source, q),
            dst_ref=piece(source, q),
            send_sem=send_sem.at[ROUTES.index((source, target)), q],
            recv_sem=recv_sem.at[source ^ target, q],
            device_id={"dp": flip(me, target)},
            device_id_type=MESH,
        )

    def arrived(source, q):
        pltpu.make_async_remote_copy(
            src_ref=piece(source, q),
            dst_ref=piece(source, q),
            send_sem=send_sem.at[0, q],
            recv_sem=recv_sem.at[source, q],
            device_id={"dp": flip(me, 1)},
            device_id_type=MESH,
        ).wait_recv()

    def load(q):
        return pltpu.make_async_copy(
            w_hbm.at[pl.ds(q * size, size)], wide.at[q % 2], load_sem.at[q % 2]
        )

    def tile(i):
        return pl.ds(pl.multiple_of(i * STEP, STEP), STEP)

    def fetch(i, slot):
        return (
            pltpu.make_async_copy(x_hbm.at[tile(i), :], x_buf.at[slot], row_sem.at[0, slot]),
            pltpu.make_async_copy(cot_hbm.at[tile(i), :], c_buf.at[slot], row_sem.at[1, slot]),
        )

    def keep(i, slot):
        return (
            pltpu.make_async_copy(h_buf.at[slot, 0], h1_hbm.at[tile(i), :], norm_sem.at[0, slot]),
            pltpu.make_async_copy(h_buf.at[slot, 1], h2_hbm.at[tile(i), :], norm_sem.at[1, slot]),
            pltpu.make_async_copy(
                table_buf.at[slot], table_hbm.at[:, tile(i), :], norm_sem.at[2, slot]
            ),
        )

    def norm_step(i, slot, first):
        for copy in fetch(i, slot):
            copy.wait()

        @pl.when(jnp.logical_not(first))
        def _():
            for copy in keep(i, slot):
                copy.wait()

        x = x_buf[slot].astype(WIDE)
        center = x - jnp.mean(x, axis=1, keepdims=True)
        scale = lax.rsqrt(jnp.mean(center * center, axis=1, keepdims=True) + norm_eps)
        xhat = center * scale
        h_buf[slot, 0] = (xhat * vec_ref[0:1, :] + vec_ref[1:2, :]).astype(LOW)
        h_buf[slot, 1] = (xhat * vec_ref[2:3, :] + vec_ref[3:4, :]).astype(LOW)
        sum_ref[0:1, :] += jnp.sum(c_buf[slot].astype(WIDE), axis=0, keepdims=True)
        row = lax.broadcasted_iota(jnp.int32, (STEP, 128), 0) + i * STEP
        first = jnp.zeros((STEP, 128), jnp.int32)
        end = jnp.int32(0)
        for j in range(len_ref.shape[0]):
            mine = place_ref[j] == me
            end = end + jnp.where(mine, len_ref[j], 0)
            first = jnp.where(row >= jnp.where(mine, end, 1 << 30), end, first)
        angle = (row - first).astype(WIDE) * freq_ref[...]
        table_buf[slot, 0] = jnp.cos(angle)
        table_buf[slot, 1] = jnp.sin(angle)
        table_buf[slot, 2] = first.astype(WIDE)
        for copy in keep(i, slot):
            copy.start()

    for q in range(2):
        load(q).start()
    for slot in range(2):
        for copy in fetch(slot, slot):
            copy.start()
    barrier = pltpu.get_barrier_semaphore()
    for target in (1, 2, 4):
        pl.semaphore_signal(
            barrier, inc=1, device_id={"dp": flip(me, target)}, device_id_type=MESH
        )
    sum_ref[...] = jnp.zeros_like(sum_ref)
    for q in range(PIECES):
        load(q).wait()
        slots[pl.ds(me * each + q * size, size)] = wide[q % 2].astype(LOW)
        if q + 2 < PIECES:
            load(q + 2).start()
        if q == 0:
            pl.semaphore_wait(barrier, 3)
        for target in (2, 4, 1):
            send(0, target, q).start()

    for q in range(PIECES):

        @pl.loop(0, steps // (2 * PIECES))
        def _(k):
            i = (q * (steps // (2 * PIECES)) + k) * 2
            for slot in range(2):
                norm_step(i + slot, slot, i == 0)

                @pl.when(i + slot + 2 < steps)
                def _():
                    for copy in fetch(i + slot + 2, slot):
                        copy.start()

        arrived(2, q)
        if q % 2:
            send(2, 4, q).start()
        send(2, 1, q).start()
        arrived(4, q)
        if q % 2 == 0:
            send(4, 2, q).start()
        send(4, 1, q).start()
    for slot in range(2):
        for copy in keep(slot, slot):
            copy.wait()
    for q in range(PIECES):
        arrived(6, q)
        send(6, 1, q).start()
    for source in (1, 3, 5, 7):
        for q in range(PIECES):
            arrived(source, q)

    for ref, skip, panels, across, block in segments(qkv_hbm, od_hbm, up_hbm):

        def panel(i, slot):
            return pltpu.make_async_copy(
                stage.at[slot, :, pl.ds(0, across * B)],
                ref.at[lane((skip + i) * B), :],
                stage_sem.at[slot],
            )

        @pl.loop(0, panels // 2)
        def _(k):
            for slot in range(2):
                i = k * 2 + slot

                @pl.when(k > 0)
                def _():
                    panel(i, slot).wait()

                for j in range(across):
                    stage[slot, :, j * B : (j + 1) * B] = slots[order_ref[block + i * across + j]]
                panel(i, slot).start()

        for slot in range(2):
            panel(slot, slot).wait()

    for source, target in ROUTES:
        for q in range(PIECES):
            if (source, target) == (2, 4) and q % 2 == 0:
                continue
            if (source, target) == (4, 2) and q % 2:
                continue
            send(source, target, q).wait_send()


def gather_weights(blocks, order, seq_len, seq_device, tokens, cotangent, vectors, shapes):
    rows, d = tokens.shape
    each = blocks.shape[0]
    half = 10000.0 ** (-2.0 * jnp.arange(ROT // 2, dtype=WIDE) / ROT)
    frequency = jnp.concatenate([half, half, jnp.zeros((128 - ROT,), WIDE)])[None]
    smem = pl.BlockSpec(memory_space=pltpu.SMEM)
    vmem = pl.BlockSpec(memory_space=pltpu.VMEM)
    return pl.pallas_call(
        gather_kernel,
        in_specs=[smem, smem, smem, vmem, vmem, ANY, ANY, ANY],
        out_specs=[ANY] * 6 + [vmem],
        out_shape=[jax.ShapeDtypeStruct(s, LOW) for s in shapes]
        + [jax.ShapeDtypeStruct((rows, d), LOW)] * 2
        + [jax.ShapeDtypeStruct((3, rows, 128), WIDE)]
        + [jax.ShapeDtypeStruct((8, d), WIDE)],
        scratch_shapes=[
            pltpu.VMEM((order.shape[0], B, B), LOW),
            pltpu.VMEM((2, each // PIECES, B, B), WIDE),
            pltpu.VMEM((2, STEP, d), LOW),
            pltpu.VMEM((2, STEP, d), LOW),
            pltpu.VMEM((2, 2, STEP, d), LOW),
            pltpu.VMEM((2, 3, STEP, 128), WIDE),
            pltpu.VMEM((2, B, d), LOW),
            pltpu.SemaphoreType.DMA((8, PIECES)),
            pltpu.SemaphoreType.DMA((8, PIECES)),
            pltpu.SemaphoreType.DMA((2,)),
            pltpu.SemaphoreType.DMA((2, 2)),
            pltpu.SemaphoreType.DMA((3, 2)),
            pltpu.SemaphoreType.DMA((2,)),
        ],
        compiler_params=pltpu.CompilerParams(
            vmem_limit_bytes=VMEM_BYTES, collective_id=3, has_side_effects=True
        ),
        cost_estimate=pl.CostEstimate(
            flops=100_000_000_000, bytes_accessed=80 << 20, transcendentals=0
        ),
        name="gather_weights",
    )(order, seq_len, seq_device, vectors, frequency, blocks, tokens, cotangent)


def turn(values, cos, sin, back=False):
    lanes = lax.broadcasted_iota(jnp.int32, values.shape, 1)
    lower, upper = pltpu.roll(values, 96, 1), pltpu.roll(values, 32, 1)
    other = jnp.where(lanes < 32, -lower, upper)
    return values * cos - other * sin if back else values * cos + other * sin


def qkv_kernel(scale, h_ref, w_ref, bias_ref, table_ref, q_ref, k_ref, v_ref):
    for j in range(w_ref.shape[1] // HD):
        head, part = divmod(j, 3)
        cols = slice(head * HD, head * HD + HD)
        proj = dot(h_ref[...], w_ref[:, j * HD : (j + 1) * HD]) + bias_ref[:, j * HD : (j + 1) * HD]
        if part == 2:
            v_ref[:, cols] = proj.astype(LOW)
            continue
        front = turn(proj[:, :128], table_ref[0], table_ref[1])
        turned = jnp.concatenate([front, proj[:, 128:]], axis=1).astype(LOW)
        if part == 0:
            q_ref[:, cols] = (turned.astype(WIDE) * scale).astype(LOW)
        else:
            k_ref[:, cols] = turned


def project_qkv(h1, qkv_w, bias, table):
    rows, d = h1.shape
    cols = qkv_w.shape[1]
    out_cols = cols // 3
    tile = 512
    row_spec = lambda width: pl.BlockSpec((tile, width), lambda i: (i, 0))
    return pl.pallas_call(
        functools.partial(qkv_kernel, 1.0 / math.sqrt(HD)),
        grid=(rows // tile,),
        in_specs=[
            row_spec(d),
            resident((d, cols)),
            resident(bias.shape),
            pl.BlockSpec((3, tile, 128), lambda i: (0, i, 0)),
        ],
        out_specs=[row_spec(out_cols)] * 3,
        out_shape=[jax.ShapeDtypeStruct((rows, out_cols), LOW)] * 3,
        compiler_params=pltpu.CompilerParams(vmem_limit_bytes=VMEM_BYTES),
        name="project_qkv",
    )(h1, qkv_w, bias, table)


def attention_kernel(tile, table_ref, q_ref, k_ref, v_ref, ctx_ref, stats_ref, s_scr):
    step = pl.program_id(0)
    heads = q_ref.shape[1] // HD
    lanes = lax.broadcasted_iota(jnp.int32, (tile, 128), 1)

    def rows(c):
        first = table_ref[0][:, 0:1].astype(jnp.int32)
        stats = jnp.broadcast_to(first.astype(WIDE), (tile, 128))
        for h in range(heads):
            cols = slice(h * HD, (h + 1) * HD)
            q = q_ref[:, cols]
            top = jnp.full((tile, 1), masked_score, WIDE)
            for j in range(c + 1):
                keys = slice(j * tile, (j + 1) * tile)
                s = dot_nt(q, k_ref[keys, cols])
                col = lax.broadcasted_iota(jnp.int32, (tile, tile), 1) + j * tile
                ok = col >= first
                if j == c:
                    row = lax.broadcasted_iota(jnp.int32, (tile, tile), 0) + c * tile
                    ok = ok & (col <= row)
                s = jnp.where(ok, s, masked_score)
                s_scr[h, :, keys] = s
                top = jnp.maximum(top, jnp.max(s, axis=1, keepdims=True))
            total = jnp.zeros((tile, 1), WIDE)
            ctx = jnp.zeros((tile, HD), WIDE)
            for j in range(c + 1):
                keys = slice(j * tile, (j + 1) * tile)
                e = jnp.exp(s_scr[h, :, keys] - top)
                total = total + jnp.sum(e, axis=1, keepdims=True)
                ctx = ctx + dot(e.astype(LOW), v_ref[keys, cols])
            ctx_ref[:, cols] = (ctx * (1.0 / total)).astype(LOW)
            stats = jnp.where(lanes == h, top + jnp.log(total), stats)
        stats_ref[...] = stats

    for c in range(k_ref.shape[0] // tile):
        pl.when(step == c)(functools.partial(rows, c))


def attention_forward_rows(table, q, k, v):
    rows, cols = q.shape
    tile = 512
    tile_spec = pl.BlockSpec((tile, cols), lambda i: (i, 0))
    full_spec = resident((rows, cols))
    flops = rows * rows * cols * 3
    return pl.pallas_call(
        functools.partial(attention_kernel, tile),
        grid=(rows // tile,),
        in_specs=[pl.BlockSpec((1, tile, 128), lambda i: (2, i, 0)), tile_spec, full_spec, full_spec],
        out_specs=[tile_spec, pl.BlockSpec((tile, 128), lambda i: (i, 0))],
        out_shape=[
            jax.ShapeDtypeStruct((rows, cols), LOW),
            jax.ShapeDtypeStruct((rows, 128), WIDE),
        ],
        scratch_shapes=[pltpu.VMEM((cols // HD, tile, rows), WIDE)],
        compiler_params=pltpu.CompilerParams(vmem_limit_bytes=VMEM_BYTES),
        cost_estimate=pl.CostEstimate(flops=flops, bytes_accessed=30 << 20, transcendentals=0),
        name="attention_forward",
    )(table, q, k, v)


class Line:
    def __init__(self, out, part, got, across, sems):
        self.out, self.part, self.got, self.across = out, part, got, across
        (
            self.up_send,
            self.up_recv,
            self.far_send,
            self.far_recv,
            self.over_send,
            self.over_recv,
            self.down_send,
            self.down_recv,
            self.relay_send,
            self.relay_recv,
            self.own,
        ) = [sems.at[i] for i in range(11)]
        z = lax.axis_index("mp")
        self.inner = (z == 1) | (z == 2)
        self.near = (z >= 2).astype(jnp.int32)
        self.far = 1 - self.near
        self.partner = jnp.where(self.inner, jnp.where(z == 1, 0, 3), jnp.where(z == 0, 1, 2))
        self.other = 3 - z

    def rows(self, pair, which):
        return self.out.at[pl.ds(pl.multiple_of(pair * (2 * SUB) + which * SUB, SUB), SUB), :]

    def greet(self):
        barrier = pltpu.get_barrier_semaphore()
        pl.semaphore_signal(barrier, inc=1, device_id={"mp": self.partner}, device_id_type=MESH)

        @pl.when(self.inner)
        def _():
            pl.semaphore_signal(barrier, inc=1, device_id={"mp": self.other}, device_id_type=MESH)
            pl.semaphore_wait(barrier, 2)

        @pl.when(jnp.logical_not(self.inner))
        def _():
            pl.semaphore_wait(barrier, 1)

    def copy(self, src, dst, send, recv, pair, target):
        return pltpu.make_async_remote_copy(
            src_ref=src,
            dst_ref=dst,
            send_sem=send.at[pair],
            recv_sem=recv.at[pair],
            device_id={"mp": target},
            device_id_type=MESH,
        )

    def up(self, pair):
        return self.copy(
            self.part.at[pair], self.got.at[pair % GOT], self.up_send, self.up_recv, pair, self.partner
        )

    def far_sum(self, pair):
        src, dst = self.part.at[pair, self.far], self.across.at[pair % ACROSS]
        return self.copy(src, dst, self.far_send, self.far_recv, pair, self.other)

    def over(self, pair, which):
        src = self.part.at[pair, self.near]
        return self.copy(src, self.rows(pair, which), self.over_send, self.over_recv, pair, self.other)

    def down(self, pair):
        src = self.part.at[pair, self.near]
        return self.copy(
            src, self.rows(pair, self.near), self.down_send, self.down_recv, pair, self.partner
        )

    def relay(self, pair):
        far = self.rows(pair, self.far)
        return self.copy(far, far, self.relay_send, self.relay_recv, pair, self.partner)

    def keep(self, pair):
        src = self.part.at[pair, self.near]
        return pltpu.make_async_copy(src, self.rows(pair, self.near), self.own.at[pair])

    def send_up(self, pair):
        @pl.when(pair >= GOT)
        def _():
            self.down(pair - GOT).wait_recv()

        self.up(pair).start()

    def add_far(self, pair):
        self.up(pair).wait_recv()
        far = self.part[pair, self.far].astype(WIDE) + self.got[pair % GOT, self.far].astype(WIDE)
        self.part[pair, self.far] = far.astype(LOW)
        self.far_sum(pair).start()

    def finish_near(self, pair, base):
        self.far_sum(pair).wait_recv()
        total = (
            self.part[pair, self.near].astype(WIDE)
            + self.got[pair % GOT, self.near].astype(WIDE)
            + self.across[pair % ACROSS].astype(WIDE)
        )
        self.part[pair, self.near] = (base + total).astype(LOW)
        self.over(pair, self.near).start()
        self.down(pair).start()
        self.keep(pair).start()

    def send_relay(self, pair):
        self.over(pair, self.far).wait_recv()
        self.relay(pair).start()

    def drain(self):
        @pl.when(self.inner)
        def _():
            @pl.loop(0, PAIRS)
            def _(pair):
                self.far_sum(pair).wait_send()
                self.over(pair, self.near).wait_send()
                self.down(pair).wait_send()
                self.relay(pair).wait_send()
                self.keep(pair).wait()

        @pl.when(jnp.logical_not(self.inner))
        def _():
            @pl.loop(0, PAIRS)
            def _(pair):
                self.up(pair).wait_send()
                self.relay(pair).wait_recv()

            @pl.loop(PAIRS - GOT, PAIRS)
            def _(pair):
                self.down(pair).wait_recv()

    def tick(self, step, lag, base):
        ahead = GOT // PER_STEP

        @pl.when(jnp.logical_not(self.inner) & (step < ahead))
        def _():
            for s in range(PER_STEP):
                self.send_up(step * PER_STEP + s)

        @pl.when(
            jnp.logical_not(self.inner) & (step >= ahead) & (step < ahead + (PAIRS - GOT) // 2)
        )
        def _():
            for s in range(2):
                self.send_up(GOT + (step - ahead) * 2 + s)

        @pl.when(self.inner & (step >= lag + 2) & (step < lag + 2 + TICKS))
        def _():
            for s in range(2):
                self.send_relay((step - lag - 2) * 2 + s)

        @pl.when(self.inner & (step >= lag + 1) & (step < lag + 1 + TICKS))
        def _():
            for s in range(2):
                self.finish_near((step - lag - 1) * 2 + s, base(s))

        @pl.when(self.inner & (step >= lag) & (step < lag + TICKS))
        def _():
            for s in range(2):
                self.add_far((step - lag) * 2 + s)


def line_scratch(d):
    return [
        pltpu.VMEM((PAIRS, 2, SUB, d), LOW),
        pltpu.VMEM((GOT, 2, SUB, d), LOW),
        pltpu.VMEM((ACROSS, SUB, d), LOW),
        pltpu.SemaphoreType.DMA((11, PAIRS)),
    ]


def now(step):
    return jnp.minimum(step, STEPS - 1)


def row_block(width):
    return pl.BlockSpec((STEP, width), lambda i: (now(i), 0))


def base_block(width, lag):
    return pl.BlockSpec((4 * SUB, width), lambda i: (jnp.clip(i - lag - 1, 0, TICKS - 1), 0))


def lane(start):
    return pl.ds(pl.multiple_of(start, B), B)


def gelu_parts(z):
    e = jnp.exp(z * z * -0.5)
    t = 1.0 / (1.0 + jnp.abs(z) * (0.3275911 * math.sqrt(0.5)))
    poly = t * (
        0.5 * 0.254829592
        + t
        * (
            0.5 * -0.284496736
            + t * (0.5 * 1.421413741 + t * (0.5 * -1.453152027 + t * (0.5 * 1.061405429)))
        )
    )
    below = poly * e
    cdf = jnp.where(z >= 0, 1.0 - below, below)
    return cdf, e * (1.0 / math.sqrt(2.0 * math.pi))


def store_part(part_ref, step, cols, value):
    value = value.astype(LOW).reshape(PER_STEP, 2, SUB, value.shape[1])
    part_ref[pl.ds(step * PER_STEP, PER_STEP), :, :, cols] = value


FORWARD_LAG = 1
FORWARD_GRID = FORWARD_LAG + TICKS + 2


def weight_unit(a_t, b_ref, cols, stage, slot):
    for n in range(cols // 512):
        part = slice(n * 512, (n + 1) * 512)
        stage[pl.ds(pl.multiple_of(slot * B, B), B), part] = dot(a_t, b_ref[:, part]).astype(LOW)


def forward_kernel(
    h_ref,
    g_ref,
    ctx_ref,
    x_ref,
    stats_ref,
    bias_ref,
    vec_ref,
    table_ref,
    up_hbm,
    od_hbm,
    h1_hbm,
    h2_hbm,
    ctx_hbm,
    cot_hbm,
    q_hbm,
    k_hbm,
    v_hbm,
    out_ref,
    hg_hbm,
    qg_hbm,
    wg_hbm,
    sums_ref,
    qkv_sums_ref,
    up_buf,
    od_buf,
    act_all,
    hg_all,
    part,
    got,
    across,
    sems,
    grad_all,
    stats,
    dq_scr,
    dk_scr,
    dv_scr,
    load_sem,
    panel_sem,
    stage_sem,
    hg_sem,
    head_sem,
):
    step = pl.program_id(0)
    line = Line(out_ref, part, got, across, sems)
    heads = ctx_ref.shape[1]
    rows, units = act_all.shape
    qkv_cols = qg_hbm.shape[1]
    width = 512
    tiles = units // width
    stage = od_buf.at[pl.ds(rows, 2 * B), :]

    def load_up(n):
        cols = pl.ds(n * width, width)
        return pltpu.make_async_copy(up_hbm.at[:, cols], up_buf.at[:, cols], load_sem.at[n])

    def load_down(n):
        part_rows = pl.ds(heads + n * width, width)
        return pltpu.make_async_copy(
            od_hbm.at[part_rows, :], od_buf.at[part_rows, :], load_sem.at[tiles + n]
        )

    def load_out():
        part_rows = pl.ds(0, heads)
        return pltpu.make_async_copy(
            od_hbm.at[part_rows, :], od_buf.at[part_rows, :], load_sem.at[2 * tiles]
        )

    def load_cot():
        return pltpu.make_async_copy(
            cot_hbm, od_buf.at[pl.ds(0, rows), :], load_sem.at[2 * tiles + 1]
        )

    def load_head(h):
        cols = pl.ds(pl.multiple_of(h * HD, HD), HD)
        return [
            pltpu.make_async_copy(
                src.at[:, cols], act_all.at[:, pl.ds(i * HD, HD)], head_sem.at[i]
            )
            for i, src in enumerate((q_hbm, k_hbm, v_hbm))
        ]

    def store_qg():
        return pltpu.make_async_copy(hg_all.at[:, pl.ds(0, qkv_cols)], qg_hbm, head_sem.at[5])

    def panel_cols(slot):
        return lane(qkv_cols + slot * B)

    def panel(src, i, slot):
        return pltpu.make_async_copy(
            src.at[:, lane(i * B)], up_buf.at[:, panel_cols(slot)], panel_sem.at[slot]
        )

    def store_hg(i):
        part_rows = pl.ds(pl.multiple_of(i * STEP, STEP), STEP)
        return pltpu.make_async_copy(
            hg_all.at[part_rows, :], hg_hbm.at[part_rows, :], hg_sem.at[i]
        )

    def stage_out(block, j, slot):
        return pltpu.make_async_copy(
            stage.at[lane(slot * B), pl.ds(j * B, B)], wg_hbm.at[block + j], stage_sem.at[slot]
        )

    def stage_wait(cols, slot):
        place = stage.at[lane(slot * B), pl.ds(0, cols)]
        pltpu.make_async_copy(place, place, stage_sem.at[slot]).wait()

    @pl.when(step == 0)
    def _():
        for n in range(tiles):
            load_up(n).start()
            load_down(n).start()
        load_out().start()
        line.greet()
        sums_ref[...] = jnp.zeros_like(sums_ref)

    @pl.when(step < STEPS)
    def _():
        here = pl.ds(pl.multiple_of(step * STEP, STEP), STEP)
        for n in range(tiles):
            cols = slice(n * width, (n + 1) * width)

            @pl.when(step == 0)
            def _():
                load_up(n).wait()
                load_down(n).wait()

            bias = bias_ref[:, qkv_cols + n * width : qkv_cols + (n + 1) * width]
            hidden = dot(h_ref[...], up_buf[:, cols]) + bias
            act_grad = dot_nt(g_ref[...], od_buf[heads + n * width : heads + (n + 1) * width, :])
            cdf, density = gelu_parts(hidden)
            act_all[here, cols] = (hidden * cdf).astype(LOW)
            grad = (act_grad * (cdf + hidden * density)).astype(LOW)
            hg_all[here, cols] = grad
            sums_ref[0:1, cols] += jnp.sum(grad.astype(WIDE), axis=0, keepdims=True)

        @pl.when(step == 0)
        def _():
            load_out().wait()

        store_hg(step).start()
        grad = dot_nt(g_ref[...], od_buf[:heads, :]).astype(LOW)
        grad_all[here, :] = grad
        lanes = lax.broadcasted_iota(jnp.int32, (STEP, 128), 1)
        info = stats_ref[...]
        for h in range(heads // HD):
            cols = slice(h * HD, (h + 1) * HD)
            both = ctx_ref[:, cols].astype(WIDE) * grad[:, cols].astype(WIDE)
            info = jnp.where(lanes == 64 + h, jnp.sum(both, axis=1, keepdims=True), info)
        stats[here, :] = info
        for n in range(od_buf.shape[1] // width):
            cols = slice(n * width, (n + 1) * width)
            value = dot(ctx_ref[...], od_buf[:heads, cols]) + dot(
                act_all[here, :], od_buf[heads:, cols]
            )
            store_part(part, step, cols, value)

    @pl.when(step == STEPS - 1)
    def _():
        panel(h2_hbm, 0, 0).start()
        load_cot().start()

    wide = od_buf.shape[1] // B
    out_first = rows // B * (qkv_cols // B)
    up_first = out_first + heads // B * wide
    down_first = up_first + rows // B * (units // B)

    def unit(index, a_t, b_ref, cols, first):
        slot = index % 2

        @pl.when(index >= 2)
        def _():
            stage_wait(cols, slot)

        weight_unit(a_t, b_ref, cols, stage, slot)
        for j in range(cols // B):
            stage_out(first + index * (cols // B), j, slot).start()

    def settle(cols):
        for slot in range(2):
            stage_wait(cols, slot)

    @pl.when((step == 8) | (step == 9))
    def _():
        @pl.loop(0, 4)
        def _(k):
            i = (step - 8) * 4 + k
            panel(h2_hbm, i, i % 2).wait()

            @pl.when(i < 7)
            def _():
                panel(h2_hbm, i + 1, (i + 1) % 2).start()

            unit(i, up_buf[:, panel_cols(i % 2)].T, hg_all, units, up_first)

    @pl.when(step == 10)
    def _():
        settle(units)
        load_cot().wait()

    @pl.when((step == 10) | (step == 11))
    def _():
        @pl.loop(0, 4)
        def _(k):
            i = (step - 10) * 4 + k
            cot = od_buf.at[pl.ds(0, rows), :]
            unit(i, act_all[:, lane(i * B)].T, cot, wide * B, down_first)

    @pl.when(step == 11)
    def _():
        for copy in load_head(0):
            copy.start()

    @pl.when(step == 12)
    def _():
        settle(wide * B)

        @pl.loop(0, STEPS)
        def _(i):
            store_hg(i).wait()

    def head_grads(h, start, stop):
        tile = 512
        count = rows // tile

        def tile_rows(i):
            return pl.ds(pl.multiple_of(i * tile, tile), tile)

        def put(i, part, values):
            cols = pl.ds(pl.multiple_of(h * 3 * HD + part * HD, HD), HD)
            hg_all[tile_rows(i), cols] = values.astype(LOW)

        def turned_back(i, values):
            front = turn(values[:, :128], table_ref[0, tile_rows(i), :], table_ref[1, tile_rows(i), :], True)
            return jnp.concatenate([front, values[:, 128:]], axis=1)

        @pl.loop(start, stop)
        def _(j):
            keys = act_all[tile_rows(j), HD : 2 * HD]
            values = act_all[tile_rows(j), 2 * HD : 3 * HD]
            dk_scr[...] = jnp.zeros_like(dk_scr)
            dv_scr[...] = jnp.zeros_like(dv_scr)

            @pl.loop(j, count)
            def _(i):
                q = act_all[tile_rows(i), 0:HD]
                g = grad_all[tile_rows(i), pl.ds(pl.multiple_of(h * HD, HD), HD)]
                info = stats[tile_rows(i), :]
                log_total = jnp.where(h == 0, info[:, 0:1], info[:, 1:2])
                delta = jnp.where(h == 0, info[:, 64:65], info[:, 65:66])
                first = info[:, 2:3].astype(jnp.int32) - j * tile
                col = lax.broadcasted_iota(jnp.int32, (tile, tile), 1)
                row = lax.broadcasted_iota(jnp.int32, (tile, tile), 0) + (i - j) * tile
                ok = (col >= first) & (col <= row)
                p = jnp.where(ok, jnp.exp(dot_nt(q, keys) - log_total), 0.0)
                ds = (p * (dot_nt(g, values) - delta)).astype(LOW)
                dv_scr[...] += dot_tn(p.astype(LOW), g)
                dk_scr[...] += dot_tn(ds, q)
                dq_scr[tile_rows(i), :] += dot(ds, keys)

            put(j, 1, turned_back(j, dk_scr[...]))
            put(j, 2, dv_scr[...])

        @pl.when(stop == count)
        def _():
            @pl.loop(0, count)
            def _(i):
                put(i, 0, turned_back(i, dq_scr[tile_rows(i), :] * (1.0 / math.sqrt(HD))))

    @pl.when((step == 12) | (step == 14))
    def _():
        for copy in load_head((step - 12) // 2):
            copy.wait()
        dq_scr[...] = jnp.zeros_like(dq_scr)

    @pl.when((step >= 12) & (step < 16))
    def _():
        second = (step - 12) % 2
        head_grads((step - 12) // 2, second, 1 + 3 * second)

    @pl.when(step == 13)
    def _():
        for copy in load_head(1):
            copy.start()

    @pl.when(step == 16)
    def _():
        store_qg().start()
        for j in range(2):
            panel(ctx_hbm, j, j).start()
        total = jnp.zeros((1, qkv_cols), WIDE)
        for i in range(rows // 512):
            part_rows = slice(i * 512, (i + 1) * 512)
            total = total + jnp.sum(hg_all[part_rows, :qkv_cols].astype(WIDE), axis=0, keepdims=True)
        qkv_sums_ref[...] = jnp.broadcast_to(total, qkv_sums_ref.shape)
        for j in range(2):
            panel(ctx_hbm, j, j).wait()

        @pl.loop(0, 2)
        def _(j):
            cot = od_buf.at[pl.ds(0, rows), :]
            unit(j, up_buf[:, panel_cols(j)].T, cot, wide * B, out_first)

        settle(wide * B)
        panel(h1_hbm, 0, 0).start()

    @pl.when((step == 17) | (step == 18))
    def _():
        @pl.loop(0, 4)
        def _(k):
            i = (step - 17) * 4 + k
            panel(h1_hbm, i, i % 2).wait()

            @pl.when(i < 7)
            def _():
                panel(h1_hbm, i + 1, (i + 1) % 2).start()

            grads = hg_all.at[:, pl.ds(0, qkv_cols)]
            unit(i, up_buf[:, panel_cols(i % 2)].T, grads, qkv_cols, 0)

    @pl.when(step == FORWARD_GRID - 1)
    def _():
        settle(qkv_cols)
        store_qg().wait()

    def base(s):
        near = pl.ds(pl.multiple_of(s * 2 * SUB + line.near * SUB, SUB), SUB)
        return x_ref[near, :].astype(WIDE) + (vec_ref[4:5, :] + vec_ref[5:6, :])

    line.tick(step, FORWARD_LAG, base)

    @pl.when(step == FORWARD_GRID - 1)
    def _():
        line.drain()


def forward_line(h1, h2, cotangent, ctx, heads, stats, table, tokens, up_w, od_w, bias, vectors):
    rows, d = tokens.shape
    units = up_w.shape[1]
    head_cols = ctx.shape[1]
    qkv_cols = 3 * head_cols
    total = (d * qkv_cols + od_w.shape[0] * d + d * units) // (B * B)
    return pl.pallas_call(
        forward_kernel,
        grid=(FORWARD_GRID,),
        in_specs=[
            row_block(d),
            row_block(d),
            row_block(head_cols),
            base_block(d, FORWARD_LAG),
            row_block(128),
            resident(bias.shape),
            resident(vectors.shape),
            resident((2, rows, 128)),
        ]
        + [ANY] * 9,
        out_specs=[ANY] * 4
        + [pl.BlockSpec((8, units), lambda i: (0, 0)), pl.BlockSpec((8, qkv_cols), lambda i: (0, 0))],
        out_shape=[
            jax.ShapeDtypeStruct((rows, d), LOW),
            jax.ShapeDtypeStruct((rows, units), LOW),
            jax.ShapeDtypeStruct((rows, qkv_cols), LOW),
            jax.ShapeDtypeStruct((total, B, B), LOW),
            jax.ShapeDtypeStruct((8, units), WIDE),
            jax.ShapeDtypeStruct((8, qkv_cols), WIDE),
        ],
        scratch_shapes=[
            pltpu.VMEM(up_w.shape, LOW),
            pltpu.VMEM(od_w.shape, LOW),
            pltpu.VMEM((rows, units), LOW),
            pltpu.VMEM((rows, units), LOW),
        ]
        + line_scratch(d)
        + [
            pltpu.VMEM((rows, head_cols), LOW),
            pltpu.VMEM((rows, 128), WIDE),
            pltpu.VMEM((rows, HD), WIDE),
            pltpu.VMEM((512, HD), WIDE),
            pltpu.VMEM((512, HD), WIDE),
            pltpu.SemaphoreType.DMA((10,)),
            pltpu.SemaphoreType.DMA((2,)),
            pltpu.SemaphoreType.DMA((2,)),
            pltpu.SemaphoreType.DMA((STEPS,)),
            pltpu.SemaphoreType.DMA((6,)),
        ],
        compiler_params=pltpu.CompilerParams(
            vmem_limit_bytes=FORWARD_VMEM, collective_id=1, has_side_effects=True
        ),
        cost_estimate=pl.CostEstimate(
            flops=200_000_000_000, bytes_accessed=80 << 20, transcendentals=0
        ),
        name="forward_line",
    )(
        h2,
        cotangent,
        ctx,
        tokens,
        stats,
        bias,
        vectors,
        table,
        up_w,
        od_w,
        h1,
        h2,
        ctx,
        cotangent,
        *heads,
    )


BACKWARD_LAG = 1
BACKWARD_GRID = BACKWARD_LAG + TICKS + 2


class Spread:
    def __init__(self, own, along_mp, along_dp, sems):
        self.own = own
        self.stages = [
            ("dp", along_dp, sems.at[0], sems.at[1]),
            ("mp", along_mp, sems.at[2], sems.at[3]),
        ]

    def others(self, stage):
        axis, buf, send, recv = self.stages[stage]
        me = lax.axis_index(axis)
        return axis, buf, send, recv, me, [lax.rem(me + k, buf.shape[0]) for k in range(1, buf.shape[0])]

    def greet(self):
        barrier = pltpu.get_barrier_semaphore()
        count = 0
        for stage in range(2):
            axis, _, _, _, _, others = self.others(stage)
            for other in others:
                pl.semaphore_signal(barrier, inc=1, device_id={axis: other}, device_id_type=MESH)
            count += len(others)
        pl.semaphore_wait(barrier, count)

    def copies(self, stage):
        axis, buf, send, recv, me, others = self.others(stage)
        return [
            (
                pltpu.make_async_remote_copy(
                    src_ref=self.own,
                    dst_ref=buf.at[me],
                    send_sem=send.at[k],
                    recv_sem=recv.at[me],
                    device_id={axis: other},
                    device_id_type=MESH,
                ),
                pltpu.make_async_remote_copy(
                    src_ref=self.own,
                    dst_ref=buf.at[other],
                    send_sem=send.at[k],
                    recv_sem=recv.at[other],
                    device_id={axis: other},
                    device_id_type=MESH,
                ),
            )
            for k, other in enumerate(others)
        ]

    def start(self, stage):
        _, buf, _, _, me, _ = self.others(stage)
        buf[me] = self.own[...]
        for out, _ in self.copies(stage):
            out.start()

    def finish(self, stage):
        _, buf, _, _, _, _ = self.others(stage)
        for out, back in self.copies(stage):
            out.wait_send()
            back.wait_recv()
        total = buf[0]
        for i in range(1, buf.shape[0]):
            total = total + buf[i]
        return total


def backward_kernel(
    qg_ref,
    hg_ref,
    x_ref,
    g_ref,
    qkv_ref,
    up_ref,
    vec_ref,
    cot_sums,
    qkv_sums,
    hidden_sums,
    sums_ref,
    out_ref,
    gc_scr,
    xhat_scr,
    own,
    along_mp,
    along_dp,
    spread_sems,
    part,
    got,
    across,
    sems,
):
    step = pl.program_id(0)
    line = Line(out_ref, part, got, across, sems)
    spread = Spread(own, along_mp, along_dp, spread_sems)
    d = x_ref.shape[1]
    width = 512

    @pl.when(step == 0)
    def _():
        spread.greet()
        own[...] = jnp.zeros_like(own)
        own[4:5, :] = cot_sums[0:1, :]
        own[5:6, : qkv_sums.shape[1]] = qkv_sums[0:1, :]
        own[6:7, : hidden_sums.shape[1]] = hidden_sums[0:1, :]

    @pl.when(step < STEPS)
    def _():
        x = x_ref[...].astype(WIDE)
        center = x - jnp.mean(x, axis=1, keepdims=True)
        scale = lax.rsqrt(jnp.mean(center * center, axis=1, keepdims=True) + norm_eps)
        xhat_scr[...] = center * scale
        mean = jnp.zeros((STEP, 1), WIDE)
        slope = jnp.zeros((STEP, 1), WIDE)
        for n in range(d // width):
            cols = slice(n * width, (n + 1) * width)
            e1 = dot_nt(qg_ref[...], qkv_ref[cols, :])
            e2 = dot_nt(hg_ref[...], up_ref[cols, :])
            xhat = xhat_scr[:, cols]
            gc = e1 * vec_ref[0:1, cols] + e2 * vec_ref[2:3, cols]
            gc_scr[:, cols] = gc
            mean = mean + jnp.sum(gc, axis=1, keepdims=True)
            slope = slope + jnp.sum(gc * xhat, axis=1, keepdims=True)
            own[0:1, cols] += jnp.sum(e1 * xhat, axis=0, keepdims=True)
            own[1:2, cols] += jnp.sum(e1, axis=0, keepdims=True)
            own[2:3, cols] += jnp.sum(e2 * xhat, axis=0, keepdims=True)
            own[3:4, cols] += jnp.sum(e2, axis=0, keepdims=True)
        mean = mean * (1.0 / d)
        slope = slope * (1.0 / d)
        for n in range(d // width):
            cols = slice(n * width, (n + 1) * width)
            value = (gc_scr[:, cols] - mean - xhat_scr[:, cols] * slope) * scale
            store_part(part, step, cols, value)

    @pl.when(step == STEPS)
    def _():
        spread.start(0)

    @pl.when(step == STEPS + 4)
    def _():
        own[...] = spread.finish(0)
        spread.start(1)

    def base(s):
        near = pl.ds(pl.multiple_of(s * 2 * SUB + line.near * SUB, SUB), SUB)
        return g_ref[near, :].astype(WIDE)

    line.tick(step, BACKWARD_LAG, base)

    @pl.when(step == BACKWARD_GRID - 1)
    def _():
        line.drain()
        total = spread.finish(1)
        row = lax.broadcasted_iota(jnp.int32, total.shape, 0)
        sums_ref[...] = jnp.where(row < 4, total, own[...])


def backward_line(qkv_grad, hidden_grad, tokens, cotangent, qkv_w, up_w, vectors, *sums):
    rows, d = tokens.shape
    small = (8, d)
    return pl.pallas_call(
        backward_kernel,
        grid=(BACKWARD_GRID,),
        in_specs=[
            row_block(qkv_grad.shape[1]),
            row_block(hidden_grad.shape[1]),
            row_block(d),
            base_block(d, BACKWARD_LAG),
            resident(qkv_w.shape),
            resident(up_w.shape),
            resident(vectors.shape),
        ]
        + [resident(part.shape) for part in sums],
        out_specs=[pl.BlockSpec(small, lambda i: (0, 0)), ANY],
        out_shape=[jax.ShapeDtypeStruct(small, WIDE), jax.ShapeDtypeStruct((rows, d), LOW)],
        scratch_shapes=[
            pltpu.VMEM((STEP, d), WIDE),
            pltpu.VMEM((STEP, d), WIDE),
            pltpu.VMEM(small, WIDE),
            pltpu.VMEM((4,) + small, WIDE),
            pltpu.VMEM((8,) + small, WIDE),
            pltpu.SemaphoreType.DMA((4, 8)),
        ]
        + line_scratch(d),
        compiler_params=pltpu.CompilerParams(
            vmem_limit_bytes=VMEM_BYTES, collective_id=2, has_side_effects=True
        ),
        cost_estimate=pl.CostEstimate(
            flops=200_000_000_000, bytes_accessed=60 << 20, transcendentals=0
        ),
        name="backward_line",
    )(
        qkv_grad, hidden_grad, tokens, cotangent, qkv_w, up_w, vectors, *sums
    )


def halves(values):
    high = values.astype(LOW)
    return high, (values - high.astype(WIDE)).astype(LOW)


def shampoo_kernel(
    g_ref,
    w_ref,
    ls_ref,
    rs_ref,
    lr_ref,
    rr_ref,
    sums_ref,
    vec_ref,
    vec_stat_ref,
    unit_ref,
    unit_stat_ref,
    one_in,
    two_in,
    grad_ref,
    left_ref,
    right_ref,
    weight_ref,
    vec_grad_out,
    vec_stat_out,
    vec_out,
    unit_grad_out,
    unit_stat_out,
    unit_out,
    one_out,
    two_out,
    hold,
    sems,
):
    step = pl.program_id(0)
    pairs = ((one_in, one_out), (two_in, two_out))
    fetch = [pltpu.make_async_copy(a, hold.at[i], sems.at[0, i]) for i, (a, _) in enumerate(pairs)]
    store = [pltpu.make_async_copy(hold.at[i], b, sems.at[1, i]) for i, (_, b) in enumerate(pairs)]

    @pl.when(step == 0)
    def _():
        for copy in fetch:
            copy.start()
        vec_grad_out[0:5, :] = sums_ref[0:5, :]
        vec_grad_out[5:6, :] = sums_ref[4:5, :]
        vec_stat_out[...], vec_out[...] = vector_update(
            vec_ref[...], vec_stat_ref[...], vec_grad_out[...]
        )
        qkv_cols = unit_ref.shape[1] * 3 // 7
        unit_grad_out[:, :qkv_cols] = sums_ref[5:6, :qkv_cols]
        unit_grad_out[:, qkv_cols:] = sums_ref[6:7, : unit_ref.shape[1] - qkv_cols]
        unit_stat_out[...], unit_out[...] = vector_update(
            unit_ref[...], unit_stat_ref[...], unit_grad_out[...]
        )

    for i in range(2):

        @pl.when(step == pl.num_programs(0) * (i + 1) // 3)
        def _():
            fetch[i].wait()
            store[i].start()

    @pl.when(step == pl.num_programs(0) - 1)
    def _():
        for copy in store:
            copy.wait()

    for n in range(g_ref.shape[0]):
        g = g_ref[n]
        grad_ref[n] = g.astype(WIDE)
        left_ref[n] = 0.5 * ls_ref[n] + 0.5 * dot_nt(g, g)
        right_ref[n] = 0.5 * rs_ref[n] + 0.5 * dot_tn(g, g)
        l_high, l_low = halves(lr_ref[n])
        r_high, r_low = halves(rr_ref[n])
        d_high, d_low = halves(dot(l_high, g) + dot(l_low, g))
        direction = dot(d_high, r_high) + dot(d_low, r_high) + dot(d_high, r_low)
        weight = w_ref[n]
        size = 1.0 / (B * B)
        weight_size = jnp.sqrt(jnp.sum(weight * weight, keepdims=True) * size)
        step_size = jnp.sqrt(jnp.sum(direction * direction, keepdims=True) * size + 1e-06)
        weight_ref[n] = weight - direction * (step_share * weight_size / step_size)


def shampoo(grads, weights, left_stat, right_stat, left_root, right_root, small, one, two):
    count = grads.shape[0]
    group = 2
    spec = pl.BlockSpec((group, B, B), lambda i: (i, 0, 0))
    results = [small[1]] * 3 + [small[3]] * 3
    return pl.pallas_call(
        shampoo_kernel,
        grid=(count // group,),
        in_specs=[spec] * 6 + [resident(part.shape) for part in small] + [ANY] * 2,
        out_specs=[spec] * 4
        + [pl.BlockSpec(part.shape, lambda i: (0, 0)) for part in results]
        + [ANY] * 2,
        out_shape=[jax.ShapeDtypeStruct((count, B, B), WIDE)] * 4
        + [jax.ShapeDtypeStruct(part.shape, part.dtype) for part in results + [one, two]],
        scratch_shapes=[
            pltpu.VMEM((2,) + one.shape, one.dtype),
            pltpu.SemaphoreType.DMA((2, 2)),
        ],
        compiler_params=pltpu.CompilerParams(vmem_limit_bytes=VMEM_BYTES),
        name="shampoo",
    )(grads, weights, left_stat, right_stat, left_root, right_root, *small, one, two)


def per_device_line(
    tokens,
    cotangent,
    seq_len,
    seq_device,
    owner_map,
    weight_blocks,
    left_stat,
    right_stat,
    left_root,
    right_root,
    vectors,
    vector_stat,
    unit_bias,
    unit_stat,
):
    groups = lax.axis_size("mp")
    d = tokens.shape[1]
    qkv_cols = 3 * d // groups
    head_cols = d // groups
    unit_cols = FF // groups
    shapes = ((d, qkv_cols), (head_cols + unit_cols, d), (d, unit_cols))
    qkv_w, od_w, up_w, normed_one, normed_two, table, cot_sums = gather_weights(
        weight_blocks[0], owner_map, seq_len, seq_device, tokens, cotangent, vectors, shapes
    )
    q, k, v = project_qkv(normed_one, qkv_w, unit_bias, table)
    ctx, stats = attention_forward_rows(table, q, k, v)
    block_out, hidden_grad, qkv_grad, weight_grads, hidden_sums, qkv_sums = forward_line(
        normed_one,
        normed_two,
        cotangent,
        ctx,
        (q, k, v),
        stats,
        table,
        tokens,
        up_w,
        od_w,
        unit_bias,
        vectors,
    )
    slots = unplace_blocks(weight_grads, owner_map)
    owned = lax.psum_scatter(slots, "dp", scatter_dimension=0, tiled=True)
    qkv_grad, hidden_grad, slots = lax.optimization_barrier((qkv_grad, hidden_grad, slots))
    sums, input_grad = backward_line(
        qkv_grad,
        hidden_grad,
        tokens,
        cotangent,
        qkv_w,
        up_w,
        vectors,
        cot_sums,
        qkv_sums,
        hidden_sums,
    )
    (
        block_grad,
        left_new,
        right_new,
        weight_new,
        vector_grad,
        vector_stat_new,
        vector_new,
        unit_grad,
        unit_stat_new,
        unit_new,
        block_out,
        input_grad,
    ) = shampoo(
        owned,
        weight_blocks[0],
        left_stat[0],
        right_stat[0],
        left_root[0],
        right_root[0],
        (sums, vectors, vector_stat, unit_bias, unit_stat),
        block_out,
        input_grad,
    )
    return (
        block_out,
        input_grad,
        block_grad[None],
        left_new[None],
        right_new[None],
        weight_new[None],
        vector_grad,
        vector_stat_new,
        vector_new,
        unit_grad,
        unit_stat_new,
        unit_new,
    )


def solution(mesh):
    placed = (
        P("dp", None),
        P("dp", None),
        P(),
        P(),
        P(),
        P("mp", "dp", None, None),
        P("mp", "dp", None, None),
        P("mp", "dp", None, None),
        P("mp", "dp", None, None),
        P("mp", "dp", None, None),
        P(),
        P(),
        P("mp", None),
        P("mp", None),
    )
    body = per_device
    if mesh.shape["dp"] == 8 and mesh.shape["mp"] == 4:
        body = per_device_line
    return jax.shard_map(
        body,
        mesh=mesh,
        in_specs=placed,
        out_specs=(
            P("dp", None),
            P("dp", None),
            P("mp", "dp", None, None),
            P("mp", "dp", None, None),
            P("mp", "dp", None, None),
            P("mp", "dp", None, None),
            P(),
            P(),
            P(),
            P("mp", None),
            P("mp", None),
            P("mp", None),
        ),
        check_vma=False,
    )
```

```python
import functools
import math

import jax
import jax.numpy as jnp
from jax import lax
from jax.experimental import pallas as pl
from jax.experimental.pallas import tpu as pltpu
from jax.sharding import PartitionSpec as P

D = 2048
HEADS = 8
HD = 256
ROT = 64
FF = 8192
B = 256


highest = lax.Precision.HIGHEST
norm_eps = 1e-05
step_share = 0.5
vector_rate = 0.15
masked_score = -1e30


def layer_norm(values, gain, shift):
    center = values - jnp.mean(values, axis=-1, keepdims=True)
    spread = jnp.mean(center * center, axis=-1, keepdims=True)
    return center * lax.rsqrt(spread + norm_eps) * gain + shift


def gelu_exact(values):
    return jax.nn.gelu(values, approximate=False)


def segment_layout(seq_len, seq_device, device, row_count):
    is_mine = seq_device == device
    lengths = jnp.where(is_mine, seq_len, 0)
    seq_ends = jnp.cumsum(lengths)
    row_index = jnp.arange(row_count, dtype=jnp.int32)
    passed = is_mine[None, :] & (seq_ends[None, :] <= row_index[:, None])
    segment = jnp.sum(passed.astype(jnp.int32), axis=1)
    seq_start = jnp.max(jnp.where(passed, seq_ends[None, :], 0), axis=1)
    return (segment, row_index - seq_start)


def rotary_tables(position):
    half_rot = ROT // 2
    frequency = 10000.0 ** (-2.0 * jnp.arange(half_rot, dtype=jnp.float32) / ROT)
    angles = position.astype(jnp.float32)[:, None] * frequency[None, :]
    cosine_table = jnp.concatenate([jnp.cos(angles), jnp.cos(angles)], axis=1)
    sine_table = jnp.concatenate([jnp.sin(angles), jnp.sin(angles)], axis=1)
    return (cosine_table, sine_table)


def rotate(values, cosine_table, sine_table):
    rot_dims = cosine_table.shape[1]
    half_rot = rot_dims // 2
    leading = values[..., :rot_dims]
    turned = jnp.concatenate([-leading[..., half_rot:], leading[..., :half_rot]], axis=-1)
    rotated = leading * cosine_table[:, None, :] + turned * sine_table[:, None, :]
    return jnp.concatenate([rotated, values[..., rot_dims:]], axis=-1)


def blocks_to_matrix(blocks, across):
    down_count = blocks.shape[0] // across
    return (
        blocks.reshape(down_count, across, B, B)
        .transpose(0, 2, 1, 3)
        .reshape(down_count * B, across * B)
    )


def matrix_to_blocks(matrix):
    down_count = matrix.shape[0] // B
    across = matrix.shape[1] // B
    return (
        matrix.reshape(down_count, B, across, B)
        .transpose(0, 2, 1, 3)
        .reshape(down_count * across, B, B)
    )


def split_blocks(blocks, qkv_cols, head_cols, unit_cols):
    qkv_end = D // B * (qkv_cols // B)
    out_end = qkv_end + head_cols // B * (D // B)
    up_end = out_end + D // B * (unit_cols // B)
    qkv_w = blocks_to_matrix(blocks[:qkv_end], qkv_cols // B)
    out_w = blocks_to_matrix(blocks[qkv_end:out_end], D // B)
    up_w = blocks_to_matrix(blocks[out_end:up_end], unit_cols // B)
    down_w = blocks_to_matrix(blocks[up_end:], D // B)
    return (qkv_w, out_w, up_w, down_w)


def apply_step(weight, direction):
    weight_size = jnp.sqrt(jnp.mean(weight * weight, axis=(-2, -1), keepdims=True))
    step_size = jnp.sqrt(jnp.mean(direction * direction, axis=(-2, -1), keepdims=True) + 1e-06)
    return weight - step_share * weight_size * direction / step_size


def vector_update(values, old_stat, gradient):
    new_stat = 0.5 * old_stat + 0.5 * gradient * gradient
    return (new_stat, values - vector_rate * gradient * lax.rsqrt(new_stat))


def block_mask(block_segment, block_row, segment, column):
    return (block_segment[:, None] == segment[None, :]) & (column[None, :] <= block_row[:, None])


def attention_forward(queries, keys_low, values_low, segment):
    row_count, head_count, head_dim = queries.shape
    block_rows = min(512, row_count)
    block_count = row_count // block_rows
    score_scale = 1.0 / math.sqrt(head_dim)
    column = jnp.arange(row_count, dtype=jnp.int32)

    def one_block(inputs):
        block_query, block_segment, block_row = inputs
        scores = (
            jnp.einsum("qhd,khd->hqk", block_query, keys_low, preferred_element_type=jnp.float32)
            * score_scale
        )
        scores = jnp.where(
            block_mask(block_segment, block_row, segment, column)[None], scores, masked_score
        )
        log_total = jax.nn.logsumexp(scores, axis=-1)
        weights = jnp.exp(scores - log_total[:, :, None]).astype(jnp.bfloat16)
        context = jnp.einsum(
            "hqk,khd->qhd", weights, values_low, preferred_element_type=jnp.float32
        )
        return (context, log_total)

    contexts, log_totals = lax.map(
        one_block,
        (
            queries.reshape(block_count, block_rows, head_count, head_dim),
            segment.reshape(block_count, block_rows),
            column.reshape(block_count, block_rows),
        ),
    )
    return (contexts.reshape(row_count, head_count, head_dim), log_totals)


def attention_backward(queries, keys_low, values_low, context_grad, log_totals, segment):
    row_count, head_count, head_dim = queries.shape
    block_rows = min(512, row_count)
    block_count = row_count // block_rows
    score_scale = 1.0 / math.sqrt(head_dim)
    column = jnp.arange(row_count, dtype=jnp.int32)

    def one_block(totals, inputs):
        key_grad, value_grad = totals
        block_query, block_grad, block_total, block_segment, block_row = inputs
        scores = (
            jnp.einsum("qhd,khd->hqk", block_query, keys_low, preferred_element_type=jnp.float32)
            * score_scale
        )
        scores = jnp.where(
            block_mask(block_segment, block_row, segment, column)[None], scores, masked_score
        )
        probs = jnp.exp(scores - block_total[:, :, None])
        weights = probs.astype(jnp.bfloat16)
        prob_grad = jnp.einsum(
            "qhd,khd->hqk", block_grad, values_low, preferred_element_type=jnp.float32
        )
        delta = jnp.sum(probs * prob_grad, axis=-1, keepdims=True)
        score_grad = (probs * (prob_grad - delta)).astype(jnp.bfloat16)
        query_grad = (
            jnp.einsum("hqk,khd->qhd", score_grad, keys_low, preferred_element_type=jnp.float32)
            * score_scale
        )
        key_grad = (
            key_grad
            + jnp.einsum(
                "hqk,qhd->khd", score_grad, block_query, preferred_element_type=jnp.float32
            )
            * score_scale
        )
        value_grad = value_grad + jnp.einsum(
            "hqk,qhd->khd", weights, block_grad, preferred_element_type=jnp.float32
        )
        return ((key_grad, value_grad), query_grad)

    zeros_start = jnp.zeros((row_count, head_count, head_dim), jnp.float32)
    (key_grad, value_grad), query_grad = lax.scan(
        one_block,
        (zeros_start, zeros_start),
        (
            queries.reshape(block_count, block_rows, head_count, head_dim),
            context_grad.reshape(block_count, block_rows, head_count, head_dim),
            log_totals,
            segment.reshape(block_count, block_rows),
            column.reshape(block_count, block_rows),
        ),
    )
    return (query_grad.reshape(row_count, head_count, head_dim), key_grad, value_grad)


def per_device(
    tokens,
    cotangent,
    seq_len,
    seq_device,
    owner_map,
    weight_blocks,
    left_stat,
    right_stat,
    left_root,
    right_root,
    vectors,
    vector_stat,
    unit_bias,
    unit_stat,
):
    groups = lax.axis_size("mp")
    device = lax.axis_index("dp")
    row_count = tokens.shape[0]
    heads_here = HEADS // groups
    qkv_cols = 3 * D // groups
    head_cols = D // groups
    unit_cols = FF // groups
    slot_count = weight_blocks.shape[1]
    sent_blocks = weight_blocks[0].astype(jnp.bfloat16)
    gathered = lax.all_gather(sent_blocks, "dp", axis=0, tiled=True)
    qkv_w, out_w, up_w, down_w = split_blocks(gathered[owner_map], qkv_cols, head_cols, unit_cols)
    segment, position = segment_layout(seq_len, seq_device, device, row_count)
    cosine_table, sine_table = rotary_tables(position)
    unit_shift = unit_bias[0]
    inputs = tokens.astype(jnp.float32)
    normed_one = layer_norm(inputs, vectors[0], vectors[1]).astype(jnp.bfloat16)
    normed_two = layer_norm(inputs, vectors[2], vectors[3]).astype(jnp.bfloat16)
    qkv_proj = (
        jnp.dot(normed_one, qkv_w, preferred_element_type=jnp.float32) + unit_shift[:qkv_cols]
    )
    qkv_proj = qkv_proj.reshape(row_count, heads_here, 3, HD)

    def turn_pair(values):
        return rotate(values.reshape(row_count, 2 * heads_here, HD), cosine_table, sine_table)

    turned, turn_back = jax.vjp(turn_pair, qkv_proj[:, :, :2])
    turned = turned.reshape(row_count, heads_here, 2, HD).astype(jnp.bfloat16)
    queries = turned[:, :, 0]
    keys_low = turned[:, :, 1]
    values_low = qkv_proj[:, :, 2].astype(jnp.bfloat16)
    context, log_totals = attention_forward(queries, keys_low, values_low, segment)
    context_low = context.reshape(row_count, head_cols).astype(jnp.bfloat16)
    hidden = jnp.dot(normed_two, up_w, preferred_element_type=jnp.float32) + unit_shift[qkv_cols:]
    active, gelu_back = jax.vjp(gelu_exact, hidden)
    active_low = active.astype(jnp.bfloat16)
    partial_out = jnp.dot(context_low, out_w, preferred_element_type=jnp.float32) + jnp.dot(
        active_low, down_w, preferred_element_type=jnp.float32
    )
    branch = lax.psum(partial_out.astype(jnp.bfloat16), "mp").astype(jnp.float32)
    block_out = (inputs + branch + (vectors[4] + vectors[5])).astype(jnp.bfloat16)
    grad_full = cotangent.astype(jnp.float32)
    act_grad = jnp.einsum("td,fd->tf", cotangent, down_w, preferred_element_type=jnp.float32)
    hidden_grad = gelu_back(act_grad)[0].astype(jnp.bfloat16)
    context_grad = jnp.einsum(
        "td,id->ti", cotangent, out_w, preferred_element_type=jnp.float32
    ).astype(jnp.bfloat16)
    query_grad, key_grad, value_grad = attention_backward(
        queries,
        keys_low,
        values_low,
        context_grad.reshape(row_count, heads_here, HD),
        log_totals,
        segment,
    )
    pair_grad = turn_back(
        jnp.stack([query_grad, key_grad], axis=2).reshape(row_count, 2 * heads_here, HD)
    )[0]
    qkv_grad = (
        jnp.concatenate([pair_grad, value_grad[:, :, None]], axis=2)
        .reshape(row_count, qkv_cols)
        .astype(jnp.bfloat16)
    )
    one_grad = jnp.einsum("te,de->td", qkv_grad, qkv_w, preferred_element_type=jnp.float32)
    two_grad = jnp.einsum("tf,df->td", hidden_grad, up_w, preferred_element_type=jnp.float32)
    norm_back_one = jax.vjp(layer_norm, inputs, vectors[0], vectors[1])[1]
    norm_back_two = jax.vjp(layer_norm, inputs, vectors[2], vectors[3])[1]
    input_one, gain_one, shift_one = norm_back_one(one_grad)
    input_two, gain_two, shift_two = norm_back_two(two_grad)
    input_part = input_one + input_two
    norm_part = jnp.stack([gain_one, shift_one, gain_two, shift_two])
    input_sum, norm_sum = lax.psum((input_part, norm_part), "mp")
    input_grad = (grad_full + input_sum).astype(jnp.bfloat16)
    qkv_w_grad = jnp.einsum("td,te->de", normed_one, qkv_grad, preferred_element_type=jnp.float32)
    out_w_grad = jnp.einsum("ti,td->id", context_low, cotangent, preferred_element_type=jnp.float32)
    up_w_grad = jnp.einsum("td,tf->df", normed_two, hidden_grad, preferred_element_type=jnp.float32)
    down_w_grad = jnp.einsum("tf,td->fd", active_low, cotangent, preferred_element_type=jnp.float32)
    canonical_grad = jnp.concatenate(
        [matrix_to_blocks(matrix) for matrix in (qkv_w_grad, out_w_grad, up_w_grad, down_w_grad)],
        axis=0,
    )
    slot_grads = canonical_grad[jnp.argsort(owner_map)]
    out_sum = jnp.sum(grad_full, axis=0)
    vector_part = jnp.concatenate([norm_sum, jnp.stack([out_sum, out_sum])], axis=0)
    unit_part = jnp.concatenate(
        [
            jnp.sum(qkv_grad.astype(jnp.float32), axis=0),
            jnp.sum(hidden_grad.astype(jnp.float32), axis=0),
        ]
    )
    summed, vector_grad, unit_grad = lax.psum((slot_grads, vector_part, unit_part), "dp")
    owned = lax.dynamic_slice_in_dim(summed, device * slot_count, slot_count, 0)
    left_new = 0.5 * left_stat[0] + 0.5 * jnp.einsum(
        "nij,nkj->nik", owned, owned, precision=highest
    )
    right_new = 0.5 * right_stat[0] + 0.5 * jnp.einsum(
        "nji,njk->nik", owned, owned, precision=highest
    )
    direction = jnp.einsum("nij,njk->nik", left_root[0], owned, precision=highest)
    direction = jnp.einsum("nij,njk->nik", direction, right_root[0], precision=highest)
    weight_new = apply_step(weight_blocks[0], direction)
    vector_stat_new, vector_new = vector_update(vectors, vector_stat, vector_grad)
    unit_stat_new, unit_new = vector_update(unit_shift, unit_stat[0], unit_grad)
    return (
        block_out,
        input_grad,
        owned[None],
        left_new[None],
        right_new[None],
        weight_new[None],
        vector_grad,
        vector_stat_new,
        vector_new,
        unit_grad[None],
        unit_stat_new[None],
        unit_new[None],
    )


LOW = jnp.bfloat16
WIDE = jnp.float32
MESH = pl.DeviceIdType.MESH
ANY = pl.BlockSpec(memory_space=pl.ANY)
STEP = 256
SUB = 32
PAIRS = 32
STEPS = 8
PER_STEP = PAIRS // STEPS
TICKS = PAIRS // 2
GOT = 8
ACROSS = 4
VMEM_BYTES = 60 * 1024 * 1024
FORWARD_VMEM = 63 * 1024 * 1024
GATHER_VMEM = 63 * 1024 * 1024


def dot(left, right):
    return lax.dot_general(left, right, (((1,), (0,)), ((), ())), preferred_element_type=WIDE)


def dot_nt(left, right):
    return lax.dot_general(left, right, (((1,), (1,)), ((), ())), preferred_element_type=WIDE)


def dot_tn(left, right):
    return lax.dot_general(left, right, (((0,), (0,)), ((), ())), preferred_element_type=WIDE)


def resident(shape):
    return pl.BlockSpec(shape, lambda *_: (0,) * len(shape), pipeline_mode=pl.Buffered(1))


def unplace_kernel(order_ref, blocks_ref, slots_ref, hold, sem_in, sem_out):
    total = blocks_ref.shape[0]
    chunk = total // sem_in.shape[0]

    def read(i):
        part = pl.ds(i * chunk, chunk)
        return pltpu.make_async_copy(blocks_ref.at[part], hold.at[part], sem_in.at[i])

    def write(b):
        return pltpu.make_async_copy(hold.at[b], slots_ref.at[order_ref[b]], sem_out.at[b])

    for i in range(total // chunk):
        read(i).start()
    for i in range(total // chunk):
        read(i).wait()
        for b in range(i * chunk, (i + 1) * chunk):
            write(b).start()
    for b in range(total):
        write(b).wait()


def unplace_blocks(blocks, order):
    total = order.shape[0]
    return pl.pallas_call(
        unplace_kernel,
        grid_spec=pltpu.PrefetchScalarGridSpec(
            num_scalar_prefetch=1,
            grid=(1,),
            in_specs=[ANY],
            out_specs=ANY,
            scratch_shapes=[
                pltpu.VMEM((total, B, B), LOW),
                pltpu.SemaphoreType.DMA((48,)),
                pltpu.SemaphoreType.DMA((total,)),
            ],
        ),
        out_shape=jax.ShapeDtypeStruct((total, B, B), LOW),
        compiler_params=pltpu.CompilerParams(vmem_limit_bytes=VMEM_BYTES),
        name="unplace_blocks",
    )(order, blocks)


def turn(values, cos, sin, back=False):
    lanes = lax.broadcasted_iota(jnp.int32, values.shape, 1)
    lower, upper = pltpu.roll(values, 96, 1), pltpu.roll(values, 32, 1)
    other = jnp.where(lanes < 32, -lower, upper)
    return values * cos - other * sin if back else values * cos + other * sin


def attention_rows(c, tile, first, q_ref, k_ref, v_ref, s_scr, ctx_ref, stats_ref):
    here = slice(c * tile, (c + 1) * tile)
    lanes = lax.broadcasted_iota(jnp.int32, (tile, 128), 1)
    stats = jnp.broadcast_to(first.astype(WIDE), (tile, 128))
    for h in range(q_ref.shape[1] // HD):
        cols = slice(h * HD, (h + 1) * HD)
        q = q_ref[here, cols]
        top = jnp.full((tile, 1), masked_score, WIDE)
        for j in range(c + 1):
            keys = slice(j * tile, (j + 1) * tile)
            s = dot_nt(q, k_ref[keys, cols])
            col = lax.broadcasted_iota(jnp.int32, (tile, tile), 1) + j * tile
            ok = col >= first
            if j == c:
                row = lax.broadcasted_iota(jnp.int32, (tile, tile), 0) + c * tile
                ok = ok & (col <= row)
            s = jnp.where(ok, s, masked_score)
            s_scr[:, keys] = s
            top = jnp.maximum(top, jnp.max(s, axis=1, keepdims=True))
        total = jnp.zeros((tile, 1), WIDE)
        ctx = jnp.zeros((tile, HD), WIDE)
        for j in range(c + 1):
            keys = slice(j * tile, (j + 1) * tile)
            e = jnp.exp(s_scr[:, keys] - top)
            total = total + jnp.sum(e, axis=1, keepdims=True)
            ctx = ctx + dot(e.astype(LOW), v_ref[keys, cols])
        ctx_ref[:, cols] = (ctx * (1.0 / total)).astype(LOW)
        stats = jnp.where(lanes == h, top + jnp.log(total), stats)
    stats_ref[...] = stats


PIECES = 4
ROUTES = ((0, 2), (0, 4), (0, 1), (2, 4), (4, 2), (2, 1), (4, 1), (6, 1))


def flip(index, mask):
    for bit in range(3):
        if mask >> bit & 1:
            unit = 2**bit
            index = index + (1 - 2 * lax.rem(lax.div(index, unit), 2)) * unit
    return index


def segments(qkv, od, up):
    wide, down = od.shape[1] // B, up.shape[1] // B
    out = od.shape[0] // B - down
    deep, cols = qkv.shape[0] // B, qkv.shape[1] // B
    starts = [deep * cols, out * wide, deep * down]
    return (
        (qkv, 0, deep, cols, 0),
        (od, 0, out, wide, starts[0]),
        (up, 0, deep, down, sum(starts[:2])),
        (od, out, down, wide, sum(starts)),
    )


def gather_kernel(
    order_ref,
    len_ref,
    place_ref,
    vec_ref,
    freq_ref,
    bias_ref,
    w_hbm,
    x_hbm,
    cot_hbm,
    qkv_hbm,
    od_hbm,
    up_hbm,
    h1_hbm,
    h2_hbm,
    table_hbm,
    q_hbm,
    k_hbm,
    v_hbm,
    ctx_hbm,
    stats_hbm,
    sum_ref,
    slots,
    wide,
    x_buf,
    c_buf,
    h_buf,
    table_all,
    stage,
    qkv_buf,
    q_all,
    k_all,
    v_all,
    s_scr,
    stats_buf,
    send_sem,
    recv_sem,
    load_sem,
    row_sem,
    norm_sem,
    stage_sem,
    out_sem,
    row_out_sem,
    q_sem,
):
    me = lax.axis_index("dp")
    each = w_hbm.shape[0]
    size = each // PIECES
    steps = x_hbm.shape[0] // STEP

    def piece(mask, q):
        return slots.at[pl.ds(flip(me, mask) * each + q * size, size)]

    def send(source, target, q):
        return pltpu.make_async_remote_copy(
            src_ref=piece(source, q),
            dst_ref=piece(source, q),
            send_sem=send_sem.at[ROUTES.index((source, target)), q],
            recv_sem=recv_sem.at[source ^ target, q],
            device_id={"dp": flip(me, target)},
            device_id_type=MESH,
        )

    def arrived(source, q):
        pltpu.make_async_remote_copy(
            src_ref=piece(source, q),
            dst_ref=piece(source, q),
            send_sem=send_sem.at[0, q],
            recv_sem=recv_sem.at[source, q],
            device_id={"dp": flip(me, 1)},
            device_id_type=MESH,
        ).wait_recv()

    def load(q):
        return pltpu.make_async_copy(
            w_hbm.at[pl.ds(q * size, size)], wide.at[q % 2], load_sem.at[q % 2]
        )

    def tile(i):
        return pl.ds(pl.multiple_of(i * STEP, STEP), STEP)

    def fetch(i, slot):
        return (
            pltpu.make_async_copy(x_hbm.at[tile(i), :], x_buf.at[slot], row_sem.at[0, slot]),
            pltpu.make_async_copy(cot_hbm.at[tile(i), :], c_buf.at[slot], row_sem.at[1, slot]),
        )

    def keep(i, slot):
        return (
            pltpu.make_async_copy(h_buf.at[slot], h1_hbm.at[tile(i), :], norm_sem.at[0, slot]),
            pltpu.make_async_copy(stage.at[slot], h2_hbm.at[tile(i), :], norm_sem.at[1, slot]),
        )

    def norm_step(i, slot, first):
        for copy in fetch(i, slot):
            copy.wait()

        @pl.when(jnp.logical_not(first))
        def _():
            for copy in keep(i, slot):
                copy.wait()

        x = x_buf[slot].astype(WIDE)
        center = x - jnp.mean(x, axis=1, keepdims=True)
        scale = lax.rsqrt(jnp.mean(center * center, axis=1, keepdims=True) + norm_eps)
        xhat = center * scale
        h_buf[slot] = (xhat * vec_ref[0:1, :] + vec_ref[1:2, :]).astype(LOW)
        stage[slot] = (xhat * vec_ref[2:3, :] + vec_ref[3:4, :]).astype(LOW)
        sum_ref[0:1, :] += jnp.sum(c_buf[slot].astype(WIDE), axis=0, keepdims=True)
        row = lax.broadcasted_iota(jnp.int32, (STEP, 128), 0) + i * STEP
        first = jnp.zeros((STEP, 128), jnp.int32)
        end = jnp.int32(0)
        for j in range(len_ref.shape[0]):
            mine = place_ref[j] == me
            end = end + jnp.where(mine, len_ref[j], 0)
            first = jnp.where(row >= jnp.where(mine, end, 1 << 30), end, first)
        angle = (row - first).astype(WIDE) * freq_ref[...]
        table_all[0, tile(i), :] = jnp.cos(angle)
        table_all[1, tile(i), :] = jnp.sin(angle)
        table_all[2, tile(i), :] = first.astype(WIDE)
        for copy in keep(i, slot):
            copy.start()

    for q in range(2):
        load(q).start()
    for slot in range(2):
        for copy in fetch(slot, slot):
            copy.start()
    barrier = pltpu.get_barrier_semaphore()
    for target in (1, 2, 4):
        pl.semaphore_signal(
            barrier, inc=1, device_id={"dp": flip(me, target)}, device_id_type=MESH
        )
    sum_ref[...] = jnp.zeros_like(sum_ref)
    for q in range(PIECES):
        load(q).wait()
        slots[pl.ds(me * each + q * size, size)] = wide[q % 2].astype(LOW)
        if q + 2 < PIECES:
            load(q + 2).start()
        if q == 0:
            pl.semaphore_wait(barrier, 3)
        for target in (2, 4, 1):
            send(0, target, q).start()

    for q in range(PIECES):

        @pl.loop(0, steps // (2 * PIECES))
        def _(k):
            i = (q * (steps // (2 * PIECES)) + k) * 2
            for slot in range(2):
                norm_step(i + slot, slot, i == 0)

                @pl.when(i + slot + 2 < steps)
                def _():
                    for copy in fetch(i + slot + 2, slot):
                        copy.start()

        arrived(2, q)
        if q % 2:
            send(2, 4, q).start()
        send(2, 1, q).start()
        arrived(4, q)
        if q % 2 == 0:
            send(4, 2, q).start()
        send(4, 1, q).start()
    for slot in range(2):
        for copy in keep(slot, slot):
            copy.wait()
    for q in range(PIECES):
        arrived(6, q)
        send(6, 1, q).start()
    for source in (1, 3, 5, 7):
        for q in range(PIECES):
            arrived(source, q)

    _, out, up, down = segments(qkv_hbm, od_hbm, up_hbm)
    qkv_across = qkv_hbm.shape[1] // B
    whole = [
        pltpu.make_async_copy(src, dst, out_sem.at[i])
        for i, (src, dst) in enumerate(
            (
                (qkv_buf, qkv_hbm),
                (table_all, table_hbm),
                (k_all, k_hbm),
                (v_all, v_hbm),
            )
        )
    ]

    def q_out(i):
        return pltpu.make_async_copy(
            q_all.at[tile(i), :], q_hbm.at[tile(i), :], q_sem.at[i]
        )

    def panel(part, i, slot):
        ref, skip = part[:2]
        return pltpu.make_async_copy(
            stage.at[slot], ref.at[lane((skip + i) * B), :], stage_sem.at[slot]
        )

    def put(part, i, slot):
        across, block = part[3:]
        for j in range(across):
            stage[slot, :, j * B : (j + 1) * B] = slots[order_ref[block + i * across + j]]
        panel(part, i, slot).start()

    def fetch_h(i, slot):
        return pltpu.make_async_copy(h1_hbm.at[tile(i), :], x_buf.at[slot], row_sem.at[0, slot])

    for slot in range(2):
        fetch_h(slot, slot).start()

    @pl.loop(0, qkv_hbm.shape[0] // B)
    def _(i):
        for j in range(qkv_across):
            qkv_buf[lane(i * B), j * B : (j + 1) * B] = slots[order_ref[i * qkv_across + j]]

    whole[0].start()
    whole[1].start()
    for slot in range(2):
        put(out, slot, slot)

    def project(i, slot):
        scale = 1.0 / math.sqrt(HD)
        for j in range(qkv_across):
            head, part = divmod(j, 3)
            cols = slice(head * HD, head * HD + HD)
            proj = dot(x_buf[slot], qkv_buf[:, j * B : (j + 1) * B])
            proj = proj + bias_ref[:, j * B : (j + 1) * B]
            if part == 2:
                v_all[tile(i), cols] = proj.astype(LOW)
                continue
            front = turn(proj[:, :128], table_all[0, tile(i), :], table_all[1, tile(i), :])
            turned = jnp.concatenate([front, proj[:, 128:]], axis=1).astype(LOW)
            if part == 0:
                q_all[tile(i), cols] = (turned.astype(WIDE) * scale).astype(LOW)
            else:
                k_all[tile(i), cols] = turned

    @pl.loop(0, steps // 2)
    def _(k):
        for slot in range(2):
            i = k * 2 + slot
            fetch_h(i, slot).wait()
            project(i, slot)
            q_out(i).start()

            @pl.when(i + 2 < steps)
            def _():
                fetch_h(i + 2, slot).start()

            panel(out, 0, 0).wait()
            put(up, i, 0)
            panel(out, 0, 1).wait()
            put(down, i, 1)

    for copy in whole[2:]:
        copy.start()
    rows = 512

    @pl.loop(0, steps)
    def _(i):
        q_out(i).wait()


    def row_out(c):
        part, slot = pl.ds(c * rows, rows), c % 2
        return (
            pltpu.make_async_copy(q_all.at[part, :], ctx_hbm.at[part, :], row_out_sem.at[0, slot]),
            pltpu.make_async_copy(
                stats_buf.at[slot], stats_hbm.at[part, :], row_out_sem.at[1, slot]
            ),
        )

    count = x_hbm.shape[0] // rows
    for c in range(count):
        if c >= 2:
            for copy in row_out(c - 2):
                copy.wait()
        first = table_all[2, c * rows : (c + 1) * rows, :][:, 0:1].astype(jnp.int32)
        place = q_all.at[pl.ds(c * rows, rows), :]
        attention_rows(c, rows, first, q_all, k_all, v_all, s_scr, place, stats_buf.at[c % 2])
        for copy in row_out(c):
            copy.start()
    for c in range(count - 2, count):
        for copy in row_out(c):
            copy.wait()
    for slot in range(2):
        panel(out, 0, slot).wait()
    for copy in whole:
        copy.wait()

    for source, target in ROUTES:
        for q in range(PIECES):
            if (source, target) == (2, 4) and q % 2 == 0:
                continue
            if (source, target) == (4, 2) and q % 2:
                continue
            send(source, target, q).wait_send()


def gather_weights(
    blocks, order, seq_len, seq_device, tokens, cotangent, vectors, bias, shapes
):
    rows, d = tokens.shape
    each = blocks.shape[0]
    half = 10000.0 ** (-2.0 * jnp.arange(ROT // 2, dtype=WIDE) / ROT)
    frequency = jnp.concatenate([half, half, jnp.zeros((128 - ROT,), WIDE)])[None]
    smem = pl.BlockSpec(memory_space=pltpu.SMEM)
    vmem = pl.BlockSpec(memory_space=pltpu.VMEM)
    return pl.pallas_call(
        gather_kernel,
        in_specs=[smem, smem, smem, vmem, vmem, vmem, ANY, ANY, ANY],
        out_specs=[ANY] * 11 + [vmem],
        out_shape=[jax.ShapeDtypeStruct(s, LOW) for s in shapes]
        + [jax.ShapeDtypeStruct((rows, d), LOW)] * 2
        + [jax.ShapeDtypeStruct((3, rows, 128), WIDE)]
        + [jax.ShapeDtypeStruct((rows, shapes[0][1] // 3), LOW)] * 4
        + [jax.ShapeDtypeStruct((rows, 128), WIDE)]
        + [jax.ShapeDtypeStruct((8, d), WIDE)],
        scratch_shapes=[
            pltpu.VMEM((order.shape[0], B, B), LOW),
            pltpu.VMEM((2, each // PIECES, B, B), WIDE),
            pltpu.VMEM((2, STEP, d), LOW),
            pltpu.VMEM((2, STEP, d), LOW),
            pltpu.VMEM((2, STEP, d), LOW),
            pltpu.VMEM((3, rows, 128), WIDE),
            pltpu.VMEM((2, B, d), LOW),
            pltpu.VMEM(shapes[0], LOW),
        ]
        + [pltpu.VMEM((rows, shapes[0][1] // 3), LOW)] * 3
        + [
            pltpu.VMEM((512, rows), WIDE),
            pltpu.VMEM((2, 512, 128), WIDE),
            pltpu.SemaphoreType.DMA((8, PIECES)),
            pltpu.SemaphoreType.DMA((8, PIECES)),
            pltpu.SemaphoreType.DMA((2,)),
            pltpu.SemaphoreType.DMA((2, 2)),
            pltpu.SemaphoreType.DMA((2, 2)),
            pltpu.SemaphoreType.DMA((2,)),
            pltpu.SemaphoreType.DMA((4,)),
            pltpu.SemaphoreType.DMA((2, 2)),
            pltpu.SemaphoreType.DMA((rows // STEP,)),
        ],
        compiler_params=pltpu.CompilerParams(
            vmem_limit_bytes=GATHER_VMEM, collective_id=3, has_side_effects=True
        ),
        cost_estimate=pl.CostEstimate(
            flops=100_000_000_000, bytes_accessed=80 << 20, transcendentals=0
        ),
        name="gather_weights",
    )(order, seq_len, seq_device, vectors, frequency, bias, blocks, tokens, cotangent)


class Line:
    def __init__(self, out, part, got, across, sems):
        self.out, self.part, self.got, self.across = out, part, got, across
        (
            self.up_send,
            self.up_recv,
            self.far_send,
            self.far_recv,
            self.over_send,
            self.over_recv,
            self.down_send,
            self.down_recv,
            self.relay_send,
            self.relay_recv,
            self.own,
        ) = [sems.at[i] for i in range(11)]
        z = lax.axis_index("mp")
        self.inner = (z == 1) | (z == 2)
        self.near = (z >= 2).astype(jnp.int32)
        self.far = 1 - self.near
        self.partner = jnp.where(self.inner, jnp.where(z == 1, 0, 3), jnp.where(z == 0, 1, 2))
        self.other = 3 - z

    def rows(self, pair, which):
        return self.out.at[pl.ds(pl.multiple_of(pair * (2 * SUB) + which * SUB, SUB), SUB), :]

    def greet(self):
        barrier = pltpu.get_barrier_semaphore()
        pl.semaphore_signal(barrier, inc=1, device_id={"mp": self.partner}, device_id_type=MESH)

        @pl.when(self.inner)
        def _():
            pl.semaphore_signal(barrier, inc=1, device_id={"mp": self.other}, device_id_type=MESH)
            pl.semaphore_wait(barrier, 2)

        @pl.when(jnp.logical_not(self.inner))
        def _():
            pl.semaphore_wait(barrier, 1)

    def copy(self, src, dst, send, recv, pair, target):
        return pltpu.make_async_remote_copy(
            src_ref=src,
            dst_ref=dst,
            send_sem=send.at[pair],
            recv_sem=recv.at[pair],
            device_id={"mp": target},
            device_id_type=MESH,
        )

    def up(self, pair):
        return self.copy(
            self.part.at[pair], self.got.at[pair % GOT], self.up_send, self.up_recv, pair, self.partner
        )

    def far_sum(self, pair):
        src, dst = self.part.at[pair, self.far], self.across.at[pair % ACROSS]
        return self.copy(src, dst, self.far_send, self.far_recv, pair, self.other)

    def over(self, pair, which):
        src = self.part.at[pair, self.near]
        return self.copy(src, self.rows(pair, which), self.over_send, self.over_recv, pair, self.other)

    def down(self, pair):
        src = self.part.at[pair, self.near]
        return self.copy(
            src, self.rows(pair, self.near), self.down_send, self.down_recv, pair, self.partner
        )

    def relay(self, pair):
        far = self.rows(pair, self.far)
        return self.copy(far, far, self.relay_send, self.relay_recv, pair, self.partner)

    def keep(self, pair):
        src = self.part.at[pair, self.near]
        return pltpu.make_async_copy(src, self.rows(pair, self.near), self.own.at[pair])

    def send_up(self, pair):
        @pl.when(pair >= GOT)
        def _():
            self.down(pair - GOT).wait_recv()

        self.up(pair).start()

    def add_far(self, pair):
        self.up(pair).wait_recv()
        far = self.part[pair, self.far].astype(WIDE) + self.got[pair % GOT, self.far].astype(WIDE)
        self.part[pair, self.far] = far.astype(LOW)
        self.far_sum(pair).start()

    def finish_near(self, pair, base):
        self.far_sum(pair).wait_recv()
        total = (
            self.part[pair, self.near].astype(WIDE)
            + self.got[pair % GOT, self.near].astype(WIDE)
            + self.across[pair % ACROSS].astype(WIDE)
        )
        self.part[pair, self.near] = (base + total).astype(LOW)
        self.over(pair, self.near).start()
        self.down(pair).start()
        self.keep(pair).start()

    def send_relay(self, pair):
        self.over(pair, self.far).wait_recv()
        self.relay(pair).start()

    def drain(self):
        @pl.when(self.inner)
        def _():
            @pl.loop(0, PAIRS)
            def _(pair):
                self.far_sum(pair).wait_send()
                self.over(pair, self.near).wait_send()
                self.down(pair).wait_send()
                self.relay(pair).wait_send()
                self.keep(pair).wait()

        @pl.when(jnp.logical_not(self.inner))
        def _():
            @pl.loop(0, PAIRS)
            def _(pair):
                self.up(pair).wait_send()
                self.relay(pair).wait_recv()

            @pl.loop(PAIRS - GOT, PAIRS)
            def _(pair):
                self.down(pair).wait_recv()

    def tick(self, step, lag, base):
        ahead = GOT // PER_STEP

        @pl.when(jnp.logical_not(self.inner) & (step < ahead))
        def _():
            for s in range(PER_STEP):
                self.send_up(step * PER_STEP + s)

        @pl.when(
            jnp.logical_not(self.inner) & (step >= ahead) & (step < ahead + (PAIRS - GOT) // 2)
        )
        def _():
            for s in range(2):
                self.send_up(GOT + (step - ahead) * 2 + s)

        @pl.when(self.inner & (step >= lag + 2) & (step < lag + 2 + TICKS))
        def _():
            for s in range(2):
                self.send_relay((step - lag - 2) * 2 + s)

        @pl.when(self.inner & (step >= lag + 1) & (step < lag + 1 + TICKS))
        def _():
            for s in range(2):
                self.finish_near((step - lag - 1) * 2 + s, base(s))

        @pl.when(self.inner & (step >= lag) & (step < lag + TICKS))
        def _():
            for s in range(2):
                self.add_far((step - lag) * 2 + s)


def line_scratch(d):
    return [
        pltpu.VMEM((PAIRS, 2, SUB, d), LOW),
        pltpu.VMEM((GOT, 2, SUB, d), LOW),
        pltpu.VMEM((ACROSS, SUB, d), LOW),
        pltpu.SemaphoreType.DMA((11, PAIRS)),
    ]


def now(step):
    return jnp.minimum(step, STEPS - 1)


def row_block(width):
    return pl.BlockSpec((STEP, width), lambda i: (now(i), 0))


def base_block(width, lag):
    return pl.BlockSpec((4 * SUB, width), lambda i: (jnp.clip(i - lag - 1, 0, TICKS - 1), 0))


def lane(start):
    return pl.ds(pl.multiple_of(start, B), B)


def gelu_parts(z):
    e = jnp.exp(z * z * -0.5)
    t = 1.0 / (1.0 + jnp.abs(z) * (0.3275911 * math.sqrt(0.5)))
    poly = t * (
        0.5 * 0.254829592
        + t
        * (
            0.5 * -0.284496736
            + t * (0.5 * 1.421413741 + t * (0.5 * -1.453152027 + t * (0.5 * 1.061405429)))
        )
    )
    below = poly * e
    cdf = jnp.where(z >= 0, 1.0 - below, below)
    return cdf, e * (1.0 / math.sqrt(2.0 * math.pi))


def store_part(part_ref, step, cols, value):
    value = value.astype(LOW).reshape(PER_STEP, 2, SUB, value.shape[1])
    part_ref[pl.ds(step * PER_STEP, PER_STEP), :, :, cols] = value


FORWARD_LAG = 1
FORWARD_GRID = FORWARD_LAG + TICKS + 2


def weight_unit(a_t, b_ref, cols, stage, slot):
    for n in range(cols // 512):
        part = slice(n * 512, (n + 1) * 512)
        stage[pl.ds(pl.multiple_of(slot * B, B), B), part] = dot(a_t, b_ref[:, part]).astype(LOW)


def forward_kernel(
    h_ref,
    g_ref,
    ctx_ref,
    x_ref,
    stats_ref,
    bias_ref,
    vec_ref,
    table_ref,
    up_hbm,
    od_hbm,
    h1_hbm,
    h2_hbm,
    ctx_hbm,
    cot_hbm,
    q_hbm,
    k_hbm,
    v_hbm,
    out_ref,
    hg_hbm,
    qg_hbm,
    wg_hbm,
    sums_ref,
    qkv_sums_ref,
    up_buf,
    od_buf,
    act_all,
    hg_all,
    part,
    got,
    across,
    sems,
    grad_all,
    stats,
    dq_scr,
    dk_scr,
    dv_scr,
    load_sem,
    panel_sem,
    stage_sem,
    hg_sem,
    head_sem,
):
    step = pl.program_id(0)
    line = Line(out_ref, part, got, across, sems)
    heads = ctx_ref.shape[1]
    rows, units = act_all.shape
    qkv_cols = qg_hbm.shape[1]
    width = 512
    tiles = units // width
    stage = od_buf.at[pl.ds(rows, 2 * B), :]

    def load_up(n):
        cols = pl.ds(n * width, width)
        return pltpu.make_async_copy(up_hbm.at[:, cols], up_buf.at[:, cols], load_sem.at[n])

    def load_down(n):
        part_rows = pl.ds(heads + n * width, width)
        return pltpu.make_async_copy(
            od_hbm.at[part_rows, :], od_buf.at[part_rows, :], load_sem.at[tiles + n]
        )

    def load_out():
        part_rows = pl.ds(0, heads)
        return pltpu.make_async_copy(
            od_hbm.at[part_rows, :], od_buf.at[part_rows, :], load_sem.at[2 * tiles]
        )

    def load_cot():
        return pltpu.make_async_copy(
            cot_hbm, od_buf.at[pl.ds(0, rows), :], load_sem.at[2 * tiles + 1]
        )

    def load_head(h):
        cols = pl.ds(pl.multiple_of(h * HD, HD), HD)
        return [
            pltpu.make_async_copy(
                src.at[:, cols], act_all.at[:, pl.ds(i * HD, HD)], head_sem.at[i]
            )
            for i, src in enumerate((q_hbm, k_hbm, v_hbm))
        ]

    def store_qg():
        return pltpu.make_async_copy(hg_all.at[:, pl.ds(0, qkv_cols)], qg_hbm, head_sem.at[5])

    def panel_cols(slot):
        return lane(qkv_cols + slot * B)

    def panel(src, i, slot):
        return pltpu.make_async_copy(
            src.at[:, lane(i * B)], up_buf.at[:, panel_cols(slot)], panel_sem.at[slot]
        )

    def store_hg(i):
        part_rows = pl.ds(pl.multiple_of(i * STEP, STEP), STEP)
        return pltpu.make_async_copy(
            hg_all.at[part_rows, :], hg_hbm.at[part_rows, :], hg_sem.at[i]
        )

    def stage_out(block, j, slot):
        return pltpu.make_async_copy(
            stage.at[lane(slot * B), pl.ds(j * B, B)], wg_hbm.at[block + j], stage_sem.at[slot]
        )

    def stage_wait(cols, slot):
        place = stage.at[lane(slot * B), pl.ds(0, cols)]
        pltpu.make_async_copy(place, place, stage_sem.at[slot]).wait()

    @pl.when(step == 0)
    def _():
        for n in range(tiles):
            load_up(n).start()
            load_down(n).start()
        load_out().start()
        line.greet()
        sums_ref[...] = jnp.zeros_like(sums_ref)

    @pl.when(step < STEPS)
    def _():
        here = pl.ds(pl.multiple_of(step * STEP, STEP), STEP)
        for n in range(tiles):
            cols = slice(n * width, (n + 1) * width)

            @pl.when(step == 0)
            def _():
                load_up(n).wait()
                load_down(n).wait()

            bias = bias_ref[:, qkv_cols + n * width : qkv_cols + (n + 1) * width]
            hidden = dot(h_ref[...], up_buf[:, cols]) + bias
            act_grad = dot_nt(g_ref[...], od_buf[heads + n * width : heads + (n + 1) * width, :])
            cdf, density = gelu_parts(hidden)
            act_all[here, cols] = (hidden * cdf).astype(LOW)
            grad = (act_grad * (cdf + hidden * density)).astype(LOW)
            hg_all[here, cols] = grad
            sums_ref[0:1, cols] += jnp.sum(grad.astype(WIDE), axis=0, keepdims=True)

        @pl.when(step == 0)
        def _():
            load_out().wait()

        store_hg(step).start()
        grad = dot_nt(g_ref[...], od_buf[:heads, :]).astype(LOW)
        grad_all[here, :] = grad
        lanes = lax.broadcasted_iota(jnp.int32, (STEP, 128), 1)
        info = stats_ref[...]
        for h in range(heads // HD):
            cols = slice(h * HD, (h + 1) * HD)
            both = ctx_ref[:, cols].astype(WIDE) * grad[:, cols].astype(WIDE)
            info = jnp.where(lanes == 64 + h, jnp.sum(both, axis=1, keepdims=True), info)
        stats[here, :] = info
        for n in range(od_buf.shape[1] // width):
            cols = slice(n * width, (n + 1) * width)
            value = dot(ctx_ref[...], od_buf[:heads, cols]) + dot(
                act_all[here, :], od_buf[heads:, cols]
            )
            store_part(part, step, cols, value)

    @pl.when(step == STEPS - 1)
    def _():
        panel(h2_hbm, 0, 0).start()
        load_cot().start()

    wide = od_buf.shape[1] // B
    out_first = rows // B * (qkv_cols // B)
    up_first = out_first + heads // B * wide
    down_first = up_first + rows // B * (units // B)

    def unit(index, a_t, b_ref, cols, first):
        slot = index % 2

        @pl.when(index >= 2)
        def _():
            stage_wait(cols, slot)

        weight_unit(a_t, b_ref, cols, stage, slot)
        for j in range(cols // B):
            stage_out(first + index * (cols // B), j, slot).start()

    def settle(cols):
        for slot in range(2):
            stage_wait(cols, slot)

    @pl.when((step == 8) | (step == 9))
    def _():
        @pl.loop(0, 4)
        def _(k):
            i = (step - 8) * 4 + k
            panel(h2_hbm, i, i % 2).wait()

            @pl.when(i < 7)
            def _():
                panel(h2_hbm, i + 1, (i + 1) % 2).start()

            unit(i, up_buf[:, panel_cols(i % 2)].T, hg_all, units, up_first)

    @pl.when(step == 10)
    def _():
        settle(units)
        load_cot().wait()

    @pl.when((step == 10) | (step == 11))
    def _():
        @pl.loop(0, 4)
        def _(k):
            i = (step - 10) * 4 + k
            cot = od_buf.at[pl.ds(0, rows), :]
            unit(i, act_all[:, lane(i * B)].T, cot, wide * B, down_first)

    @pl.when(step == 11)
    def _():
        for copy in load_head(0):
            copy.start()

    @pl.when(step == 12)
    def _():
        settle(wide * B)

        @pl.loop(0, STEPS)
        def _(i):
            store_hg(i).wait()

    def head_grads(h, start, stop):
        tile = 512
        count = rows // tile

        def tile_rows(i):
            return pl.ds(pl.multiple_of(i * tile, tile), tile)

        def put(i, part, values):
            cols = pl.ds(pl.multiple_of(h * 3 * HD + part * HD, HD), HD)
            hg_all[tile_rows(i), cols] = values.astype(LOW)

        def turned_back(i, values):
            front = turn(values[:, :128], table_ref[0, tile_rows(i), :], table_ref[1, tile_rows(i), :], True)
            return jnp.concatenate([front, values[:, 128:]], axis=1)

        @pl.loop(start, stop)
        def _(j):
            keys = act_all[tile_rows(j), HD : 2 * HD]
            values = act_all[tile_rows(j), 2 * HD : 3 * HD]
            dk_scr[...] = jnp.zeros_like(dk_scr)
            dv_scr[...] = jnp.zeros_like(dv_scr)

            @pl.loop(j, count)
            def _(i):
                q = act_all[tile_rows(i), 0:HD]
                g = grad_all[tile_rows(i), pl.ds(pl.multiple_of(h * HD, HD), HD)]
                info = stats[tile_rows(i), :]
                log_total = jnp.where(h == 0, info[:, 0:1], info[:, 1:2])
                delta = jnp.where(h == 0, info[:, 64:65], info[:, 65:66])
                first = info[:, 2:3].astype(jnp.int32) - j * tile
                col = lax.broadcasted_iota(jnp.int32, (tile, tile), 1)
                row = lax.broadcasted_iota(jnp.int32, (tile, tile), 0) + (i - j) * tile
                ok = (col >= first) & (col <= row)
                p = jnp.where(ok, jnp.exp(dot_nt(q, keys) - log_total), 0.0)
                ds = (p * (dot_nt(g, values) - delta)).astype(LOW)
                dv_scr[...] += dot_tn(p.astype(LOW), g)
                dk_scr[...] += dot_tn(ds, q)
                dq_scr[tile_rows(i), :] += dot(ds, keys)

            put(j, 1, turned_back(j, dk_scr[...]))
            put(j, 2, dv_scr[...])

        @pl.when(stop == count)
        def _():
            @pl.loop(0, count)
            def _(i):
                put(i, 0, turned_back(i, dq_scr[tile_rows(i), :] * (1.0 / math.sqrt(HD))))

    @pl.when((step == 12) | (step == 14))
    def _():
        for copy in load_head((step - 12) // 2):
            copy.wait()
        dq_scr[...] = jnp.zeros_like(dq_scr)

    @pl.when((step >= 12) & (step < 16))
    def _():
        second = (step - 12) % 2
        head_grads((step - 12) // 2, second, 1 + 3 * second)

    @pl.when(step == 13)
    def _():
        for copy in load_head(1):
            copy.start()

    @pl.when(step == 16)
    def _():
        store_qg().start()
        for j in range(2):
            panel(ctx_hbm, j, j).start()
        total = jnp.zeros((1, qkv_cols), WIDE)
        for i in range(rows // 512):
            part_rows = slice(i * 512, (i + 1) * 512)
            total = total + jnp.sum(hg_all[part_rows, :qkv_cols].astype(WIDE), axis=0, keepdims=True)
        qkv_sums_ref[...] = jnp.broadcast_to(total, qkv_sums_ref.shape)
        for j in range(2):
            panel(ctx_hbm, j, j).wait()

        @pl.loop(0, 2)
        def _(j):
            cot = od_buf.at[pl.ds(0, rows), :]
            unit(j, up_buf[:, panel_cols(j)].T, cot, wide * B, out_first)

        settle(wide * B)
        panel(h1_hbm, 0, 0).start()

    @pl.when((step == 17) | (step == 18))
    def _():
        @pl.loop(0, 4)
        def _(k):
            i = (step - 17) * 4 + k
            panel(h1_hbm, i, i % 2).wait()

            @pl.when(i < 7)
            def _():
                panel(h1_hbm, i + 1, (i + 1) % 2).start()

            grads = hg_all.at[:, pl.ds(0, qkv_cols)]
            unit(i, up_buf[:, panel_cols(i % 2)].T, grads, qkv_cols, 0)

    @pl.when(step == FORWARD_GRID - 1)
    def _():
        settle(qkv_cols)
        store_qg().wait()

    def base(s):
        near = pl.ds(pl.multiple_of(s * 2 * SUB + line.near * SUB, SUB), SUB)
        return x_ref[near, :].astype(WIDE) + (vec_ref[4:5, :] + vec_ref[5:6, :])

    line.tick(step, FORWARD_LAG, base)

    @pl.when(step == FORWARD_GRID - 1)
    def _():
        line.drain()


def forward_line(h1, h2, cotangent, ctx, heads, stats, table, tokens, up_w, od_w, bias, vectors):
    rows, d = tokens.shape
    units = up_w.shape[1]
    head_cols = ctx.shape[1]
    qkv_cols = 3 * head_cols
    total = (d * qkv_cols + od_w.shape[0] * d + d * units) // (B * B)
    return pl.pallas_call(
        forward_kernel,
        grid=(FORWARD_GRID,),
        in_specs=[
            row_block(d),
            row_block(d),
            row_block(head_cols),
            base_block(d, FORWARD_LAG),
            row_block(128),
            resident(bias.shape),
            resident(vectors.shape),
            resident((2, rows, 128)),
        ]
        + [ANY] * 9,
        out_specs=[ANY] * 4
        + [pl.BlockSpec((8, units), lambda i: (0, 0)), pl.BlockSpec((8, qkv_cols), lambda i: (0, 0))],
        out_shape=[
            jax.ShapeDtypeStruct((rows, d), LOW),
            jax.ShapeDtypeStruct((rows, units), LOW),
            jax.ShapeDtypeStruct((rows, qkv_cols), LOW),
            jax.ShapeDtypeStruct((total, B, B), LOW),
            jax.ShapeDtypeStruct((8, units), WIDE),
            jax.ShapeDtypeStruct((8, qkv_cols), WIDE),
        ],
        scratch_shapes=[
            pltpu.VMEM(up_w.shape, LOW),
            pltpu.VMEM(od_w.shape, LOW),
            pltpu.VMEM((rows, units), LOW),
            pltpu.VMEM((rows, units), LOW),
        ]
        + line_scratch(d)
        + [
            pltpu.VMEM((rows, head_cols), LOW),
            pltpu.VMEM((rows, 128), WIDE),
            pltpu.VMEM((rows, HD), WIDE),
            pltpu.VMEM((512, HD), WIDE),
            pltpu.VMEM((512, HD), WIDE),
            pltpu.SemaphoreType.DMA((10,)),
            pltpu.SemaphoreType.DMA((2,)),
            pltpu.SemaphoreType.DMA((2,)),
            pltpu.SemaphoreType.DMA((STEPS,)),
            pltpu.SemaphoreType.DMA((6,)),
        ],
        compiler_params=pltpu.CompilerParams(
            vmem_limit_bytes=FORWARD_VMEM, collective_id=1, has_side_effects=True
        ),
        cost_estimate=pl.CostEstimate(
            flops=200_000_000_000, bytes_accessed=80 << 20, transcendentals=0
        ),
        name="forward_line",
    )(
        h2,
        cotangent,
        ctx,
        tokens,
        stats,
        bias,
        vectors,
        table,
        up_w,
        od_w,
        h1,
        h2,
        ctx,
        cotangent,
        *heads,
    )


BACKWARD_LAG = 1
BACKWARD_GRID = BACKWARD_LAG + TICKS + 2


class Spread:
    def __init__(self, own, along_mp, along_dp, sems):
        self.own = own
        self.stages = [
            ("dp", along_dp, sems.at[0], sems.at[1]),
            ("mp", along_mp, sems.at[2], sems.at[3]),
        ]

    def others(self, stage):
        axis, buf, send, recv = self.stages[stage]
        me = lax.axis_index(axis)
        return axis, buf, send, recv, me, [lax.rem(me + k, buf.shape[0]) for k in range(1, buf.shape[0])]

    def greet(self):
        barrier = pltpu.get_barrier_semaphore()
        count = 0
        for stage in range(2):
            axis, _, _, _, _, others = self.others(stage)
            for other in others:
                pl.semaphore_signal(barrier, inc=1, device_id={axis: other}, device_id_type=MESH)
            count += len(others)
        pl.semaphore_wait(barrier, count)

    def copies(self, stage):
        axis, buf, send, recv, me, others = self.others(stage)
        return [
            (
                pltpu.make_async_remote_copy(
                    src_ref=self.own,
                    dst_ref=buf.at[me],
                    send_sem=send.at[k],
                    recv_sem=recv.at[me],
                    device_id={axis: other},
                    device_id_type=MESH,
                ),
                pltpu.make_async_remote_copy(
                    src_ref=self.own,
                    dst_ref=buf.at[other],
                    send_sem=send.at[k],
                    recv_sem=recv.at[other],
                    device_id={axis: other},
                    device_id_type=MESH,
                ),
            )
            for k, other in enumerate(others)
        ]

    def start(self, stage):
        _, buf, _, _, me, _ = self.others(stage)
        buf[me] = self.own[...]
        for out, _ in self.copies(stage):
            out.start()

    def finish(self, stage):
        _, buf, _, _, _, _ = self.others(stage)
        for out, back in self.copies(stage):
            out.wait_send()
            back.wait_recv()
        total = buf[0]
        for i in range(1, buf.shape[0]):
            total = total + buf[i]
        return total


def backward_kernel(
    qg_ref,
    hg_ref,
    x_ref,
    g_ref,
    vec_ref,
    cot_sums,
    qkv_sums,
    hidden_sums,
    qkv_hbm,
    up_hbm,
    sums_ref,
    out_ref,
    qkv_ref,
    up_ref,
    load_sem,
    gc_scr,
    xhat_scr,
    own,
    along_mp,
    along_dp,
    spread_sems,
    part,
    got,
    across,
    sems,
):
    step = pl.program_id(0)
    line = Line(out_ref, part, got, across, sems)
    spread = Spread(own, along_mp, along_dp, spread_sems)
    d = x_ref.shape[1]
    width = 512

    def load(n):
        part_rows = pl.ds(n * width, width)
        return (
            pltpu.make_async_copy(
                qkv_hbm.at[part_rows, :], qkv_ref.at[part_rows, :], load_sem.at[0, n]
            ),
            pltpu.make_async_copy(
                up_hbm.at[part_rows, :], up_ref.at[part_rows, :], load_sem.at[1, n]
            ),
        )

    @pl.when(step == 0)
    def _():
        for n in range(d // width):
            for copy in load(n):
                copy.start()
        spread.greet()
        own[...] = jnp.zeros_like(own)
        own[4:5, :] = cot_sums[0:1, :]
        own[5:6, : qkv_sums.shape[1]] = qkv_sums[0:1, :]
        own[6:7, : hidden_sums.shape[1]] = hidden_sums[0:1, :]

    @pl.when(step < STEPS)
    def _():
        x = x_ref[...].astype(WIDE)
        center = x - jnp.mean(x, axis=1, keepdims=True)
        scale = lax.rsqrt(jnp.mean(center * center, axis=1, keepdims=True) + norm_eps)
        xhat_scr[...] = center * scale
        mean = jnp.zeros((STEP, 1), WIDE)
        slope = jnp.zeros((STEP, 1), WIDE)
        for n in range(d // width):
            cols = slice(n * width, (n + 1) * width)

            @pl.when(step == 0)
            def _():
                for copy in load(n):
                    copy.wait()

            e1 = dot_nt(qg_ref[...], qkv_ref[cols, :])
            e2 = dot_nt(hg_ref[...], up_ref[cols, :])
            xhat = xhat_scr[:, cols]
            gc = e1 * vec_ref[0:1, cols] + e2 * vec_ref[2:3, cols]
            gc_scr[:, cols] = gc
            mean = mean + jnp.sum(gc, axis=1, keepdims=True)
            slope = slope + jnp.sum(gc * xhat, axis=1, keepdims=True)
            own[0:1, cols] += jnp.sum(e1 * xhat, axis=0, keepdims=True)
            own[1:2, cols] += jnp.sum(e1, axis=0, keepdims=True)
            own[2:3, cols] += jnp.sum(e2 * xhat, axis=0, keepdims=True)
            own[3:4, cols] += jnp.sum(e2, axis=0, keepdims=True)
        mean = mean * (1.0 / d)
        slope = slope * (1.0 / d)
        for n in range(d // width):
            cols = slice(n * width, (n + 1) * width)
            value = (gc_scr[:, cols] - mean - xhat_scr[:, cols] * slope) * scale
            store_part(part, step, cols, value)

    @pl.when(step == STEPS)
    def _():
        spread.start(0)

    @pl.when(step == STEPS + 4)
    def _():
        own[...] = spread.finish(0)
        spread.start(1)

    def base(s):
        near = pl.ds(pl.multiple_of(s * 2 * SUB + line.near * SUB, SUB), SUB)
        return g_ref[near, :].astype(WIDE)

    line.tick(step, BACKWARD_LAG, base)

    @pl.when(step == BACKWARD_GRID - 1)
    def _():
        line.drain()
        total = spread.finish(1)
        row = lax.broadcasted_iota(jnp.int32, total.shape, 0)
        sums_ref[...] = jnp.where(row < 4, total, own[...])


def backward_line(qkv_grad, hidden_grad, tokens, cotangent, qkv_w, up_w, vectors, *sums):
    rows, d = tokens.shape
    small = (8, d)
    return pl.pallas_call(
        backward_kernel,
        grid=(BACKWARD_GRID,),
        in_specs=[
            row_block(qkv_grad.shape[1]),
            row_block(hidden_grad.shape[1]),
            row_block(d),
            base_block(d, BACKWARD_LAG),
            resident(vectors.shape),
        ]
        + [resident(part.shape) for part in sums]
        + [ANY] * 2,
        out_specs=[pl.BlockSpec(small, lambda i: (0, 0)), ANY],
        out_shape=[jax.ShapeDtypeStruct(small, WIDE), jax.ShapeDtypeStruct((rows, d), LOW)],
        scratch_shapes=[
            pltpu.VMEM(qkv_w.shape, LOW),
            pltpu.VMEM(up_w.shape, LOW),
            pltpu.SemaphoreType.DMA((2, d // 512)),
            pltpu.VMEM((STEP, d), WIDE),
            pltpu.VMEM((STEP, d), WIDE),
            pltpu.VMEM(small, WIDE),
            pltpu.VMEM((4,) + small, WIDE),
            pltpu.VMEM((8,) + small, WIDE),
            pltpu.SemaphoreType.DMA((4, 8)),
        ]
        + line_scratch(d),
        compiler_params=pltpu.CompilerParams(
            vmem_limit_bytes=VMEM_BYTES, collective_id=2, has_side_effects=True
        ),
        cost_estimate=pl.CostEstimate(
            flops=200_000_000_000, bytes_accessed=60 << 20, transcendentals=0
        ),
        name="backward_line",
    )(
        qkv_grad, hidden_grad, tokens, cotangent, vectors, *sums, qkv_w, up_w
    )


def halves(values):
    high = values.astype(LOW)
    return high, (values - high.astype(WIDE)).astype(LOW)


def shampoo_kernel(
    g_ref,
    w_ref,
    ls_ref,
    rs_ref,
    lr_ref,
    rr_ref,
    sums_ref,
    vec_ref,
    vec_stat_ref,
    unit_ref,
    unit_stat_ref,
    one_in,
    two_in,
    grad_ref,
    left_ref,
    right_ref,
    weight_ref,
    vec_grad_out,
    vec_stat_out,
    vec_out,
    unit_grad_out,
    unit_stat_out,
    unit_out,
    one_out,
    two_out,
    hold,
    sems,
):
    step = pl.program_id(0)
    pairs = ((one_in, one_out), (two_in, two_out))
    fetch = [pltpu.make_async_copy(a, hold.at[i], sems.at[0, i]) for i, (a, _) in enumerate(pairs)]
    store = [pltpu.make_async_copy(hold.at[i], b, sems.at[1, i]) for i, (_, b) in enumerate(pairs)]

    @pl.when(step == 0)
    def _():
        for copy in fetch:
            copy.start()
        vec_grad_out[0:5, :] = sums_ref[0:5, :]
        vec_grad_out[5:6, :] = sums_ref[4:5, :]
        vec_stat_out[...], vec_out[...] = vector_update(
            vec_ref[...], vec_stat_ref[...], vec_grad_out[...]
        )
        qkv_cols = unit_ref.shape[1] * 3 // 7
        unit_grad_out[:, :qkv_cols] = sums_ref[5:6, :qkv_cols]
        unit_grad_out[:, qkv_cols:] = sums_ref[6:7, : unit_ref.shape[1] - qkv_cols]
        unit_stat_out[...], unit_out[...] = vector_update(
            unit_ref[...], unit_stat_ref[...], unit_grad_out[...]
        )

    for i in range(2):

        @pl.when(step == pl.num_programs(0) * (i + 1) // 3)
        def _():
            fetch[i].wait()
            store[i].start()

    @pl.when(step == pl.num_programs(0) - 1)
    def _():
        for copy in store:
            copy.wait()

    for n in range(g_ref.shape[0]):
        g = g_ref[n]
        grad_ref[n] = g.astype(WIDE)
        left_ref[n] = 0.5 * ls_ref[n] + 0.5 * dot_nt(g, g)
        right_ref[n] = 0.5 * rs_ref[n] + 0.5 * dot_tn(g, g)
        l_high, l_low = halves(lr_ref[n])
        r_high, r_low = halves(rr_ref[n])
        d_high, d_low = halves(dot(l_high, g) + dot(l_low, g))
        direction = dot(d_high, r_high) + dot(d_low, r_high) + dot(d_high, r_low)
        weight = w_ref[n]
        size = 1.0 / (B * B)
        weight_size = jnp.sqrt(jnp.sum(weight * weight, keepdims=True) * size)
        step_size = jnp.sqrt(jnp.sum(direction * direction, keepdims=True) * size + 1e-06)
        weight_ref[n] = weight - direction * (step_share * weight_size / step_size)


def shampoo(grads, weights, left_stat, right_stat, left_root, right_root, small, one, two):
    count = grads.shape[0]
    group = 2
    spec = pl.BlockSpec((group, B, B), lambda i: (i, 0, 0))
    results = [small[1]] * 3 + [small[3]] * 3
    return pl.pallas_call(
        shampoo_kernel,
        grid=(count // group,),
        in_specs=[spec] * 6 + [resident(part.shape) for part in small] + [ANY] * 2,
        out_specs=[spec] * 4
        + [pl.BlockSpec(part.shape, lambda i: (0, 0)) for part in results]
        + [ANY] * 2,
        out_shape=[jax.ShapeDtypeStruct((count, B, B), WIDE)] * 4
        + [jax.ShapeDtypeStruct(part.shape, part.dtype) for part in results + [one, two]],
        scratch_shapes=[
            pltpu.VMEM((2,) + one.shape, one.dtype),
            pltpu.SemaphoreType.DMA((2, 2)),
        ],
        compiler_params=pltpu.CompilerParams(vmem_limit_bytes=VMEM_BYTES),
        name="shampoo",
    )(grads, weights, left_stat, right_stat, left_root, right_root, *small, one, two)


def per_device_line(
    tokens,
    cotangent,
    seq_len,
    seq_device,
    owner_map,
    weight_blocks,
    left_stat,
    right_stat,
    left_root,
    right_root,
    vectors,
    vector_stat,
    unit_bias,
    unit_stat,
):
    groups = lax.axis_size("mp")
    d = tokens.shape[1]
    qkv_cols = 3 * d // groups
    head_cols = d // groups
    unit_cols = FF // groups
    shapes = ((d, qkv_cols), (head_cols + unit_cols, d), (d, unit_cols))
    (
        qkv_w,
        od_w,
        up_w,
        normed_one,
        normed_two,
        table,
        q,
        k,
        v,
        ctx,
        stats,
        cot_sums,
    ) = gather_weights(
        weight_blocks[0],
        owner_map,
        seq_len,
        seq_device,
        tokens,
        cotangent,
        vectors,
        unit_bias,
        shapes,
    )
    block_out, hidden_grad, qkv_grad, weight_grads, hidden_sums, qkv_sums = forward_line(
        normed_one,
        normed_two,
        cotangent,
        ctx,
        (q, k, v),
        stats,
        table,
        tokens,
        up_w,
        od_w,
        unit_bias,
        vectors,
    )
    slots = unplace_blocks(weight_grads, owner_map)
    owned = lax.psum_scatter(slots, "dp", scatter_dimension=0, tiled=True)
    qkv_grad, hidden_grad, slots = lax.optimization_barrier((qkv_grad, hidden_grad, slots))
    sums, input_grad = backward_line(
        qkv_grad,
        hidden_grad,
        tokens,
        cotangent,
        qkv_w,
        up_w,
        vectors,
        cot_sums,
        qkv_sums,
        hidden_sums,
    )
    (
        block_grad,
        left_new,
        right_new,
        weight_new,
        vector_grad,
        vector_stat_new,
        vector_new,
        unit_grad,
        unit_stat_new,
        unit_new,
        block_out,
        input_grad,
    ) = shampoo(
        owned,
        weight_blocks[0],
        left_stat[0],
        right_stat[0],
        left_root[0],
        right_root[0],
        (sums, vectors, vector_stat, unit_bias, unit_stat),
        block_out,
        input_grad,
    )
    return (
        block_out,
        input_grad,
        block_grad[None],
        left_new[None],
        right_new[None],
        weight_new[None],
        vector_grad,
        vector_stat_new,
        vector_new,
        unit_grad,
        unit_stat_new,
        unit_new,
    )


def solution(mesh):
    placed = (
        P("dp", None),
        P("dp", None),
        P(),
        P(),
        P(),
        P("mp", "dp", None, None),
        P("mp", "dp", None, None),
        P("mp", "dp", None, None),
        P("mp", "dp", None, None),
        P("mp", "dp", None, None),
        P(),
        P(),
        P("mp", None),
        P("mp", None),
    )
    body = per_device
    if mesh.shape["dp"] == 8 and mesh.shape["mp"] == 4:
        body = per_device_line
    return jax.shard_map(
        body,
        mesh=mesh,
        in_specs=placed,
        out_specs=(
            P("dp", None),
            P("dp", None),
            P("mp", "dp", None, None),
            P("mp", "dp", None, None),
            P("mp", "dp", None, None),
            P("mp", "dp", None, None),
            P(),
            P(),
            P(),
            P("mp", None),
            P("mp", None),
            P("mp", None),
        ),
        check_vma=False,
    )
```

```python
import functools
import math

import jax
import jax.numpy as jnp
from jax import lax
from jax.experimental import pallas as pl
from jax.experimental.pallas import tpu as pltpu
from jax.sharding import PartitionSpec as P

D = 2048
HEADS = 8
HD = 256
ROT = 64
FF = 8192
B = 256


highest = lax.Precision.HIGHEST
norm_eps = 1e-05
step_share = 0.5
vector_rate = 0.15
masked_score = -1e30


def layer_norm(values, gain, shift):
    center = values - jnp.mean(values, axis=-1, keepdims=True)
    spread = jnp.mean(center * center, axis=-1, keepdims=True)
    return center * lax.rsqrt(spread + norm_eps) * gain + shift


def gelu_exact(values):
    return jax.nn.gelu(values, approximate=False)


def segment_layout(seq_len, seq_device, device, row_count):
    is_mine = seq_device == device
    lengths = jnp.where(is_mine, seq_len, 0)
    seq_ends = jnp.cumsum(lengths)
    row_index = jnp.arange(row_count, dtype=jnp.int32)
    passed = is_mine[None, :] & (seq_ends[None, :] <= row_index[:, None])
    segment = jnp.sum(passed.astype(jnp.int32), axis=1)
    seq_start = jnp.max(jnp.where(passed, seq_ends[None, :], 0), axis=1)
    return (segment, row_index - seq_start)


def rotary_tables(position):
    half_rot = ROT // 2
    frequency = 10000.0 ** (-2.0 * jnp.arange(half_rot, dtype=jnp.float32) / ROT)
    angles = position.astype(jnp.float32)[:, None] * frequency[None, :]
    cosine_table = jnp.concatenate([jnp.cos(angles), jnp.cos(angles)], axis=1)
    sine_table = jnp.concatenate([jnp.sin(angles), jnp.sin(angles)], axis=1)
    return (cosine_table, sine_table)


def rotate(values, cosine_table, sine_table):
    rot_dims = cosine_table.shape[1]
    half_rot = rot_dims // 2
    leading = values[..., :rot_dims]
    turned = jnp.concatenate([-leading[..., half_rot:], leading[..., :half_rot]], axis=-1)
    rotated = leading * cosine_table[:, None, :] + turned * sine_table[:, None, :]
    return jnp.concatenate([rotated, values[..., rot_dims:]], axis=-1)


def blocks_to_matrix(blocks, across):
    down_count = blocks.shape[0] // across
    return (
        blocks.reshape(down_count, across, B, B)
        .transpose(0, 2, 1, 3)
        .reshape(down_count * B, across * B)
    )


def matrix_to_blocks(matrix):
    down_count = matrix.shape[0] // B
    across = matrix.shape[1] // B
    return (
        matrix.reshape(down_count, B, across, B)
        .transpose(0, 2, 1, 3)
        .reshape(down_count * across, B, B)
    )


def split_blocks(blocks, qkv_cols, head_cols, unit_cols):
    qkv_end = D // B * (qkv_cols // B)
    out_end = qkv_end + head_cols // B * (D // B)
    up_end = out_end + D // B * (unit_cols // B)
    qkv_w = blocks_to_matrix(blocks[:qkv_end], qkv_cols // B)
    out_w = blocks_to_matrix(blocks[qkv_end:out_end], D // B)
    up_w = blocks_to_matrix(blocks[out_end:up_end], unit_cols // B)
    down_w = blocks_to_matrix(blocks[up_end:], D // B)
    return (qkv_w, out_w, up_w, down_w)


def apply_step(weight, direction):
    weight_size = jnp.sqrt(jnp.mean(weight * weight, axis=(-2, -1), keepdims=True))
    step_size = jnp.sqrt(jnp.mean(direction * direction, axis=(-2, -1), keepdims=True) + 1e-06)
    return weight - step_share * weight_size * direction / step_size


def vector_update(values, old_stat, gradient):
    new_stat = 0.5 * old_stat + 0.5 * gradient * gradient
    return (new_stat, values - vector_rate * gradient * lax.rsqrt(new_stat))


def block_mask(block_segment, block_row, segment, column):
    return (block_segment[:, None] == segment[None, :]) & (column[None, :] <= block_row[:, None])


def attention_forward(queries, keys_low, values_low, segment):
    row_count, head_count, head_dim = queries.shape
    block_rows = min(512, row_count)
    block_count = row_count // block_rows
    score_scale = 1.0 / math.sqrt(head_dim)
    column = jnp.arange(row_count, dtype=jnp.int32)

    def one_block(inputs):
        block_query, block_segment, block_row = inputs
        scores = (
            jnp.einsum("qhd,khd->hqk", block_query, keys_low, preferred_element_type=jnp.float32)
            * score_scale
        )
        scores = jnp.where(
            block_mask(block_segment, block_row, segment, column)[None], scores, masked_score
        )
        log_total = jax.nn.logsumexp(scores, axis=-1)
        weights = jnp.exp(scores - log_total[:, :, None]).astype(jnp.bfloat16)
        context = jnp.einsum(
            "hqk,khd->qhd", weights, values_low, preferred_element_type=jnp.float32
        )
        return (context, log_total)

    contexts, log_totals = lax.map(
        one_block,
        (
            queries.reshape(block_count, block_rows, head_count, head_dim),
            segment.reshape(block_count, block_rows),
            column.reshape(block_count, block_rows),
        ),
    )
    return (contexts.reshape(row_count, head_count, head_dim), log_totals)


def attention_backward(queries, keys_low, values_low, context_grad, log_totals, segment):
    row_count, head_count, head_dim = queries.shape
    block_rows = min(512, row_count)
    block_count = row_count // block_rows
    score_scale = 1.0 / math.sqrt(head_dim)
    column = jnp.arange(row_count, dtype=jnp.int32)

    def one_block(totals, inputs):
        key_grad, value_grad = totals
        block_query, block_grad, block_total, block_segment, block_row = inputs
        scores = (
            jnp.einsum("qhd,khd->hqk", block_query, keys_low, preferred_element_type=jnp.float32)
            * score_scale
        )
        scores = jnp.where(
            block_mask(block_segment, block_row, segment, column)[None], scores, masked_score
        )
        probs = jnp.exp(scores - block_total[:, :, None])
        weights = probs.astype(jnp.bfloat16)
        prob_grad = jnp.einsum(
            "qhd,khd->hqk", block_grad, values_low, preferred_element_type=jnp.float32
        )
        delta = jnp.sum(probs * prob_grad, axis=-1, keepdims=True)
        score_grad = (probs * (prob_grad - delta)).astype(jnp.bfloat16)
        query_grad = (
            jnp.einsum("hqk,khd->qhd", score_grad, keys_low, preferred_element_type=jnp.float32)
            * score_scale
        )
        key_grad = (
            key_grad
            + jnp.einsum(
                "hqk,qhd->khd", score_grad, block_query, preferred_element_type=jnp.float32
            )
            * score_scale
        )
        value_grad = value_grad + jnp.einsum(
            "hqk,qhd->khd", weights, block_grad, preferred_element_type=jnp.float32
        )
        return ((key_grad, value_grad), query_grad)

    zeros_start = jnp.zeros((row_count, head_count, head_dim), jnp.float32)
    (key_grad, value_grad), query_grad = lax.scan(
        one_block,
        (zeros_start, zeros_start),
        (
            queries.reshape(block_count, block_rows, head_count, head_dim),
            context_grad.reshape(block_count, block_rows, head_count, head_dim),
            log_totals,
            segment.reshape(block_count, block_rows),
            column.reshape(block_count, block_rows),
        ),
    )
    return (query_grad.reshape(row_count, head_count, head_dim), key_grad, value_grad)


def per_device(
    tokens,
    cotangent,
    seq_len,
    seq_device,
    owner_map,
    weight_blocks,
    left_stat,
    right_stat,
    left_root,
    right_root,
    vectors,
    vector_stat,
    unit_bias,
    unit_stat,
):
    groups = lax.axis_size("mp")
    device = lax.axis_index("dp")
    row_count = tokens.shape[0]
    heads_here = HEADS // groups
    qkv_cols = 3 * D // groups
    head_cols = D // groups
    unit_cols = FF // groups
    slot_count = weight_blocks.shape[1]
    sent_blocks = weight_blocks[0].astype(jnp.bfloat16)
    gathered = lax.all_gather(sent_blocks, "dp", axis=0, tiled=True)
    qkv_w, out_w, up_w, down_w = split_blocks(gathered[owner_map], qkv_cols, head_cols, unit_cols)
    segment, position = segment_layout(seq_len, seq_device, device, row_count)
    cosine_table, sine_table = rotary_tables(position)
    unit_shift = unit_bias[0]
    inputs = tokens.astype(jnp.float32)
    normed_one = layer_norm(inputs, vectors[0], vectors[1]).astype(jnp.bfloat16)
    normed_two = layer_norm(inputs, vectors[2], vectors[3]).astype(jnp.bfloat16)
    qkv_proj = (
        jnp.dot(normed_one, qkv_w, preferred_element_type=jnp.float32) + unit_shift[:qkv_cols]
    )
    qkv_proj = qkv_proj.reshape(row_count, heads_here, 3, HD)

    def turn_pair(values):
        return rotate(values.reshape(row_count, 2 * heads_here, HD), cosine_table, sine_table)

    turned, turn_back = jax.vjp(turn_pair, qkv_proj[:, :, :2])
    turned = turned.reshape(row_count, heads_here, 2, HD).astype(jnp.bfloat16)
    queries = turned[:, :, 0]
    keys_low = turned[:, :, 1]
    values_low = qkv_proj[:, :, 2].astype(jnp.bfloat16)
    context, log_totals = attention_forward(queries, keys_low, values_low, segment)
    context_low = context.reshape(row_count, head_cols).astype(jnp.bfloat16)
    hidden = jnp.dot(normed_two, up_w, preferred_element_type=jnp.float32) + unit_shift[qkv_cols:]
    active, gelu_back = jax.vjp(gelu_exact, hidden)
    active_low = active.astype(jnp.bfloat16)
    partial_out = jnp.dot(context_low, out_w, preferred_element_type=jnp.float32) + jnp.dot(
        active_low, down_w, preferred_element_type=jnp.float32
    )
    branch = lax.psum(partial_out.astype(jnp.bfloat16), "mp").astype(jnp.float32)
    block_out = (inputs + branch + (vectors[4] + vectors[5])).astype(jnp.bfloat16)
    grad_full = cotangent.astype(jnp.float32)
    act_grad = jnp.einsum("td,fd->tf", cotangent, down_w, preferred_element_type=jnp.float32)
    hidden_grad = gelu_back(act_grad)[0].astype(jnp.bfloat16)
    context_grad = jnp.einsum(
        "td,id->ti", cotangent, out_w, preferred_element_type=jnp.float32
    ).astype(jnp.bfloat16)
    query_grad, key_grad, value_grad = attention_backward(
        queries,
        keys_low,
        values_low,
        context_grad.reshape(row_count, heads_here, HD),
        log_totals,
        segment,
    )
    pair_grad = turn_back(
        jnp.stack([query_grad, key_grad], axis=2).reshape(row_count, 2 * heads_here, HD)
    )[0]
    qkv_grad = (
        jnp.concatenate([pair_grad, value_grad[:, :, None]], axis=2)
        .reshape(row_count, qkv_cols)
        .astype(jnp.bfloat16)
    )
    one_grad = jnp.einsum("te,de->td", qkv_grad, qkv_w, preferred_element_type=jnp.float32)
    two_grad = jnp.einsum("tf,df->td", hidden_grad, up_w, preferred_element_type=jnp.float32)
    norm_back_one = jax.vjp(layer_norm, inputs, vectors[0], vectors[1])[1]
    norm_back_two = jax.vjp(layer_norm, inputs, vectors[2], vectors[3])[1]
    input_one, gain_one, shift_one = norm_back_one(one_grad)
    input_two, gain_two, shift_two = norm_back_two(two_grad)
    input_part = input_one + input_two
    norm_part = jnp.stack([gain_one, shift_one, gain_two, shift_two])
    input_sum, norm_sum = lax.psum((input_part, norm_part), "mp")
    input_grad = (grad_full + input_sum).astype(jnp.bfloat16)
    qkv_w_grad = jnp.einsum("td,te->de", normed_one, qkv_grad, preferred_element_type=jnp.float32)
    out_w_grad = jnp.einsum("ti,td->id", context_low, cotangent, preferred_element_type=jnp.float32)
    up_w_grad = jnp.einsum("td,tf->df", normed_two, hidden_grad, preferred_element_type=jnp.float32)
    down_w_grad = jnp.einsum("tf,td->fd", active_low, cotangent, preferred_element_type=jnp.float32)
    canonical_grad = jnp.concatenate(
        [matrix_to_blocks(matrix) for matrix in (qkv_w_grad, out_w_grad, up_w_grad, down_w_grad)],
        axis=0,
    )
    slot_grads = canonical_grad[jnp.argsort(owner_map)]
    out_sum = jnp.sum(grad_full, axis=0)
    vector_part = jnp.concatenate([norm_sum, jnp.stack([out_sum, out_sum])], axis=0)
    unit_part = jnp.concatenate(
        [
            jnp.sum(qkv_grad.astype(jnp.float32), axis=0),
            jnp.sum(hidden_grad.astype(jnp.float32), axis=0),
        ]
    )
    summed, vector_grad, unit_grad = lax.psum((slot_grads, vector_part, unit_part), "dp")
    owned = lax.dynamic_slice_in_dim(summed, device * slot_count, slot_count, 0)
    left_new = 0.5 * left_stat[0] + 0.5 * jnp.einsum(
        "nij,nkj->nik", owned, owned, precision=highest
    )
    right_new = 0.5 * right_stat[0] + 0.5 * jnp.einsum(
        "nji,njk->nik", owned, owned, precision=highest
    )
    direction = jnp.einsum("nij,njk->nik", left_root[0], owned, precision=highest)
    direction = jnp.einsum("nij,njk->nik", direction, right_root[0], precision=highest)
    weight_new = apply_step(weight_blocks[0], direction)
    vector_stat_new, vector_new = vector_update(vectors, vector_stat, vector_grad)
    unit_stat_new, unit_new = vector_update(unit_shift, unit_stat[0], unit_grad)
    return (
        block_out,
        input_grad,
        owned[None],
        left_new[None],
        right_new[None],
        weight_new[None],
        vector_grad,
        vector_stat_new,
        vector_new,
        unit_grad[None],
        unit_stat_new[None],
        unit_new[None],
    )


LOW = jnp.bfloat16
WIDE = jnp.float32
MESH = pl.DeviceIdType.MESH
ANY = pl.BlockSpec(memory_space=pl.ANY)
STEP = 256
SUB = 32
PAIRS = 32
STEPS = 8
PER_STEP = PAIRS // STEPS
TICKS = PAIRS // 2
GOT = 8
ACROSS = 4
VMEM_BYTES = 60 * 1024 * 1024
FORWARD_VMEM = 63 * 1024 * 1024
GATHER_VMEM = 63 * 1024 * 1024


def dot(left, right):
    return lax.dot_general(left, right, (((1,), (0,)), ((), ())), preferred_element_type=WIDE)


def dot_nt(left, right):
    return lax.dot_general(left, right, (((1,), (1,)), ((), ())), preferred_element_type=WIDE)


def dot_tn(left, right):
    return lax.dot_general(left, right, (((0,), (0,)), ((), ())), preferred_element_type=WIDE)


def resident(shape):
    return pl.BlockSpec(shape, lambda *_: (0,) * len(shape), pipeline_mode=pl.Buffered(1))


def unplace_kernel(order_ref, blocks_ref, slots_ref, hold, sem_in, sem_out):
    total = blocks_ref.shape[0]
    chunk = total // sem_in.shape[0]

    def read(i):
        part = pl.ds(i * chunk, chunk)
        return pltpu.make_async_copy(blocks_ref.at[part], hold.at[part], sem_in.at[i])

    def write(b):
        return pltpu.make_async_copy(hold.at[b], slots_ref.at[order_ref[b]], sem_out.at[b])

    for i in range(total // chunk):
        read(i).start()
    for i in range(total // chunk):
        read(i).wait()
        for b in range(i * chunk, (i + 1) * chunk):
            write(b).start()
    for b in range(total):
        write(b).wait()


def unplace_blocks(blocks, order):
    total = order.shape[0]
    return pl.pallas_call(
        unplace_kernel,
        grid_spec=pltpu.PrefetchScalarGridSpec(
            num_scalar_prefetch=1,
            grid=(1,),
            in_specs=[ANY],
            out_specs=ANY,
            scratch_shapes=[
                pltpu.VMEM((total, B, B), LOW),
                pltpu.SemaphoreType.DMA((48,)),
                pltpu.SemaphoreType.DMA((total,)),
            ],
        ),
        out_shape=jax.ShapeDtypeStruct((total, B, B), LOW),
        compiler_params=pltpu.CompilerParams(vmem_limit_bytes=VMEM_BYTES),
        name="unplace_blocks",
    )(order, blocks)


def turn(values, cos, sin, back=False):
    lanes = lax.broadcasted_iota(jnp.int32, values.shape, 1)
    lower, upper = pltpu.roll(values, 96, 1), pltpu.roll(values, 32, 1)
    other = jnp.where(lanes < 32, -lower, upper)
    return values * cos - other * sin if back else values * cos + other * sin


def attention_rows(c, tile, first, q_ref, k_ref, v_ref, s_scr, ctx_ref, stats_ref):
    here = slice(c * tile, (c + 1) * tile)
    lanes = lax.broadcasted_iota(jnp.int32, (tile, 128), 1)
    stats = jnp.broadcast_to(first.astype(WIDE), (tile, 128))
    for h in range(q_ref.shape[1] // HD):
        cols = slice(h * HD, (h + 1) * HD)
        q = q_ref[here, cols]
        top = jnp.full((tile, 1), masked_score, WIDE)
        for j in range(c + 1):
            keys = slice(j * tile, (j + 1) * tile)
            s = dot_nt(q, k_ref[keys, cols])
            col = lax.broadcasted_iota(jnp.int32, (tile, tile), 1) + j * tile
            ok = col >= first
            if j == c:
                row = lax.broadcasted_iota(jnp.int32, (tile, tile), 0) + c * tile
                ok = ok & (col <= row)
            s = jnp.where(ok, s, masked_score)
            s_scr[:, keys] = s
            top = jnp.maximum(top, jnp.max(s, axis=1, keepdims=True))
        total = jnp.zeros((tile, 1), WIDE)
        ctx = jnp.zeros((tile, HD), WIDE)
        for j in range(c + 1):
            keys = slice(j * tile, (j + 1) * tile)
            e = jnp.exp(s_scr[:, keys] - top)
            total = total + jnp.sum(e, axis=1, keepdims=True)
            ctx = ctx + dot(e.astype(LOW), v_ref[keys, cols])
        ctx_ref[:, cols] = (ctx * (1.0 / total)).astype(LOW)
        stats = jnp.where(lanes == h, top + jnp.log(total), stats)
    stats_ref[...] = stats


PIECES = 4
ROUTES = ((0, 2), (0, 4), (0, 1), (2, 4), (4, 2), (2, 1), (4, 1), (6, 1))


def flip(index, mask):
    for bit in range(3):
        if mask >> bit & 1:
            unit = 2**bit
            index = index + (1 - 2 * lax.rem(lax.div(index, unit), 2)) * unit
    return index


def segments(qkv, od, up):
    wide, down = od.shape[1] // B, up.shape[1] // B
    out = od.shape[0] // B - down
    deep, cols = qkv.shape[0] // B, qkv.shape[1] // B
    starts = [deep * cols, out * wide, deep * down]
    return (
        (qkv, 0, deep, cols, 0),
        (od, 0, out, wide, starts[0]),
        (up, 0, deep, down, sum(starts[:2])),
        (od, out, down, wide, sum(starts)),
    )


def gather_kernel(
    order_ref,
    len_ref,
    place_ref,
    vec_ref,
    freq_ref,
    bias_ref,
    w_hbm,
    x_hbm,
    cot_hbm,
    qkv_hbm,
    od_hbm,
    up_hbm,
    h1_hbm,
    h2_hbm,
    table_hbm,
    q_hbm,
    k_hbm,
    v_hbm,
    ctx_hbm,
    stats_hbm,
    sum_ref,
    slots,
    wide,
    x_buf,
    c_buf,
    h_buf,
    table_all,
    stage,
    qkv_buf,
    q_all,
    k_all,
    v_all,
    s_scr,
    stats_buf,
    send_sem,
    recv_sem,
    load_sem,
    row_sem,
    norm_sem,
    stage_sem,
    out_sem,
    row_out_sem,
    q_sem,
):
    me = lax.axis_index("dp")
    each = w_hbm.shape[0]
    size = each // PIECES
    steps = x_hbm.shape[0] // STEP

    def piece(mask, q):
        return slots.at[pl.ds(flip(me, mask) * each + q * size, size)]

    def send(source, target, q):
        return pltpu.make_async_remote_copy(
            src_ref=piece(source, q),
            dst_ref=piece(source, q),
            send_sem=send_sem.at[ROUTES.index((source, target)), q],
            recv_sem=recv_sem.at[source ^ target, q],
            device_id={"dp": flip(me, target)},
            device_id_type=MESH,
        )

    def arrived(source, q):
        pltpu.make_async_remote_copy(
            src_ref=piece(source, q),
            dst_ref=piece(source, q),
            send_sem=send_sem.at[0, q],
            recv_sem=recv_sem.at[source, q],
            device_id={"dp": flip(me, 1)},
            device_id_type=MESH,
        ).wait_recv()

    def load(q):
        return pltpu.make_async_copy(
            w_hbm.at[pl.ds(q * size, size)], wide.at[q % 2], load_sem.at[q % 2]
        )

    def tile(i):
        return pl.ds(pl.multiple_of(i * STEP, STEP), STEP)

    def fetch(i, slot):
        return (
            pltpu.make_async_copy(x_hbm.at[tile(i), :], x_buf.at[slot], row_sem.at[0, slot]),
            pltpu.make_async_copy(cot_hbm.at[tile(i), :], c_buf.at[slot], row_sem.at[1, slot]),
        )

    def keep(i, slot):
        return (
            pltpu.make_async_copy(h_buf.at[slot], h1_hbm.at[tile(i), :], norm_sem.at[0, slot]),
            pltpu.make_async_copy(stage.at[slot], h2_hbm.at[tile(i), :], norm_sem.at[1, slot]),
        )

    def norm_step(i, slot, first):
        for copy in fetch(i, slot):
            copy.wait()

        @pl.when(jnp.logical_not(first))
        def _():
            for copy in keep(i, slot):
                copy.wait()

        x = x_buf[slot].astype(WIDE)
        center = x - jnp.mean(x, axis=1, keepdims=True)
        scale = lax.rsqrt(jnp.mean(center * center, axis=1, keepdims=True) + norm_eps)
        xhat = center * scale
        h_buf[slot] = (xhat * vec_ref[0:1, :] + vec_ref[1:2, :]).astype(LOW)
        stage[slot] = (xhat * vec_ref[2:3, :] + vec_ref[3:4, :]).astype(LOW)
        sum_ref[0:1, :] += jnp.sum(c_buf[slot].astype(WIDE), axis=0, keepdims=True)
        row = lax.broadcasted_iota(jnp.int32, (STEP, 128), 0) + i * STEP
        first = jnp.zeros((STEP, 128), jnp.int32)
        end = jnp.int32(0)
        for j in range(len_ref.shape[0]):
            mine = place_ref[j] == me
            end = end + jnp.where(mine, len_ref[j], 0)
            first = jnp.where(row >= jnp.where(mine, end, 1 << 30), end, first)
        angle = (row - first).astype(WIDE) * freq_ref[...]
        table_all[0, tile(i), :] = jnp.cos(angle)
        table_all[1, tile(i), :] = jnp.sin(angle)
        table_all[2, tile(i), :] = first.astype(WIDE)
        for copy in keep(i, slot):
            copy.start()

    for q in range(2):
        load(q).start()
    for slot in range(2):
        for copy in fetch(slot, slot):
            copy.start()
    barrier = pltpu.get_barrier_semaphore()
    for target in (1, 2, 4):
        pl.semaphore_signal(
            barrier, inc=1, device_id={"dp": flip(me, target)}, device_id_type=MESH
        )
    sum_ref[...] = jnp.zeros_like(sum_ref)
    for q in range(PIECES):
        load(q).wait()
        slots[pl.ds(me * each + q * size, size)] = wide[q % 2].astype(LOW)
        if q + 2 < PIECES:
            load(q + 2).start()
        if q == 0:
            pl.semaphore_wait(barrier, 3)
        for target in (2, 4, 1):
            send(0, target, q).start()

    for q in range(PIECES):

        @pl.loop(0, steps // (2 * PIECES))
        def _(k):
            i = (q * (steps // (2 * PIECES)) + k) * 2
            for slot in range(2):
                norm_step(i + slot, slot, i == 0)

                @pl.when(i + slot + 2 < steps)
                def _():
                    for copy in fetch(i + slot + 2, slot):
                        copy.start()

        arrived(2, q)
        if q % 2:
            send(2, 4, q).start()
        send(2, 1, q).start()
        arrived(4, q)
        if q % 2 == 0:
            send(4, 2, q).start()
        send(4, 1, q).start()
    for slot in range(2):
        for copy in keep(slot, slot):
            copy.wait()
    for q in range(PIECES):
        arrived(6, q)
        send(6, 1, q).start()
    for source in (1, 3, 5, 7):
        for q in range(PIECES):
            arrived(source, q)

    _, out, up, down = segments(qkv_hbm, od_hbm, up_hbm)
    qkv_across = qkv_hbm.shape[1] // B
    whole = [
        pltpu.make_async_copy(src, dst, out_sem.at[i])
        for i, (src, dst) in enumerate(
            (
                (qkv_buf, qkv_hbm),
                (table_all, table_hbm),
                (k_all, k_hbm),
                (v_all, v_hbm),
            )
        )
    ]

    def q_out(i):
        return pltpu.make_async_copy(
            q_all.at[tile(i), :], q_hbm.at[tile(i), :], q_sem.at[i]
        )

    def panel(part, i, slot):
        ref, skip = part[:2]
        return pltpu.make_async_copy(
            stage.at[slot], ref.at[lane((skip + i) * B), :], stage_sem.at[slot]
        )

    def put(part, i, slot):
        across, block = part[3:]
        for j in range(across):
            stage[slot, :, j * B : (j + 1) * B] = slots[order_ref[block + i * across + j]]
        panel(part, i, slot).start()

    def fetch_h(i, slot):
        return pltpu.make_async_copy(h1_hbm.at[tile(i), :], x_buf.at[slot], row_sem.at[0, slot])

    for slot in range(2):
        fetch_h(slot, slot).start()

    @pl.loop(0, qkv_hbm.shape[0] // B)
    def _(i):
        for j in range(qkv_across):
            qkv_buf[lane(i * B), j * B : (j + 1) * B] = slots[order_ref[i * qkv_across + j]]

    whole[0].start()
    whole[1].start()
    for slot in range(2):
        put(out, slot, slot)

    def project(i, slot):
        scale = 1.0 / math.sqrt(HD)
        for j in range(qkv_across):
            head, part = divmod(j, 3)
            cols = slice(head * HD, head * HD + HD)
            proj = dot(x_buf[slot], qkv_buf[:, j * B : (j + 1) * B])
            proj = proj + bias_ref[:, j * B : (j + 1) * B]
            if part == 2:
                v_all[tile(i), cols] = proj.astype(LOW)
                continue
            front = turn(proj[:, :128], table_all[0, tile(i), :], table_all[1, tile(i), :])
            turned = jnp.concatenate([front, proj[:, 128:]], axis=1).astype(LOW)
            if part == 0:
                q_all[tile(i), cols] = (turned.astype(WIDE) * scale).astype(LOW)
            else:
                k_all[tile(i), cols] = turned

    @pl.loop(0, steps // 2)
    def _(k):
        for slot in range(2):
            i = k * 2 + slot
            fetch_h(i, slot).wait()
            project(i, slot)
            q_out(i).start()

            @pl.when(i + 2 < steps)
            def _():
                fetch_h(i + 2, slot).start()

            panel(out, 0, 0).wait()
            put(up, i, 0)
            panel(out, 0, 1).wait()
            put(down, i, 1)

    for copy in whole[2:]:
        copy.start()
    rows = 512

    @pl.loop(0, steps)
    def _(i):
        q_out(i).wait()


    def row_out(c):
        part, slot = pl.ds(c * rows, rows), c % 2
        return (
            pltpu.make_async_copy(q_all.at[part, :], ctx_hbm.at[part, :], row_out_sem.at[0, slot]),
            pltpu.make_async_copy(
                stats_buf.at[slot], stats_hbm.at[part, :], row_out_sem.at[1, slot]
            ),
        )

    count = x_hbm.shape[0] // rows
    for c in range(count):
        if c >= 2:
            for copy in row_out(c - 2):
                copy.wait()
        first = table_all[2, c * rows : (c + 1) * rows, :][:, 0:1].astype(jnp.int32)
        place = q_all.at[pl.ds(c * rows, rows), :]
        attention_rows(c, rows, first, q_all, k_all, v_all, s_scr, place, stats_buf.at[c % 2])
        for copy in row_out(c):
            copy.start()
    for c in range(count - 2, count):
        for copy in row_out(c):
            copy.wait()
    for slot in range(2):
        panel(out, 0, slot).wait()
    for copy in whole:
        copy.wait()

    for source, target in ROUTES:
        for q in range(PIECES):
            if (source, target) == (2, 4) and q % 2 == 0:
                continue
            if (source, target) == (4, 2) and q % 2:
                continue
            send(source, target, q).wait_send()


def gather_weights(
    blocks, order, seq_len, seq_device, tokens, cotangent, vectors, bias, shapes
):
    rows, d = tokens.shape
    each = blocks.shape[0]
    half = 10000.0 ** (-2.0 * jnp.arange(ROT // 2, dtype=WIDE) / ROT)
    frequency = jnp.concatenate([half, half, jnp.zeros((128 - ROT,), WIDE)])[None]
    smem = pl.BlockSpec(memory_space=pltpu.SMEM)
    vmem = pl.BlockSpec(memory_space=pltpu.VMEM)
    return pl.pallas_call(
        gather_kernel,
        in_specs=[smem, smem, smem, vmem, vmem, vmem, ANY, ANY, ANY],
        out_specs=[ANY] * 11 + [vmem],
        out_shape=[jax.ShapeDtypeStruct(s, LOW) for s in shapes]
        + [jax.ShapeDtypeStruct((rows, d), LOW)] * 2
        + [jax.ShapeDtypeStruct((3, rows, 128), WIDE)]
        + [jax.ShapeDtypeStruct((rows, shapes[0][1] // 3), LOW)] * 4
        + [jax.ShapeDtypeStruct((rows, 128), WIDE)]
        + [jax.ShapeDtypeStruct((8, d), WIDE)],
        scratch_shapes=[
            pltpu.VMEM((order.shape[0], B, B), LOW),
            pltpu.VMEM((2, each // PIECES, B, B), WIDE),
            pltpu.VMEM((2, STEP, d), LOW),
            pltpu.VMEM((2, STEP, d), LOW),
            pltpu.VMEM((2, STEP, d), LOW),
            pltpu.VMEM((3, rows, 128), WIDE),
            pltpu.VMEM((2, B, d), LOW),
            pltpu.VMEM(shapes[0], LOW),
        ]
        + [pltpu.VMEM((rows, shapes[0][1] // 3), LOW)] * 3
        + [
            pltpu.VMEM((512, rows), WIDE),
            pltpu.VMEM((2, 512, 128), WIDE),
            pltpu.SemaphoreType.DMA((8, PIECES)),
            pltpu.SemaphoreType.DMA((8, PIECES)),
            pltpu.SemaphoreType.DMA((2,)),
            pltpu.SemaphoreType.DMA((2, 2)),
            pltpu.SemaphoreType.DMA((2, 2)),
            pltpu.SemaphoreType.DMA((2,)),
            pltpu.SemaphoreType.DMA((4,)),
            pltpu.SemaphoreType.DMA((2, 2)),
            pltpu.SemaphoreType.DMA((rows // STEP,)),
        ],
        compiler_params=pltpu.CompilerParams(
            vmem_limit_bytes=GATHER_VMEM, collective_id=3, has_side_effects=True
        ),
        cost_estimate=pl.CostEstimate(
            flops=100_000_000_000, bytes_accessed=80 << 20, transcendentals=0
        ),
        name="gather_weights",
    )(order, seq_len, seq_device, vectors, frequency, bias, blocks, tokens, cotangent)


class Line:
    def __init__(self, out, part, got, across, sems):
        self.out, self.part, self.got, self.across = out, part, got, across
        (
            self.up_send,
            self.up_recv,
            self.far_send,
            self.far_recv,
            self.over_send,
            self.over_recv,
            self.down_send,
            self.down_recv,
            self.relay_send,
            self.relay_recv,
            self.own,
        ) = [sems.at[i] for i in range(11)]
        z = lax.axis_index("mp")
        self.inner = (z == 1) | (z == 2)
        self.near = (z >= 2).astype(jnp.int32)
        self.far = 1 - self.near
        self.partner = jnp.where(self.inner, jnp.where(z == 1, 0, 3), jnp.where(z == 0, 1, 2))
        self.other = 3 - z

    def rows(self, pair, which):
        return self.out.at[pl.ds(pl.multiple_of(pair * (2 * SUB) + which * SUB, SUB), SUB), :]

    def greet(self):
        barrier = pltpu.get_barrier_semaphore()
        pl.semaphore_signal(barrier, inc=1, device_id={"mp": self.partner}, device_id_type=MESH)

        @pl.when(self.inner)
        def _():
            pl.semaphore_signal(barrier, inc=1, device_id={"mp": self.other}, device_id_type=MESH)
            pl.semaphore_wait(barrier, 2)

        @pl.when(jnp.logical_not(self.inner))
        def _():
            pl.semaphore_wait(barrier, 1)

    def copy(self, src, dst, send, recv, pair, target):
        return pltpu.make_async_remote_copy(
            src_ref=src,
            dst_ref=dst,
            send_sem=send.at[pair],
            recv_sem=recv.at[pair],
            device_id={"mp": target},
            device_id_type=MESH,
        )

    def up(self, pair):
        return self.copy(
            self.part.at[pair], self.got.at[pair % GOT], self.up_send, self.up_recv, pair, self.partner
        )

    def far_sum(self, pair):
        src, dst = self.part.at[pair, self.far], self.across.at[pair % ACROSS]
        return self.copy(src, dst, self.far_send, self.far_recv, pair, self.other)

    def over(self, pair, which):
        src = self.part.at[pair, self.near]
        return self.copy(src, self.rows(pair, which), self.over_send, self.over_recv, pair, self.other)

    def down(self, pair):
        src = self.part.at[pair, self.near]
        return self.copy(
            src, self.rows(pair, self.near), self.down_send, self.down_recv, pair, self.partner
        )

    def relay(self, pair):
        far = self.rows(pair, self.far)
        return self.copy(far, far, self.relay_send, self.relay_recv, pair, self.partner)

    def keep(self, pair):
        src = self.part.at[pair, self.near]
        return pltpu.make_async_copy(src, self.rows(pair, self.near), self.own.at[pair])

    def send_up(self, pair):
        @pl.when(pair >= GOT)
        def _():
            self.down(pair - GOT).wait_recv()

        self.up(pair).start()

    def add_far(self, pair):
        self.up(pair).wait_recv()
        far = self.part[pair, self.far].astype(WIDE) + self.got[pair % GOT, self.far].astype(WIDE)
        self.part[pair, self.far] = far.astype(LOW)
        self.far_sum(pair).start()

    def finish_near(self, pair, base):
        self.far_sum(pair).wait_recv()
        total = (
            self.part[pair, self.near].astype(WIDE)
            + self.got[pair % GOT, self.near].astype(WIDE)
            + self.across[pair % ACROSS].astype(WIDE)
        )
        self.part[pair, self.near] = (base + total).astype(LOW)
        self.over(pair, self.near).start()
        self.down(pair).start()
        self.keep(pair).start()

    def send_relay(self, pair):
        self.over(pair, self.far).wait_recv()
        self.relay(pair).start()

    def drain(self):
        @pl.when(self.inner)
        def _():
            @pl.loop(0, PAIRS)
            def _(pair):
                self.far_sum(pair).wait_send()
                self.over(pair, self.near).wait_send()
                self.down(pair).wait_send()
                self.relay(pair).wait_send()
                self.keep(pair).wait()

        @pl.when(jnp.logical_not(self.inner))
        def _():
            @pl.loop(0, PAIRS)
            def _(pair):
                self.up(pair).wait_send()
                self.relay(pair).wait_recv()

            @pl.loop(PAIRS - GOT, PAIRS)
            def _(pair):
                self.down(pair).wait_recv()

    def tick(self, step, lag, base):
        ahead = GOT // PER_STEP

        @pl.when(jnp.logical_not(self.inner) & (step < ahead))
        def _():
            for s in range(PER_STEP):
                self.send_up(step * PER_STEP + s)

        @pl.when(
            jnp.logical_not(self.inner) & (step >= ahead) & (step < ahead + (PAIRS - GOT) // 2)
        )
        def _():
            for s in range(2):
                self.send_up(GOT + (step - ahead) * 2 + s)

        @pl.when(self.inner & (step >= lag + 2) & (step < lag + 2 + TICKS))
        def _():
            for s in range(2):
                self.send_relay((step - lag - 2) * 2 + s)

        @pl.when(self.inner & (step >= lag + 1) & (step < lag + 1 + TICKS))
        def _():
            for s in range(2):
                self.finish_near((step - lag - 1) * 2 + s, base(s))

        @pl.when(self.inner & (step >= lag) & (step < lag + TICKS))
        def _():
            for s in range(2):
                self.add_far((step - lag) * 2 + s)


def line_scratch(d):
    return [
        pltpu.VMEM((PAIRS, 2, SUB, d), LOW),
        pltpu.VMEM((GOT, 2, SUB, d), LOW),
        pltpu.VMEM((ACROSS, SUB, d), LOW),
        pltpu.SemaphoreType.DMA((11, PAIRS)),
    ]


def now(step):
    return jnp.minimum(step, STEPS - 1)


def row_block(width):
    return pl.BlockSpec((STEP, width), lambda i: (now(i), 0))


def base_block(width, lag):
    return pl.BlockSpec((4 * SUB, width), lambda i: (jnp.clip(i - lag - 1, 0, TICKS - 1), 0))


def lane(start):
    return pl.ds(pl.multiple_of(start, B), B)


def gelu_parts(z):
    e = jnp.exp(z * z * -0.5)
    t = 1.0 / (1.0 + jnp.abs(z) * (0.3275911 * math.sqrt(0.5)))
    poly = t * (
        0.5 * 0.254829592
        + t
        * (
            0.5 * -0.284496736
            + t * (0.5 * 1.421413741 + t * (0.5 * -1.453152027 + t * (0.5 * 1.061405429)))
        )
    )
    below = poly * e
    cdf = jnp.where(z >= 0, 1.0 - below, below)
    return cdf, e * (1.0 / math.sqrt(2.0 * math.pi))


def store_part(part_ref, step, cols, value):
    value = value.astype(LOW).reshape(PER_STEP, 2, SUB, value.shape[1])
    part_ref[pl.ds(step * PER_STEP, PER_STEP), :, :, cols] = value


FORWARD_LAG = 1
FORWARD_GRID = FORWARD_LAG + TICKS + 2


def weight_unit(a_t, b_ref, cols, stage, slot):
    for n in range(cols // 512):
        part = slice(n * 512, (n + 1) * 512)
        stage[pl.ds(pl.multiple_of(slot * B, B), B), part] = dot(a_t, b_ref[:, part]).astype(LOW)


def forward_kernel(
    h_ref,
    g_ref,
    ctx_ref,
    x_ref,
    stats_ref,
    bias_ref,
    vec_ref,
    table_ref,
    up_hbm,
    od_hbm,
    h1_hbm,
    h2_hbm,
    ctx_hbm,
    cot_hbm,
    q_hbm,
    k_hbm,
    v_hbm,
    out_ref,
    hg_hbm,
    qg_hbm,
    wg_hbm,
    sums_ref,
    qkv_sums_ref,
    up_buf,
    od_buf,
    act_all,
    hg_all,
    part,
    got,
    across,
    sems,
    grad_all,
    stats,
    dq_scr,
    dk_scr,
    dv_scr,
    load_sem,
    panel_sem,
    stage_sem,
    hg_sem,
    head_sem,
):
    step = pl.program_id(0)
    line = Line(out_ref, part, got, across, sems)
    heads = ctx_ref.shape[1]
    rows, units = act_all.shape
    qkv_cols = qg_hbm.shape[1]
    width = 512
    tiles = units // width
    stage = od_buf.at[pl.ds(rows, 2 * B), :]

    def load_up(n):
        cols = pl.ds(n * width, width)
        return pltpu.make_async_copy(up_hbm.at[:, cols], up_buf.at[:, cols], load_sem.at[n])

    def load_down(n):
        part_rows = pl.ds(heads + n * width, width)
        return pltpu.make_async_copy(
            od_hbm.at[part_rows, :], od_buf.at[part_rows, :], load_sem.at[tiles + n]
        )

    def load_out():
        part_rows = pl.ds(0, heads)
        return pltpu.make_async_copy(
            od_hbm.at[part_rows, :], od_buf.at[part_rows, :], load_sem.at[2 * tiles]
        )

    def load_cot():
        return pltpu.make_async_copy(
            cot_hbm, od_buf.at[pl.ds(0, rows), :], load_sem.at[2 * tiles + 1]
        )

    def load_head(h):
        cols = pl.ds(pl.multiple_of(h * HD, HD), HD)
        return [
            pltpu.make_async_copy(
                src.at[:, cols], act_all.at[:, pl.ds(i * HD, HD)], head_sem.at[i]
            )
            for i, src in enumerate((q_hbm, k_hbm, v_hbm))
        ]

    def store_qg():
        return pltpu.make_async_copy(hg_all.at[:, pl.ds(0, qkv_cols)], qg_hbm, head_sem.at[5])

    def panel_cols(slot):
        return lane(qkv_cols + slot * B)

    def panel(src, i, slot):
        return pltpu.make_async_copy(
            src.at[:, lane(i * B)], up_buf.at[:, panel_cols(slot)], panel_sem.at[slot]
        )

    def store_hg(i):
        part_rows = pl.ds(pl.multiple_of(i * STEP, STEP), STEP)
        return pltpu.make_async_copy(
            hg_all.at[part_rows, :], hg_hbm.at[part_rows, :], hg_sem.at[i]
        )

    def stage_out(block, j, slot):
        return pltpu.make_async_copy(
            stage.at[lane(slot * B), pl.ds(j * B, B)], wg_hbm.at[block + j], stage_sem.at[slot]
        )

    def stage_wait(cols, slot):
        place = stage.at[lane(slot * B), pl.ds(0, cols)]
        pltpu.make_async_copy(place, place, stage_sem.at[slot]).wait()

    @pl.when(step == 0)
    def _():
        for n in range(tiles):
            load_up(n).start()
            load_down(n).start()
        load_out().start()
        line.greet()
        sums_ref[...] = jnp.zeros_like(sums_ref)

    @pl.when(step < STEPS)
    def _():
        here = pl.ds(pl.multiple_of(step * STEP, STEP), STEP)
        for n in range(tiles):
            cols = slice(n * width, (n + 1) * width)

            @pl.when(step == 0)
            def _():
                load_up(n).wait()
                load_down(n).wait()

            bias = bias_ref[:, qkv_cols + n * width : qkv_cols + (n + 1) * width]
            hidden = dot(h_ref[...], up_buf[:, cols]) + bias
            act_grad = dot_nt(g_ref[...], od_buf[heads + n * width : heads + (n + 1) * width, :])
            cdf, density = gelu_parts(hidden)
            act_all[here, cols] = (hidden * cdf).astype(LOW)
            grad = (act_grad * (cdf + hidden * density)).astype(LOW)
            hg_all[here, cols] = grad
            sums_ref[0:1, cols] += jnp.sum(grad.astype(WIDE), axis=0, keepdims=True)

        @pl.when(step == 0)
        def _():
            load_out().wait()

        store_hg(step).start()
        grad = dot_nt(g_ref[...], od_buf[:heads, :]).astype(LOW)
        grad_all[here, :] = grad
        lanes = lax.broadcasted_iota(jnp.int32, (STEP, 128), 1)
        info = stats_ref[...]
        for h in range(heads // HD):
            cols = slice(h * HD, (h + 1) * HD)
            both = ctx_ref[:, cols].astype(WIDE) * grad[:, cols].astype(WIDE)
            info = jnp.where(lanes == 64 + h, jnp.sum(both, axis=1, keepdims=True), info)
        stats[here, :] = info
        for n in range(od_buf.shape[1] // width):
            cols = slice(n * width, (n + 1) * width)
            value = dot(ctx_ref[...], od_buf[:heads, cols]) + dot(
                act_all[here, :], od_buf[heads:, cols]
            )
            store_part(part, step, cols, value)

    @pl.when(step == STEPS - 1)
    def _():
        panel(h2_hbm, 0, 0).start()
        load_cot().start()

    wide = od_buf.shape[1] // B
    out_first = rows // B * (qkv_cols // B)
    up_first = out_first + heads // B * wide
    down_first = up_first + rows // B * (units // B)

    def unit(index, a_t, b_ref, cols, first):
        slot = index % 2

        @pl.when(index >= 2)
        def _():
            stage_wait(cols, slot)

        weight_unit(a_t, b_ref, cols, stage, slot)
        for j in range(cols // B):
            stage_out(first + index * (cols // B), j, slot).start()

    def settle(cols):
        for slot in range(2):
            stage_wait(cols, slot)

    @pl.when((step == 8) | (step == 9))
    def _():
        @pl.loop(0, 4)
        def _(k):
            i = (step - 8) * 4 + k
            panel(h2_hbm, i, i % 2).wait()

            @pl.when(i < 7)
            def _():
                panel(h2_hbm, i + 1, (i + 1) % 2).start()

            unit(i, up_buf[:, panel_cols(i % 2)].T, hg_all, units, up_first)

    @pl.when(step == 10)
    def _():
        settle(units)
        load_cot().wait()

    @pl.when((step == 10) | (step == 11))
    def _():
        @pl.loop(0, 4)
        def _(k):
            i = (step - 10) * 4 + k
            cot = od_buf.at[pl.ds(0, rows), :]
            unit(i, act_all[:, lane(i * B)].T, cot, wide * B, down_first)

    @pl.when(step == 11)
    def _():
        for copy in load_head(0):
            copy.start()

    @pl.when(step == 12)
    def _():
        settle(wide * B)

        @pl.loop(0, STEPS)
        def _(i):
            store_hg(i).wait()

    def head_grads(h, start, stop):
        tile = 512
        count = rows // tile

        def tile_rows(i):
            return pl.ds(pl.multiple_of(i * tile, tile), tile)

        def put(i, part, values):
            cols = pl.ds(pl.multiple_of(h * 3 * HD + part * HD, HD), HD)
            hg_all[tile_rows(i), cols] = values.astype(LOW)

        def turned_back(i, values):
            front = turn(values[:, :128], table_ref[0, tile_rows(i), :], table_ref[1, tile_rows(i), :], True)
            return jnp.concatenate([front, values[:, 128:]], axis=1)

        @pl.loop(start, stop)
        def _(j):
            keys = act_all[tile_rows(j), HD : 2 * HD]
            values = act_all[tile_rows(j), 2 * HD : 3 * HD]
            dk_scr[...] = jnp.zeros_like(dk_scr)
            dv_scr[...] = jnp.zeros_like(dv_scr)

            @pl.loop(j, count)
            def _(i):
                q = act_all[tile_rows(i), 0:HD]
                g = grad_all[tile_rows(i), pl.ds(pl.multiple_of(h * HD, HD), HD)]
                info = stats[tile_rows(i), :]
                log_total = jnp.where(h == 0, info[:, 0:1], info[:, 1:2])
                delta = jnp.where(h == 0, info[:, 64:65], info[:, 65:66])
                first = info[:, 2:3].astype(jnp.int32) - j * tile
                col = lax.broadcasted_iota(jnp.int32, (tile, tile), 1)
                row = lax.broadcasted_iota(jnp.int32, (tile, tile), 0) + (i - j) * tile
                ok = (col >= first) & (col <= row)
                p = jnp.where(ok, jnp.exp(dot_nt(q, keys) - log_total), 0.0)
                ds = (p * (dot_nt(g, values) - delta)).astype(LOW)
                dv_scr[...] += dot_tn(p.astype(LOW), g)
                dk_scr[...] += dot_tn(ds, q)
                dq_scr[tile_rows(i), :] += dot(ds, keys)

            put(j, 1, turned_back(j, dk_scr[...]))
            put(j, 2, dv_scr[...])

        @pl.when(stop == count)
        def _():
            @pl.loop(0, count)
            def _(i):
                put(i, 0, turned_back(i, dq_scr[tile_rows(i), :] * (1.0 / math.sqrt(HD))))

    @pl.when((step == 12) | (step == 14))
    def _():
        for copy in load_head((step - 12) // 2):
            copy.wait()
        dq_scr[...] = jnp.zeros_like(dq_scr)

    @pl.when((step >= 12) & (step < 16))
    def _():
        second = (step - 12) % 2
        head_grads((step - 12) // 2, second, 1 + 3 * second)

    @pl.when(step == 13)
    def _():
        for copy in load_head(1):
            copy.start()

    @pl.when(step == 16)
    def _():
        store_qg().start()
        for j in range(2):
            panel(ctx_hbm, j, j).start()
        total = jnp.zeros((1, qkv_cols), WIDE)
        for i in range(rows // 512):
            part_rows = slice(i * 512, (i + 1) * 512)
            total = total + jnp.sum(hg_all[part_rows, :qkv_cols].astype(WIDE), axis=0, keepdims=True)
        qkv_sums_ref[...] = jnp.broadcast_to(total, qkv_sums_ref.shape)
        for j in range(2):
            panel(ctx_hbm, j, j).wait()

        @pl.loop(0, 2)
        def _(j):
            cot = od_buf.at[pl.ds(0, rows), :]
            unit(j, up_buf[:, panel_cols(j)].T, cot, wide * B, out_first)

        settle(wide * B)
        panel(h1_hbm, 0, 0).start()

    @pl.when((step == 17) | (step == 18))
    def _():
        @pl.loop(0, 4)
        def _(k):
            i = (step - 17) * 4 + k
            panel(h1_hbm, i, i % 2).wait()

            @pl.when(i < 7)
            def _():
                panel(h1_hbm, i + 1, (i + 1) % 2).start()

            grads = hg_all.at[:, pl.ds(0, qkv_cols)]
            unit(i, up_buf[:, panel_cols(i % 2)].T, grads, qkv_cols, 0)

    @pl.when(step == FORWARD_GRID - 1)
    def _():
        settle(qkv_cols)
        store_qg().wait()

    def base(s):
        near = pl.ds(pl.multiple_of(s * 2 * SUB + line.near * SUB, SUB), SUB)
        return x_ref[near, :].astype(WIDE) + (vec_ref[4:5, :] + vec_ref[5:6, :])

    line.tick(step, FORWARD_LAG, base)

    @pl.when(step == FORWARD_GRID - 1)
    def _():
        line.drain()


def forward_line(h1, h2, cotangent, ctx, heads, stats, table, tokens, up_w, od_w, bias, vectors):
    rows, d = tokens.shape
    units = up_w.shape[1]
    head_cols = ctx.shape[1]
    qkv_cols = 3 * head_cols
    total = (d * qkv_cols + od_w.shape[0] * d + d * units) // (B * B)
    return pl.pallas_call(
        forward_kernel,
        grid=(FORWARD_GRID,),
        in_specs=[
            row_block(d),
            row_block(d),
            row_block(head_cols),
            base_block(d, FORWARD_LAG),
            row_block(128),
            resident(bias.shape),
            resident(vectors.shape),
            resident((2, rows, 128)),
        ]
        + [ANY] * 9,
        out_specs=[ANY] * 4
        + [pl.BlockSpec((8, units), lambda i: (0, 0)), pl.BlockSpec((8, qkv_cols), lambda i: (0, 0))],
        out_shape=[
            jax.ShapeDtypeStruct((rows, d), LOW),
            jax.ShapeDtypeStruct((rows, units), LOW),
            jax.ShapeDtypeStruct((rows, qkv_cols), LOW),
            jax.ShapeDtypeStruct((total, B, B), LOW),
            jax.ShapeDtypeStruct((8, units), WIDE),
            jax.ShapeDtypeStruct((8, qkv_cols), WIDE),
        ],
        scratch_shapes=[
            pltpu.VMEM(up_w.shape, LOW),
            pltpu.VMEM(od_w.shape, LOW),
            pltpu.VMEM((rows, units), LOW),
            pltpu.VMEM((rows, units), LOW),
        ]
        + line_scratch(d)
        + [
            pltpu.VMEM((rows, head_cols), LOW),
            pltpu.VMEM((rows, 128), WIDE),
            pltpu.VMEM((rows, HD), WIDE),
            pltpu.VMEM((512, HD), WIDE),
            pltpu.VMEM((512, HD), WIDE),
            pltpu.SemaphoreType.DMA((10,)),
            pltpu.SemaphoreType.DMA((2,)),
            pltpu.SemaphoreType.DMA((2,)),
            pltpu.SemaphoreType.DMA((STEPS,)),
            pltpu.SemaphoreType.DMA((6,)),
        ],
        compiler_params=pltpu.CompilerParams(
            vmem_limit_bytes=FORWARD_VMEM, collective_id=1, has_side_effects=True
        ),
        cost_estimate=pl.CostEstimate(
            flops=200_000_000_000, bytes_accessed=80 << 20, transcendentals=0
        ),
        name="forward_line",
    )(
        h2,
        cotangent,
        ctx,
        tokens,
        stats,
        bias,
        vectors,
        table,
        up_w,
        od_w,
        h1,
        h2,
        ctx,
        cotangent,
        *heads,
    )


BACKWARD_LAG = 1
BACKWARD_GRID = BACKWARD_LAG + TICKS + 2


class Spread:
    def __init__(self, own, along_mp, along_dp, sems):
        self.own = own
        self.stages = [
            ("dp", along_dp, sems.at[0], sems.at[1]),
            ("mp", along_mp, sems.at[2], sems.at[3]),
        ]

    def others(self, stage):
        axis, buf, send, recv = self.stages[stage]
        me = lax.axis_index(axis)
        return axis, buf, send, recv, me, [lax.rem(me + k, buf.shape[0]) for k in range(1, buf.shape[0])]

    def greet(self):
        barrier = pltpu.get_barrier_semaphore()
        count = 0
        for stage in range(2):
            axis, _, _, _, _, others = self.others(stage)
            for other in others:
                pl.semaphore_signal(barrier, inc=1, device_id={axis: other}, device_id_type=MESH)
            count += len(others)
        pl.semaphore_wait(barrier, count)

    def copies(self, stage):
        axis, buf, send, recv, me, others = self.others(stage)
        return [
            (
                pltpu.make_async_remote_copy(
                    src_ref=self.own,
                    dst_ref=buf.at[me],
                    send_sem=send.at[k],
                    recv_sem=recv.at[me],
                    device_id={axis: other},
                    device_id_type=MESH,
                ),
                pltpu.make_async_remote_copy(
                    src_ref=self.own,
                    dst_ref=buf.at[other],
                    send_sem=send.at[k],
                    recv_sem=recv.at[other],
                    device_id={axis: other},
                    device_id_type=MESH,
                ),
            )
            for k, other in enumerate(others)
        ]

    def start(self, stage):
        _, buf, _, _, me, _ = self.others(stage)
        buf[me] = self.own[...]
        for out, _ in self.copies(stage):
            out.start()

    def finish(self, stage):
        _, buf, _, _, _, _ = self.others(stage)
        for out, back in self.copies(stage):
            out.wait_send()
            back.wait_recv()
        total = buf[0]
        for i in range(1, buf.shape[0]):
            total = total + buf[i]
        return total


def backward_kernel(
    qg_ref,
    hg_ref,
    x_ref,
    g_ref,
    vec_ref,
    cot_sums,
    qkv_sums,
    hidden_sums,
    qkv_hbm,
    up_hbm,
    sums_ref,
    out_ref,
    qkv_ref,
    up_ref,
    load_sem,
    gc_scr,
    xhat_scr,
    own,
    along_mp,
    along_dp,
    spread_sems,
    part,
    got,
    across,
    sems,
):
    step = pl.program_id(0)
    line = Line(out_ref, part, got, across, sems)
    spread = Spread(own, along_mp, along_dp, spread_sems)
    d = x_ref.shape[1]
    width = 512

    def load(n):
        part_rows = pl.ds(n * width, width)
        return (
            pltpu.make_async_copy(
                qkv_hbm.at[part_rows, :], qkv_ref.at[part_rows, :], load_sem.at[0, n]
            ),
            pltpu.make_async_copy(
                up_hbm.at[part_rows, :], up_ref.at[part_rows, :], load_sem.at[1, n]
            ),
        )

    @pl.when(step == 0)
    def _():
        for n in range(d // width):
            for copy in load(n):
                copy.start()
        spread.greet()
        own[...] = jnp.zeros_like(own)
        own[4:5, :] = cot_sums[0:1, :]
        own[5:6, : qkv_sums.shape[1]] = qkv_sums[0:1, :]
        own[6:7, : hidden_sums.shape[1]] = hidden_sums[0:1, :]

    @pl.when(step < STEPS)
    def _():
        x = x_ref[...].astype(WIDE)
        center = x - jnp.mean(x, axis=1, keepdims=True)
        scale = lax.rsqrt(jnp.mean(center * center, axis=1, keepdims=True) + norm_eps)
        xhat_scr[...] = center * scale
        mean = jnp.zeros((STEP, 1), WIDE)
        slope = jnp.zeros((STEP, 1), WIDE)
        for n in range(d // width):
            cols = slice(n * width, (n + 1) * width)

            @pl.when(step == 0)
            def _():
                for copy in load(n):
                    copy.wait()

            e1 = dot_nt(qg_ref[...], qkv_ref[cols, :])
            e2 = dot_nt(hg_ref[...], up_ref[cols, :])
            xhat = xhat_scr[:, cols]
            gc = e1 * vec_ref[0:1, cols] + e2 * vec_ref[2:3, cols]
            gc_scr[:, cols] = gc
            mean = mean + jnp.sum(gc, axis=1, keepdims=True)
            slope = slope + jnp.sum(gc * xhat, axis=1, keepdims=True)
            own[0:1, cols] += jnp.sum(e1 * xhat, axis=0, keepdims=True)
            own[1:2, cols] += jnp.sum(e1, axis=0, keepdims=True)
            own[2:3, cols] += jnp.sum(e2 * xhat, axis=0, keepdims=True)
            own[3:4, cols] += jnp.sum(e2, axis=0, keepdims=True)
        mean = mean * (1.0 / d)
        slope = slope * (1.0 / d)
        for n in range(d // width):
            cols = slice(n * width, (n + 1) * width)
            value = (gc_scr[:, cols] - mean - xhat_scr[:, cols] * slope) * scale
            store_part(part, step, cols, value)

    @pl.when(step == STEPS)
    def _():
        spread.start(0)

    @pl.when(step == STEPS + 4)
    def _():
        own[...] = spread.finish(0)
        spread.start(1)

    def base(s):
        near = pl.ds(pl.multiple_of(s * 2 * SUB + line.near * SUB, SUB), SUB)
        return g_ref[near, :].astype(WIDE)

    line.tick(step, BACKWARD_LAG, base)

    @pl.when(step == BACKWARD_GRID - 1)
    def _():
        line.drain()
        total = spread.finish(1)
        row = lax.broadcasted_iota(jnp.int32, total.shape, 0)
        sums_ref[...] = jnp.where(row < 4, total, own[...])


def backward_line(qkv_grad, hidden_grad, tokens, cotangent, qkv_w, up_w, vectors, *sums):
    rows, d = tokens.shape
    small = (8, d)
    return pl.pallas_call(
        backward_kernel,
        grid=(BACKWARD_GRID,),
        in_specs=[
            row_block(qkv_grad.shape[1]),
            row_block(hidden_grad.shape[1]),
            row_block(d),
            base_block(d, BACKWARD_LAG),
            resident(vectors.shape),
        ]
        + [resident(part.shape) for part in sums]
        + [ANY] * 2,
        out_specs=[pl.BlockSpec(small, lambda i: (0, 0)), ANY],
        out_shape=[jax.ShapeDtypeStruct(small, WIDE), jax.ShapeDtypeStruct((rows, d), LOW)],
        scratch_shapes=[
            pltpu.VMEM(qkv_w.shape, LOW),
            pltpu.VMEM(up_w.shape, LOW),
            pltpu.SemaphoreType.DMA((2, d // 512)),
            pltpu.VMEM((STEP, d), WIDE),
            pltpu.VMEM((STEP, d), WIDE),
            pltpu.VMEM(small, WIDE),
            pltpu.VMEM((4,) + small, WIDE),
            pltpu.VMEM((8,) + small, WIDE),
            pltpu.SemaphoreType.DMA((4, 8)),
        ]
        + line_scratch(d),
        compiler_params=pltpu.CompilerParams(
            vmem_limit_bytes=VMEM_BYTES, collective_id=2, has_side_effects=True
        ),
        cost_estimate=pl.CostEstimate(
            flops=200_000_000_000, bytes_accessed=60 << 20, transcendentals=0
        ),
        name="backward_line",
    )(
        qkv_grad, hidden_grad, tokens, cotangent, vectors, *sums, qkv_w, up_w
    )


def halves(values):
    high = values.astype(LOW)
    return high, (values - high.astype(WIDE)).astype(LOW)


def shampoo_kernel(
    g_ref,
    w_ref,
    ls_ref,
    rs_ref,
    lr_ref,
    rr_ref,
    sums_ref,
    vec_ref,
    vec_stat_ref,
    unit_ref,
    unit_stat_ref,
    one_in,
    two_in,
    grad_ref,
    left_ref,
    right_ref,
    weight_ref,
    vec_grad_out,
    vec_stat_out,
    vec_out,
    unit_grad_out,
    unit_stat_out,
    unit_out,
    one_out,
    two_out,
    hold,
    sems,
):
    step = pl.program_id(0)
    pairs = ((one_in, one_out), (two_in, two_out))
    fetch = [pltpu.make_async_copy(a, hold.at[i], sems.at[0, i]) for i, (a, _) in enumerate(pairs)]
    store = [pltpu.make_async_copy(hold.at[i], b, sems.at[1, i]) for i, (_, b) in enumerate(pairs)]

    @pl.when(step == 0)
    def _():
        for copy in fetch:
            copy.start()
        vec_grad_out[0:5, :] = sums_ref[0:5, :]
        vec_grad_out[5:6, :] = sums_ref[4:5, :]
        vec_stat_out[...], vec_out[...] = vector_update(
            vec_ref[...], vec_stat_ref[...], vec_grad_out[...]
        )
        qkv_cols = unit_ref.shape[1] * 3 // 7
        unit_grad_out[:, :qkv_cols] = sums_ref[5:6, :qkv_cols]
        unit_grad_out[:, qkv_cols:] = sums_ref[6:7, : unit_ref.shape[1] - qkv_cols]
        unit_stat_out[...], unit_out[...] = vector_update(
            unit_ref[...], unit_stat_ref[...], unit_grad_out[...]
        )

    for i in range(2):

        @pl.when(step == pl.num_programs(0) * (i + 1) // 3)
        def _():
            fetch[i].wait()
            store[i].start()

    @pl.when(step == pl.num_programs(0) - 1)
    def _():
        for copy in store:
            copy.wait()

    for n in range(g_ref.shape[0]):
        g = g_ref[n]
        grad_ref[n] = g.astype(WIDE)
        left_ref[n] = 0.5 * ls_ref[n] + 0.5 * dot_nt(g, g)
        right_ref[n] = 0.5 * rs_ref[n] + 0.5 * dot_tn(g, g)
        l_high, l_low = halves(lr_ref[n])
        r_high, r_low = halves(rr_ref[n])
        d_high, d_low = halves(dot(l_high, g) + dot(l_low, g))
        direction = dot(d_high, r_high) + dot(d_low, r_high) + dot(d_high, r_low)
        weight = w_ref[n]
        size = 1.0 / (B * B)
        weight_size = jnp.sqrt(jnp.sum(weight * weight, keepdims=True) * size)
        step_size = jnp.sqrt(jnp.sum(direction * direction, keepdims=True) * size + 1e-06)
        weight_ref[n] = weight - direction * (step_share * weight_size / step_size)


def shampoo(grads, weights, left_stat, right_stat, left_root, right_root, small, one, two):
    count = grads.shape[0]
    group = 4
    spec = pl.BlockSpec((group, B, B), lambda i: (i, 0, 0))
    results = [small[1]] * 3 + [small[3]] * 3
    return pl.pallas_call(
        shampoo_kernel,
        grid=(count // group,),
        in_specs=[spec] * 6 + [resident(part.shape) for part in small] + [ANY] * 2,
        out_specs=[spec] * 4
        + [pl.BlockSpec(part.shape, lambda i: (0, 0)) for part in results]
        + [ANY] * 2,
        out_shape=[jax.ShapeDtypeStruct((count, B, B), WIDE)] * 4
        + [jax.ShapeDtypeStruct(part.shape, part.dtype) for part in results + [one, two]],
        scratch_shapes=[
            pltpu.VMEM((2,) + one.shape, one.dtype),
            pltpu.SemaphoreType.DMA((2, 2)),
        ],
        compiler_params=pltpu.CompilerParams(vmem_limit_bytes=VMEM_BYTES),
        name="shampoo",
    )(grads, weights, left_stat, right_stat, left_root, right_root, *small, one, two)


def per_device_line(
    tokens,
    cotangent,
    seq_len,
    seq_device,
    owner_map,
    weight_blocks,
    left_stat,
    right_stat,
    left_root,
    right_root,
    vectors,
    vector_stat,
    unit_bias,
    unit_stat,
):
    groups = lax.axis_size("mp")
    d = tokens.shape[1]
    qkv_cols = 3 * d // groups
    head_cols = d // groups
    unit_cols = FF // groups
    shapes = ((d, qkv_cols), (head_cols + unit_cols, d), (d, unit_cols))
    (
        qkv_w,
        od_w,
        up_w,
        normed_one,
        normed_two,
        table,
        q,
        k,
        v,
        ctx,
        stats,
        cot_sums,
    ) = gather_weights(
        weight_blocks[0],
        owner_map,
        seq_len,
        seq_device,
        tokens,
        cotangent,
        vectors,
        unit_bias,
        shapes,
    )
    block_out, hidden_grad, qkv_grad, weight_grads, hidden_sums, qkv_sums = forward_line(
        normed_one,
        normed_two,
        cotangent,
        ctx,
        (q, k, v),
        stats,
        table,
        tokens,
        up_w,
        od_w,
        unit_bias,
        vectors,
    )
    slots = unplace_blocks(weight_grads, owner_map)
    owned = lax.psum_scatter(slots, "dp", scatter_dimension=0, tiled=True)
    qkv_grad, hidden_grad, slots = lax.optimization_barrier((qkv_grad, hidden_grad, slots))
    sums, input_grad = backward_line(
        qkv_grad,
        hidden_grad,
        tokens,
        cotangent,
        qkv_w,
        up_w,
        vectors,
        cot_sums,
        qkv_sums,
        hidden_sums,
    )
    (
        block_grad,
        left_new,
        right_new,
        weight_new,
        vector_grad,
        vector_stat_new,
        vector_new,
        unit_grad,
        unit_stat_new,
        unit_new,
        block_out,
        input_grad,
    ) = shampoo(
        owned,
        weight_blocks[0],
        left_stat[0],
        right_stat[0],
        left_root[0],
        right_root[0],
        (sums, vectors, vector_stat, unit_bias, unit_stat),
        block_out,
        input_grad,
    )
    return (
        block_out,
        input_grad,
        block_grad[None],
        left_new[None],
        right_new[None],
        weight_new[None],
        vector_grad,
        vector_stat_new,
        vector_new,
        unit_grad,
        unit_stat_new,
        unit_new,
    )


def solution(mesh):
    placed = (
        P("dp", None),
        P("dp", None),
        P(),
        P(),
        P(),
        P("mp", "dp", None, None),
        P("mp", "dp", None, None),
        P("mp", "dp", None, None),
        P("mp", "dp", None, None),
        P("mp", "dp", None, None),
        P(),
        P(),
        P("mp", None),
        P("mp", None),
    )
    body = per_device
    if mesh.shape["dp"] == 8 and mesh.shape["mp"] == 4:
        body = per_device_line
    return jax.shard_map(
        body,
        mesh=mesh,
        in_specs=placed,
        out_specs=(
            P("dp", None),
            P("dp", None),
            P("mp", "dp", None, None),
            P("mp", "dp", None, None),
            P("mp", "dp", None, None),
            P("mp", "dp", None, None),
            P(),
            P(),
            P(),
            P("mp", None),
            P("mp", None),
            P("mp", None),
        ),
        check_vma=False,
    )
```

```python
import functools
import math

import jax
import jax.numpy as jnp
from jax import lax
from jax.experimental import pallas as pl
from jax.experimental.pallas import tpu as pltpu
from jax.sharding import PartitionSpec as P

D = 2048
HEADS = 8
HD = 256
ROT = 64
FF = 8192
B = 256


highest = lax.Precision.HIGHEST
norm_eps = 1e-05
step_share = 0.5
vector_rate = 0.15
masked_score = -1e30


def layer_norm(values, gain, shift):
    center = values - jnp.mean(values, axis=-1, keepdims=True)
    spread = jnp.mean(center * center, axis=-1, keepdims=True)
    return center * lax.rsqrt(spread + norm_eps) * gain + shift


def gelu_exact(values):
    return jax.nn.gelu(values, approximate=False)


def segment_layout(seq_len, seq_device, device, row_count):
    is_mine = seq_device == device
    lengths = jnp.where(is_mine, seq_len, 0)
    seq_ends = jnp.cumsum(lengths)
    row_index = jnp.arange(row_count, dtype=jnp.int32)
    passed = is_mine[None, :] & (seq_ends[None, :] <= row_index[:, None])
    segment = jnp.sum(passed.astype(jnp.int32), axis=1)
    seq_start = jnp.max(jnp.where(passed, seq_ends[None, :], 0), axis=1)
    return (segment, row_index - seq_start)


def rotary_tables(position):
    half_rot = ROT // 2
    frequency = 10000.0 ** (-2.0 * jnp.arange(half_rot, dtype=jnp.float32) / ROT)
    angles = position.astype(jnp.float32)[:, None] * frequency[None, :]
    cosine_table = jnp.concatenate([jnp.cos(angles), jnp.cos(angles)], axis=1)
    sine_table = jnp.concatenate([jnp.sin(angles), jnp.sin(angles)], axis=1)
    return (cosine_table, sine_table)


def rotate(values, cosine_table, sine_table):
    rot_dims = cosine_table.shape[1]
    half_rot = rot_dims // 2
    leading = values[..., :rot_dims]
    turned = jnp.concatenate([-leading[..., half_rot:], leading[..., :half_rot]], axis=-1)
    rotated = leading * cosine_table[:, None, :] + turned * sine_table[:, None, :]
    return jnp.concatenate([rotated, values[..., rot_dims:]], axis=-1)


def blocks_to_matrix(blocks, across):
    down_count = blocks.shape[0] // across
    return (
        blocks.reshape(down_count, across, B, B)
        .transpose(0, 2, 1, 3)
        .reshape(down_count * B, across * B)
    )


def matrix_to_blocks(matrix):
    down_count = matrix.shape[0] // B
    across = matrix.shape[1] // B
    return (
        matrix.reshape(down_count, B, across, B)
        .transpose(0, 2, 1, 3)
        .reshape(down_count * across, B, B)
    )


def split_blocks(blocks, qkv_cols, head_cols, unit_cols):
    qkv_end = D // B * (qkv_cols // B)
    out_end = qkv_end + head_cols // B * (D // B)
    up_end = out_end + D // B * (unit_cols // B)
    qkv_w = blocks_to_matrix(blocks[:qkv_end], qkv_cols // B)
    out_w = blocks_to_matrix(blocks[qkv_end:out_end], D // B)
    up_w = blocks_to_matrix(blocks[out_end:up_end], unit_cols // B)
    down_w = blocks_to_matrix(blocks[up_end:], D // B)
    return (qkv_w, out_w, up_w, down_w)


def apply_step(weight, direction):
    weight_size = jnp.sqrt(jnp.mean(weight * weight, axis=(-2, -1), keepdims=True))
    step_size = jnp.sqrt(jnp.mean(direction * direction, axis=(-2, -1), keepdims=True) + 1e-06)
    return weight - step_share * weight_size * direction / step_size


def vector_update(values, old_stat, gradient):
    new_stat = 0.5 * old_stat + 0.5 * gradient * gradient
    return (new_stat, values - vector_rate * gradient * lax.rsqrt(new_stat))


def block_mask(block_segment, block_row, segment, column):
    return (block_segment[:, None] == segment[None, :]) & (column[None, :] <= block_row[:, None])


def attention_forward(queries, keys_low, values_low, segment):
    row_count, head_count, head_dim = queries.shape
    block_rows = min(512, row_count)
    block_count = row_count // block_rows
    score_scale = 1.0 / math.sqrt(head_dim)
    column = jnp.arange(row_count, dtype=jnp.int32)

    def one_block(inputs):
        block_query, block_segment, block_row = inputs
        scores = (
            jnp.einsum("qhd,khd->hqk", block_query, keys_low, preferred_element_type=jnp.float32)
            * score_scale
        )
        scores = jnp.where(
            block_mask(block_segment, block_row, segment, column)[None], scores, masked_score
        )
        log_total = jax.nn.logsumexp(scores, axis=-1)
        weights = jnp.exp(scores - log_total[:, :, None]).astype(jnp.bfloat16)
        context = jnp.einsum(
            "hqk,khd->qhd", weights, values_low, preferred_element_type=jnp.float32
        )
        return (context, log_total)

    contexts, log_totals = lax.map(
        one_block,
        (
            queries.reshape(block_count, block_rows, head_count, head_dim),
            segment.reshape(block_count, block_rows),
            column.reshape(block_count, block_rows),
        ),
    )
    return (contexts.reshape(row_count, head_count, head_dim), log_totals)


def attention_backward(queries, keys_low, values_low, context_grad, log_totals, segment):
    row_count, head_count, head_dim = queries.shape
    block_rows = min(512, row_count)
    block_count = row_count // block_rows
    score_scale = 1.0 / math.sqrt(head_dim)
    column = jnp.arange(row_count, dtype=jnp.int32)

    def one_block(totals, inputs):
        key_grad, value_grad = totals
        block_query, block_grad, block_total, block_segment, block_row = inputs
        scores = (
            jnp.einsum("qhd,khd->hqk", block_query, keys_low, preferred_element_type=jnp.float32)
            * score_scale
        )
        scores = jnp.where(
            block_mask(block_segment, block_row, segment, column)[None], scores, masked_score
        )
        probs = jnp.exp(scores - block_total[:, :, None])
        weights = probs.astype(jnp.bfloat16)
        prob_grad = jnp.einsum(
            "qhd,khd->hqk", block_grad, values_low, preferred_element_type=jnp.float32
        )
        delta = jnp.sum(probs * prob_grad, axis=-1, keepdims=True)
        score_grad = (probs * (prob_grad - delta)).astype(jnp.bfloat16)
        query_grad = (
            jnp.einsum("hqk,khd->qhd", score_grad, keys_low, preferred_element_type=jnp.float32)
            * score_scale
        )
        key_grad = (
            key_grad
            + jnp.einsum(
                "hqk,qhd->khd", score_grad, block_query, preferred_element_type=jnp.float32
            )
            * score_scale
        )
        value_grad = value_grad + jnp.einsum(
            "hqk,qhd->khd", weights, block_grad, preferred_element_type=jnp.float32
        )
        return ((key_grad, value_grad), query_grad)

    zeros_start = jnp.zeros((row_count, head_count, head_dim), jnp.float32)
    (key_grad, value_grad), query_grad = lax.scan(
        one_block,
        (zeros_start, zeros_start),
        (
            queries.reshape(block_count, block_rows, head_count, head_dim),
            context_grad.reshape(block_count, block_rows, head_count, head_dim),
            log_totals,
            segment.reshape(block_count, block_rows),
            column.reshape(block_count, block_rows),
        ),
    )
    return (query_grad.reshape(row_count, head_count, head_dim), key_grad, value_grad)


def per_device(
    tokens,
    cotangent,
    seq_len,
    seq_device,
    owner_map,
    weight_blocks,
    left_stat,
    right_stat,
    left_root,
    right_root,
    vectors,
    vector_stat,
    unit_bias,
    unit_stat,
):
    groups = lax.axis_size("mp")
    device = lax.axis_index("dp")
    row_count = tokens.shape[0]
    heads_here = HEADS // groups
    qkv_cols = 3 * D // groups
    head_cols = D // groups
    unit_cols = FF // groups
    slot_count = weight_blocks.shape[1]
    sent_blocks = weight_blocks[0].astype(jnp.bfloat16)
    gathered = lax.all_gather(sent_blocks, "dp", axis=0, tiled=True)
    qkv_w, out_w, up_w, down_w = split_blocks(gathered[owner_map], qkv_cols, head_cols, unit_cols)
    segment, position = segment_layout(seq_len, seq_device, device, row_count)
    cosine_table, sine_table = rotary_tables(position)
    unit_shift = unit_bias[0]
    inputs = tokens.astype(jnp.float32)
    normed_one = layer_norm(inputs, vectors[0], vectors[1]).astype(jnp.bfloat16)
    normed_two = layer_norm(inputs, vectors[2], vectors[3]).astype(jnp.bfloat16)
    qkv_proj = (
        jnp.dot(normed_one, qkv_w, preferred_element_type=jnp.float32) + unit_shift[:qkv_cols]
    )
    qkv_proj = qkv_proj.reshape(row_count, heads_here, 3, HD)

    def turn_pair(values):
        return rotate(values.reshape(row_count, 2 * heads_here, HD), cosine_table, sine_table)

    turned, turn_back = jax.vjp(turn_pair, qkv_proj[:, :, :2])
    turned = turned.reshape(row_count, heads_here, 2, HD).astype(jnp.bfloat16)
    queries = turned[:, :, 0]
    keys_low = turned[:, :, 1]
    values_low = qkv_proj[:, :, 2].astype(jnp.bfloat16)
    context, log_totals = attention_forward(queries, keys_low, values_low, segment)
    context_low = context.reshape(row_count, head_cols).astype(jnp.bfloat16)
    hidden = jnp.dot(normed_two, up_w, preferred_element_type=jnp.float32) + unit_shift[qkv_cols:]
    active, gelu_back = jax.vjp(gelu_exact, hidden)
    active_low = active.astype(jnp.bfloat16)
    partial_out = jnp.dot(context_low, out_w, preferred_element_type=jnp.float32) + jnp.dot(
        active_low, down_w, preferred_element_type=jnp.float32
    )
    branch = lax.psum(partial_out.astype(jnp.bfloat16), "mp").astype(jnp.float32)
    block_out = (inputs + branch + (vectors[4] + vectors[5])).astype(jnp.bfloat16)
    grad_full = cotangent.astype(jnp.float32)
    act_grad = jnp.einsum("td,fd->tf", cotangent, down_w, preferred_element_type=jnp.float32)
    hidden_grad = gelu_back(act_grad)[0].astype(jnp.bfloat16)
    context_grad = jnp.einsum(
        "td,id->ti", cotangent, out_w, preferred_element_type=jnp.float32
    ).astype(jnp.bfloat16)
    query_grad, key_grad, value_grad = attention_backward(
        queries,
        keys_low,
        values_low,
        context_grad.reshape(row_count, heads_here, HD),
        log_totals,
        segment,
    )
    pair_grad = turn_back(
        jnp.stack([query_grad, key_grad], axis=2).reshape(row_count, 2 * heads_here, HD)
    )[0]
    qkv_grad = (
        jnp.concatenate([pair_grad, value_grad[:, :, None]], axis=2)
        .reshape(row_count, qkv_cols)
        .astype(jnp.bfloat16)
    )
    one_grad = jnp.einsum("te,de->td", qkv_grad, qkv_w, preferred_element_type=jnp.float32)
    two_grad = jnp.einsum("tf,df->td", hidden_grad, up_w, preferred_element_type=jnp.float32)
    norm_back_one = jax.vjp(layer_norm, inputs, vectors[0], vectors[1])[1]
    norm_back_two = jax.vjp(layer_norm, inputs, vectors[2], vectors[3])[1]
    input_one, gain_one, shift_one = norm_back_one(one_grad)
    input_two, gain_two, shift_two = norm_back_two(two_grad)
    input_part = input_one + input_two
    norm_part = jnp.stack([gain_one, shift_one, gain_two, shift_two])
    input_sum, norm_sum = lax.psum((input_part, norm_part), "mp")
    input_grad = (grad_full + input_sum).astype(jnp.bfloat16)
    qkv_w_grad = jnp.einsum("td,te->de", normed_one, qkv_grad, preferred_element_type=jnp.float32)
    out_w_grad = jnp.einsum("ti,td->id", context_low, cotangent, preferred_element_type=jnp.float32)
    up_w_grad = jnp.einsum("td,tf->df", normed_two, hidden_grad, preferred_element_type=jnp.float32)
    down_w_grad = jnp.einsum("tf,td->fd", active_low, cotangent, preferred_element_type=jnp.float32)
    canonical_grad = jnp.concatenate(
        [matrix_to_blocks(matrix) for matrix in (qkv_w_grad, out_w_grad, up_w_grad, down_w_grad)],
        axis=0,
    )
    slot_grads = canonical_grad[jnp.argsort(owner_map)]
    out_sum = jnp.sum(grad_full, axis=0)
    vector_part = jnp.concatenate([norm_sum, jnp.stack([out_sum, out_sum])], axis=0)
    unit_part = jnp.concatenate(
        [
            jnp.sum(qkv_grad.astype(jnp.float32), axis=0),
            jnp.sum(hidden_grad.astype(jnp.float32), axis=0),
        ]
    )
    summed, vector_grad, unit_grad = lax.psum((slot_grads, vector_part, unit_part), "dp")
    owned = lax.dynamic_slice_in_dim(summed, device * slot_count, slot_count, 0)
    left_new = 0.5 * left_stat[0] + 0.5 * jnp.einsum(
        "nij,nkj->nik", owned, owned, precision=highest
    )
    right_new = 0.5 * right_stat[0] + 0.5 * jnp.einsum(
        "nji,njk->nik", owned, owned, precision=highest
    )
    direction = jnp.einsum("nij,njk->nik", left_root[0], owned, precision=highest)
    direction = jnp.einsum("nij,njk->nik", direction, right_root[0], precision=highest)
    weight_new = apply_step(weight_blocks[0], direction)
    vector_stat_new, vector_new = vector_update(vectors, vector_stat, vector_grad)
    unit_stat_new, unit_new = vector_update(unit_shift, unit_stat[0], unit_grad)
    return (
        block_out,
        input_grad,
        owned[None],
        left_new[None],
        right_new[None],
        weight_new[None],
        vector_grad,
        vector_stat_new,
        vector_new,
        unit_grad[None],
        unit_stat_new[None],
        unit_new[None],
    )


LOW = jnp.bfloat16
WIDE = jnp.float32
MESH = pl.DeviceIdType.MESH
ANY = pl.BlockSpec(memory_space=pl.ANY)
STEP = 256
SUB = 32
PAIRS = 32
STEPS = 8
PER_STEP = PAIRS // STEPS
TICKS = PAIRS // 2
GOT = 8
ACROSS = 4
VMEM_BYTES = 60 * 1024 * 1024
FORWARD_VMEM = 63 * 1024 * 1024
GATHER_VMEM = 63 * 1024 * 1024


def dot(left, right):
    return lax.dot_general(left, right, (((1,), (0,)), ((), ())), preferred_element_type=WIDE)


def dot_nt(left, right):
    return lax.dot_general(left, right, (((1,), (1,)), ((), ())), preferred_element_type=WIDE)


def dot_tn(left, right):
    return lax.dot_general(left, right, (((0,), (0,)), ((), ())), preferred_element_type=WIDE)


def resident(shape):
    return pl.BlockSpec(shape, lambda *_: (0,) * len(shape), pipeline_mode=pl.Buffered(1))


def unplace_kernel(order_ref, blocks_ref, slots_ref, hold, sem_in, sem_out):
    total = blocks_ref.shape[0]
    chunk = total // sem_in.shape[0]

    def read(i):
        part = pl.ds(i * chunk, chunk)
        return pltpu.make_async_copy(blocks_ref.at[part], hold.at[part], sem_in.at[i])

    def write(b):
        return pltpu.make_async_copy(hold.at[b], slots_ref.at[order_ref[b]], sem_out.at[b])

    for i in range(total // chunk):
        read(i).start()
    for i in range(total // chunk):
        read(i).wait()
        for b in range(i * chunk, (i + 1) * chunk):
            write(b).start()
    for b in range(total):
        write(b).wait()


def unplace_blocks(blocks, order):
    total = order.shape[0]
    return pl.pallas_call(
        unplace_kernel,
        grid_spec=pltpu.PrefetchScalarGridSpec(
            num_scalar_prefetch=1,
            grid=(1,),
            in_specs=[ANY],
            out_specs=ANY,
            scratch_shapes=[
                pltpu.VMEM((total, B, B), LOW),
                pltpu.SemaphoreType.DMA((48,)),
                pltpu.SemaphoreType.DMA((total,)),
            ],
        ),
        out_shape=jax.ShapeDtypeStruct((total, B, B), LOW),
        compiler_params=pltpu.CompilerParams(vmem_limit_bytes=VMEM_BYTES),
        name="unplace_blocks",
    )(order, blocks)


def turn(values, cos, sin, back=False):
    lanes = lax.broadcasted_iota(jnp.int32, values.shape, 1)
    lower, upper = pltpu.roll(values, 96, 1), pltpu.roll(values, 32, 1)
    other = jnp.where(lanes < 32, -lower, upper)
    return values * cos - other * sin if back else values * cos + other * sin


def attention_rows(c, tile, first, q_ref, k_ref, v_ref, s_scr, ctx_ref, stats_ref):
    here = slice(c * tile, (c + 1) * tile)
    lanes = lax.broadcasted_iota(jnp.int32, (tile, 128), 1)
    stats = jnp.broadcast_to(first.astype(WIDE), (tile, 128))
    for h in range(q_ref.shape[1] // HD):
        cols = slice(h * HD, (h + 1) * HD)
        q = q_ref[here, cols]
        top = jnp.full((tile, 1), masked_score, WIDE)
        for j in range(c + 1):
            keys = slice(j * tile, (j + 1) * tile)
            s = dot_nt(q, k_ref[keys, cols])
            col = lax.broadcasted_iota(jnp.int32, (tile, tile), 1) + j * tile
            ok = col >= first
            if j == c:
                row = lax.broadcasted_iota(jnp.int32, (tile, tile), 0) + c * tile
                ok = ok & (col <= row)
            s = jnp.where(ok, s, masked_score)
            s_scr[:, keys] = s
            top = jnp.maximum(top, jnp.max(s, axis=1, keepdims=True))
        total = jnp.zeros((tile, 1), WIDE)
        ctx = jnp.zeros((tile, HD), WIDE)
        for j in range(c + 1):
            keys = slice(j * tile, (j + 1) * tile)
            e = jnp.exp(s_scr[:, keys] - top)
            total = total + jnp.sum(e, axis=1, keepdims=True)
            ctx = ctx + dot(e.astype(LOW), v_ref[keys, cols])
        ctx_ref[:, cols] = (ctx * (1.0 / total)).astype(LOW)
        stats = jnp.where(lanes == h, top + jnp.log(total), stats)
    stats_ref[...] = stats


PIECES = 4
ROUTES = ((0, 2), (0, 4), (0, 1), (2, 4), (4, 2), (2, 1), (4, 1), (6, 1))


def flip(index, mask):
    for bit in range(3):
        if mask >> bit & 1:
            unit = 2**bit
            index = index + (1 - 2 * lax.rem(lax.div(index, unit), 2)) * unit
    return index


def segments(qkv, od, up):
    wide, down = od.shape[1] // B, up.shape[1] // B
    out = od.shape[0] // B - down
    deep, cols = qkv.shape[0] // B, qkv.shape[1] // B
    starts = [deep * cols, out * wide, deep * down]
    return (
        (qkv, 0, deep, cols, 0),
        (od, 0, out, wide, starts[0]),
        (up, 0, deep, down, sum(starts[:2])),
        (od, out, down, wide, sum(starts)),
    )


def gather_kernel(
    order_ref,
    len_ref,
    place_ref,
    vec_ref,
    freq_ref,
    bias_ref,
    w_hbm,
    x_hbm,
    cot_hbm,
    qkv_hbm,
    od_hbm,
    up_hbm,
    h1_hbm,
    h2_hbm,
    table_hbm,
    q_hbm,
    k_hbm,
    v_hbm,
    ctx_hbm,
    stats_hbm,
    sum_ref,
    slots,
    wide,
    x_buf,
    c_buf,
    h_buf,
    table_all,
    stage,
    qkv_buf,
    q_all,
    k_all,
    v_all,
    s_scr,
    stats_buf,
    send_sem,
    recv_sem,
    load_sem,
    row_sem,
    norm_sem,
    stage_sem,
    out_sem,
    row_out_sem,
    q_sem,
):
    me = lax.axis_index("dp")
    each = w_hbm.shape[0]
    size = each // PIECES
    steps = x_hbm.shape[0] // STEP

    def piece(mask, q):
        return slots.at[pl.ds(flip(me, mask) * each + q * size, size)]

    def send(source, target, q):
        return pltpu.make_async_remote_copy(
            src_ref=piece(source, q),
            dst_ref=piece(source, q),
            send_sem=send_sem.at[ROUTES.index((source, target)), q],
            recv_sem=recv_sem.at[source ^ target, q],
            device_id={"dp": flip(me, target)},
            device_id_type=MESH,
        )

    def arrived(source, q):
        pltpu.make_async_remote_copy(
            src_ref=piece(source, q),
            dst_ref=piece(source, q),
            send_sem=send_sem.at[0, q],
            recv_sem=recv_sem.at[source, q],
            device_id={"dp": flip(me, 1)},
            device_id_type=MESH,
        ).wait_recv()

    def load(q):
        return pltpu.make_async_copy(
            w_hbm.at[pl.ds(q * size, size)], wide.at[q % 2], load_sem.at[q % 2]
        )

    def tile(i):
        return pl.ds(pl.multiple_of(i * STEP, STEP), STEP)

    def fetch(i, slot):
        return (
            pltpu.make_async_copy(x_hbm.at[tile(i), :], x_buf.at[slot], row_sem.at[0, slot]),
            pltpu.make_async_copy(cot_hbm.at[tile(i), :], c_buf.at[slot], row_sem.at[1, slot]),
        )

    def keep(i, slot):
        return (
            pltpu.make_async_copy(h_buf.at[slot], h1_hbm.at[tile(i), :], norm_sem.at[0, slot]),
            pltpu.make_async_copy(stage.at[slot], h2_hbm.at[tile(i), :], norm_sem.at[1, slot]),
        )

    def norm_step(i, slot, first):
        for copy in fetch(i, slot):
            copy.wait()

        @pl.when(jnp.logical_not(first))
        def _():
            for copy in keep(i, slot):
                copy.wait()

        x = x_buf[slot].astype(WIDE)
        center = x - jnp.mean(x, axis=1, keepdims=True)
        scale = lax.rsqrt(jnp.mean(center * center, axis=1, keepdims=True) + norm_eps)
        xhat = center * scale
        h_buf[slot] = (xhat * vec_ref[0:1, :] + vec_ref[1:2, :]).astype(LOW)
        stage[slot] = (xhat * vec_ref[2:3, :] + vec_ref[3:4, :]).astype(LOW)
        sum_ref[0:1, :] += jnp.sum(c_buf[slot].astype(WIDE), axis=0, keepdims=True)
        row = lax.broadcasted_iota(jnp.int32, (STEP, 128), 0) + i * STEP
        first = jnp.zeros((STEP, 128), jnp.int32)
        end = jnp.int32(0)
        for j in range(len_ref.shape[0]):
            mine = place_ref[j] == me
            end = end + jnp.where(mine, len_ref[j], 0)
            first = jnp.where(row >= jnp.where(mine, end, 1 << 30), end, first)
        angle = (row - first).astype(WIDE) * freq_ref[...]
        table_all[0, tile(i), :] = jnp.cos(angle)
        table_all[1, tile(i), :] = jnp.sin(angle)
        table_all[2, tile(i), :] = first.astype(WIDE)
        for copy in keep(i, slot):
            copy.start()

    for q in range(2):
        load(q).start()
    for slot in range(2):
        for copy in fetch(slot, slot):
            copy.start()
    barrier = pltpu.get_barrier_semaphore()
    for target in (1, 2, 4):
        pl.semaphore_signal(
            barrier, inc=1, device_id={"dp": flip(me, target)}, device_id_type=MESH
        )
    sum_ref[...] = jnp.zeros_like(sum_ref)
    for q in range(PIECES):
        load(q).wait()
        slots[pl.ds(me * each + q * size, size)] = wide[q % 2].astype(LOW)
        if q + 2 < PIECES:
            load(q + 2).start()
        if q == 0:
            pl.semaphore_wait(barrier, 3)
        for target in (2, 4, 1):
            send(0, target, q).start()

    for q in range(PIECES):

        @pl.loop(0, steps // (2 * PIECES))
        def _(k):
            i = (q * (steps // (2 * PIECES)) + k) * 2
            for slot in range(2):
                norm_step(i + slot, slot, i == 0)

                @pl.when(i + slot + 2 < steps)
                def _():
                    for copy in fetch(i + slot + 2, slot):
                        copy.start()

        arrived(2, q)
        if q % 2:
            send(2, 4, q).start()
        send(2, 1, q).start()
        arrived(4, q)
        if q % 2 == 0:
            send(4, 2, q).start()
        send(4, 1, q).start()
    for slot in range(2):
        for copy in keep(slot, slot):
            copy.wait()
    for q in range(PIECES):
        arrived(6, q)
        send(6, 1, q).start()
    for source in (1, 3, 5, 7):
        for q in range(PIECES):
            arrived(source, q)

    _, out, up, down = segments(qkv_hbm, od_hbm, up_hbm)
    qkv_across = qkv_hbm.shape[1] // B
    whole = [
        pltpu.make_async_copy(src, dst, out_sem.at[i])
        for i, (src, dst) in enumerate(
            (
                (qkv_buf, qkv_hbm),
                (table_all, table_hbm),
                (k_all, k_hbm),
                (v_all, v_hbm),
            )
        )
    ]

    def q_out(i):
        return pltpu.make_async_copy(
            q_all.at[tile(i), :], q_hbm.at[tile(i), :], q_sem.at[i]
        )

    def panel(part, i, slot):
        ref, skip = part[:2]
        return pltpu.make_async_copy(
            stage.at[slot], ref.at[lane((skip + i) * B), :], stage_sem.at[slot]
        )

    def put(part, i, slot):
        across, block = part[3:]
        for j in range(across):
            stage[slot, :, j * B : (j + 1) * B] = slots[order_ref[block + i * across + j]]
        panel(part, i, slot).start()

    def fetch_h(i, slot):
        return pltpu.make_async_copy(h1_hbm.at[tile(i), :], x_buf.at[slot], row_sem.at[0, slot])

    for slot in range(2):
        fetch_h(slot, slot).start()

    @pl.loop(0, qkv_hbm.shape[0] // B)
    def _(i):
        for j in range(qkv_across):
            qkv_buf[lane(i * B), j * B : (j + 1) * B] = slots[order_ref[i * qkv_across + j]]

    whole[0].start()
    whole[1].start()
    for slot in range(2):
        put(out, slot, slot)

    def project(i, slot):
        scale = 1.0 / math.sqrt(HD)
        for j in range(qkv_across):
            head, part = divmod(j, 3)
            cols = slice(head * HD, head * HD + HD)
            proj = dot(x_buf[slot], qkv_buf[:, j * B : (j + 1) * B])
            proj = proj + bias_ref[:, j * B : (j + 1) * B]
            if part == 2:
                v_all[tile(i), cols] = proj.astype(LOW)
                continue
            front = turn(proj[:, :128], table_all[0, tile(i), :], table_all[1, tile(i), :])
            turned = jnp.concatenate([front, proj[:, 128:]], axis=1).astype(LOW)
            if part == 0:
                q_all[tile(i), cols] = (turned.astype(WIDE) * scale).astype(LOW)
            else:
                k_all[tile(i), cols] = turned

    @pl.loop(0, steps // 2)
    def _(k):
        for slot in range(2):
            i = k * 2 + slot
            fetch_h(i, slot).wait()
            project(i, slot)
            q_out(i).start()

            @pl.when(i + 2 < steps)
            def _():
                fetch_h(i + 2, slot).start()

            panel(out, 0, 0).wait()
            put(up, i, 0)
            panel(out, 0, 1).wait()
            put(down, i, 1)

    for copy in whole[2:]:
        copy.start()
    rows = 512

    @pl.loop(0, steps)
    def _(i):
        q_out(i).wait()


    def row_out(c):
        part, slot = pl.ds(c * rows, rows), c % 2
        return (
            pltpu.make_async_copy(q_all.at[part, :], ctx_hbm.at[part, :], row_out_sem.at[0, slot]),
            pltpu.make_async_copy(
                stats_buf.at[slot], stats_hbm.at[part, :], row_out_sem.at[1, slot]
            ),
        )

    count = x_hbm.shape[0] // rows
    for c in range(count):
        if c >= 2:
            for copy in row_out(c - 2):
                copy.wait()
        first = table_all[2, c * rows : (c + 1) * rows, :][:, 0:1].astype(jnp.int32)
        place = q_all.at[pl.ds(c * rows, rows), :]
        attention_rows(c, rows, first, q_all, k_all, v_all, s_scr, place, stats_buf.at[c % 2])
        for copy in row_out(c):
            copy.start()
    for c in range(count - 2, count):
        for copy in row_out(c):
            copy.wait()
    for slot in range(2):
        panel(out, 0, slot).wait()
    for copy in whole:
        copy.wait()

    for source, target in ROUTES:
        for q in range(PIECES):
            if (source, target) == (2, 4) and q % 2 == 0:
                continue
            if (source, target) == (4, 2) and q % 2:
                continue
            send(source, target, q).wait_send()


def gather_weights(
    blocks, order, seq_len, seq_device, tokens, cotangent, vectors, bias, shapes
):
    rows, d = tokens.shape
    each = blocks.shape[0]
    half = 10000.0 ** (-2.0 * jnp.arange(ROT // 2, dtype=WIDE) / ROT)
    frequency = jnp.concatenate([half, half, jnp.zeros((128 - ROT,), WIDE)])[None]
    smem = pl.BlockSpec(memory_space=pltpu.SMEM)
    vmem = pl.BlockSpec(memory_space=pltpu.VMEM)
    return pl.pallas_call(
        gather_kernel,
        in_specs=[smem, smem, smem, vmem, vmem, vmem, ANY, ANY, ANY],
        out_specs=[ANY] * 11 + [vmem],
        out_shape=[jax.ShapeDtypeStruct(s, LOW) for s in shapes]
        + [jax.ShapeDtypeStruct((rows, d), LOW)] * 2
        + [jax.ShapeDtypeStruct((3, rows, 128), WIDE)]
        + [jax.ShapeDtypeStruct((rows, shapes[0][1] // 3), LOW)] * 4
        + [jax.ShapeDtypeStruct((rows, 128), WIDE)]
        + [jax.ShapeDtypeStruct((8, d), WIDE)],
        scratch_shapes=[
            pltpu.VMEM((order.shape[0], B, B), LOW),
            pltpu.VMEM((2, each // PIECES, B, B), WIDE),
            pltpu.VMEM((2, STEP, d), LOW),
            pltpu.VMEM((2, STEP, d), LOW),
            pltpu.VMEM((2, STEP, d), LOW),
            pltpu.VMEM((3, rows, 128), WIDE),
            pltpu.VMEM((2, B, d), LOW),
            pltpu.VMEM(shapes[0], LOW),
        ]
        + [pltpu.VMEM((rows, shapes[0][1] // 3), LOW)] * 3
        + [
            pltpu.VMEM((512, rows), WIDE),
            pltpu.VMEM((2, 512, 128), WIDE),
            pltpu.SemaphoreType.DMA((8, PIECES)),
            pltpu.SemaphoreType.DMA((8, PIECES)),
            pltpu.SemaphoreType.DMA((2,)),
            pltpu.SemaphoreType.DMA((2, 2)),
            pltpu.SemaphoreType.DMA((2, 2)),
            pltpu.SemaphoreType.DMA((2,)),
            pltpu.SemaphoreType.DMA((4,)),
            pltpu.SemaphoreType.DMA((2, 2)),
            pltpu.SemaphoreType.DMA((rows // STEP,)),
        ],
        compiler_params=pltpu.CompilerParams(
            vmem_limit_bytes=GATHER_VMEM, collective_id=3, has_side_effects=True
        ),
        cost_estimate=pl.CostEstimate(
            flops=100_000_000_000, bytes_accessed=80 << 20, transcendentals=0
        ),
        name="gather_weights",
    )(order, seq_len, seq_device, vectors, frequency, bias, blocks, tokens, cotangent)


class Line:
    def __init__(self, out, part, got, across, sems):
        self.out, self.part, self.got, self.across = out, part, got, across
        (
            self.up_send,
            self.up_recv,
            self.far_send,
            self.far_recv,
            self.over_send,
            self.over_recv,
            self.down_send,
            self.down_recv,
            self.relay_send,
            self.relay_recv,
            self.own,
        ) = [sems.at[i] for i in range(11)]
        z = lax.axis_index("mp")
        self.inner = (z == 1) | (z == 2)
        self.near = (z >= 2).astype(jnp.int32)
        self.far = 1 - self.near
        self.partner = jnp.where(self.inner, jnp.where(z == 1, 0, 3), jnp.where(z == 0, 1, 2))
        self.other = 3 - z

    def rows(self, pair, which):
        return self.out.at[pl.ds(pl.multiple_of(pair * (2 * SUB) + which * SUB, SUB), SUB), :]

    def greet(self):
        barrier = pltpu.get_barrier_semaphore()
        pl.semaphore_signal(barrier, inc=1, device_id={"mp": self.partner}, device_id_type=MESH)

        @pl.when(self.inner)
        def _():
            pl.semaphore_signal(barrier, inc=1, device_id={"mp": self.other}, device_id_type=MESH)
            pl.semaphore_wait(barrier, 2)

        @pl.when(jnp.logical_not(self.inner))
        def _():
            pl.semaphore_wait(barrier, 1)

    def copy(self, src, dst, send, recv, pair, target):
        return pltpu.make_async_remote_copy(
            src_ref=src,
            dst_ref=dst,
            send_sem=send.at[pair],
            recv_sem=recv.at[pair],
            device_id={"mp": target},
            device_id_type=MESH,
        )

    def up(self, pair):
        return self.copy(
            self.part.at[pair], self.got.at[pair % GOT], self.up_send, self.up_recv, pair, self.partner
        )

    def far_sum(self, pair):
        src, dst = self.part.at[pair, self.far], self.across.at[pair % ACROSS]
        return self.copy(src, dst, self.far_send, self.far_recv, pair, self.other)

    def over(self, pair, which):
        src = self.part.at[pair, self.near]
        return self.copy(src, self.rows(pair, which), self.over_send, self.over_recv, pair, self.other)

    def down(self, pair):
        src = self.part.at[pair, self.near]
        return self.copy(
            src, self.rows(pair, self.near), self.down_send, self.down_recv, pair, self.partner
        )

    def relay(self, pair):
        far = self.rows(pair, self.far)
        return self.copy(far, far, self.relay_send, self.relay_recv, pair, self.partner)

    def keep(self, pair):
        src = self.part.at[pair, self.near]
        return pltpu.make_async_copy(src, self.rows(pair, self.near), self.own.at[pair])

    def send_up(self, pair):
        @pl.when(pair >= GOT)
        def _():
            self.down(pair - GOT).wait_recv()

        self.up(pair).start()

    def add_far(self, pair):
        self.up(pair).wait_recv()
        far = self.part[pair, self.far].astype(WIDE) + self.got[pair % GOT, self.far].astype(WIDE)
        self.part[pair, self.far] = far.astype(LOW)
        self.far_sum(pair).start()

    def finish_near(self, pair, base):
        self.far_sum(pair).wait_recv()
        total = (
            self.part[pair, self.near].astype(WIDE)
            + self.got[pair % GOT, self.near].astype(WIDE)
            + self.across[pair % ACROSS].astype(WIDE)
        )
        self.part[pair, self.near] = (base + total).astype(LOW)
        self.over(pair, self.near).start()
        self.down(pair).start()
        self.keep(pair).start()

    def send_relay(self, pair):
        self.over(pair, self.far).wait_recv()
        self.relay(pair).start()

    def drain(self):
        @pl.when(self.inner)
        def _():
            @pl.loop(0, PAIRS)
            def _(pair):
                self.far_sum(pair).wait_send()
                self.over(pair, self.near).wait_send()
                self.down(pair).wait_send()
                self.relay(pair).wait_send()
                self.keep(pair).wait()

        @pl.when(jnp.logical_not(self.inner))
        def _():
            @pl.loop(0, PAIRS)
            def _(pair):
                self.up(pair).wait_send()
                self.relay(pair).wait_recv()

            @pl.loop(PAIRS - GOT, PAIRS)
            def _(pair):
                self.down(pair).wait_recv()

    def tick(self, step, lag, base):
        ahead = GOT // PER_STEP

        @pl.when(jnp.logical_not(self.inner) & (step < ahead))
        def _():
            for s in range(PER_STEP):
                self.send_up(step * PER_STEP + s)

        @pl.when(
            jnp.logical_not(self.inner) & (step >= ahead) & (step < ahead + (PAIRS - GOT) // 2)
        )
        def _():
            for s in range(2):
                self.send_up(GOT + (step - ahead) * 2 + s)

        @pl.when(self.inner & (step >= lag + 2) & (step < lag + 2 + TICKS))
        def _():
            for s in range(2):
                self.send_relay((step - lag - 2) * 2 + s)

        @pl.when(self.inner & (step >= lag + 1) & (step < lag + 1 + TICKS))
        def _():
            for s in range(2):
                self.finish_near((step - lag - 1) * 2 + s, base(s))

        @pl.when(self.inner & (step >= lag) & (step < lag + TICKS))
        def _():
            for s in range(2):
                self.add_far((step - lag) * 2 + s)


def line_scratch(d):
    return [
        pltpu.VMEM((PAIRS, 2, SUB, d), LOW),
        pltpu.VMEM((GOT, 2, SUB, d), LOW),
        pltpu.VMEM((ACROSS, SUB, d), LOW),
        pltpu.SemaphoreType.DMA((11, PAIRS)),
    ]


def now(step):
    return jnp.minimum(step, STEPS - 1)


def row_block(width):
    return pl.BlockSpec((STEP, width), lambda i: (now(i), 0))


def base_block(width, lag):
    return pl.BlockSpec((4 * SUB, width), lambda i: (jnp.clip(i - lag - 1, 0, TICKS - 1), 0))


def lane(start):
    return pl.ds(pl.multiple_of(start, B), B)


def gelu_parts(z):
    e = jnp.exp(z * z * -0.5)
    t = 1.0 / (1.0 + jnp.abs(z) * (0.3275911 * math.sqrt(0.5)))
    poly = t * (
        0.5 * 0.254829592
        + t
        * (
            0.5 * -0.284496736
            + t * (0.5 * 1.421413741 + t * (0.5 * -1.453152027 + t * (0.5 * 1.061405429)))
        )
    )
    below = poly * e
    cdf = jnp.where(z >= 0, 1.0 - below, below)
    return cdf, e * (1.0 / math.sqrt(2.0 * math.pi))


def store_part(part_ref, step, cols, value):
    value = value.astype(LOW).reshape(PER_STEP, 2, SUB, value.shape[1])
    part_ref[pl.ds(step * PER_STEP, PER_STEP), :, :, cols] = value


FORWARD_LAG = 1
FORWARD_GRID = FORWARD_LAG + TICKS + 2


def weight_unit(a_t, b_ref, cols, stage, slot):
    for n in range(cols // 512):
        part = slice(n * 512, (n + 1) * 512)
        stage[pl.ds(pl.multiple_of(slot * B, B), B), part] = dot(a_t, b_ref[:, part]).astype(LOW)


def forward_kernel(
    h_ref,
    g_ref,
    ctx_ref,
    x_ref,
    stats_ref,
    bias_ref,
    vec_ref,
    table_ref,
    up_hbm,
    od_hbm,
    h1_hbm,
    h2_hbm,
    ctx_hbm,
    cot_hbm,
    q_hbm,
    k_hbm,
    v_hbm,
    out_ref,
    hg_hbm,
    qg_hbm,
    wg_hbm,
    sums_ref,
    qkv_sums_ref,
    up_buf,
    od_buf,
    act_all,
    hg_all,
    part,
    got,
    across,
    sems,
    grad_all,
    stats,
    dq_scr,
    dk_scr,
    dv_scr,
    load_sem,
    panel_sem,
    stage_sem,
    hg_sem,
    head_sem,
):
    step = pl.program_id(0)
    line = Line(out_ref, part, got, across, sems)
    heads = ctx_ref.shape[1]
    rows, units = act_all.shape
    qkv_cols = qg_hbm.shape[1]
    width = 512
    tiles = units // width
    stage = od_buf.at[pl.ds(rows, 2 * B), :]

    def load_up(n):
        cols = pl.ds(n * width, width)
        return pltpu.make_async_copy(up_hbm.at[:, cols], up_buf.at[:, cols], load_sem.at[n])

    def load_down(n):
        part_rows = pl.ds(heads + n * width, width)
        return pltpu.make_async_copy(
            od_hbm.at[part_rows, :], od_buf.at[part_rows, :], load_sem.at[tiles + n]
        )

    def load_out():
        part_rows = pl.ds(0, heads)
        return pltpu.make_async_copy(
            od_hbm.at[part_rows, :], od_buf.at[part_rows, :], load_sem.at[2 * tiles]
        )

    def load_cot():
        return pltpu.make_async_copy(
            cot_hbm, od_buf.at[pl.ds(0, rows), :], load_sem.at[2 * tiles + 1]
        )

    def load_head(h):
        cols = pl.ds(pl.multiple_of(h * HD, HD), HD)
        return [
            pltpu.make_async_copy(
                src.at[:, cols], act_all.at[:, pl.ds(i * HD, HD)], head_sem.at[i]
            )
            for i, src in enumerate((q_hbm, k_hbm, v_hbm))
        ]

    def store_qg():
        return pltpu.make_async_copy(hg_all.at[:, pl.ds(0, qkv_cols)], qg_hbm, head_sem.at[5])

    def panel_cols(slot):
        return lane(qkv_cols + slot * B)

    def panel(src, i, slot):
        return pltpu.make_async_copy(
            src.at[:, lane(i * B)], up_buf.at[:, panel_cols(slot)], panel_sem.at[slot]
        )

    def store_hg(i):
        part_rows = pl.ds(pl.multiple_of(i * STEP, STEP), STEP)
        return pltpu.make_async_copy(
            hg_all.at[part_rows, :], hg_hbm.at[part_rows, :], hg_sem.at[i]
        )

    def stage_out(block, j, slot):
        return pltpu.make_async_copy(
            stage.at[lane(slot * B), pl.ds(j * B, B)], wg_hbm.at[block + j], stage_sem.at[slot]
        )

    def stage_wait(cols, slot):
        place = stage.at[lane(slot * B), pl.ds(0, cols)]
        pltpu.make_async_copy(place, place, stage_sem.at[slot]).wait()

    @pl.when(step == 0)
    def _():
        for n in range(tiles):
            load_up(n).start()
            load_down(n).start()
        load_out().start()
        line.greet()
        sums_ref[...] = jnp.zeros_like(sums_ref)

    @pl.when(step < STEPS)
    def _():
        here = pl.ds(pl.multiple_of(step * STEP, STEP), STEP)
        for n in range(tiles):
            cols = slice(n * width, (n + 1) * width)

            @pl.when(step == 0)
            def _():
                load_up(n).wait()
                load_down(n).wait()

            bias = bias_ref[:, qkv_cols + n * width : qkv_cols + (n + 1) * width]
            hidden = dot(h_ref[...], up_buf[:, cols]) + bias
            act_grad = dot_nt(g_ref[...], od_buf[heads + n * width : heads + (n + 1) * width, :])
            cdf, density = gelu_parts(hidden)
            act_all[here, cols] = (hidden * cdf).astype(LOW)
            grad = (act_grad * (cdf + hidden * density)).astype(LOW)
            hg_all[here, cols] = grad
            sums_ref[0:1, cols] += jnp.sum(grad.astype(WIDE), axis=0, keepdims=True)

        @pl.when(step == 0)
        def _():
            load_out().wait()

        store_hg(step).start()
        grad = dot_nt(g_ref[...], od_buf[:heads, :]).astype(LOW)
        grad_all[here, :] = grad
        lanes = lax.broadcasted_iota(jnp.int32, (STEP, 128), 1)
        info = stats_ref[...]
        for h in range(heads // HD):
            cols = slice(h * HD, (h + 1) * HD)
            both = ctx_ref[:, cols].astype(WIDE) * grad[:, cols].astype(WIDE)
            info = jnp.where(lanes == 64 + h, jnp.sum(both, axis=1, keepdims=True), info)
        stats[here, :] = info
        for n in range(od_buf.shape[1] // width):
            cols = slice(n * width, (n + 1) * width)
            value = dot(ctx_ref[...], od_buf[:heads, cols]) + dot(
                act_all[here, :], od_buf[heads:, cols]
            )
            store_part(part, step, cols, value)

    @pl.when(step == STEPS - 1)
    def _():
        panel(h2_hbm, 0, 0).start()
        load_cot().start()

    wide = od_buf.shape[1] // B
    out_first = rows // B * (qkv_cols // B)
    up_first = out_first + heads // B * wide
    down_first = up_first + rows // B * (units // B)

    def unit(index, a_t, b_ref, cols, first):
        slot = index % 2

        @pl.when(index >= 2)
        def _():
            stage_wait(cols, slot)

        weight_unit(a_t, b_ref, cols, stage, slot)
        for j in range(cols // B):
            stage_out(first + index * (cols // B), j, slot).start()

    def settle(cols):
        for slot in range(2):
            stage_wait(cols, slot)

    @pl.when((step == 8) | (step == 9))
    def _():
        @pl.loop(0, 4)
        def _(k):
            i = (step - 8) * 4 + k
            panel(h2_hbm, i, i % 2).wait()

            @pl.when(i < 7)
            def _():
                panel(h2_hbm, i + 1, (i + 1) % 2).start()

            unit(i, up_buf[:, panel_cols(i % 2)].T, hg_all, units, up_first)

    @pl.when(step == 10)
    def _():
        settle(units)
        load_cot().wait()

    @pl.when((step == 10) | (step == 11))
    def _():
        @pl.loop(0, 4)
        def _(k):
            i = (step - 10) * 4 + k
            cot = od_buf.at[pl.ds(0, rows), :]
            unit(i, act_all[:, lane(i * B)].T, cot, wide * B, down_first)

    @pl.when(step == 11)
    def _():
        for copy in load_head(0):
            copy.start()

    @pl.when(step == 12)
    def _():
        settle(wide * B)

        @pl.loop(0, STEPS)
        def _(i):
            store_hg(i).wait()

    def head_grads(h, second):
        tile = 512
        count = rows // tile

        def tile_rows(i):
            return pl.ds(pl.multiple_of(i * tile, tile), tile)

        def put(i, part, values):
            cols = pl.ds(pl.multiple_of(h * 3 * HD + part * HD, HD), HD)
            hg_all[tile_rows(i), cols] = values.astype(LOW)

        def turned_back(i, values):
            front = turn(values[:, :128], table_ref[0, tile_rows(i), :], table_ref[1, tile_rows(i), :], True)
            return jnp.concatenate([front, values[:, 128:]], axis=1)

        @pl.loop(0, 2)
        def _(turn_index):
            j = second + turn_index * (3 - 2 * second)
            keys = act_all[tile_rows(j), HD : 2 * HD]
            values = act_all[tile_rows(j), 2 * HD : 3 * HD]
            dk_scr[...] = jnp.zeros_like(dk_scr)
            dv_scr[...] = jnp.zeros_like(dv_scr)

            @pl.loop(j, count)
            def _(i):
                q = act_all[tile_rows(i), 0:HD]
                g = grad_all[tile_rows(i), pl.ds(pl.multiple_of(h * HD, HD), HD)]
                info = stats[tile_rows(i), :]
                log_total = jnp.where(h == 0, info[:, 0:1], info[:, 1:2])
                delta = jnp.where(h == 0, info[:, 64:65], info[:, 65:66])
                first = info[:, 2:3].astype(jnp.int32) - j * tile
                col = lax.broadcasted_iota(jnp.int32, (tile, tile), 1)
                row = lax.broadcasted_iota(jnp.int32, (tile, tile), 0) + (i - j) * tile
                ok = (col >= first) & (col <= row)
                p = jnp.where(ok, jnp.exp(dot_nt(q, keys) - log_total), 0.0)
                ds = (p * (dot_nt(g, values) - delta)).astype(LOW)
                dv_scr[...] += dot_tn(p.astype(LOW), g)
                dk_scr[...] += dot_tn(ds, q)
                dq_scr[tile_rows(i), :] += dot(ds, keys)

            put(j, 1, turned_back(j, dk_scr[...]))
            put(j, 2, dv_scr[...])

        @pl.when(second == 1)
        def _():
            @pl.loop(0, count)
            def _(i):
                put(i, 0, turned_back(i, dq_scr[tile_rows(i), :] * (1.0 / math.sqrt(HD))))

    @pl.when((step == 12) | (step == 14))
    def _():
        for copy in load_head((step - 12) // 2):
            copy.wait()
        dq_scr[...] = jnp.zeros_like(dq_scr)

    @pl.when((step >= 12) & (step < 16))
    def _():
        second = (step - 12) % 2
        head_grads((step - 12) // 2, second)

    @pl.when(step == 13)
    def _():
        for copy in load_head(1):
            copy.start()

    @pl.when(step == 16)
    def _():
        store_qg().start()
        for j in range(2):
            panel(ctx_hbm, j, j).start()
        total = jnp.zeros((1, qkv_cols), WIDE)
        for i in range(rows // 512):
            part_rows = slice(i * 512, (i + 1) * 512)
            total = total + jnp.sum(hg_all[part_rows, :qkv_cols].astype(WIDE), axis=0, keepdims=True)
        qkv_sums_ref[...] = jnp.broadcast_to(total, qkv_sums_ref.shape)
        for j in range(2):
            panel(ctx_hbm, j, j).wait()

        @pl.loop(0, 2)
        def _(j):
            cot = od_buf.at[pl.ds(0, rows), :]
            unit(j, up_buf[:, panel_cols(j)].T, cot, wide * B, out_first)

        settle(wide * B)
        panel(h1_hbm, 0, 0).start()

    @pl.when((step == 17) | (step == 18))
    def _():
        @pl.loop(0, 4)
        def _(k):
            i = (step - 17) * 4 + k
            panel(h1_hbm, i, i % 2).wait()

            @pl.when(i < 7)
            def _():
                panel(h1_hbm, i + 1, (i + 1) % 2).start()

            grads = hg_all.at[:, pl.ds(0, qkv_cols)]
            unit(i, up_buf[:, panel_cols(i % 2)].T, grads, qkv_cols, 0)

    @pl.when(step == FORWARD_GRID - 1)
    def _():
        settle(qkv_cols)
        store_qg().wait()

    def base(s):
        near = pl.ds(pl.multiple_of(s * 2 * SUB + line.near * SUB, SUB), SUB)
        return x_ref[near, :].astype(WIDE) + (vec_ref[4:5, :] + vec_ref[5:6, :])

    line.tick(step, FORWARD_LAG, base)

    @pl.when(step == FORWARD_GRID - 1)
    def _():
        line.drain()


def forward_line(h1, h2, cotangent, ctx, heads, stats, table, tokens, up_w, od_w, bias, vectors):
    rows, d = tokens.shape
    units = up_w.shape[1]
    head_cols = ctx.shape[1]
    qkv_cols = 3 * head_cols
    total = (d * qkv_cols + od_w.shape[0] * d + d * units) // (B * B)
    return pl.pallas_call(
        forward_kernel,
        grid=(FORWARD_GRID,),
        in_specs=[
            row_block(d),
            row_block(d),
            row_block(head_cols),
            base_block(d, FORWARD_LAG),
            row_block(128),
            resident(bias.shape),
            resident(vectors.shape),
            resident((2, rows, 128)),
        ]
        + [ANY] * 9,
        out_specs=[ANY] * 4
        + [pl.BlockSpec((8, units), lambda i: (0, 0)), pl.BlockSpec((8, qkv_cols), lambda i: (0, 0))],
        out_shape=[
            jax.ShapeDtypeStruct((rows, d), LOW),
            jax.ShapeDtypeStruct((rows, units), LOW),
            jax.ShapeDtypeStruct((rows, qkv_cols), LOW),
            jax.ShapeDtypeStruct((total, B, B), LOW),
            jax.ShapeDtypeStruct((8, units), WIDE),
            jax.ShapeDtypeStruct((8, qkv_cols), WIDE),
        ],
        scratch_shapes=[
            pltpu.VMEM(up_w.shape, LOW),
            pltpu.VMEM(od_w.shape, LOW),
            pltpu.VMEM((rows, units), LOW),
            pltpu.VMEM((rows, units), LOW),
        ]
        + line_scratch(d)
        + [
            pltpu.VMEM((rows, head_cols), LOW),
            pltpu.VMEM((rows, 128), WIDE),
            pltpu.VMEM((rows, HD), WIDE),
            pltpu.VMEM((512, HD), WIDE),
            pltpu.VMEM((512, HD), WIDE),
            pltpu.SemaphoreType.DMA((10,)),
            pltpu.SemaphoreType.DMA((2,)),
            pltpu.SemaphoreType.DMA((2,)),
            pltpu.SemaphoreType.DMA((STEPS,)),
            pltpu.SemaphoreType.DMA((6,)),
        ],
        compiler_params=pltpu.CompilerParams(
            vmem_limit_bytes=FORWARD_VMEM, collective_id=1, has_side_effects=True
        ),
        cost_estimate=pl.CostEstimate(
            flops=200_000_000_000, bytes_accessed=80 << 20, transcendentals=0
        ),
        name="forward_line",
    )(
        h2,
        cotangent,
        ctx,
        tokens,
        stats,
        bias,
        vectors,
        table,
        up_w,
        od_w,
        h1,
        h2,
        ctx,
        cotangent,
        *heads,
    )


BACKWARD_LAG = 1
BACKWARD_GRID = BACKWARD_LAG + TICKS + 2


class Spread:
    def __init__(self, own, along_mp, along_dp, sems):
        self.own = own
        self.stages = [
            ("dp", along_dp, sems.at[0], sems.at[1]),
            ("mp", along_mp, sems.at[2], sems.at[3]),
        ]

    def others(self, stage):
        axis, buf, send, recv = self.stages[stage]
        me = lax.axis_index(axis)
        return axis, buf, send, recv, me, [lax.rem(me + k, buf.shape[0]) for k in range(1, buf.shape[0])]

    def greet(self):
        barrier = pltpu.get_barrier_semaphore()
        count = 0
        for stage in range(2):
            axis, _, _, _, _, others = self.others(stage)
            for other in others:
                pl.semaphore_signal(barrier, inc=1, device_id={axis: other}, device_id_type=MESH)
            count += len(others)
        pl.semaphore_wait(barrier, count)

    def copies(self, stage):
        axis, buf, send, recv, me, others = self.others(stage)
        return [
            (
                pltpu.make_async_remote_copy(
                    src_ref=self.own,
                    dst_ref=buf.at[me],
                    send_sem=send.at[k],
                    recv_sem=recv.at[me],
                    device_id={axis: other},
                    device_id_type=MESH,
                ),
                pltpu.make_async_remote_copy(
                    src_ref=self.own,
                    dst_ref=buf.at[other],
                    send_sem=send.at[k],
                    recv_sem=recv.at[other],
                    device_id={axis: other},
                    device_id_type=MESH,
                ),
            )
            for k, other in enumerate(others)
        ]

    def start(self, stage):
        _, buf, _, _, me, _ = self.others(stage)
        buf[me] = self.own[...]
        for out, _ in self.copies(stage):
            out.start()

    def finish(self, stage):
        _, buf, _, _, _, _ = self.others(stage)
        for out, back in self.copies(stage):
            out.wait_send()
            back.wait_recv()
        total = buf[0]
        for i in range(1, buf.shape[0]):
            total = total + buf[i]
        return total


def backward_kernel(
    qg_ref,
    hg_ref,
    x_ref,
    g_ref,
    vec_ref,
    cot_sums,
    qkv_sums,
    hidden_sums,
    qkv_hbm,
    up_hbm,
    sums_ref,
    out_ref,
    qkv_ref,
    up_ref,
    load_sem,
    gc_scr,
    xhat_scr,
    own,
    along_mp,
    along_dp,
    spread_sems,
    part,
    got,
    across,
    sems,
):
    step = pl.program_id(0)
    line = Line(out_ref, part, got, across, sems)
    spread = Spread(own, along_mp, along_dp, spread_sems)
    d = x_ref.shape[1]
    width = 512

    def load(n):
        part_rows = pl.ds(n * width, width)
        return (
            pltpu.make_async_copy(
                qkv_hbm.at[part_rows, :], qkv_ref.at[part_rows, :], load_sem.at[0, n]
            ),
            pltpu.make_async_copy(
                up_hbm.at[part_rows, :], up_ref.at[part_rows, :], load_sem.at[1, n]
            ),
        )

    @pl.when(step == 0)
    def _():
        for n in range(d // width):
            for copy in load(n):
                copy.start()
        spread.greet()
        own[...] = jnp.zeros_like(own)
        own[4:5, :] = cot_sums[0:1, :]
        own[5:6, : qkv_sums.shape[1]] = qkv_sums[0:1, :]
        own[6:7, : hidden_sums.shape[1]] = hidden_sums[0:1, :]

    @pl.when(step < STEPS)
    def _():
        x = x_ref[...].astype(WIDE)
        center = x - jnp.mean(x, axis=1, keepdims=True)
        scale = lax.rsqrt(jnp.mean(center * center, axis=1, keepdims=True) + norm_eps)
        xhat_scr[...] = center * scale
        mean = jnp.zeros((STEP, 1), WIDE)
        slope = jnp.zeros((STEP, 1), WIDE)
        for n in range(d // width):
            cols = slice(n * width, (n + 1) * width)

            @pl.when(step == 0)
            def _():
                for copy in load(n):
                    copy.wait()

            e1 = dot_nt(qg_ref[...], qkv_ref[cols, :])
            e2 = dot_nt(hg_ref[...], up_ref[cols, :])
            xhat = xhat_scr[:, cols]
            gc = e1 * vec_ref[0:1, cols] + e2 * vec_ref[2:3, cols]
            gc_scr[:, cols] = gc
            mean = mean + jnp.sum(gc, axis=1, keepdims=True)
            slope = slope + jnp.sum(gc * xhat, axis=1, keepdims=True)
            own[0:1, cols] += jnp.sum(e1 * xhat, axis=0, keepdims=True)
            own[1:2, cols] += jnp.sum(e1, axis=0, keepdims=True)
            own[2:3, cols] += jnp.sum(e2 * xhat, axis=0, keepdims=True)
            own[3:4, cols] += jnp.sum(e2, axis=0, keepdims=True)
        mean = mean * (1.0 / d)
        slope = slope * (1.0 / d)
        for n in range(d // width):
            cols = slice(n * width, (n + 1) * width)
            value = (gc_scr[:, cols] - mean - xhat_scr[:, cols] * slope) * scale
            store_part(part, step, cols, value)

    @pl.when(step == STEPS)
    def _():
        spread.start(0)

    @pl.when(step == STEPS + 4)
    def _():
        own[...] = spread.finish(0)
        spread.start(1)

    def base(s):
        near = pl.ds(pl.multiple_of(s * 2 * SUB + line.near * SUB, SUB), SUB)
        return g_ref[near, :].astype(WIDE)

    line.tick(step, BACKWARD_LAG, base)

    @pl.when(step == BACKWARD_GRID - 1)
    def _():
        line.drain()
        total = spread.finish(1)
        row = lax.broadcasted_iota(jnp.int32, total.shape, 0)
        sums_ref[...] = jnp.where(row < 4, total, own[...])


def backward_line(qkv_grad, hidden_grad, tokens, cotangent, qkv_w, up_w, vectors, *sums):
    rows, d = tokens.shape
    small = (8, d)
    return pl.pallas_call(
        backward_kernel,
        grid=(BACKWARD_GRID,),
        in_specs=[
            row_block(qkv_grad.shape[1]),
            row_block(hidden_grad.shape[1]),
            row_block(d),
            base_block(d, BACKWARD_LAG),
            resident(vectors.shape),
        ]
        + [resident(part.shape) for part in sums]
        + [ANY] * 2,
        out_specs=[pl.BlockSpec(small, lambda i: (0, 0)), ANY],
        out_shape=[jax.ShapeDtypeStruct(small, WIDE), jax.ShapeDtypeStruct((rows, d), LOW)],
        scratch_shapes=[
            pltpu.VMEM(qkv_w.shape, LOW),
            pltpu.VMEM(up_w.shape, LOW),
            pltpu.SemaphoreType.DMA((2, d // 512)),
            pltpu.VMEM((STEP, d), WIDE),
            pltpu.VMEM((STEP, d), WIDE),
            pltpu.VMEM(small, WIDE),
            pltpu.VMEM((4,) + small, WIDE),
            pltpu.VMEM((8,) + small, WIDE),
            pltpu.SemaphoreType.DMA((4, 8)),
        ]
        + line_scratch(d),
        compiler_params=pltpu.CompilerParams(
            vmem_limit_bytes=VMEM_BYTES, collective_id=2, has_side_effects=True
        ),
        cost_estimate=pl.CostEstimate(
            flops=200_000_000_000, bytes_accessed=60 << 20, transcendentals=0
        ),
        name="backward_line",
    )(
        qkv_grad, hidden_grad, tokens, cotangent, vectors, *sums, qkv_w, up_w
    )


def halves(values):
    high = values.astype(LOW)
    return high, (values - high.astype(WIDE)).astype(LOW)


def shampoo_kernel(
    g_ref,
    w_ref,
    ls_ref,
    rs_ref,
    lr_ref,
    rr_ref,
    sums_ref,
    vec_ref,
    vec_stat_ref,
    unit_ref,
    unit_stat_ref,
    one_in,
    two_in,
    grad_ref,
    left_ref,
    right_ref,
    weight_ref,
    vec_grad_out,
    vec_stat_out,
    vec_out,
    unit_grad_out,
    unit_stat_out,
    unit_out,
    one_out,
    two_out,
    hold,
    sems,
):
    step = pl.program_id(0)
    pairs = ((one_in, one_out), (two_in, two_out))
    fetch = [pltpu.make_async_copy(a, hold.at[i], sems.at[0, i]) for i, (a, _) in enumerate(pairs)]
    store = [pltpu.make_async_copy(hold.at[i], b, sems.at[1, i]) for i, (_, b) in enumerate(pairs)]

    @pl.when(step == 0)
    def _():
        for copy in fetch:
            copy.start()
        vec_grad_out[0:5, :] = sums_ref[0:5, :]
        vec_grad_out[5:6, :] = sums_ref[4:5, :]
        vec_stat_out[...], vec_out[...] = vector_update(
            vec_ref[...], vec_stat_ref[...], vec_grad_out[...]
        )
        qkv_cols = unit_ref.shape[1] * 3 // 7
        unit_grad_out[:, :qkv_cols] = sums_ref[5:6, :qkv_cols]
        unit_grad_out[:, qkv_cols:] = sums_ref[6:7, : unit_ref.shape[1] - qkv_cols]
        unit_stat_out[...], unit_out[...] = vector_update(
            unit_ref[...], unit_stat_ref[...], unit_grad_out[...]
        )

    for i in range(2):

        @pl.when(step == pl.num_programs(0) * (i + 1) // 3)
        def _():
            fetch[i].wait()
            store[i].start()

    @pl.when(step == pl.num_programs(0) - 1)
    def _():
        for copy in store:
            copy.wait()

    for n in range(g_ref.shape[0]):
        g = g_ref[n]
        grad_ref[n] = g.astype(WIDE)
        left_ref[n] = 0.5 * ls_ref[n] + 0.5 * dot_nt(g, g)
        right_ref[n] = 0.5 * rs_ref[n] + 0.5 * dot_tn(g, g)
        l_high, l_low = halves(lr_ref[n])
        r_high, r_low = halves(rr_ref[n])
        d_high, d_low = halves(dot(l_high, g) + dot(l_low, g))
        direction = dot(d_high, r_high) + dot(d_low, r_high) + dot(d_high, r_low)
        weight = w_ref[n]
        size = 1.0 / (B * B)
        weight_size = jnp.sqrt(jnp.sum(weight * weight, keepdims=True) * size)
        step_size = jnp.sqrt(jnp.sum(direction * direction, keepdims=True) * size + 1e-06)
        weight_ref[n] = weight - direction * (step_share * weight_size / step_size)


def shampoo(grads, weights, left_stat, right_stat, left_root, right_root, small, one, two):
    count = grads.shape[0]
    group = 4
    spec = pl.BlockSpec((group, B, B), lambda i: (i, 0, 0))
    results = [small[1]] * 3 + [small[3]] * 3
    return pl.pallas_call(
        shampoo_kernel,
        grid=(count // group,),
        in_specs=[spec] * 6 + [resident(part.shape) for part in small] + [ANY] * 2,
        out_specs=[spec] * 4
        + [pl.BlockSpec(part.shape, lambda i: (0, 0)) for part in results]
        + [ANY] * 2,
        out_shape=[jax.ShapeDtypeStruct((count, B, B), WIDE)] * 4
        + [jax.ShapeDtypeStruct(part.shape, part.dtype) for part in results + [one, two]],
        scratch_shapes=[
            pltpu.VMEM((2,) + one.shape, one.dtype),
            pltpu.SemaphoreType.DMA((2, 2)),
        ],
        compiler_params=pltpu.CompilerParams(vmem_limit_bytes=VMEM_BYTES),
        name="shampoo",
    )(grads, weights, left_stat, right_stat, left_root, right_root, *small, one, two)


def per_device_line(
    tokens,
    cotangent,
    seq_len,
    seq_device,
    owner_map,
    weight_blocks,
    left_stat,
    right_stat,
    left_root,
    right_root,
    vectors,
    vector_stat,
    unit_bias,
    unit_stat,
):
    groups = lax.axis_size("mp")
    d = tokens.shape[1]
    qkv_cols = 3 * d // groups
    head_cols = d // groups
    unit_cols = FF // groups
    shapes = ((d, qkv_cols), (head_cols + unit_cols, d), (d, unit_cols))
    (
        qkv_w,
        od_w,
        up_w,
        normed_one,
        normed_two,
        table,
        q,
        k,
        v,
        ctx,
        stats,
        cot_sums,
    ) = gather_weights(
        weight_blocks[0],
        owner_map,
        seq_len,
        seq_device,
        tokens,
        cotangent,
        vectors,
        unit_bias,
        shapes,
    )
    block_out, hidden_grad, qkv_grad, weight_grads, hidden_sums, qkv_sums = forward_line(
        normed_one,
        normed_two,
        cotangent,
        ctx,
        (q, k, v),
        stats,
        table,
        tokens,
        up_w,
        od_w,
        unit_bias,
        vectors,
    )
    slots = unplace_blocks(weight_grads, owner_map)
    owned = lax.psum_scatter(slots, "dp", scatter_dimension=0, tiled=True)
    qkv_grad, hidden_grad, slots = lax.optimization_barrier((qkv_grad, hidden_grad, slots))
    sums, input_grad = backward_line(
        qkv_grad,
        hidden_grad,
        tokens,
        cotangent,
        qkv_w,
        up_w,
        vectors,
        cot_sums,
        qkv_sums,
        hidden_sums,
    )
    (
        block_grad,
        left_new,
        right_new,
        weight_new,
        vector_grad,
        vector_stat_new,
        vector_new,
        unit_grad,
        unit_stat_new,
        unit_new,
        block_out,
        input_grad,
    ) = shampoo(
        owned,
        weight_blocks[0],
        left_stat[0],
        right_stat[0],
        left_root[0],
        right_root[0],
        (sums, vectors, vector_stat, unit_bias, unit_stat),
        block_out,
        input_grad,
    )
    return (
        block_out,
        input_grad,
        block_grad[None],
        left_new[None],
        right_new[None],
        weight_new[None],
        vector_grad,
        vector_stat_new,
        vector_new,
        unit_grad,
        unit_stat_new,
        unit_new,
    )


def solution(mesh):
    placed = (
        P("dp", None),
        P("dp", None),
        P(),
        P(),
        P(),
        P("mp", "dp", None, None),
        P("mp", "dp", None, None),
        P("mp", "dp", None, None),
        P("mp", "dp", None, None),
        P("mp", "dp", None, None),
        P(),
        P(),
        P("mp", None),
        P("mp", None),
    )
    body = per_device
    if mesh.shape["dp"] == 8 and mesh.shape["mp"] == 4:
        body = per_device_line
    return jax.shard_map(
        body,
        mesh=mesh,
        in_specs=placed,
        out_specs=(
            P("dp", None),
            P("dp", None),
            P("mp", "dp", None, None),
            P("mp", "dp", None, None),
            P("mp", "dp", None, None),
            P("mp", "dp", None, None),
            P(),
            P(),
            P(),
            P("mp", None),
            P("mp", None),
            P("mp", None),
        ),
        check_vma=False,
    )
```
